32 devices in a mesh: dp: 8 (over y, x, core), tensor: 4 (over z).
Axes of the slice: x: 2, y: 2, z: 4, core: 2. Of those that a mesh axis runs over, the one named last changes fastest.
Arguments:
- hidden_in: bfloat16 [2048, 2048], P('dp'), may hold values from -6 to 6
- out_grad: bfloat16 [2048, 2048], P('dp'), may hold values from -6 to 6
- parents: int32 [8], replicated, may hold values from -1 to 3, as said below
- routes: int32 [2048, 4], P('dp'), may hold values from 0 to 7, all different within a row; in each aligned block of 256 rows (0 to 255, 256 to 511, ...) at most 256 rows name the same one
- attn_gain: float32 [2048], replicated, may hold values from 0.5 to 1.5
- w_query: bfloat16 [2048, 2048], P(None, 'tensor'), may hold values from -0.1875 to 0.1875
- w_key: bfloat16 [2048, 2048], P(None, 'tensor'), may hold values from -0.125 to 0.125
- w_value: bfloat16 [2048, 2048], P(None, 'tensor'), may hold values from -0.125 to 0.125
- b_query: float32 [16, 128], P('tensor'), may hold values from -0.625 to 0.625
- b_key: float32 [16, 128], P('tensor'), may hold values from -0.625 to 0.625
- b_value: float32 [16, 128], P('tensor'), may hold values from -0.125 to 0.125
- w_out: bfloat16 [2048, 2048], P(None, 'tensor'), may hold values from -2 to 2
- ffn_gain: float32 [2048], replicated, may hold values from 0.5 to 1.5
- w_router: bfloat16 [2048, 8], replicated, may hold values from -0.0625 to 0.0625
- shared_gate: bfloat16 [2048], replicated, may hold values from -0.125 to 0.125
- shared_w_gate: bfloat16 [2048, 5632], P(None, 'tensor'), may hold values from -0.125 to 0.125
- shared_w_up: bfloat16 [2048, 5632], P(None, 'tensor'), may hold values from -0.125 to 0.125
- shared_w_down: bfloat16 [2048, 5632], P(None, 'tensor'), may hold values from -0.25 to 0.25
- expert_w_gate: bfloat16 [8, 2048, 1408], P('dp', None, 'tensor'), may hold values from -0.125 to 0.125
- expert_w_up: bfloat16 [8, 2048, 1408], P('dp', None, 'tensor'), may hold values from -0.125 to 0.125
- expert_w_down: bfloat16 [8, 2048, 1408], P('dp', None, 'tensor'), may hold values from -1 to 1
Outputs:
- hidden_out: bfloat16 [2048, 2048], P('dp')
- hidden_in_grad: bfloat16 [2048, 2048], P('dp')
- attn_gain_grad: float32 [2048], P('dp')
- w_query_grad: float32 [2048, 2048], P('dp', 'tensor')
- w_key_grad: float32 [2048, 2048], P('dp', 'tensor')
- w_value_grad: float32 [2048, 2048], P('dp', 'tensor')
- b_query_grad: float32 [16, 128], P('tensor', 'dp')
- b_key_grad: float32 [16, 128], P('tensor', 'dp')
- b_value_grad: float32 [16, 128], P('tensor', 'dp')
- w_out_grad: float32 [2048, 2048], P('dp', 'tensor')
- ffn_gain_grad: float32 [2048], P('dp')
- w_router_grad: float32 [2048, 8], P('dp')
- shared_gate_grad: float32 [2048], P('dp')
- shared_w_gate_grad: float32 [2048, 5632], P('dp', 'tensor')
- shared_w_up_grad: float32 [2048, 5632], P('dp', 'tensor')
- shared_w_down_grad: float32 [2048, 5632], P('dp', 'tensor')
- expert_w_gate_grad: float32 [8, 2048, 1408], P('dp', None, 'tensor')
- expert_w_up_grad: float32 [8, 2048, 1408], P('dp', None, 'tensor')
- expert_w_down_grad: float32 [8, 2048, 1408], P('dp', None, 'tensor')
The draws below stay inside these ranges and needn't reach their ends.
Inputs may be any that keep to these rules, and one draw needn't show every extreme that they name: `parents`: the segments form 1 trees. Each tree has a chain of 2 trunk segments whose first has parent -1, 2 branch segments whose parent is the tree's last trunk segment, and 2 leaf segments under each branch. The trunks come first, tree after tree, then the branches in the same order of trees, then the leaves in the reversed order of trees. `routes`: each row names 4 different experts. Among the rows of one index of dp no expert is named more than 256 times, and in every draw some expert is named exactly that often by the rows of some index.
All inputs are finite; a program needn't handle non-finite values.
Results may differ from the reference program's by a relative error of at most 0.019.
Values may be sent and summed in bfloat16 or wider, within the bound.
A program may use at most 384 MiB of HBM per device.

```python
import math
import jax
import jax.numpy as jnp
import numpy as np
from jax import lax

D = 2048
HEADS = 16
HEAD_DIM = 128
HQ = 2048
FFE = 1408
FFS = 5632
TOPK = 4
TOK_DEV = 256
SEG = 256
TRUNK = 2
BRANCHES = 2
LEAVES = 2
TOKENS = 2048
NSEG = 8
TREES = 1
EXPERTS = 8
CAPACITY = 1280
ROUTE_CAP = 256


def draw_parents(key, part):
    key = jax.random.fold_in(key, 7)
    leaf_span = BRANCHES * LEAVES
    seg_index = jnp.arange(NSEG, dtype=jnp.int32)
    trunk_end = TREES * TRUNK
    branch_end = trunk_end + TREES * BRANCHES
    tree_keys = jax.random.split(key, TREES)
    orders = jax.vmap(lambda one_key: jax.random.permutation(one_key, leaf_span))(tree_keys).astype(jnp.int32)
    trunk_parent = jnp.where(seg_index % TRUNK == 0, -1, seg_index - 1)
    branch_tree = jnp.clip((seg_index - trunk_end) // BRANCHES, 0, TREES - 1)
    branch_parent = branch_tree * TRUNK + TRUNK - 1
    leaf_index = jnp.clip(seg_index - branch_end, 0, TREES * leaf_span - 1)
    leaf_tree = TREES - 1 - leaf_index // leaf_span
    leaf_slot = leaf_index % leaf_span
    owner = orders[leaf_tree, leaf_slot] // LEAVES
    leaf_parent = trunk_end + leaf_tree * BRANCHES + owner
    parent_pick = jnp.where(seg_index < trunk_end, trunk_parent, jnp.where(seg_index < branch_end, branch_parent, leaf_parent))
    return parent_pick.astype(jnp.int32)


def levels(stream_key, shape, cuts, least, largest):
    factor_of = 1.0
    for position, parts in cuts:
        steps = jax.random.uniform(jax.random.fold_in(jax.random.fold_in(stream_key, 6), position), (parts,), jnp.float32, least / len(cuts), largest / len(cuts))
        factor_of = factor_of * jnp.repeat(jnp.exp(steps), shape[position] // parts).reshape((-1,) + (1,) * (len(shape) - 1 - position))
    return factor_of


def assign_block(rng, own, number, rows, count, top, most, lean):
    order = jax.random.permutation(rng, count)
    crowded, common = shares(count, rows * top, most, lean, True), shares(count, rows * top, most, lean, False)
    places = jnp.arange(count)

    def named(lengths, offset_by):
        used = int((lengths > 0).sum())
        fixed = max(1, used // 4)
        passed = fixed + (places - fixed + offset_by * (used - fixed)) % max(1, count - fixed)
        return jnp.zeros((count,), jnp.int32).at[order[jnp.where(places < fixed, places, passed)]].set(jnp.asarray(lengths, jnp.int32))

    lengths = jnp.where(number % 4 == 0, named(crowded, number // 4), named(common, number - number // 4 - 1))
    mixed = jax.random.permutation(jax.random.fold_in(own, 3), count)
    donor, taker = mixed[0:count // 2 * 2:2], mixed[1:count // 2 * 2:2]
    slack = jnp.minimum(lengths[donor] - 1, most - lengths[taker]) // 2
    slack = jnp.where((donor == order[0]) | (taker == order[0]) | (lengths[taker] == 0), 0, jnp.maximum(slack, 0))
    passed = jax.random.randint(jax.random.fold_in(own, 4), (count // 2,), 0, 1 << 20) % (slack + 1)
    lengths = lengths.at[donor].add(-passed).at[taker].add(passed)
    items = jnp.searchsorted(jnp.cumsum(lengths), jnp.arange(rows * top), side="right").astype(jnp.int32)
    grid = items.reshape(top, rows).T
    grid = grid[jax.random.permutation(jax.random.fold_in(own, 1), rows)]
    offset_by = jax.random.randint(jax.random.fold_in(own, 2), (rows, 1), 0, top)
    return jnp.take_along_axis(grid, (jnp.arange(top)[None, :] + offset_by) % top, axis=1)


def shares(count, total, limit, skew, full):
    loads = [(1 << 20) // math.isqrt(rank ** skew) + 1 for rank in range(1, count + 1)]
    largest = limit if full else min(limit, max(-(-total // count), total * loads[0] // sum(loads)))
    least = 1 if total - largest >= count - 1 else 0
    given, surplus = [largest] + [least] * (count - 1), total - largest - least * (count - 1)
    while surplus > 0:
        candidates = [i for i in range(1, count) if given[i] < largest] or [i for i in range(1, count) if given[i] < limit]
        pool, left = sum([loads[i] for i in candidates]), surplus
        for i in candidates:
            more = min(limit - given[i], max(1, left * loads[i] // pool), surplus)
            given[i] = given[i] + more
            surplus = surplus - more
    return np.array(given)


def normal_values(own_key, dims, deviation, bound, shards=(), held_as=jnp.bfloat16):
    result = jax.random.normal(own_key, dims, jnp.float32) * deviation
    if len(shards) > 0:
        result = levels(own_key, dims, shards, -0.22, 0.18) * result
    return jnp.clip(result, min=-bound, max=bound).astype(held_as)


def setup_inputs(seed: int = 0) -> dict:
    streams_of = jax.random.split(jax.random.key(seed), 22)
    hidden_in = normal_values(streams_of[0], (TOKENS, D), 1.0, 6.0, ((0, 8),))
    out_grad = normal_values(streams_of[1], (TOKENS, D), 1.0, 6.0, ((0, 8),))
    parents = draw_parents(jax.random.fold_in(streams_of[21], 71), 0)
    routes_keys = jax.random.split(jax.random.fold_in(streams_of[3], 1), TOKENS // TOK_DEV)
    routes_turns = jax.random.permutation(jax.random.fold_in(streams_of[3], 3), TOKENS // TOK_DEV)
    routes = jax.vmap(lambda own, number: assign_block(jax.random.fold_in(streams_of[3], 2), own, number, TOK_DEV, EXPERTS, TOPK, ROUTE_CAP, 2))(routes_keys, routes_turns).reshape((TOKENS, TOPK))
    attn_gain = jnp.clip(1.0 + 0.1 * jax.random.normal(streams_of[4], (D,), jnp.float32), 0.5, 1.5)
    w_query = normal_values(streams_of[5], (D, HQ), (1.5 / D ** 0.5), 0.1875, ((1, 4),))
    w_key = normal_values(streams_of[6], (D, HQ), D ** -0.5, 0.125, ((1, 4),))
    w_value = normal_values(streams_of[7], (D, HQ), D ** -0.5, 0.125, ((1, 4),))
    b_query = normal_values(streams_of[8], (HEADS, HEAD_DIM), 0.1, 0.625, ((0, 4),), jnp.float32)
    b_key = normal_values(streams_of[9], (HEADS, HEAD_DIM), 0.1, 0.625, ((0, 4),), jnp.float32)
    b_value = normal_values(streams_of[10], (HEADS, HEAD_DIM), 0.02, 0.125, ((0, 4),), jnp.float32)
    w_out = normal_values(streams_of[11], (D, HQ), (16 / HQ ** 0.5), 2.0, ((1, 4),))
    ffn_gain = jnp.clip(1.0 + 0.1 * jax.random.normal(streams_of[12], (D,), jnp.float32), 0.5, 1.5)
    w_router = normal_values(streams_of[13], (D, EXPERTS), (0.5 / D ** 0.5), 0.0625)
    shared_gate = normal_values(streams_of[14], (D,), D ** -0.5, 0.125)
    shared_w_gate = normal_values(streams_of[15], (D, FFS), D ** -0.5, 0.125, ((1, 4),))
    shared_w_up = normal_values(streams_of[16], (D, FFS), D ** -0.5, 0.125, ((1, 4),))
    shared_w_down = normal_values(streams_of[17], (D, FFS), (3.3 / FFS ** 0.5), 0.25, ((1, 4),))
    expert_w_gate = normal_values(streams_of[18], (EXPERTS, D, FFE), D ** -0.5, 0.125, ((0, 8), (2, 4)))
    expert_w_up = normal_values(streams_of[19], (EXPERTS, D, FFE), D ** -0.5, 0.125, ((0, 8), (2, 4)))
    expert_w_down = normal_values(streams_of[20], (EXPERTS, D, FFE), (EXPERTS / (1.2 * FFE ** 0.5)), 1.0, ((0, 8), (2, 4)))
    return {"hidden_in": hidden_in, "out_grad": out_grad, "parents": parents, "routes": routes, "attn_gain": attn_gain, "w_query": w_query, "w_key": w_key, "w_value": w_value, "b_query": b_query, "b_key": b_key, "b_value": b_value, "w_out": w_out, "ffn_gain": ffn_gain, "w_router": w_router, "shared_gate": shared_gate, "shared_w_gate": shared_w_gate, "shared_w_up": shared_w_up, "shared_w_down": shared_w_down, "expert_w_gate": expert_w_gate, "expert_w_up": expert_w_up, "expert_w_down": expert_w_down}


epsilon = 1e-06
rope_base = 1000000.0
highest = lax.Precision.HIGHEST

@jax.custom_vjp
def low(v):
    return lax.optimization_barrier(v.astype(jnp.bfloat16)).astype(jnp.float32)

@jax.custom_vjp
def low_back(v):
    return v

def low_keep(v):
    return (low(v), None)

def low_pass(kept, grad):
    return (grad,)

def back_keep(v):
    return (v, None)

def back_low(kept, grad):
    return (low(grad),)
low.defvjp(low_keep, low_pass)
low_back.defvjp(back_keep, back_low)

def matmul(left, right):
    return jnp.dot(left, right, precision=highest)

def ancestry(parents):
    seg_count = parents.shape[0]
    labels = jnp.arange(seg_count, dtype=jnp.int32)

    def climb(level, carry):
        current, reach = carry
        upward = jnp.where(current >= 0, parents[jnp.maximum(current, 0)], -1).astype(jnp.int32)
        reach = jnp.maximum(reach, (upward[:, None] == labels[None, :]).astype(jnp.float32))
        return (upward, reach)
    start = (labels, jnp.eye(seg_count, dtype=jnp.float32))
    return lax.fori_loop(0, seg_count, climb, start)[1]

def rope_tables(positions):
    freqs = rope_base ** (-jnp.arange(0, HEAD_DIM, 2, dtype=jnp.float32) / HEAD_DIM)
    angles = positions[:, None] * freqs[None, :]
    angles = jnp.concatenate([angles, angles], 1)
    return (jnp.cos(angles)[:, None, :], jnp.sin(angles)[:, None, :])

def rotate(values, cosine, sine):
    half = values.shape[-1] // 2
    turned = jnp.concatenate([-values[..., half:], values[..., :half]], -1)
    return values * cosine + turned * sine

def rms_norm(values, gain):
    return values * lax.rsqrt(lax.optimization_barrier(jnp.mean(values * values, -1, keepdims=True)) + epsilon) * gain

def reference(hidden_in, out_grad, parents, routes, attn_gain, w_query, w_key, w_value, b_query, b_key, b_value, w_out, ffn_gain, w_router, shared_gate, shared_w_gate, shared_w_up, shared_w_down, expert_w_gate, expert_w_up, expert_w_down):
    total_rows = hidden_in.shape[0]
    reach = ancestry(parents)
    token_ids = jnp.arange(total_rows, dtype=jnp.int32)
    segments = token_ids // SEG
    token_reach = reach[segments]
    positions = (lax.optimization_barrier(jnp.sum(token_reach, 1)) - 1.0) * SEG + (token_ids % SEG).astype(jnp.float32)
    cosine, sine = rope_tables(positions)
    score_scale = HEAD_DIM ** (-0.5)
    block_rows = math.gcd(512, total_rows)
    expert_ids = jnp.arange(EXPERTS, dtype=jnp.int32)
    pair_onehot = routes[:, :, None] == expert_ids[None, None, :]
    token_hits = lax.optimization_barrier(jnp.sum(pair_onehot.astype(jnp.int32), 1)).astype(jnp.int32)
    earlier = (jnp.cumsum(token_hits, 0).astype(jnp.int32) - token_hits).astype(jnp.int32)
    slot = lax.optimization_barrier(jnp.sum(jnp.where(pair_onehot, earlier[:, None, :], 0), 2)).astype(jnp.int32)
    keep = slot < CAPACITY
    table = jnp.full((EXPERTS, CAPACITY), total_rows, jnp.int32)
    fill_ids = jnp.where(keep, token_ids[:, None], total_rows).astype(jnp.int32)
    table = table.at[routes, slot].set(fill_ids, mode='drop')

    def forward(hidden_f, attn_gain_f, wq, wk, wv, bq, bk, bv, wo, ffn_gain_f, wr, wsg, swg, swu, swd, ewg, ewu, ewd):
        attn_normed = low(rms_norm(hidden_f, attn_gain_f))
        query = low(rotate(low_back(matmul(attn_normed, wq) + bq.reshape(-1)).reshape(total_rows, HEADS, HEAD_DIM), cosine, sine))
        key = low(rotate(low_back(matmul(attn_normed, wk) + bk.reshape(-1)).reshape(total_rows, HEADS, HEAD_DIM), cosine, sine))
        value = low(low_back(matmul(attn_normed, wv) + bv.reshape(-1))).reshape(total_rows, HEADS, HEAD_DIM)

        def attend_block(start):
            query_block = lax.dynamic_slice_in_dim(query, start, block_rows, 0)
            reach_block = lax.dynamic_slice_in_dim(token_reach, start, block_rows, 0)
            rows_block = start + jnp.arange(block_rows, dtype=jnp.int32)
            allowed = jnp.repeat(reach_block > 0.5, SEG, axis=1) & (token_ids[None, :] <= rows_block[:, None])
            scores = low_back(jnp.einsum('qhd,khd->hqk', query_block, key, precision=highest) * score_scale)
            weights = jax.nn.softmax(jnp.where(allowed[None], scores, -jnp.inf), -1)
            return jnp.einsum('hqk,khd->qhd', low(weights), value, precision=highest)
        starts = jnp.arange(0, total_rows, block_rows, dtype=jnp.int32)
        attended = lax.map(jax.checkpoint(attend_block), starts).reshape(total_rows, HEADS * HEAD_DIM)
        attended = low(low_back(attended))
        residual = hidden_f + low_back(matmul(attended, wo.T))
        ffn_normed = low(rms_norm(residual, ffn_gain_f))
        probs = jax.nn.softmax(low_back(matmul(ffn_normed, wr)), -1)
        shared_weight = jax.nn.sigmoid(low_back(matmul(ffn_normed, wsg)))
        shared_hidden = low(jax.nn.silu(low_back(matmul(ffn_normed, swg))) * low_back(matmul(ffn_normed, swu)))
        shared_out = low_back(matmul(shared_hidden, swd.T))
        padded_normed = jnp.concatenate([ffn_normed, jnp.zeros((1, D), ffn_normed.dtype)], 0)
        padded_probs = jnp.concatenate([probs, jnp.zeros((1, EXPERTS), probs.dtype)], 0)
        slot_gates = padded_probs[table, expert_ids[:, None]]

        def expert_step(items):
            rows_idx, gates, wgate, wup, wdown = items
            inputs = padded_normed[rows_idx]
            hidden = low(jax.nn.silu(low_back(matmul(inputs, wgate))) * low_back(matmul(inputs, wup)))
            outputs = low_back(matmul(hidden, wdown.T))
            return gates[:, None] * outputs
        gated = lax.map(jax.checkpoint(expert_step), (table, slot_gates, ewg, ewu, ewd))
        mixed = jnp.zeros((total_rows + 1, D), hidden_f.dtype).at[table].add(gated)
        return residual + mixed[:total_rows] + shared_weight[:, None] * shared_out
    layer_out, pullback = jax.vjp(forward, hidden_in.astype(jnp.float32), attn_gain, w_query.astype(jnp.float32), w_key.astype(jnp.float32), w_value.astype(jnp.float32), b_query, b_key, b_value, w_out.astype(jnp.float32), ffn_gain, w_router.astype(jnp.float32), shared_gate.astype(jnp.float32), shared_w_gate.astype(jnp.float32), shared_w_up.astype(jnp.float32), shared_w_down.astype(jnp.float32), expert_w_gate.astype(jnp.float32), expert_w_up.astype(jnp.float32), expert_w_down.astype(jnp.float32))
    grads = pullback(out_grad.astype(jnp.float32))
    return (layer_out.astype(jnp.bfloat16), grads[0].astype(jnp.bfloat16), grads[1], grads[2], grads[3], grads[4], grads[5], grads[6], grads[7], grads[8], grads[9], grads[10], grads[11], grads[12], grads[13], grads[14], grads[15], grads[16], grads[17])
```

```python
import jax
import jax.numpy as jnp
from jax import lax
from jax.sharding import PartitionSpec as P

HEAD_DIM = 128
SEG = 256


epsilon = 1e-06
rope_base = 1000000.0
highest = lax.Precision.HIGHEST


def product(left, right):
    return jnp.dot(left, right, preferred_element_type=jnp.float32)


def product_tn(left, right):
    return lax.dot_general(
        left, right, (((0,), (0,)), ((), ())), preferred_element_type=jnp.float32
    )


def product_nt(left, right):
    return lax.dot_general(
        left, right, (((1,), (1,)), ((), ())), preferred_element_type=jnp.float32
    )


def ancestry(parents):
    seg_count = parents.shape[0]
    labels = jnp.arange(seg_count, dtype=jnp.int32)

    def climb(level, carry):
        current, reach = carry
        upward = jnp.where(current >= 0, parents[jnp.maximum(current, 0)], -1)
        reach = jnp.maximum(reach, (upward[:, None] == labels[None, :]).astype(jnp.float32))
        return (upward, reach)

    start = (labels, jnp.eye(seg_count, dtype=jnp.float32))
    return lax.fori_loop(0, seg_count, climb, start)[1]


def rope_tables(positions):
    freqs = rope_base ** (-jnp.arange(0, HEAD_DIM, 2, dtype=jnp.float32) / HEAD_DIM)
    angles = positions[:, None] * freqs[None, :]
    angles = jnp.concatenate([angles, angles], 1)
    return (jnp.cos(angles)[:, None, :], jnp.sin(angles)[:, None, :])


def turn_heads(matrix, cosine, sine, sign_value):
    shaped = matrix.reshape(matrix.shape[0], matrix.shape[1] // HEAD_DIM, HEAD_DIM)
    half = HEAD_DIM // 2
    turned = jnp.concatenate([-shaped[..., half:], shaped[..., :half]], -1)
    return (shaped * cosine + sign_value * turned * sine).reshape(matrix.shape)


def norm_parts(values):
    scale_rows = lax.rsqrt(jnp.mean(values * values, 1, keepdims=True) + epsilon)
    return (scale_rows, values * scale_rows)


def norm_back(grad_rows, unit_rows, scale_rows, gain):
    unit_grad = grad_rows * gain
    return scale_rows * (unit_grad - unit_rows * jnp.mean(unit_grad * unit_rows, 1, keepdims=True))


LEVELS = 4


def gather_dp(rows):
    return lax.all_gather(rows, "dp", axis=0, tiled=True)


def gather_tensor(rows):
    return lax.all_gather(rows, "tensor", axis=0, tiled=True)


def gather_all(rows):
    return gather_dp(gather_tensor(rows))


def scatter_dp(rows):
    return lax.psum_scatter(rows, "dp", scatter_dimension=0, tiled=True)


def scatter_tensor(rows):
    return lax.psum_scatter(rows, "tensor", scatter_dimension=0, tiled=True)


def scatter_all(rows):
    return scatter_tensor(scatter_dp(rows))


def path_of(parents, segment):
    path = [segment]
    for _ in range(LEVELS - 1):
        last = path[-1]
        path.append(jnp.where(last >= 0, parents[jnp.maximum(last, 0)], -1))
    return jnp.stack(path)


def heads_of(matrix):
    return matrix.reshape(matrix.shape[0], -1, HEAD_DIM)


def attend_forward(query_rot, key_path, value_path, allowed, score_scale):
    scores = (
        jnp.einsum(
            "qhd,khd->hqk",
            heads_of(query_rot),
            heads_of(key_path),
            preferred_element_type=jnp.float32,
        )
        * score_scale
    )
    scores = jnp.where(allowed[None], scores, -jnp.inf)
    peak = jnp.max(scores, 2, keepdims=True)
    log_total = peak + jnp.log(jnp.sum(jnp.exp(scores - peak), 2, keepdims=True))
    weights = jnp.exp(scores - log_total).astype(jnp.bfloat16)
    attended = jnp.einsum(
        "hqk,khd->qhd", weights, heads_of(value_path), preferred_element_type=jnp.float32
    )
    return attended.reshape(query_rot.shape), log_total


def attend_backward(
    query_rot, key_path, value_path, allowed, log_total, attended_grad, score_scale
):
    query, key, value = heads_of(query_rot), heads_of(key_path), heads_of(value_path)
    grad = heads_of(attended_grad)
    scores = jnp.einsum("qhd,khd->hqk", query, key, preferred_element_type=jnp.float32)
    weights = jnp.exp(jnp.where(allowed[None], scores * score_scale, -jnp.inf) - log_total)
    weight_grad = jnp.einsum("qhd,khd->hqk", grad, value, preferred_element_type=jnp.float32)
    center = jnp.sum(weights * weight_grad, 2, keepdims=True)
    score_grad = (weights * (weight_grad - center)).astype(jnp.bfloat16)
    query_grad = (
        jnp.einsum("hqk,khd->qhd", score_grad, key, preferred_element_type=jnp.float32)
        * score_scale
    )
    key_grad = (
        jnp.einsum("hqk,qhd->khd", score_grad, query, preferred_element_type=jnp.float32)
        * score_scale
    )
    value_grad = jnp.einsum(
        "hqk,qhd->khd",
        weights.astype(jnp.bfloat16),
        grad,
        preferred_element_type=jnp.float32,
    )
    return (
        query_grad.reshape(query_rot.shape),
        key_grad.reshape(key_path.shape),
        value_grad.reshape(value_path.shape),
    )


def on_device(
    hidden_in,
    out_grad,
    parents,
    routes,
    attn_gain,
    w_query,
    w_key,
    w_value,
    b_query,
    b_key,
    b_value,
    w_out,
    ffn_gain,
    w_router,
    shared_gate,
    shared_w_gate,
    shared_w_up,
    shared_w_down,
    expert_w_gate,
    expert_w_up,
    expert_w_down,
):
    tok_rows, model_width = hidden_in.shape
    devices = lax.axis_size("dp")
    columns = lax.axis_size("tensor")
    place, column = lax.axis_index("dp"), lax.axis_index("tensor")
    all_rows = tok_rows * devices
    part_rows = tok_rows // columns
    local_width = w_query.shape[1]
    experts = w_router.shape[1]
    top_count = routes.shape[1]
    capacity = 5 * tok_rows * top_count // 4
    score_scale = HEAD_DIM ** (-0.5)
    bf16, f32 = jnp.bfloat16, jnp.float32

    expert_units = expert_w_gate.shape[2]
    shared_units = shared_w_gate.shape[1] // devices
    units = expert_units + shared_units
    units_pad = -(-(units + experts + 1) // 128) * 128

    def own_units(matrix):
        return lax.dynamic_slice_in_dim(matrix, place * shared_units, shared_units, 1)

    def pad_to(parts):
        joined = jnp.concatenate(parts, 1)
        return jnp.pad(joined, ((0, 0), (0, units_pad - joined.shape[1])))

    w_pre = jnp.concatenate(
        [
            pad_to([expert_w_gate[0], own_units(shared_w_gate), w_router, shared_gate[:, None]]),
            pad_to([expert_w_up[0], own_units(shared_w_up)]),
        ],
        1,
    )
    w_down = pad_to([expert_w_down[0], own_units(shared_w_down)])

    out_all = gather_dp(out_grad)

    routes_all = lax.all_gather(routes, "dp", axis=0, tiled=True)
    pair_onehot = routes_all[:, :, None] == jnp.arange(experts, dtype=jnp.int32)[None, None, :]
    hits = jnp.any(pair_onehot, 1)
    hit_blocks = hits.astype(bf16).reshape(devices, tok_rows, experts)
    below = (
        jnp.arange(tok_rows)[None, :] < jnp.arange(tok_rows)[:, None]
    ).astype(bf16)
    within = jnp.einsum("ij,bje->bie", below, hit_blocks, preferred_element_type=f32)
    block_sums = jnp.sum(hit_blocks.astype(f32), 1)
    before = jnp.cumsum(block_sums, 0) - block_sums
    slots = (within + before[:, None, :]).reshape(all_rows, experts)
    kept = (hits & (slots < capacity)).astype(f32)

    path = path_of(parents, place * tok_rows // SEG)
    reachable = path >= 0
    path_rows = jnp.maximum(path, 0)
    row_ids = jnp.arange(tok_rows, dtype=jnp.int32)
    depth = jnp.sum(reachable.astype(f32)) - 1.0
    cosine, sine = rope_tables(depth * SEG + row_ids.astype(f32))
    allowed = jnp.concatenate(
        [
            row_ids[:, None] >= row_ids[None, :],
            jnp.broadcast_to(
                jnp.repeat(reachable[1:], tok_rows)[None, :], (tok_rows, (LEVELS - 1) * tok_rows)
            ),
        ],
        1,
    )
    hidden_f = hidden_in.astype(f32)
    attn_scale, attn_unit = norm_parts(hidden_f)
    attn_normed = (attn_unit * attn_gain).astype(bf16)
    query_rot = turn_heads(
        product(attn_normed, w_query) + b_query.reshape(-1), cosine, sine, 1.0
    ).astype(bf16)
    key_rot = turn_heads(
        product(attn_normed, w_key) + b_key.reshape(-1), cosine, sine, 1.0
    ).astype(bf16)
    value_rows = (product(attn_normed, w_value) + b_value.reshape(-1)).astype(bf16)
    gathered = gather_dp(jnp.concatenate([key_rot, value_rows], 1))
    kv_blocks = gathered.reshape(devices, tok_rows, 2 * local_width)
    kv_path = jnp.take(kv_blocks, path_rows, axis=0).reshape(LEVELS * tok_rows, 2 * local_width)
    key_path, value_path = kv_path[:, :local_width], kv_path[:, local_width:]
    attended, log_total = attend_forward(query_rot, key_path, value_path, allowed, score_scale)
    attended_low = attended.astype(bf16)
    attn_part = scatter_tensor(product_nt(attended_low, w_out).astype(bf16))

    hidden_own = lax.dynamic_slice_in_dim(hidden_f, column * part_rows, part_rows, 0)
    out_own = lax.dynamic_slice_in_dim(out_grad, column * part_rows, part_rows, 0).astype(f32)
    residual = hidden_own + attn_part.astype(f32)
    ffn_scale, ffn_unit = norm_parts(residual)
    ffn_normed = (ffn_unit * ffn_gain).astype(bf16)
    normed_all = gather_all(ffn_normed)

    pre = product(normed_all, w_pre)
    pre_gate, pre_up = pre[:, :units_pad], pre[:, units_pad:]
    logits = pre[:, units : units + experts]
    probs = jax.nn.softmax(logits, 1)
    shared_weight = jax.nn.sigmoid(pre[:, units + experts])
    own_expert = jnp.arange(experts, dtype=jnp.int32)[None, :] == place
    gate_own = jnp.sum(jnp.where(own_expert, probs * kept, 0.0), 1)
    lane = jnp.arange(units_pad)[None, :]
    weight = jnp.where(
        lane < expert_units,
        gate_own[:, None],
        jnp.where(lane < units, shared_weight[:, None], 0.0),
    )
    down_back = product(out_all, w_down)
    sigmoid_gate = jax.nn.sigmoid(pre_gate)
    hidden = (pre_gate * sigmoid_gate * pre_up).astype(bf16).astype(f32)
    hidden_scaled = (hidden * weight).astype(bf16)
    hidden_grad = down_back * weight
    up_rows = (hidden_grad * pre_gate * sigmoid_gate).astype(bf16)
    gate_rows = (
        hidden_grad * pre_up * sigmoid_gate * (1.0 + pre_gate * (1.0 - sigmoid_gate))
    ).astype(bf16)
    both_rows = jnp.concatenate([gate_rows, up_rows], 1)
    dots = hidden * down_back
    gate_dot = jnp.sum(jnp.where(lane < expert_units, dots, 0.0), 1)
    shared_dot = jnp.sum(jnp.where((lane >= expert_units) & (lane < units), dots, 0.0), 1)
    dot_parts = jnp.concatenate(
        [jnp.where(own_expert, gate_dot[:, None] * kept, 0.0), shared_dot[:, None]], 1
    )
    ffn_part = product_nt(hidden_scaled, w_down).astype(bf16)
    normed_part = product_nt(both_rows, w_pre).astype(bf16)
    grad_pre = product_tn(normed_all, both_rows)
    grad_down = product_tn(out_all, hidden_scaled)

    dot_own = scatter_all(dot_parts)
    ffn_own = scatter_all(ffn_part).astype(f32)
    normed_own = scatter_all(normed_part).astype(f32)
    hidden_out = gather_tensor((residual + ffn_own).astype(bf16))

    first = (place * tok_rows) + column * part_rows
    own = lambda array: lax.dynamic_slice_in_dim(array, first, part_rows, 0)
    probs_own, shared_own = own(probs), own(shared_weight)
    prob_grad = dot_own[:, :experts]
    logit_grad = (
        probs_own * (prob_grad - jnp.sum(probs_own * prob_grad, 1, keepdims=True))
    ).astype(bf16)
    weight_logit_grad = (dot_own[:, experts] * shared_own * (1.0 - shared_own)).astype(bf16)
    side_grad = jnp.concatenate([logit_grad, weight_logit_grad[:, None]], 1)
    side_w = jnp.concatenate([w_router, shared_gate[:, None]], 1)
    normed_grad = normed_own + product_nt(side_grad, side_w)
    grad_side = product_tn(ffn_normed, side_grad)
    grad_ffn_gain = jnp.sum(normed_grad * ffn_unit, 0)
    residual_grad = out_own + norm_back(normed_grad, ffn_unit, ffn_scale, ffn_gain)
    residual_low = gather_tensor(residual_grad.astype(bf16))
    grad_out_proj = product_tn(residual_low, attended_low)
    attended_grad = product(residual_low, w_out).astype(bf16)

    query_grad, key_grad, value_grad = attend_backward(
        query_rot, key_path, value_path, allowed, log_total, attended_grad, score_scale
    )
    kv_grad = jnp.concatenate([key_grad, value_grad], 1).reshape(
        LEVELS, tok_rows, 2 * local_width
    )
    kv_all = jnp.zeros((devices, tok_rows, 2 * local_width), f32)
    for level in range(LEVELS):
        kv_all = kv_all.at[path_rows[level]].add(kv_grad[level])
    kv_own = scatter_dp(
        kv_all.reshape(all_rows, 2 * local_width).astype(bf16)
    ).astype(f32)
    query_pre_grad = turn_heads(query_grad, cosine, sine, -1.0).astype(bf16)
    key_pre_grad = turn_heads(kv_own[:, :local_width], cosine, sine, -1.0).astype(bf16)
    value_pre_grad = kv_own[:, local_width:].astype(bf16)
    qkv_pre_grad = jnp.concatenate([query_pre_grad, key_pre_grad, value_pre_grad], 1)
    grad_qkv = product_tn(attn_normed, qkv_pre_grad)
    bias_grads = jnp.sum(qkv_pre_grad.astype(f32), 0).reshape(3, -1, HEAD_DIM)
    attn_part_grad = (
        product_nt(query_pre_grad, w_query)
        + product_nt(key_pre_grad, w_key)
        + product_nt(value_pre_grad, w_value)
    )
    grad_attn_gain = jnp.sum(attn_part_grad * attn_unit, 0)
    attn_own_grad = scatter_tensor(attn_part_grad.astype(bf16)).astype(f32)
    own_rows = lambda array: lax.dynamic_slice_in_dim(
        array, column * part_rows, part_rows, 0
    )
    hidden_in_grad = gather_tensor(
        (
            residual_grad
            + norm_back(attn_own_grad, own_rows(attn_unit), own_rows(attn_scale), attn_gain)
        ).astype(bf16)
    )

    small = jnp.concatenate(
        [grad_side, grad_ffn_gain[:, None], grad_attn_gain[:, None]], 1
    )
    small = scatter_dp(lax.psum(small, "tensor"))
    bias_sums = lax.psum_scatter(bias_grads, "dp", scatter_dimension=2, tiled=True)
    grad_attn = scatter_dp(jnp.concatenate([grad_qkv, grad_out_proj], 1).astype(bf16)).astype(f32)
    shared_grads = jnp.stack(
        [
            grad_pre[:, expert_units:units],
            grad_pre[:, units_pad + expert_units : units_pad + units],
            grad_down[:, expert_units:units],
        ]
    ).astype(bf16)
    shared_grads = lax.all_to_all(
        shared_grads, "dp", split_axis=1, concat_axis=2, tiled=True
    ).astype(f32)
    return (
        hidden_out,
        hidden_in_grad,
        small[:, experts + 2],
        grad_attn[:, :local_width],
        grad_attn[:, local_width : 2 * local_width],
        grad_attn[:, 2 * local_width : 3 * local_width],
        bias_sums[0],
        bias_sums[1],
        bias_sums[2],
        grad_attn[:, 3 * local_width :],
        small[:, experts + 1],
        small[:, :experts],
        small[:, experts],
        shared_grads[0],
        shared_grads[1],
        shared_grads[2],
        grad_pre[None, :, :expert_units],
        grad_pre[None, :, units_pad : units_pad + expert_units],
        grad_down[None, :, :expert_units],
    )


def solution(mesh):
    return jax.shard_map(
        on_device,
        mesh=mesh,
        in_specs=(
            P("dp", None),
            P("dp", None),
            P(),
            P("dp", None),
            P(),
            P(None, "tensor"),
            P(None, "tensor"),
            P(None, "tensor"),
            P("tensor", None),
            P("tensor", None),
            P("tensor", None),
            P(None, "tensor"),
            P(),
            P(),
            P(),
            P(None, "tensor"),
            P(None, "tensor"),
            P(None, "tensor"),
            P("dp", None, "tensor"),
            P("dp", None, "tensor"),
            P("dp", None, "tensor"),
        ),
        out_specs=(
            P("dp", None),
            P("dp", None),
            P("dp"),
            P("dp", "tensor"),
            P("dp", "tensor"),
            P("dp", "tensor"),
            P("tensor", "dp"),
            P("tensor", "dp"),
            P("tensor", "dp"),
            P("dp", "tensor"),
            P("dp"),
            P("dp", None),
            P("dp"),
            P("dp", "tensor"),
            P("dp", "tensor"),
            P("dp", "tensor"),
            P("dp", None, "tensor"),
            P("dp", None, "tensor"),
            P("dp", None, "tensor"),
        ),
        check_vma=False,
    )
```

```python
import functools

import jax
import jax.numpy as jnp
from jax import lax
from jax.experimental import pallas as pl
from jax.experimental.pallas import tpu as pltpu
from jax.sharding import PartitionSpec as P

HEAD_DIM = 128
SEG = 256
MESH = pl.DeviceIdType.MESH


epsilon = 1e-06
rope_base = 1000000.0
highest = lax.Precision.HIGHEST


def product(left, right):
    return jnp.dot(left, right, preferred_element_type=jnp.float32)


def product_tn(left, right):
    return lax.dot_general(
        left, right, (((0,), (0,)), ((), ())), preferred_element_type=jnp.float32
    )


def product_nt(left, right):
    return lax.dot_general(
        left, right, (((1,), (1,)), ((), ())), preferred_element_type=jnp.float32
    )


def ancestry(parents):
    seg_count = parents.shape[0]
    labels = jnp.arange(seg_count, dtype=jnp.int32)

    def climb(level, carry):
        current, reach = carry
        upward = jnp.where(current >= 0, parents[jnp.maximum(current, 0)], -1)
        reach = jnp.maximum(reach, (upward[:, None] == labels[None, :]).astype(jnp.float32))
        return (upward, reach)

    start = (labels, jnp.eye(seg_count, dtype=jnp.float32))
    return lax.fori_loop(0, seg_count, climb, start)[1]


def rope_tables(positions):
    freqs = rope_base ** (-jnp.arange(0, HEAD_DIM, 2, dtype=jnp.float32) / HEAD_DIM)
    angles = positions[:, None] * freqs[None, :]
    angles = jnp.concatenate([angles, angles], 1)
    return (jnp.cos(angles)[:, None, :], jnp.sin(angles)[:, None, :])


def turn_heads(matrix, cosine, sine, sign_value):
    shaped = matrix.reshape(matrix.shape[0], matrix.shape[1] // HEAD_DIM, HEAD_DIM)
    half = HEAD_DIM // 2
    turned = jnp.concatenate([-shaped[..., half:], shaped[..., :half]], -1)
    return (shaped * cosine + sign_value * turned * sine).reshape(matrix.shape)


def norm_parts(values):
    scale_rows = lax.rsqrt(jnp.mean(values * values, 1, keepdims=True) + epsilon)
    return (scale_rows, values * scale_rows)


def norm_back(grad_rows, unit_rows, scale_rows, gain):
    unit_grad = grad_rows * gain
    return scale_rows * (unit_grad - unit_rows * jnp.mean(unit_grad * unit_rows, 1, keepdims=True))


LEVELS = 4


def gather_dp(rows):
    return lax.all_gather(rows, "dp", axis=0, tiled=True)


def gather_tensor(rows):
    return lax.all_gather(rows, "tensor", axis=0, tiled=True)


def gather_all(rows):
    return gather_dp(gather_tensor(rows))


def scatter_dp(rows):
    return lax.psum_scatter(rows, "dp", scatter_dimension=0, tiled=True)


def scatter_tensor(rows):
    return lax.psum_scatter(rows, "tensor", scatter_dimension=0, tiled=True)


def scatter_all(rows):
    return scatter_tensor(scatter_dp(rows))


def path_of(parents, segment):
    path = [segment]
    for _ in range(LEVELS - 1):
        last = path[-1]
        path.append(jnp.where(last >= 0, parents[jnp.maximum(last, 0)], -1))
    return jnp.stack(path)


def heads_of(matrix):
    return matrix.reshape(matrix.shape[0], -1, HEAD_DIM)


def attend_forward(query_rot, key_path, value_path, allowed, score_scale):
    scores = (
        jnp.einsum(
            "qhd,khd->hqk",
            heads_of(query_rot),
            heads_of(key_path),
            preferred_element_type=jnp.float32,
        )
        * score_scale
    )
    scores = jnp.where(allowed[None], scores, -jnp.inf)
    peak = jnp.max(scores, 2, keepdims=True)
    log_total = peak + jnp.log(jnp.sum(jnp.exp(scores - peak), 2, keepdims=True))
    weights = jnp.exp(scores - log_total).astype(jnp.bfloat16)
    attended = jnp.einsum(
        "hqk,khd->qhd", weights, heads_of(value_path), preferred_element_type=jnp.float32
    )
    return attended.reshape(query_rot.shape), log_total


def attend_backward(
    query_rot, key_path, value_path, allowed, log_total, attended_grad, score_scale
):
    query, key, value = heads_of(query_rot), heads_of(key_path), heads_of(value_path)
    grad = heads_of(attended_grad)
    scores = jnp.einsum("qhd,khd->hqk", query, key, preferred_element_type=jnp.float32)
    weights = jnp.exp(jnp.where(allowed[None], scores * score_scale, -jnp.inf) - log_total)
    weight_grad = jnp.einsum("qhd,khd->hqk", grad, value, preferred_element_type=jnp.float32)
    center = jnp.sum(weights * weight_grad, 2, keepdims=True)
    score_grad = (weights * (weight_grad - center)).astype(jnp.bfloat16)
    query_grad = (
        jnp.einsum("hqk,khd->qhd", score_grad, key, preferred_element_type=jnp.float32)
        * score_scale
    )
    key_grad = (
        jnp.einsum("hqk,qhd->khd", score_grad, query, preferred_element_type=jnp.float32)
        * score_scale
    )
    value_grad = jnp.einsum(
        "hqk,qhd->khd",
        weights.astype(jnp.bfloat16),
        grad,
        preferred_element_type=jnp.float32,
    )
    return (
        query_grad.reshape(query_rot.shape),
        key_grad.reshape(key_path.shape),
        value_grad.reshape(value_path.shape),
    )


def ffn_plain(attn_part, hidden_own, grad_own, ffn_gain, kept, out_all, w_pre, w_down, layout):
    shared_pad, expert_units, experts, units_pad = layout
    units = shared_pad + expert_units
    bf16, f32 = jnp.bfloat16, jnp.float32
    place, column = lax.axis_index("dp"), lax.axis_index("tensor")
    columns, part_rows = lax.axis_size("tensor"), hidden_own.shape[0]
    out_own = grad_own.astype(f32)
    residual = hidden_own.astype(f32) + scatter_tensor(attn_part).astype(f32)
    ffn_scale, ffn_unit = norm_parts(residual)
    ffn_normed = (ffn_unit * ffn_gain).astype(bf16)
    normed_all = gather_all(ffn_normed)

    pre = product(normed_all, w_pre)
    pre_gate, pre_up = pre[:, :units_pad], pre[:, units_pad:]
    logits = pre[:, units : units + experts]
    probs = jax.nn.softmax(logits, 1)
    shared_weight = jax.nn.sigmoid(pre[:, units + experts])
    own_expert = jnp.arange(experts, dtype=jnp.int32)[None, :] == place
    gate_own = jnp.sum(jnp.where(own_expert, probs * kept, 0.0), 1)
    lane = jnp.arange(units_pad)[None, :]
    weight = jnp.where(
        lane < shared_pad,
        shared_weight[:, None],
        jnp.where(lane < units, gate_own[:, None], 0.0),
    )
    down_back = product(out_all, w_down)
    sigmoid_gate = jax.nn.sigmoid(pre_gate)
    hidden = (pre_gate * sigmoid_gate * pre_up).astype(bf16).astype(f32)
    hidden_scaled = (hidden * weight).astype(bf16)
    hidden_grad = down_back * weight
    up_rows = (hidden_grad * pre_gate * sigmoid_gate).astype(bf16)
    gate_rows = (
        hidden_grad * pre_up * sigmoid_gate * (1.0 + pre_gate * (1.0 - sigmoid_gate))
    ).astype(bf16)
    both_rows = jnp.concatenate([gate_rows, up_rows], 1)
    dots = hidden * down_back
    gate_dot = jnp.sum(jnp.where((lane >= shared_pad) & (lane < units), dots, 0.0), 1)
    shared_dot = jnp.sum(jnp.where(lane < shared_pad, dots, 0.0), 1)
    dot_parts = jnp.concatenate(
        [jnp.where(own_expert, gate_dot[:, None] * kept, 0.0), shared_dot[:, None]], 1
    )
    ffn_part = product_nt(hidden_scaled, w_down).astype(bf16)
    normed_part = product_nt(both_rows, w_pre).astype(bf16)
    grad_pre = product_tn(normed_all, both_rows)
    grad_down = product_tn(out_all, hidden_scaled)

    dot_own = scatter_all(dot_parts)
    normed_own = scatter_all(normed_part).astype(f32)

    first = (place * columns + column) * part_rows
    own = lambda array: lax.dynamic_slice_in_dim(array, first, part_rows, 0)
    probs_own, shared_own = own(probs), own(shared_weight)
    prob_grad = dot_own[:, :experts]
    logit_grad = (
        probs_own * (prob_grad - jnp.sum(probs_own * prob_grad, 1, keepdims=True))
    ).astype(bf16)
    weight_logit_grad = (dot_own[:, experts] * shared_own * (1.0 - shared_own)).astype(bf16)
    side_grad = jnp.concatenate([logit_grad, weight_logit_grad[:, None]], 1)
    side_w = w_pre[:, units : units + experts + 1]
    normed_grad = normed_own + product_nt(side_grad, side_w)
    grad_side = product_tn(ffn_normed, side_grad)
    grad_ffn_gain = jnp.sum(normed_grad * ffn_unit, 0)
    residual_grad = out_own + norm_back(normed_grad, ffn_unit, ffn_scale, ffn_gain)
    expert = slice(shared_pad, units)
    expert_up = slice(units_pad + shared_pad, units_pad + units)
    grad_shared = jnp.stack(
        [
            grad_pre[:, : shared_pad],
            grad_pre[:, units_pad : units_pad + shared_pad],
            grad_down[:, : shared_pad],
        ]
    ).astype(bf16)
    return (
        residual,
        residual_grad,
        residual_grad.astype(bf16),
        ffn_part,
        grad_pre[:, expert],
        grad_pre[:, expert_up],
        grad_down[:, expert],
        grad_shared,
        grad_side,
        grad_ffn_gain,
    )


def flip(bit):
    return 1 - bit


def other(index, step):
    result, place = index, 1
    while place <= step:
        if step & place:
            result = result + place - 2 * place * ((index // place) % 2)
        place *= 2
    return result


def ffn_kernel(
    units,
    part_ref,
    hidden_ref,
    grad_ref,
    gain_ref,
    kept_ref,
    grad_all_ref,
    w_pre_ref,
    w_down_ref,
    residual_ref,
    res_grad_ref,
    res_low_ref,
    ffn_part_ref,
    e_gate_ref,
    e_up_ref,
    e_down_ref,
    shared_ref,
    side_ref,
    gain_grad_ref,
    rows_all,
    dy_all,
    w_pre,
    w_down,
    both_all,
    scaled_all,
    sums,
    got_core,
    got_x1,
    got_y1,
    got_y2,
    got_x2,
    got_z,
    attn_z,
    ffn_chunk,
    tile_gate,
    tile_up,
    tile_down,
    tile_shared,
    load_sems,
    store_sems,
    tile_sems,
    attn_sems,
    zs,
    links,
    cores,
    rs_core,
    rs_links,
    rs_z,
):
    shared_pad, expert_units, experts, unit_pad, half, wide = units
    bf16, f32 = jnp.bfloat16, jnp.float32
    place, column = lax.axis_index("dp"), lax.axis_index("tensor")
    core, east, north = place % 2, (place // 2) % 2, place // 4
    rows, width = hidden_ref.shape
    sibling = {"dp": other(place, 1)}
    x_side = {"dp": other(place, 2)}
    y_side = {"dp": other(place, 4)}
    levels = [{"tensor": other(column, k)} for k in range(4)]

    def level_of(k):
        low_i, high_i, low_k, high_k = column % 2, column // 2, k % 2, k // 2
        return (low_i + low_k - 2 * low_i * low_k) + 2 * (high_i + high_k - 2 * high_i * high_k)

    def remote(src, dst, sems, which, device):
        return pltpu.make_async_remote_copy(
            src_ref=src,
            dst_ref=dst,
            send_sem=sems.at[(0, *which)],
            recv_sem=sems.at[(1, *which)],
            device_id=device,
            device_id_type=MESH,
        )

    load_pre = pltpu.make_async_copy(w_pre_ref, w_pre, load_sems.at[0])
    load_down = pltpu.make_async_copy(w_down_ref, w_down, load_sems.at[1])
    load_pre.start()
    load_down.start()

    def load_grad(c, z):
        return pltpu.make_async_copy(
            grad_all_ref.at[:, :, c, z], dy_all.at[z, c], load_sems.at[2 + c * 4 + z]
        )

    for c in range(2):
        for z in range(4):
            load_grad(c, z).start()

    barrier = pltpu.get_barrier_semaphore()
    partners = [sibling, x_side, y_side] + levels[1:]
    for partner in partners:
        pl.semaphore_signal(barrier, inc=1, device_id=partner, device_id_type=MESH)
    pl.semaphore_wait(barrier, len(partners))

    attn_copies = []
    for k in (3, 2, 1):
        copy = remote(
            part_ref.at[other(column, k)], attn_z.at[k], attn_sems, (k,), levels[k]
        )
        copy.start()
        attn_copies.append(copy)
    own_part = pltpu.make_async_copy(part_ref.at[column], attn_z.at[0], load_sems.at[10])
    own_part.start()
    own_part.wait()
    for copy in attn_copies:
        copy.wait()
    attn = attn_z[0].astype(f32)
    for k in range(1, 4):
        attn = attn + attn_z[k].astype(f32)
    residual = hidden_ref[...].astype(f32) + attn
    residual_ref[...] = residual
    scale_rows = lax.rsqrt(jnp.mean(residual * residual, 1, keepdims=True) + epsilon)
    normed = (residual * scale_rows * gain_ref[...]).astype(bf16)
    rows_all[column, core, north, east] = normed

    own_slot = rows_all.at[column, core, north, east]

    def z_copy(k):
        return remote(own_slot, own_slot, zs, (k,), levels[k])

    def block(k, c, y, x, cols=slice(None)):
        return rows_all.at[level_of(k), c, y, x, :, cols]

    first_half, second_half = pl.ds(0, half), pl.ds(half, width - half)

    def direct_copies(k):
        own = block(k, core, north, east)
        return [
            remote(own, own, links, (0, k), x_side),
            remote(own, own, links, (1, k), y_side),
            remote(own, own, cores, (0, k), sibling),
        ]

    def forward_copies(k):
        from_x = block(k, core, north, flip(east), first_half)
        from_y = block(k, core, flip(north), east, second_half)
        all_x = block(k, core, north, flip(east))
        all_y = block(k, core, flip(north), east)
        return [
            remote(from_x, from_x, links, (2, k), y_side),
            remote(from_y, from_y, links, (3, k), x_side),
            remote(all_x, all_x, cores, (1, k), sibling),
            remote(all_y, all_y, cores, (2, k), sibling),
        ]

    def corner_copy(k):
        corner = block(k, core, flip(north), flip(east))
        return remote(corner, corner, cores, (3, k), sibling)

    def start_direct(k):
        for copy in direct_copies(k):
            copy.start()

    def start_forward(k):
        for copy in direct_copies(k)[:2]:
            copy.wait_recv()
        for copy in forward_copies(k):
            copy.start()

    def start_corner(k):
        for copy in forward_copies(k)[:2]:
            copy.wait_recv()
        corner_copy(k).start()

    def finish_gather(k):
        direct_copies(k)[2].wait_recv()
        for copy in forward_copies(k)[2:]:
            copy.wait_recv()
        corner_copy(k).wait_recv()

    def core_copy(k):
        return remote(sums.at[k, flip(core)], got_core.at[k], rs_core, (k,), sibling)

    left, right = pl.ds(0, half), pl.ds(half, wide - half)

    def first_copies(k):
        return [
            remote(
                sums.at[k, core, :, flip(east), :, left],
                got_x1.at[k],
                rs_links, (0, k),
                x_side,
            ),
            remote(
                sums.at[k, core, flip(north), :, :, right],
                got_y1.at[k],
                rs_links, (1, k),
                y_side,
            ),
        ]

    def second_copies(k):
        return [
            remote(
                sums.at[k, core, flip(north), east, :, left],
                got_y2.at[k],
                rs_links, (2, k),
                y_side,
            ),
            remote(
                sums.at[k, core, north, flip(east), :, right],
                got_x2.at[k],
                rs_links, (3, k),
                x_side,
            ),
        ]

    def level_copy(k, device):
        return remote(sums.at[k, core, north, east], got_z.at[k], rs_z, (k,), device)

    def add(ref, value):
        ref[...] = (ref[...].astype(f32) + value.astype(f32)).astype(bf16)

    def after_core(k):
        core_copy(k).wait_recv()
        for y in range(2):
            for x in range(2):
                add(sums.at[k, core, y, x], got_core[k, y, x])
        for copy in first_copies(k):
            copy.start()

    def after_first(k):
        x_copy, y_copy = first_copies(k)
        x_copy.wait_recv()
        for y in range(2):
            add(sums.at[k, core, y, east, :, left], got_x1[k, y])
        y_copy.wait_recv()
        for x in range(2):
            add(sums.at[k, core, north, x, :, right], got_y1[k, x])
        for copy in second_copies(k):
            copy.start()

    def after_second(k):
        y_copy, x_copy = second_copies(k)
        y_copy.wait_recv()
        add(sums.at[k, core, north, east, :, left], got_y2[k])
        x_copy.wait_recv()
        add(sums.at[k, core, north, east, :, right], got_x2[k])
        for level in range(1, 4):

            @pl.when(k == level)
            def _():
                level_copy(k, levels[level]).start()

    for k in (1, 2, 3):
        z_copy(k).start()
    start_direct(0)
    load_pre.wait()
    load_down.wait()
    for c in range(2):
        for z in range(4):
            load_grad(c, z).wait()
    start_forward(0)
    z_copy(1).wait_recv()
    start_direct(1)
    start_corner(0)

    last = unit_pad - 128
    lane = lax.broadcasted_iota(jnp.int32, (1, 128), 1)
    first_lane = shared_pad + expert_units - last
    in_router = (lane >= first_lane) & (lane < first_lane + experts)
    is_shared = lane == first_lane + experts

    def routing(logit_block):
        top = jnp.max(jnp.where(in_router, logit_block, -jnp.inf), 1, keepdims=True)
        powers = jnp.where(in_router, jnp.exp(jnp.where(in_router, logit_block - top, 0.0)), 0.0)
        probs = powers / jnp.sum(powers, 1, keepdims=True)
        shared_logit = jnp.sum(jnp.where(is_shared, logit_block, 0.0), 1, keepdims=True)
        return probs, jax.nn.sigmoid(shared_logit)

    def compute(k, c):
        z = level_of(k)
        row_block = rows_all[z, c].reshape(4 * rows, width)
        dy_block = dy_all[z, c].reshape(4 * rows, width)
        pre_gate = product(row_block, w_pre[:, :unit_pad])
        pre_up = product(row_block, w_pre[:, unit_pad:])
        down_back = product(dy_block, w_down[...])
        probs, shared_weight = routing(pre_gate[:, last:])
        kept = kept_ref[z, c]
        gate = (
            jnp.sum(jnp.where(lane == first_lane + place, probs, 0.0), 1, keepdims=True) * kept
        )
        dots = []
        for begin, end, weight in (
            (0, shared_pad, shared_weight),
            (shared_pad, unit_pad, gate),
        ):
            cols = slice(begin, end)
            a, b, back = pre_gate[:, cols], pre_up[:, cols], down_back[:, cols]
            sig = jax.nn.sigmoid(a)
            silu = a * sig
            hidden = (silu * b).astype(bf16).astype(f32)
            dots.append(jnp.sum(hidden * back, 1, keepdims=True))
            scaled_all[z, c, :, begin:end] = (hidden * weight).astype(bf16)
            grad = back * weight
            both_all[z, c, :, unit_pad + begin : unit_pad + end] = (grad * silu).astype(bf16)
            both_all[z, c, :, begin:end] = (
                grad * b * sig * (1.0 + a * (1.0 - sig))
            ).astype(bf16)
        dot_block = jnp.where(is_shared, dots[0], 0.0) + jnp.where(
            lane == first_lane + place, dots[1] * kept, 0.0
        )
        normed_grad = product_nt(both_all[z, c], w_pre[...]).astype(bf16)
        sums[k, c, :, :, :, 0:width] = normed_grad.reshape(2, 2, rows, width)
        sums[k, c, :, :, :, width:wide] = dot_block.astype(bf16).reshape(2, 2, rows, wide - width)

    def store_chunk(k, c):
        return pltpu.make_async_copy(
            ffn_chunk, ffn_part_ref.at[level_of(k), c], store_sems.at[c]
        )

    def chunk(k, carry):
        @pl.when(k < 3)
        def _():
            start_forward(k + 1)

        @pl.when(k < 2)
        def _():
            for level in (2, 3):

                @pl.when(k + 2 == level)
                def _():
                    z_copy(level).wait_recv()

            start_direct(k + 2)

        finish_gather(k)
        def rows_of(i, carry):
            compute(k, (i + 1 + core) % 2)

            @pl.when(i == 0)
            def _():
                core_copy(k).start()

            return carry

        lax.fori_loop(0, 2, rows_of, 0)

        @pl.when(k >= 1)
        def _():
            after_first(k - 1)
            store_chunk(k - 1, 1).wait()

        def outputs(c, carry):
            part = product_nt(scaled_all[level_of(k), c], w_down[...]).astype(bf16)

            @pl.when(c == 1)
            def _():
                store_chunk(k, 0).wait()

            ffn_chunk[...] = part.reshape(2, 2, rows, width)
            store_chunk(k, c).start()
            return carry

        lax.fori_loop(0, 2, outputs, 0)

        @pl.when(k < 3)
        def _():
            start_corner(k + 1)

        after_core(k)

        @pl.when(k >= 1)
        def _():
            after_second(k - 1)

        return carry

    lax.fori_loop(0, 4, chunk, 0)
    store_chunk(3, 1).wait()

    tile = tile_gate.shape[1]
    tiles = width // tile

    def tile_copies(i, slot):
        window = pl.ds(pl.multiple_of(i * tile, tile), tile)
        return [
            pltpu.make_async_copy(tile_gate.at[slot], e_gate_ref.at[window], tile_sems.at[slot, 0]),
            pltpu.make_async_copy(tile_up.at[slot], e_up_ref.at[window], tile_sems.at[slot, 1]),
            pltpu.make_async_copy(tile_down.at[slot], e_down_ref.at[window], tile_sems.at[slot, 2]),
            pltpu.make_async_copy(
                tile_shared.at[slot], shared_ref.at[:, window], tile_sems.at[slot, 3]
            ),
        ]

    tokens = rows * 32

    def weight_tile(i, carry):
        slot = i % 2

        @pl.when(i >= 2)
        def _():
            for copy in tile_copies(i - 2, slot):
                copy.wait()

        window = pl.ds(pl.multiple_of(i * tile, tile), tile)
        expert = slice(shared_pad, shared_pad + expert_units)
        lhs = rows_all[:, :, :, :, :, window].reshape(tokens, tile)
        grad = product_tn(lhs, both_all[...].reshape(tokens, 2 * unit_pad))
        tile_gate[slot] = grad[:, expert]
        tile_shared[slot, 0] = grad[:, :shared_pad].astype(bf16)
        tile_up[slot] = grad[:, unit_pad + shared_pad : unit_pad + shared_pad + expert_units]
        tile_shared[slot, 1] = grad[:, unit_pad : unit_pad + shared_pad].astype(bf16)
        lhs = dy_all[:, :, :, :, :, window].reshape(tokens, tile)
        grad = product_tn(lhs, scaled_all[...].reshape(tokens, unit_pad))
        tile_down[slot] = grad[:, expert]
        tile_shared[slot, 2] = grad[:, :shared_pad].astype(bf16)
        for copy in tile_copies(i, slot):
            copy.start()

        @pl.when(i == 1)
        def _():
            after_first(3)

        @pl.when(i == 3)
        def _():
            after_second(3)

        return carry

    lax.fori_loop(0, tiles, weight_tile, 0)
    for i in (tiles - 2, tiles - 1):
        for copy in tile_copies(i, i % 2):
            copy.wait()

    total = sums[0, core, north, east].astype(f32)
    for k in (1, 2, 3):
        level_copy(k, levels[k]).wait_recv()
        total = total + got_z[k].astype(f32)
    dots = total[:, width:]
    unit = residual_ref[...] * scale_rows
    own_normed = rows_all[column, core, north, east]
    side_w = w_pre[:, last:unit_pad]
    probs, shared_weight = routing(product(own_normed, side_w))
    router_dots = jnp.where(in_router, dots, 0.0)
    center = jnp.sum(probs * router_dots, 1, keepdims=True)
    side = jnp.where(in_router, probs * (router_dots - center), 0.0) + jnp.where(
        is_shared, dots * shared_weight * (1.0 - shared_weight), 0.0
    )
    side = side.astype(bf16)
    normed_grad = total[:, :width] + product_nt(side, side_w)
    side_ref[...] = product_tn(own_normed, side)
    gain_grad_ref[...] = jnp.sum(normed_grad * unit, 0, keepdims=True)
    grad_f = grad_ref[...].astype(f32) + norm_back(normed_grad, unit, scale_rows, gain_ref[...])
    res_grad_ref[...] = grad_f
    res_low_ref[...] = grad_f.astype(bf16)

    for k in (1, 2, 3):
        z_copy(k).wait_send()
        level_copy(k, levels[k]).wait_send()
    for k in range(4):
        for copy in direct_copies(k) + forward_copies(k) + [corner_copy(k), core_copy(k)]:
            copy.wait_send()
        for copy in first_copies(k) + second_copies(k):
            copy.wait_send()


def ffn_layer(
    attn_part, hidden_own, grad_own, ffn_gain, kept, grad_all, w_pre, w_down, layout
):
    shared_pad, expert_units, experts, unit_pad = layout
    rows, width = hidden_own.shape
    bf16, f32 = jnp.bfloat16, jnp.float32
    half = width // 2
    wide = width + 128
    tile = 256
    shape = jax.ShapeDtypeStruct
    vmem, anywhere = pl.BlockSpec(memory_space=pltpu.VMEM), pl.BlockSpec(memory_space=pl.ANY)
    dma = pltpu.SemaphoreType.DMA
    cost = pl.CostEstimate(
        flops=2 * 24 * 2048 * 2048 * 256, bytes_accessed=60 * 2**20, transcendentals=3 * 2**20
    )
    return pl.pallas_call(
        functools.partial(
            ffn_kernel, (shared_pad, expert_units, experts, unit_pad, half, wide)
        ),
        out_shape=[
            shape((rows, width), f32),
            shape((rows, width), f32),
            shape((rows, width), bf16),
            shape((4, 2, 2, 2, rows, width), bf16),
            shape((width, expert_units), f32),
            shape((width, expert_units), f32),
            shape((width, expert_units), f32),
            shape((3, width, shared_pad), bf16),
            shape((width, 128), f32),
            shape((1, width), f32),
        ],
        in_specs=[anywhere, vmem, vmem, vmem, vmem, anywhere, anywhere, anywhere],
        out_specs=[vmem, vmem, vmem] + [anywhere] * 5 + [vmem, vmem],
        scratch_shapes=[
            pltpu.VMEM((4, 2, 2, 2, rows, width), bf16),
            pltpu.VMEM((4, 2, 2, 2, rows, width), bf16),
            pltpu.VMEM(w_pre.shape, bf16),
            pltpu.VMEM(w_down.shape, bf16),
            pltpu.VMEM((4, 2, 4 * rows, 2 * unit_pad), bf16),
            pltpu.VMEM((4, 2, 4 * rows, unit_pad), bf16),
            pltpu.VMEM((4, 2, 2, 2, rows, wide), bf16),
            pltpu.VMEM((4, 2, 2, rows, wide), bf16),
            pltpu.VMEM((4, 2, rows, half), bf16),
            pltpu.VMEM((4, 2, rows, wide - half), bf16),
            pltpu.VMEM((4, rows, half), bf16),
            pltpu.VMEM((4, rows, wide - half), bf16),
            pltpu.VMEM((4, rows, wide), bf16),
            pltpu.VMEM((4, rows, width), bf16),
            pltpu.VMEM((2, 2, rows, width), bf16),
            pltpu.VMEM((2, tile, expert_units), f32),
            pltpu.VMEM((2, tile, expert_units), f32),
            pltpu.VMEM((2, tile, expert_units), f32),
            pltpu.VMEM((2, 3, tile, shared_pad), bf16),
            dma((11,)),
            dma((2,)),
            dma((2, 4)),
            dma((2, 4)),
            dma((2, 4)),
            dma((2, 4, 4)),
            dma((2, 4, 4)),
            dma((2, 4)),
            dma((2, 4, 4)),
            dma((2, 4)),
        ],
        compiler_params=pltpu.CompilerParams(
            collective_id=0, has_side_effects=True, vmem_limit_bytes=63 * 2**20
        ),
        cost_estimate=cost,
    )(attn_part, hidden_own, grad_own, ffn_gain, kept, grad_all, w_pre, w_down)


def on_device(
    hidden_in,
    out_grad,
    parents,
    routes,
    attn_gain,
    w_query,
    w_key,
    w_value,
    b_query,
    b_key,
    b_value,
    w_out,
    ffn_gain,
    w_router,
    shared_gate,
    shared_w_gate,
    shared_w_up,
    shared_w_down,
    expert_w_gate,
    expert_w_up,
    expert_w_down,
):
    tok_rows, model_width = hidden_in.shape
    devices = lax.axis_size("dp")
    columns = lax.axis_size("tensor")
    place, column = lax.axis_index("dp"), lax.axis_index("tensor")
    all_rows = tok_rows * devices
    part_rows = tok_rows // columns
    local_width = w_query.shape[1]
    experts = w_router.shape[1]
    top_count = routes.shape[1]
    capacity = 5 * tok_rows * top_count // 4
    score_scale = HEAD_DIM ** (-0.5)
    bf16, f32 = jnp.bfloat16, jnp.float32

    expert_units = expert_w_gate.shape[2]
    shared_units = shared_w_gate.shape[1] // devices
    shared_pad = -(-shared_units // 128) * 128
    units = shared_pad + expert_units
    units_pad = -(-(units + experts + 1) // 128) * 128

    def own_units(matrix):
        return lax.dynamic_slice_in_dim(matrix, place * shared_units, shared_units, 1)

    def pad_to(matrix, columns):
        return jnp.pad(matrix, ((0, 0), (0, columns - matrix.shape[1])))

    def side_by_side(shared, expert):
        joined = jnp.concatenate([pad_to(own_units(shared), shared_pad), expert[0]], 1)
        return joined

    w_pre = jnp.concatenate(
        [
            pad_to(
                jnp.concatenate(
                    [side_by_side(shared_w_gate, expert_w_gate), w_router, shared_gate[:, None]], 1
                ),
                units_pad,
            ),
            pad_to(side_by_side(shared_w_up, expert_w_up), units_pad),
        ],
        1,
    )
    w_down = pad_to(side_by_side(shared_w_down, expert_w_down), units_pad)

    out_all = gather_dp(out_grad)

    routes_all = lax.all_gather(routes, "dp", axis=0, tiled=True)
    pair_onehot = routes_all[:, :, None] == jnp.arange(experts, dtype=jnp.int32)[None, None, :]
    hits = jnp.any(pair_onehot, 1)
    hit_blocks = hits.astype(bf16).reshape(devices, tok_rows, experts)
    below = (
        jnp.arange(tok_rows)[None, :] < jnp.arange(tok_rows)[:, None]
    ).astype(bf16)
    within = jnp.einsum("ij,bje->bie", below, hit_blocks, preferred_element_type=f32)
    block_sums = jnp.sum(hit_blocks.astype(f32), 1)
    before = jnp.cumsum(block_sums, 0) - block_sums
    slots = (within + before[:, None, :]).reshape(all_rows, experts)
    kept = (hits & (slots < capacity)).astype(f32)

    path = path_of(parents, place * tok_rows // SEG)
    reachable = path >= 0
    path_rows = jnp.maximum(path, 0)
    row_ids = jnp.arange(tok_rows, dtype=jnp.int32)
    depth = jnp.sum(reachable.astype(f32)) - 1.0
    cosine, sine = rope_tables(depth * SEG + row_ids.astype(f32))
    allowed = jnp.concatenate(
        [
            row_ids[:, None] >= row_ids[None, :],
            jnp.broadcast_to(
                jnp.repeat(reachable[1:], tok_rows)[None, :], (tok_rows, (LEVELS - 1) * tok_rows)
            ),
        ],
        1,
    )
    hidden_f = hidden_in.astype(f32)
    attn_scale, attn_unit = norm_parts(hidden_f)
    attn_normed = (attn_unit * attn_gain).astype(bf16)
    query_rot = turn_heads(
        product(attn_normed, w_query) + b_query.reshape(-1), cosine, sine, 1.0
    ).astype(bf16)
    key_rot = turn_heads(
        product(attn_normed, w_key) + b_key.reshape(-1), cosine, sine, 1.0
    ).astype(bf16)
    value_rows = (product(attn_normed, w_value) + b_value.reshape(-1)).astype(bf16)
    gathered = gather_dp(jnp.concatenate([key_rot, value_rows], 1))
    kv_blocks = gathered.reshape(devices, tok_rows, 2 * local_width)
    kv_path = jnp.take(kv_blocks, path_rows, axis=0).reshape(LEVELS * tok_rows, 2 * local_width)
    key_path, value_path = kv_path[:, :local_width], kv_path[:, local_width:]
    attended, log_total = attend_forward(query_rot, key_path, value_path, allowed, score_scale)
    attended_low = attended.astype(bf16)
    attn_part = product_nt(attended_low, w_out).astype(bf16)

    hidden_own = lax.dynamic_slice_in_dim(hidden_in, column * part_rows, part_rows, 0)
    grad_own = lax.dynamic_slice_in_dim(out_grad, column * part_rows, part_rows, 0)
    layout = (shared_pad, expert_units, experts, units_pad)
    cube = devices == 8 and columns == 4
    if cube and all_rows * model_width <= 2**22:
        kept_own = jnp.sum(jnp.where(jnp.arange(experts)[None, :] == place, kept, 0.0), 1)
        kept_own = kept_own.reshape(2, 2, 2, columns, part_rows).transpose(3, 2, 0, 1, 4)
        (
            residual,
            residual_grad,
            residual_low,
            ffn_part,
            grad_expert_gate,
            grad_expert_up,
            grad_expert_down,
            grad_shared,
            grad_side,
            grad_ffn_gain,
        ) = ffn_layer(
            attn_part.reshape(columns, part_rows, model_width),
            hidden_own,
            grad_own,
            ffn_gain[None, :],
            kept_own.reshape(columns, 2, 4 * part_rows, 1),
            out_all.reshape(2, 2, 2, columns, part_rows, model_width),
            w_pre,
            w_down,
            layout,
        )
        ffn_part = ffn_part.transpose(2, 3, 1, 0, 4, 5).reshape(all_rows, model_width)
        grad_ffn_gain = grad_ffn_gain[0]
        side_first = units - (units_pad - 128)
        grad_side = grad_side[:, side_first : side_first + experts + 1]
        grad_shared = grad_shared[:, :, :shared_units]
    else:
        (
            residual,
            residual_grad,
            residual_low,
            ffn_part,
            grad_expert_gate,
            grad_expert_up,
            grad_expert_down,
            grad_shared,
            grad_side,
            grad_ffn_gain,
        ) = ffn_plain(
            attn_part, hidden_own, grad_own, ffn_gain, kept, out_all, w_pre, w_down, layout
        )
        grad_shared = grad_shared[:, :, :shared_units]
    ffn_own = scatter_all(ffn_part).astype(f32)
    hidden_out = gather_tensor((residual + ffn_own).astype(bf16))
    residual_low = gather_tensor(residual_low)
    grad_out_proj = product_tn(residual_low, attended_low)
    attended_grad = product(residual_low, w_out).astype(bf16)

    query_grad, key_grad, value_grad = attend_backward(
        query_rot, key_path, value_path, allowed, log_total, attended_grad, score_scale
    )
    kv_grad = jnp.concatenate([key_grad, value_grad], 1).reshape(
        LEVELS, tok_rows, 2 * local_width
    )
    kv_all = jnp.zeros((devices, tok_rows, 2 * local_width), f32)
    for level in range(LEVELS):
        kv_all = kv_all.at[path_rows[level]].add(kv_grad[level])
    kv_own = scatter_dp(
        kv_all.reshape(all_rows, 2 * local_width).astype(bf16)
    ).astype(f32)
    query_pre_grad = turn_heads(query_grad, cosine, sine, -1.0).astype(bf16)
    key_pre_grad = turn_heads(kv_own[:, :local_width], cosine, sine, -1.0).astype(bf16)
    value_pre_grad = kv_own[:, local_width:].astype(bf16)
    qkv_pre_grad = jnp.concatenate([query_pre_grad, key_pre_grad, value_pre_grad], 1)
    grad_qkv = product_tn(attn_normed, qkv_pre_grad)
    bias_grads = jnp.sum(qkv_pre_grad.astype(f32), 0).reshape(3, -1, HEAD_DIM)
    attn_part_grad = (
        product_nt(query_pre_grad, w_query)
        + product_nt(key_pre_grad, w_key)
        + product_nt(value_pre_grad, w_value)
    )
    grad_attn_gain = jnp.sum(attn_part_grad * attn_unit, 0)
    attn_own_grad = scatter_tensor(attn_part_grad.astype(bf16)).astype(f32)
    own_rows = lambda array: lax.dynamic_slice_in_dim(
        array, column * part_rows, part_rows, 0
    )
    hidden_in_grad = gather_tensor(
        (
            residual_grad
            + norm_back(attn_own_grad, own_rows(attn_unit), own_rows(attn_scale), attn_gain)
        ).astype(bf16)
    )

    small = jnp.concatenate(
        [grad_side, grad_ffn_gain[:, None], grad_attn_gain[:, None]], 1
    )
    small = scatter_dp(lax.psum(small, "tensor"))
    bias_sums = lax.psum_scatter(bias_grads, "dp", scatter_dimension=2, tiled=True)
    grad_attn = scatter_dp(jnp.concatenate([grad_qkv, grad_out_proj], 1).astype(bf16)).astype(f32)
    shared_grads = lax.all_to_all(
        grad_shared, "dp", split_axis=1, concat_axis=2, tiled=True
    ).astype(f32)
    return (
        hidden_out,
        hidden_in_grad,
        small[:, experts + 2],
        grad_attn[:, :local_width],
        grad_attn[:, local_width : 2 * local_width],
        grad_attn[:, 2 * local_width : 3 * local_width],
        bias_sums[0],
        bias_sums[1],
        bias_sums[2],
        grad_attn[:, 3 * local_width :],
        small[:, experts + 1],
        small[:, :experts],
        small[:, experts],
        shared_grads[0],
        shared_grads[1],
        shared_grads[2],
        grad_expert_gate[None],
        grad_expert_up[None],
        grad_expert_down[None],
    )


def solution(mesh):
    return jax.shard_map(
        on_device,
        mesh=mesh,
        in_specs=(
            P("dp", None),
            P("dp", None),
            P(),
            P("dp", None),
            P(),
            P(None, "tensor"),
            P(None, "tensor"),
            P(None, "tensor"),
            P("tensor", None),
            P("tensor", None),
            P("tensor", None),
            P(None, "tensor"),
            P(),
            P(),
            P(),
            P(None, "tensor"),
            P(None, "tensor"),
            P(None, "tensor"),
            P("dp", None, "tensor"),
            P("dp", None, "tensor"),
            P("dp", None, "tensor"),
        ),
        out_specs=(
            P("dp", None),
            P("dp", None),
            P("dp"),
            P("dp", "tensor"),
            P("dp", "tensor"),
            P("dp", "tensor"),
            P("tensor", "dp"),
            P("tensor", "dp"),
            P("tensor", "dp"),
            P("dp", "tensor"),
            P("dp"),
            P("dp", None),
            P("dp"),
            P("dp", "tensor"),
            P("dp", "tensor"),
            P("dp", "tensor"),
            P("dp", None, "tensor"),
            P("dp", None, "tensor"),
            P("dp", None, "tensor"),
        ),
        check_vma=False,
    )
```

```python
import functools

import jax
import jax.numpy as jnp
from jax import lax
from jax.experimental import pallas as pl
from jax.experimental.pallas import tpu as pltpu
from jax.sharding import PartitionSpec as P

HEAD_DIM = 128
SEG = 256
MESH = pl.DeviceIdType.MESH


epsilon = 1e-06
rope_base = 1000000.0
highest = lax.Precision.HIGHEST


def product(left, right):
    return jnp.dot(left, right, preferred_element_type=jnp.float32)


def product_tn(left, right):
    return lax.dot_general(
        left, right, (((0,), (0,)), ((), ())), preferred_element_type=jnp.float32
    )


def product_nt(left, right):
    return lax.dot_general(
        left, right, (((1,), (1,)), ((), ())), preferred_element_type=jnp.float32
    )


def ancestry(parents):
    seg_count = parents.shape[0]
    labels = jnp.arange(seg_count, dtype=jnp.int32)

    def climb(level, carry):
        current, reach = carry
        upward = jnp.where(current >= 0, parents[jnp.maximum(current, 0)], -1)
        reach = jnp.maximum(reach, (upward[:, None] == labels[None, :]).astype(jnp.float32))
        return (upward, reach)

    start = (labels, jnp.eye(seg_count, dtype=jnp.float32))
    return lax.fori_loop(0, seg_count, climb, start)[1]


def rope_tables(positions):
    freqs = rope_base ** (-jnp.arange(0, HEAD_DIM, 2, dtype=jnp.float32) / HEAD_DIM)
    angles = positions[:, None] * freqs[None, :]
    angles = jnp.concatenate([angles, angles], 1)
    return (jnp.cos(angles)[:, None, :], jnp.sin(angles)[:, None, :])


def turn_heads(matrix, cosine, sine, sign_value):
    shaped = matrix.reshape(matrix.shape[0], matrix.shape[1] // HEAD_DIM, HEAD_DIM)
    half = HEAD_DIM // 2
    turned = jnp.concatenate([-shaped[..., half:], shaped[..., :half]], -1)
    return (shaped * cosine + sign_value * turned * sine).reshape(matrix.shape)


def norm_parts(values):
    scale_rows = lax.rsqrt(jnp.mean(values * values, 1, keepdims=True) + epsilon)
    return (scale_rows, values * scale_rows)


def norm_back(grad_rows, unit_rows, scale_rows, gain):
    unit_grad = grad_rows * gain
    return scale_rows * (unit_grad - unit_rows * jnp.mean(unit_grad * unit_rows, 1, keepdims=True))


LEVELS = 4


def gather_dp(rows):
    return lax.all_gather(rows, "dp", axis=0, tiled=True)


def gather_tensor(rows):
    return lax.all_gather(rows, "tensor", axis=0, tiled=True)


def gather_all(rows):
    return gather_dp(gather_tensor(rows))


def scatter_dp(rows):
    return lax.psum_scatter(rows, "dp", scatter_dimension=0, tiled=True)


def scatter_tensor(rows):
    return lax.psum_scatter(rows, "tensor", scatter_dimension=0, tiled=True)


def scatter_all(rows):
    return scatter_tensor(scatter_dp(rows))


def path_of(parents, segment):
    path = [segment]
    for _ in range(LEVELS - 1):
        last = path[-1]
        path.append(jnp.where(last >= 0, parents[jnp.maximum(last, 0)], -1))
    return jnp.stack(path)


def heads_of(matrix):
    return matrix.reshape(matrix.shape[0], -1, HEAD_DIM)


def attend_forward(query_rot, key_path, value_path, allowed, score_scale):
    scores = (
        jnp.einsum(
            "qhd,khd->hqk",
            heads_of(query_rot),
            heads_of(key_path),
            preferred_element_type=jnp.float32,
        )
        * score_scale
    )
    scores = jnp.where(allowed[None], scores, -jnp.inf)
    peak = jnp.max(scores, 2, keepdims=True)
    log_total = peak + jnp.log(jnp.sum(jnp.exp(scores - peak), 2, keepdims=True))
    weights = jnp.exp(scores - log_total).astype(jnp.bfloat16)
    attended = jnp.einsum(
        "hqk,khd->qhd", weights, heads_of(value_path), preferred_element_type=jnp.float32
    )
    return attended.reshape(query_rot.shape), log_total


def attend_backward(
    query_rot, key_path, value_path, allowed, log_total, attended_grad, score_scale
):
    query, key, value = heads_of(query_rot), heads_of(key_path), heads_of(value_path)
    grad = heads_of(attended_grad)
    scores = jnp.einsum("qhd,khd->hqk", query, key, preferred_element_type=jnp.float32)
    weights = jnp.exp(jnp.where(allowed[None], scores * score_scale, -jnp.inf) - log_total)
    weight_grad = jnp.einsum("qhd,khd->hqk", grad, value, preferred_element_type=jnp.float32)
    center = jnp.sum(weights * weight_grad, 2, keepdims=True)
    score_grad = (weights * (weight_grad - center)).astype(jnp.bfloat16)
    query_grad = (
        jnp.einsum("hqk,khd->qhd", score_grad, key, preferred_element_type=jnp.float32)
        * score_scale
    )
    key_grad = (
        jnp.einsum("hqk,qhd->khd", score_grad, query, preferred_element_type=jnp.float32)
        * score_scale
    )
    value_grad = jnp.einsum(
        "hqk,qhd->khd",
        weights.astype(jnp.bfloat16),
        grad,
        preferred_element_type=jnp.float32,
    )
    return (
        query_grad.reshape(query_rot.shape),
        key_grad.reshape(key_path.shape),
        value_grad.reshape(value_path.shape),
    )


def ffn_plain(attn_part, hidden_own, grad_own, ffn_gain, kept, out_all, w_pre, w_down, layout):
    _, shared_pad, expert_units, experts, units_pad = layout
    units = shared_pad + expert_units
    bf16, f32 = jnp.bfloat16, jnp.float32
    place, column = lax.axis_index("dp"), lax.axis_index("tensor")
    columns, part_rows = lax.axis_size("tensor"), hidden_own.shape[0]
    out_own = grad_own.astype(f32)
    residual = hidden_own.astype(f32) + scatter_tensor(attn_part).astype(f32)
    ffn_scale, ffn_unit = norm_parts(residual)
    ffn_normed = (ffn_unit * ffn_gain).astype(bf16)
    normed_all = gather_all(ffn_normed)

    pre = product(normed_all, w_pre)
    pre_gate, pre_up = pre[:, :units_pad], pre[:, units_pad:]
    logits = pre[:, units : units + experts]
    probs = jax.nn.softmax(logits, 1)
    shared_weight = jax.nn.sigmoid(pre[:, units + experts])
    own_expert = jnp.arange(experts, dtype=jnp.int32)[None, :] == place
    gate_own = jnp.sum(jnp.where(own_expert, probs * kept, 0.0), 1)
    lane = jnp.arange(units_pad)[None, :]
    weight = jnp.where(
        lane < shared_pad,
        shared_weight[:, None],
        jnp.where(lane < units, gate_own[:, None], 0.0),
    )
    down_back = product(out_all, w_down)
    sigmoid_gate = jax.nn.sigmoid(pre_gate)
    hidden = (pre_gate * sigmoid_gate * pre_up).astype(bf16).astype(f32)
    hidden_scaled = (hidden * weight).astype(bf16)
    hidden_grad = down_back * weight
    up_rows = (hidden_grad * pre_gate * sigmoid_gate).astype(bf16)
    gate_rows = (
        hidden_grad * pre_up * sigmoid_gate * (1.0 + pre_gate * (1.0 - sigmoid_gate))
    ).astype(bf16)
    both_rows = jnp.concatenate([gate_rows, up_rows], 1)
    dots = hidden * down_back
    gate_dot = jnp.sum(jnp.where((lane >= shared_pad) & (lane < units), dots, 0.0), 1)
    shared_dot = jnp.sum(jnp.where(lane < shared_pad, dots, 0.0), 1)
    dot_parts = jnp.concatenate(
        [jnp.where(own_expert, gate_dot[:, None] * kept, 0.0), shared_dot[:, None]], 1
    )
    ffn_part = product_nt(hidden_scaled, w_down).astype(bf16)
    normed_part = product_nt(both_rows, w_pre).astype(bf16)
    grad_pre = product_tn(normed_all, both_rows)
    grad_down = product_tn(out_all, hidden_scaled)

    dot_own = scatter_all(dot_parts)
    normed_own = scatter_all(normed_part).astype(f32)

    first = (place * columns + column) * part_rows
    own = lambda array: lax.dynamic_slice_in_dim(array, first, part_rows, 0)
    probs_own, shared_own = own(probs), own(shared_weight)
    prob_grad = dot_own[:, :experts]
    logit_grad = (
        probs_own * (prob_grad - jnp.sum(probs_own * prob_grad, 1, keepdims=True))
    ).astype(bf16)
    weight_logit_grad = (dot_own[:, experts] * shared_own * (1.0 - shared_own)).astype(bf16)
    side_grad = jnp.concatenate([logit_grad, weight_logit_grad[:, None]], 1)
    side_w = w_pre[:, units : units + experts + 1]
    normed_grad = normed_own + product_nt(side_grad, side_w)
    grad_side = product_tn(ffn_normed, side_grad)
    grad_ffn_gain = jnp.sum(normed_grad * ffn_unit, 0)
    residual_grad = out_own + norm_back(normed_grad, ffn_unit, ffn_scale, ffn_gain)
    expert = slice(shared_pad, units)
    expert_up = slice(units_pad + shared_pad, units_pad + units)
    grad_shared = jnp.stack(
        [
            grad_pre[:, : shared_pad],
            grad_pre[:, units_pad : units_pad + shared_pad],
            grad_down[:, : shared_pad],
        ]
    ).astype(bf16)
    return (
        residual,
        residual_grad,
        residual_grad.astype(bf16),
        ffn_part,
        grad_pre[:, expert],
        grad_pre[:, expert_up],
        grad_down[:, expert],
        grad_shared,
        grad_side,
        grad_ffn_gain,
    )


def flip(bit):
    return 1 - bit


def other(index, step):
    result, place = index, 1
    while place <= step:
        if step & place:
            result = result + place - 2 * place * ((index // place) % 2)
        place *= 2
    return result


def ffn_kernel(
    units,
    part_ref,
    hidden_ref,
    grad_ref,
    gain_ref,
    kept_ref,
    grad_all_ref,
    w_pre_ref,
    w_down_ref,
    residual_ref,
    res_grad_ref,
    res_low_ref,
    ffn_part_ref,
    e_gate_ref,
    e_up_ref,
    e_down_ref,
    shared_ref,
    small_ref,
    rows_all,
    dy_all,
    w_pre,
    w_down,
    both_all,
    scaled_all,
    sums,
    got_core,
    got_x1,
    got_y1,
    got_y2,
    got_x2,
    got_z,
    attn_z,
    ffn_chunk,
    tile_gate,
    tile_up,
    tile_down,
    tile_shared,
    load_sems,
    store_sems,
    tile_sems,
    attn_sems,
    zs,
    links,
    cores,
    rs_core,
    rs_links,
    rs_z,
):
    shared_units, shared_pad, expert_units, experts, unit_pad, half, wide = units
    bf16, f32 = jnp.bfloat16, jnp.float32
    place, column = lax.axis_index("dp"), lax.axis_index("tensor")
    core, east, north = place % 2, (place // 2) % 2, place // 4
    rows, width = hidden_ref.shape
    sibling = {"dp": other(place, 1)}
    x_side = {"dp": other(place, 2)}
    y_side = {"dp": other(place, 4)}
    levels = [{"tensor": other(column, k)} for k in range(4)]

    def level_of(k):
        low_i, high_i, low_k, high_k = column % 2, column // 2, k % 2, k // 2
        return (low_i + low_k - 2 * low_i * low_k) + 2 * (high_i + high_k - 2 * high_i * high_k)

    def remote(src, dst, sems, which, device):
        return pltpu.make_async_remote_copy(
            src_ref=src,
            dst_ref=dst,
            send_sem=sems.at[(0, *which)],
            recv_sem=sems.at[(1, *which)],
            device_id=device,
            device_id_type=MESH,
        )

    load_pre = pltpu.make_async_copy(w_pre_ref, w_pre, load_sems.at[0])
    load_down = pltpu.make_async_copy(w_down_ref, w_down, load_sems.at[1])
    load_pre.start()
    load_down.start()

    def load_grad(c, z):
        return pltpu.make_async_copy(
            grad_all_ref.at[:, :, c, z], dy_all.at[z, c], load_sems.at[2 + c * 4 + z]
        )

    for c in range(2):
        for z in range(4):
            load_grad(c, z).start()

    barrier = pltpu.get_barrier_semaphore()
    partners = [sibling, x_side, y_side] + levels[1:]
    for partner in partners:
        pl.semaphore_signal(barrier, inc=1, device_id=partner, device_id_type=MESH)
    pl.semaphore_wait(barrier, len(partners))

    attn_copies = []
    for k in (3, 2, 1):
        copy = remote(
            part_ref.at[other(column, k)], attn_z.at[k], attn_sems, (k,), levels[k]
        )
        copy.start()
        attn_copies.append(copy)
    own_part = pltpu.make_async_copy(part_ref.at[column], attn_z.at[0], load_sems.at[10])
    own_part.start()
    own_part.wait()
    for copy in attn_copies:
        copy.wait()
    attn = attn_z[0].astype(f32)
    for k in range(1, 4):
        attn = attn + attn_z[k].astype(f32)
    residual = hidden_ref[...].astype(f32) + attn
    residual_ref[...] = residual
    scale_rows = lax.rsqrt(jnp.mean(residual * residual, 1, keepdims=True) + epsilon)
    normed = (residual * scale_rows * gain_ref[...]).astype(bf16)
    rows_all[column, core, north, east] = normed

    own_slot = rows_all.at[column, core, north, east]

    def z_copy(k):
        return remote(own_slot, own_slot, zs, (k,), levels[k])

    def block(k, c, y, x, cols=slice(None)):
        return rows_all.at[level_of(k), c, y, x, :, cols]

    first_half, second_half = pl.ds(0, half), pl.ds(half, width - half)

    def direct_copies(k):
        own = block(k, core, north, east)
        return [
            remote(own, own, links, (0, k), x_side),
            remote(own, own, links, (1, k), y_side),
            remote(own, own, cores, (0, k), sibling),
        ]

    def forward_copies(k):
        from_x = block(k, core, north, flip(east), first_half)
        from_y = block(k, core, flip(north), east, second_half)
        all_x = block(k, core, north, flip(east))
        all_y = block(k, core, flip(north), east)
        return [
            remote(from_x, from_x, links, (2, k), y_side),
            remote(from_y, from_y, links, (3, k), x_side),
            remote(all_x, all_x, cores, (1, k), sibling),
            remote(all_y, all_y, cores, (2, k), sibling),
        ]

    def corner_copy(k):
        corner = block(k, core, flip(north), flip(east))
        return remote(corner, corner, cores, (3, k), sibling)

    def start_direct(k):
        for copy in direct_copies(k):
            copy.start()

    def start_forward(k):
        for copy in direct_copies(k)[:2]:
            copy.wait_recv()
        for copy in forward_copies(k):
            copy.start()

    def start_corner(k):
        for copy in forward_copies(k)[:2]:
            copy.wait_recv()
        corner_copy(k).start()

    def finish_gather(k):
        direct_copies(k)[2].wait_recv()
        for copy in forward_copies(k)[2:]:
            copy.wait_recv()
        corner_copy(k).wait_recv()

    def core_copy(k):
        return remote(sums.at[k, flip(core)], got_core.at[k], rs_core, (k,), sibling)

    left, right = pl.ds(0, half), pl.ds(half, wide - half)

    def first_copies(k):
        return [
            remote(
                sums.at[k, core, :, flip(east), :, left],
                got_x1.at[k],
                rs_links, (0, k),
                x_side,
            ),
            remote(
                sums.at[k, core, flip(north), :, :, right],
                got_y1.at[k],
                rs_links, (1, k),
                y_side,
            ),
        ]

    def second_copies(k):
        return [
            remote(
                sums.at[k, core, flip(north), east, :, left],
                got_y2.at[k],
                rs_links, (2, k),
                y_side,
            ),
            remote(
                sums.at[k, core, north, flip(east), :, right],
                got_x2.at[k],
                rs_links, (3, k),
                x_side,
            ),
        ]

    def level_copy(k, device):
        return remote(sums.at[k, core, north, east], got_z.at[k], rs_z, (k,), device)

    def add(ref, value):
        ref[...] = (ref[...].astype(f32) + value.astype(f32)).astype(bf16)

    def after_core(k):
        core_copy(k).wait_recv()
        for y in range(2):
            for x in range(2):
                add(sums.at[k, core, y, x], got_core[k, y, x])
        for copy in first_copies(k):
            copy.start()

    def after_first(k):
        x_copy, y_copy = first_copies(k)
        x_copy.wait_recv()
        for y in range(2):
            add(sums.at[k, core, y, east, :, left], got_x1[k, y])
        y_copy.wait_recv()
        for x in range(2):
            add(sums.at[k, core, north, x, :, right], got_y1[k, x])
        for copy in second_copies(k):
            copy.start()

    def after_second(k):
        y_copy, x_copy = second_copies(k)
        y_copy.wait_recv()
        add(sums.at[k, core, north, east, :, left], got_y2[k])
        x_copy.wait_recv()
        add(sums.at[k, core, north, east, :, right], got_x2[k])
        for level in range(1, 4):

            @pl.when(k == level)
            def _():
                level_copy(k, levels[level]).start()

    for k in (1, 2, 3):
        z_copy(k).start()
    start_direct(0)
    load_pre.wait()
    load_down.wait()
    for c in range(2):
        for z in range(4):
            load_grad(c, z).wait()
    start_forward(0)
    z_copy(1).wait_recv()
    start_direct(1)
    start_corner(0)

    last = unit_pad - 128
    lane = lax.broadcasted_iota(jnp.int32, (1, 128), 1)
    first_lane = shared_pad + expert_units - last
    in_router = (lane >= first_lane) & (lane < first_lane + experts)
    is_shared = lane == first_lane + experts

    def routing(logit_block):
        top = jnp.max(jnp.where(in_router, logit_block, -jnp.inf), 1, keepdims=True)
        powers = jnp.where(in_router, jnp.exp(jnp.where(in_router, logit_block - top, 0.0)), 0.0)
        probs = powers / jnp.sum(powers, 1, keepdims=True)
        shared_logit = jnp.sum(jnp.where(is_shared, logit_block, 0.0), 1, keepdims=True)
        return probs, jax.nn.sigmoid(shared_logit)

    def compute(k, c):
        z = level_of(k)
        row_block = rows_all[z, c].reshape(4 * rows, width)
        dy_block = dy_all[z, c].reshape(4 * rows, width)
        pre_gate = product(row_block, w_pre[:, :unit_pad])
        pre_up = product(row_block, w_pre[:, unit_pad:])
        down_back = product(dy_block, w_down[...])
        probs, shared_weight = routing(pre_gate[:, last:])
        kept = kept_ref[z, c]
        gate = (
            jnp.sum(jnp.where(lane == first_lane + place, probs, 0.0), 1, keepdims=True) * kept
        )
        dots = []
        for begin, end, weight in (
            (0, shared_pad, shared_weight),
            (shared_pad, unit_pad, gate),
        ):
            cols = slice(begin, end)
            a, b, back = pre_gate[:, cols], pre_up[:, cols], down_back[:, cols]
            sig = jax.nn.sigmoid(a)
            silu = a * sig
            hidden = (silu * b).astype(bf16).astype(f32)
            dots.append(jnp.sum(hidden * back, 1, keepdims=True))
            scaled_all[z, c, :, begin:end] = (hidden * weight).astype(bf16)
            grad = back * weight
            both_all[z, c, :, unit_pad + begin : unit_pad + end] = (grad * silu).astype(bf16)
            both_all[z, c, :, begin:end] = (
                grad * b * sig * (1.0 + a * (1.0 - sig))
            ).astype(bf16)
        dot_block = jnp.where(is_shared, dots[0], 0.0) + jnp.where(
            lane == first_lane + place, dots[1] * kept, 0.0
        )
        normed_grad = product_nt(both_all[z, c], w_pre[...]).astype(bf16)
        sums[k, c, :, :, :, 0:width] = normed_grad.reshape(2, 2, rows, width)
        sums[k, c, :, :, :, width:wide] = dot_block.astype(bf16).reshape(2, 2, rows, wide - width)

    def store_chunk(k, c):
        return pltpu.make_async_copy(
            ffn_chunk, ffn_part_ref.at[level_of(k), c], store_sems.at[c]
        )

    def chunk(k, carry):
        @pl.when(k < 3)
        def _():
            start_forward(k + 1)

        @pl.when(k < 2)
        def _():
            for level in (2, 3):

                @pl.when(k + 2 == level)
                def _():
                    z_copy(level).wait_recv()

            start_direct(k + 2)

        finish_gather(k)
        def rows_of(i, carry):
            compute(k, (i + 1 + core) % 2)

            @pl.when(i == 0)
            def _():
                core_copy(k).start()

            return carry

        lax.fori_loop(0, 2, rows_of, 0)

        @pl.when(k >= 1)
        def _():
            after_first(k - 1)
            store_chunk(k - 1, 1).wait()

        def outputs(c, carry):
            part = product_nt(scaled_all[level_of(k), c], w_down[...]).astype(bf16)

            @pl.when(c == 1)
            def _():
                store_chunk(k, 0).wait()

            ffn_chunk[...] = part.reshape(2, 2, rows, width)
            store_chunk(k, c).start()
            return carry

        lax.fori_loop(0, 2, outputs, 0)

        @pl.when(k < 3)
        def _():
            start_corner(k + 1)

        after_core(k)

        @pl.when(k >= 1)
        def _():
            after_second(k - 1)

        return carry

    lax.fori_loop(0, 4, chunk, 0)
    store_chunk(3, 1).wait()

    tile = tile_gate.shape[1]
    tiles = width // tile

    def tile_copies(i, slot):
        window = pl.ds(pl.multiple_of(i * tile, tile), tile)
        return [
            pltpu.make_async_copy(tile_gate.at[slot], e_gate_ref.at[window], tile_sems.at[slot, 0]),
            pltpu.make_async_copy(tile_up.at[slot], e_up_ref.at[window], tile_sems.at[slot, 1]),
            pltpu.make_async_copy(tile_down.at[slot], e_down_ref.at[window], tile_sems.at[slot, 2]),
            pltpu.make_async_copy(
                tile_shared.at[slot], shared_ref.at[i], tile_sems.at[slot, 3]
            ),
        ]

    tokens = rows * 32

    def weight_tile(i, carry):
        slot = i % 2

        @pl.when(i >= 2)
        def _():
            for copy in tile_copies(i - 2, slot):
                copy.wait()

        window = pl.ds(pl.multiple_of(i * tile, tile), tile)
        expert = slice(shared_pad, shared_pad + expert_units)
        lhs = rows_all[:, :, :, :, :, window].reshape(tokens, tile)
        grad = product_tn(lhs, both_all[...].reshape(tokens, 2 * unit_pad))
        tile_gate[slot] = grad[:, expert]
        tile_shared[slot, 0] = grad[:, :shared_pad].T[:shared_units].astype(bf16)
        tile_up[slot] = grad[:, unit_pad + shared_pad : unit_pad + shared_pad + expert_units]
        tile_shared[slot, 1] = grad[:, unit_pad : unit_pad + shared_pad].T[:shared_units].astype(bf16)
        lhs = dy_all[:, :, :, :, :, window].reshape(tokens, tile)
        grad = product_tn(lhs, scaled_all[...].reshape(tokens, unit_pad))
        tile_down[slot] = grad[:, expert]
        tile_shared[slot, 2] = grad[:, :shared_pad].T[:shared_units].astype(bf16)
        for copy in tile_copies(i, slot):
            copy.start()

        @pl.when(i == 1)
        def _():
            after_first(3)

        @pl.when(i == 3)
        def _():
            after_second(3)

        return carry

    lax.fori_loop(0, tiles, weight_tile, 0)
    for i in (tiles - 2, tiles - 1):
        for copy in tile_copies(i, i % 2):
            copy.wait()

    total = sums[0, core, north, east].astype(f32)
    for k in (1, 2, 3):
        level_copy(k, levels[k]).wait_recv()
        total = total + got_z[k].astype(f32)
    dots = total[:, width:]
    unit = residual_ref[...] * scale_rows
    own_normed = rows_all[column, core, north, east]
    side_w = w_pre[:, last:unit_pad]
    probs, shared_weight = routing(product(own_normed, side_w))
    router_dots = jnp.where(in_router, dots, 0.0)
    center = jnp.sum(probs * router_dots, 1, keepdims=True)
    side = jnp.where(in_router, probs * (router_dots - center), 0.0) + jnp.where(
        is_shared, dots * shared_weight * (1.0 - shared_weight), 0.0
    )
    side = side.astype(bf16)
    normed_grad = total[:, :width] + product_nt(side, side_w)
    side_rows = product_tn(side, own_normed)
    small_ref[...] = side_rows[first_lane : first_lane + small_ref.shape[0]]
    small_ref[experts + 1 : experts + 2, :] = jnp.sum(normed_grad * unit, 0, keepdims=True)
    grad_f = grad_ref[...].astype(f32) + norm_back(normed_grad, unit, scale_rows, gain_ref[...])
    res_grad_ref[...] = grad_f
    res_low_ref[...] = grad_f.astype(bf16)

    for k in (1, 2, 3):
        z_copy(k).wait_send()
        level_copy(k, levels[k]).wait_send()
    for k in range(4):
        for copy in direct_copies(k) + forward_copies(k) + [corner_copy(k), core_copy(k)]:
            copy.wait_send()
        for copy in first_copies(k) + second_copies(k):
            copy.wait_send()


def ffn_layer(
    attn_part, hidden_own, grad_own, ffn_gain, kept, grad_all, w_pre, w_down, layout
):
    shared_units, shared_pad, expert_units, experts, unit_pad = layout
    rows, width = hidden_own.shape
    bf16, f32 = jnp.bfloat16, jnp.float32
    half = width // 2
    wide = width + 128
    tile = 256
    shape = jax.ShapeDtypeStruct
    vmem, anywhere = pl.BlockSpec(memory_space=pltpu.VMEM), pl.BlockSpec(memory_space=pl.ANY)
    dma = pltpu.SemaphoreType.DMA
    cost = pl.CostEstimate(
        flops=2 * 24 * 2048 * 2048 * 256, bytes_accessed=60 * 2**20, transcendentals=3 * 2**20
    )
    return pl.pallas_call(
        functools.partial(
            ffn_kernel, (shared_units, shared_pad, expert_units, experts, unit_pad, half, wide)
        ),
        out_shape=[
            shape((rows, width), f32),
            shape((rows, width), f32),
            shape((rows, width), bf16),
            shape((4, 2, 2, 2, rows, width), bf16),
            shape((width, expert_units), f32),
            shape((width, expert_units), f32),
            shape((width, expert_units), f32),
            shape((width // tile, 3, shared_units, tile), bf16),
            shape((16, width), f32),
        ],
        in_specs=[anywhere, vmem, vmem, vmem, vmem, anywhere, anywhere, anywhere],
        out_specs=[vmem, vmem, vmem] + [anywhere] * 5 + [vmem],
        scratch_shapes=[
            pltpu.VMEM((4, 2, 2, 2, rows, width), bf16),
            pltpu.VMEM((4, 2, 2, 2, rows, width), bf16),
            pltpu.VMEM(w_pre.shape, bf16),
            pltpu.VMEM(w_down.shape, bf16),
            pltpu.VMEM((4, 2, 4 * rows, 2 * unit_pad), bf16),
            pltpu.VMEM((4, 2, 4 * rows, unit_pad), bf16),
            pltpu.VMEM((4, 2, 2, 2, rows, wide), bf16),
            pltpu.VMEM((4, 2, 2, rows, wide), bf16),
            pltpu.VMEM((4, 2, rows, half), bf16),
            pltpu.VMEM((4, 2, rows, wide - half), bf16),
            pltpu.VMEM((4, rows, half), bf16),
            pltpu.VMEM((4, rows, wide - half), bf16),
            pltpu.VMEM((4, rows, wide), bf16),
            pltpu.VMEM((4, rows, width), bf16),
            pltpu.VMEM((2, 2, rows, width), bf16),
            pltpu.VMEM((2, tile, expert_units), f32),
            pltpu.VMEM((2, tile, expert_units), f32),
            pltpu.VMEM((2, tile, expert_units), f32),
            pltpu.VMEM((2, 3, shared_units, tile), bf16),
            dma((11,)),
            dma((2,)),
            dma((2, 4)),
            dma((2, 4)),
            dma((2, 4)),
            dma((2, 4, 4)),
            dma((2, 4, 4)),
            dma((2, 4)),
            dma((2, 4, 4)),
            dma((2, 4)),
        ],
        compiler_params=pltpu.CompilerParams(
            collective_id=0, has_side_effects=True, vmem_limit_bytes=63 * 2**20
        ),
        cost_estimate=cost,
    )(attn_part, hidden_own, grad_own, ffn_gain, kept, grad_all, w_pre, w_down)


class PlaneSum:
    def __init__(self, mine, theirs, got_core, got_x1, got_y1, got_y2, got_x2, core_sems, sems):
        self.mine, self.theirs = mine, theirs
        self.got = (got_core, got_x1, got_y1, got_y2, got_x2)
        self.core_sems, self.sems = core_sems, sems
        self.wide = got_core.shape[-1]
        self.half = got_x1.shape[-1]
        self.left, self.right = pl.ds(0, self.half), pl.ds(self.half, self.wide - self.half)
        place = lax.axis_index("dp")
        self.core, self.east, self.north = place % 2, (place // 2) % 2, place // 4
        self.sibling = {"dp": other(place, 1)}
        self.x_side, self.y_side = {"dp": other(place, 2)}, {"dp": other(place, 4)}

    def remote(self, src, dst, sems, which, device):
        return pltpu.make_async_remote_copy(
            src_ref=src,
            dst_ref=dst,
            send_sem=sems.at[(0, *which)],
            recv_sem=sems.at[(1, *which)],
            device_id=device,
            device_id_type=MESH,
        )

    def core_copy(self, k):
        return self.remote(
            self.theirs(k), self.got[0].at[k], self.core_sems, (k,), self.sibling
        )

    def first_copies(self, k):
        mine = self.mine(k)
        return [
            self.remote(
                mine.at[:, flip(self.east), :, self.left],
                self.got[1].at[k],
                self.sems,
                (0, k),
                self.x_side,
            ),
            self.remote(
                mine.at[flip(self.north), :, :, self.right],
                self.got[2].at[k],
                self.sems,
                (1, k),
                self.y_side,
            ),
        ]

    def second_copies(self, k):
        mine = self.mine(k)
        return [
            self.remote(
                mine.at[flip(self.north), self.east, :, self.left],
                self.got[3].at[k],
                self.sems,
                (2, k),
                self.y_side,
            ),
            self.remote(
                mine.at[self.north, flip(self.east), :, self.right],
                self.got[4].at[k],
                self.sems,
                (3, k),
                self.x_side,
            ),
        ]

    def add(self, ref, value):
        ref[...] = (ref[...].astype(jnp.float32) + value.astype(jnp.float32)).astype(jnp.bfloat16)

    def start(self, k):
        self.core_copy(k).start()

    def after_core(self, k):
        self.core_copy(k).wait_recv()
        mine = self.mine(k)
        for y in range(2):
            for x in range(2):
                self.add(mine.at[y, x], self.got[0][k, y, x])
        for copy in self.first_copies(k):
            copy.start()

    def after_first(self, k):
        x_copy, y_copy = self.first_copies(k)
        mine = self.mine(k)
        x_copy.wait_recv()
        for y in range(2):
            self.add(mine.at[y, self.east, :, self.left], self.got[1][k, y])
        y_copy.wait_recv()
        for x in range(2):
            self.add(mine.at[self.north, x, :, self.right], self.got[2][k, x])
        for copy in self.second_copies(k):
            copy.start()

    def after_second(self, k):
        y_copy, x_copy = self.second_copies(k)
        own = self.mine(k).at[self.north, self.east]
        y_copy.wait_recv()
        self.add(own.at[:, self.left], self.got[3][k])
        x_copy.wait_recv()
        self.add(own.at[:, self.right], self.got[4][k])
        return own

    def wait_sends(self, k):
        self.core_copy(k).wait_send()
        for copy in self.first_copies(k) + self.second_copies(k):
            copy.wait_send()


def plane_scratch(count, rows, wide):
    half = wide // 2
    bf16, dma = jnp.bfloat16, pltpu.SemaphoreType.DMA
    return [
        pltpu.VMEM((count, 2, 2, rows, wide), bf16),
        pltpu.VMEM((count, 2, rows, half), bf16),
        pltpu.VMEM((count, 2, rows, wide - half), bf16),
        pltpu.VMEM((count, rows, half), bf16),
        pltpu.VMEM((count, rows, wide - half), bf16),
        dma((2, count)),
        dma((2, 4, count)),
    ]


def unturn(grad, cosine, sine):
    heads = []
    for begin in range(0, grad.shape[1], HEAD_DIM):
        head = grad[:, begin : begin + HEAD_DIM]
        heads.append(head * cosine - pltpu.roll(head, HEAD_DIM // 2, 1) * sine)
    return jnp.concatenate(heads, 1)


def back_kernel(
    score_scale,
    gain_row,
    residual_ref,
    res_grad_ref,
    res_low_ref,
    ffn_part_ref,
    shared_ref,
    small_ref,
    query_ref,
    key_ref,
    value_ref,
    level_mask_ref,
    level_spots_ref,
    log_total_ref,
    attended_ref,
    normed_ref,
    hidden_ref,
    gain_ref,
    cosine_ref,
    sine_ref,
    w_out_ref,
    w_query_ref,
    w_key_ref,
    w_value_ref,
    hidden_out_ref,
    hidden_grad_ref,
    grad_query_ref,
    grad_key_ref,
    grad_value_ref,
    grad_out_ref,
    grad_shared_ref,
    small_out_ref,
    bias_out_ref,
    low_all,
    w_qkv,
    out_mine,
    out_z,
    kv_sums,
    w_sums,
    kv_path,
    attended_grad,
    query_grad,
    pre_grads,
    part,
    part_send,
    part_z,
    hidden_stage,
    shared_got,
    shared_stage,
    small_send,
    small_got,
    small_z,
    *rest,
):
    bf16, f32 = jnp.bfloat16, jnp.float32
    out_scr, rest = rest[:7], rest[7:]
    kv_scr, rest = rest[:7], rest[7:]
    w_scr, rest = rest[:7], rest[7:]
    wkv_sems, rest = rest[:2], rest[2:]
    load_sems, low_sems, out_sems, part_sems, end_sems, shared_sems, small_sems, small_z_sems = rest
    place, column = lax.axis_index("dp"), lax.axis_index("tensor")
    core, east, north = place % 2, (place // 2) % 2, place // 4
    rows, width = residual_ref.shape
    tok_rows, local_width = query_ref.shape
    levels = [{"tensor": other(column, k)} for k in range(4)]
    peers = [{"dp": other(place, j)} for j in range(8)]

    def remote(src, dst, sems, which, device):
        return pltpu.make_async_remote_copy(
            src_ref=src,
            dst_ref=dst,
            send_sem=sems.at[(0, *which)],
            recv_sem=sems.at[(1, *which)],
            device_id=device,
            device_id_type=MESH,
        )

    def load_out(z):
        return pltpu.make_async_copy(ffn_part_ref.at[z, core], out_mine.at[z], load_sems.at[z])

    loads = [
        pltpu.make_async_copy(w_query_ref, w_qkv.at[0], load_sems.at[5]),
        pltpu.make_async_copy(w_key_ref, w_qkv.at[1], load_sems.at[6]),
        pltpu.make_async_copy(w_out_ref, w_qkv.at[2], load_sems.at[4]),
    ]
    load_value = pltpu.make_async_copy(w_value_ref, w_qkv.at[2], load_sems.at[7])
    for z in range(4):
        load_out(z).start()
    for copy in loads:
        copy.start()

    barrier = pltpu.get_barrier_semaphore()
    partners = peers[1:] + levels[1:]
    for partner in partners:
        pl.semaphore_signal(barrier, inc=1, device_id=partner, device_id_type=MESH)
    pl.semaphore_wait(barrier, len(partners))

    out_sum = PlaneSum(
        lambda k: out_mine.at[k], lambda k: ffn_part_ref.at[k, flip(core)], *out_scr
    )
    kv_sum = PlaneSum(
        lambda k: kv_sums.at[core], lambda k: kv_sums.at[flip(core)], *kv_scr
    )
    w_sum = PlaneSum(
        lambda k: w_sums.at[k, core], lambda k: w_sums.at[k, flip(core)], *w_scr
    )
    wkv_sum = PlaneSum(
        lambda k: kv_sums.at[core], lambda k: kv_sums.at[flip(core)], *kv_scr[:5], *wkv_sems
    )

    low_all[column] = res_low_ref[...]
    own_low = low_all.at[column]
    low_copies = [remote(own_low, own_low, low_sems, (k,), levels[k]) for k in (3, 2, 1)]
    for copy in low_copies:
        copy.start()
    for z in range(4):
        out_sum.start(z)
    for z in range(4):
        load_out(z).wait()
        out_sum.after_core(z)
    for copy in loads:
        copy.wait()
    for copy in low_copies:
        copy.wait_recv()

    low_rows = low_all[...].reshape(tok_rows, width)
    attended_grad[...] = product(low_rows, w_qkv[2]).astype(bf16)
    load_value.start()

    def block_index(place_of):
        return place_of % 2, place_of // 4, (place_of // 2) % 2

    def out_weights(i, carry):
        c, y, x = block_index(i)
        window = pl.ds(pl.multiple_of(i * tok_rows, tok_rows), tok_rows)
        lhs = low_all[:, :, window].reshape(tok_rows, tok_rows)
        w_sums[0, c, y, x] = product_tn(lhs, attended_ref[...]).astype(bf16)
        return carry

    lax.fori_loop(0, 8, out_weights, 0)
    w_sum.start(0)

    key_rows = key_ref.shape[0]
    row_id = lax.broadcasted_iota(jnp.int32, (tok_rows, key_rows), 0)
    col_id = lax.broadcasted_iota(jnp.int32, (tok_rows, key_rows), 1)

    def head(h, carry):
        cols = pl.ds(pl.multiple_of(h * HEAD_DIM, HEAD_DIM), HEAD_DIM)
        value_cols = pl.ds(pl.multiple_of(local_width + h * HEAD_DIM, HEAD_DIM), HEAD_DIM)
        query, key, value = query_ref[:, cols], key_ref[:, cols], value_ref[:, cols]
        grad = attended_grad[:, cols]
        scores = product_nt(query, key) * score_scale + level_mask_ref[...]
        scores = jnp.where((col_id >= tok_rows) | (row_id >= col_id), scores, -jnp.inf)
        weights = jnp.exp(scores - log_total_ref[h])
        weight_grad = product_nt(grad, value)
        center = jnp.sum(weights * weight_grad, 1, keepdims=True)
        score_grad = (weights * (weight_grad - center)).astype(bf16)
        query_grad[:, cols] = product(score_grad, key) * score_scale
        kv_path[:, cols] = (product_tn(score_grad, query) * score_scale).astype(bf16)
        kv_path[:, value_cols] = product_tn(weights.astype(bf16), grad).astype(bf16)
        return carry

    lax.fori_loop(0, 2, head, 0)
    for z in range(4):
        out_sum.after_first(z)
    w_sum.after_core(0)
    lax.fori_loop(2, 4, head, 0)

    def kv_blocks(q, c):
        y, x = q // 2, q % 2
        segment = 4 * y + 2 * x + c
        total = jnp.zeros((tok_rows, 2 * local_width), f32)
        for level in range(1, LEVELS):
            spot = level_spots_ref[segment * LEVELS + level]
            total = total + spot * kv_path[level * tok_rows : (level + 1) * tok_rows].astype(f32)
        kv_sums[c, y, x] = total.astype(bf16)
        return c

    lax.fori_loop(0, 4, kv_blocks, flip(core))
    kv_sum.start(0)
    lax.fori_loop(0, 4, kv_blocks, core)
    own_kv = kv_sums.at[core, north, east]
    own_kv[...] = (own_kv[...].astype(f32) + kv_path[0:tok_rows].astype(f32)).astype(bf16)
    kv_sum.after_core(0)

    def cast_pre(which, grad):
        low = grad.astype(bf16)
        pre_grads[which] = low
        bias = jnp.sum(low.astype(f32), 0, keepdims=True)
        for h in range(local_width // HEAD_DIM):
            small_send[0, 4 * which + h : 4 * which + h + 1, 2 * HEAD_DIM :] = bias[
                :, h * HEAD_DIM : (h + 1) * HEAD_DIM
            ]

    small_send[0, :, 2 * HEAD_DIM :] = jnp.zeros((16, HEAD_DIM), f32)
    cast_pre(0, unturn(query_grad[...], cosine_ref[...], sine_ref[...]))

    def query_weights(i, carry):
        c, y, x = block_index(i)
        window = pl.ds(pl.multiple_of(i * tok_rows, tok_rows), tok_rows)
        w_sums[1, c, y, x] = product_tn(normed_ref[:, window], pre_grads[0]).astype(bf16)
        return carry

    lax.fori_loop(0, 8, query_weights, 0)
    w_sum.start(1)
    part[...] = product_nt(pre_grads[0], w_qkv[0])
    kv_sum.after_first(0)

    def out_level(k):
        return remote(
            out_mine.at[other(column, k), north, east],
            out_z.at[k],
            out_sems,
            (0, k),
            levels[k],
        )

    w_sum.after_first(0)
    for z in range(4):
        out_sum.after_second(z)
    for k in (3, 2, 1):
        out_level(k).start()
    w_sum.after_core(1)

    own_kv = kv_sum.after_second(0)
    cast_pre(1, unturn(own_kv[:, :local_width].astype(f32), cosine_ref[...], sine_ref[...]))
    cast_pre(2, own_kv[:, local_width:].astype(f32))
    load_value.wait()
    for which in (1, 2):
        part[...] += product_nt(pre_grads[which], w_qkv[which])

    hidden_f = hidden_ref[...].astype(f32)
    unit_scale = lax.rsqrt(jnp.mean(hidden_f * hidden_f, 1, keepdims=True) + epsilon)
    part_send[...] = part[...].astype(bf16).reshape(4, rows, width)

    def part_copy(k):
        return remote(part_send.at[other(column, k)], part_z.at[k], part_sems, (k,), levels[k])

    for k in (3, 2, 1):
        part_copy(k).start()
    attn_gain_row = jnp.sum(part[...] * (hidden_f * unit_scale), 0, keepdims=True)

    kv_sum.wait_sends(0)

    def key_value_weights(i, carry):
        c, y, x = block_index(i)
        window = pl.ds(pl.multiple_of(i * tok_rows, tok_rows), tok_rows)
        lhs = normed_ref[:, window]
        kv_sums[c, y, x, :, :local_width] = product_tn(lhs, pre_grads[1]).astype(bf16)
        kv_sums[c, y, x, :, local_width:] = product_tn(lhs, pre_grads[2]).astype(bf16)
        return carry

    lax.fori_loop(0, 8, key_value_weights, 0)
    wkv_sum.start(0)

    bias_rows = small_send[0, :, 2 * HEAD_DIM :]
    for d in range(8):
        small_send[d, :, : 2 * HEAD_DIM] = small_ref[:, d * tok_rows : (d + 1) * tok_rows]
        small_send[d, gain_row : gain_row + 1, : 2 * HEAD_DIM] = attn_gain_row[
            :, d * tok_rows : (d + 1) * tok_rows
        ]
        small_send[d, :, 2 * HEAD_DIM :] = bias_rows

    def small_copy(j):
        return remote(
            small_send.at[other(place, j)], small_got.at[j], small_sems, (j,), peers[j]
        )

    for j in range(1, 8):
        small_copy(j).start()

    def shared_copy(j):
        return remote(
            shared_ref.at[other(place, j)], shared_got.at[place], shared_sems, (j,), peers[j]
        )

    w_sum.after_first(1)
    wkv_sum.after_core(0)
    grad_out_ref[...] = w_sum.after_second(0)[...].astype(f32)
    for j in (6, 7, 2, 3, 4, 5, 1):
        shared_copy(j).start()
    own_shared = pltpu.make_async_copy(shared_ref.at[place], shared_got.at[place], load_sems.at[8])
    own_shared.start()

    total = small_send[place]
    for j in range(1, 8):
        small_copy(j).wait_recv()
        total = total + small_got[j]
    bias_out_ref[...] = total[:, 2 * HEAD_DIM :]
    small_z[column] = total[:, : 2 * HEAD_DIM]
    own_small = small_z.at[column]
    small_levels = [
        remote(own_small, own_small, small_z_sems, (k,), levels[k]) for k in (1, 2, 3)
    ]
    for copy in small_levels:
        copy.start()

    mine = pl.ds(pl.multiple_of(column * rows, rows), rows)
    attn_grad = part_send[column].astype(f32)
    for k in (1, 2, 3):
        part_copy(k).wait_recv()
        attn_grad = attn_grad + part_z[k].astype(f32)
    own_hidden = hidden_ref[mine, :].astype(f32)
    own_scale = lax.rsqrt(jnp.mean(own_hidden * own_hidden, 1, keepdims=True) + epsilon)
    hidden_stage[0, column] = (
        res_grad_ref[...] + norm_back(attn_grad, own_hidden * own_scale, own_scale, gain_ref[...])
    ).astype(bf16)

    def end_copy(which, k):
        own = hidden_stage.at[which, column]
        return remote(own, own, end_sems, (which, k), levels[k])

    for k in (3, 2, 1):
        end_copy(0, k).start()

    out = residual_ref[...] + out_mine[column, north, east].astype(f32)
    for k in (1, 2, 3):
        out_level(k).wait_recv()
        out = out + out_z[k].astype(f32)
    hidden_stage[1, column] = out.astype(bf16)
    for k in (3, 2, 1):
        end_copy(1, k).start()

    wkv_sum.after_first(0)
    grad_query_ref[...] = w_sum.after_second(1)[...].astype(f32)
    for copy in small_levels:
        copy.wait_recv()
    small_out_ref[...] = (small_z[0] + small_z[1]) + (small_z[2] + small_z[3])
    own_wkv = wkv_sum.after_second(0)
    grad_key_ref[...] = own_wkv[:, :local_width].astype(f32)
    grad_value_ref[...] = own_wkv[:, local_width:].astype(f32)

    own_shared.wait()
    for j in range(1, 8):
        shared_copy(j).wait_recv()

    def store_shared(which):
        return pltpu.make_async_copy(
            shared_stage, grad_shared_ref.at[which], load_sems.at[9]
        )

    for which in range(3):
        units = shared_got[:, which].astype(f32)
        turned = units.reshape(-1, units.shape[-1]).T
        if which:
            store_shared(which - 1).wait()
        shared_stage[...] = turned
        store_shared(which).start()

    for k in (1, 2, 3):
        end_copy(0, k).wait_recv()
        end_copy(1, k).wait_recv()
    ends = [
        pltpu.make_async_copy(hidden_stage.at[0], hidden_grad_ref, load_sems.at[10]),
        pltpu.make_async_copy(hidden_stage.at[1], hidden_out_ref, load_sems.at[11]),
    ]
    for copy in ends:
        copy.start()
    store_shared(2).wait()
    for copy in ends:
        copy.wait()

    for copy in low_copies + small_levels:
        copy.wait_send()
    for z in range(4):
        out_sum.wait_sends(z)
    for k in (1, 2, 3):
        out_level(k).wait_send()
        part_copy(k).wait_send()
        end_copy(0, k).wait_send()
        end_copy(1, k).wait_send()
    for k in range(2):
        w_sum.wait_sends(k)
    wkv_sum.wait_sends(0)
    for j in range(1, 8):
        small_copy(j).wait_send()
        shared_copy(j).wait_send()


def back_layer(score_scale, gain_row, operands):
    (
        residual,
        res_grad,
        res_low,
        ffn_part,
        grad_shared,
        small,
        query,
        key,
        value,
        level_mask,
        level_spots,
        log_total,
        attended,
        normed,
        hidden,
        gain,
        cosine,
        sine,
        w_out,
        w_query,
        w_key,
        w_value,
    ) = operands
    rows, width = residual.shape
    tok_rows, local_width = query.shape
    units = grad_shared.shape[2]
    bf16, f32 = jnp.bfloat16, jnp.float32
    shape = jax.ShapeDtypeStruct
    vmem, anywhere = pl.BlockSpec(memory_space=pltpu.VMEM), pl.BlockSpec(memory_space=pl.ANY)
    smem = pl.BlockSpec(memory_space=pltpu.SMEM)
    dma = pltpu.SemaphoreType.DMA
    return pl.pallas_call(
        functools.partial(back_kernel, score_scale, gain_row),
        out_shape=[
            shape((4, rows, width), bf16),
            shape((4, rows, width), bf16),
            shape((tok_rows, local_width), f32),
            shape((tok_rows, local_width), f32),
            shape((tok_rows, local_width), f32),
            shape((tok_rows, local_width), f32),
            shape((3, tok_rows, 8 * units), f32),
            shape((16, tok_rows), f32),
            shape((16, HEAD_DIM), f32),
        ],
        in_specs=[vmem, vmem, vmem, anywhere, anywhere, vmem]
        + [vmem] * 4
        + [smem]
        + [vmem] * 7
        + [anywhere] * 4,
        out_specs=[anywhere] * 2 + [vmem] * 4 + [anywhere, vmem, vmem],
        scratch_shapes=[
            pltpu.VMEM((4, rows, width), bf16),
            pltpu.VMEM((3, width, local_width), bf16),
            pltpu.VMEM((4, 2, 2, rows, width), bf16),
            pltpu.VMEM((4, rows, width), bf16),
            pltpu.VMEM((2, 2, 2, tok_rows, 2 * local_width), bf16),
            pltpu.VMEM((2, 2, 2, 2, tok_rows, local_width), bf16),
            pltpu.VMEM((LEVELS * tok_rows, 2 * local_width), bf16),
            pltpu.VMEM((tok_rows, local_width), bf16),
            pltpu.VMEM((tok_rows, local_width), f32),
            pltpu.VMEM((3, tok_rows, local_width), bf16),
            pltpu.VMEM((tok_rows, width), f32),
            pltpu.VMEM((4, rows, width), bf16),
            pltpu.VMEM((4, rows, width), bf16),
            pltpu.VMEM((2, 4, rows, width), bf16),
            pltpu.VMEM((8, 3, units, tok_rows), bf16),
            pltpu.VMEM((tok_rows, 8 * units), f32),
            pltpu.VMEM((8, 16, 2 * HEAD_DIM + HEAD_DIM), f32),
            pltpu.VMEM((8, 16, 2 * HEAD_DIM + HEAD_DIM), f32),
            pltpu.VMEM((4, 16, 2 * HEAD_DIM), f32),
        ]
        + plane_scratch(4, rows, width)
        + plane_scratch(1, tok_rows, 2 * local_width)
        + plane_scratch(2, tok_rows, local_width)
        + plane_scratch(1, tok_rows, 2 * local_width)[5:]
        + [
            dma((12,)),
            dma((2, 4)),
            dma((2, 1, 4)),
            dma((2, 4)),
            dma((2, 2, 4)),
            dma((2, 8)),
            dma((2, 8)),
            dma((2, 4)),
        ],
        compiler_params=pltpu.CompilerParams(
            collective_id=1, has_side_effects=True, vmem_limit_bytes=63 * 2**20
        ),
        cost_estimate=pl.CostEstimate(
            flops=2 * 12 * 2**30, bytes_accessed=40 * 2**20, transcendentals=2**20
        ),
    )(*operands)


def on_device(
    hidden_in,
    out_grad,
    parents,
    routes,
    attn_gain,
    w_query,
    w_key,
    w_value,
    b_query,
    b_key,
    b_value,
    w_out,
    ffn_gain,
    w_router,
    shared_gate,
    shared_w_gate,
    shared_w_up,
    shared_w_down,
    expert_w_gate,
    expert_w_up,
    expert_w_down,
):
    tok_rows, model_width = hidden_in.shape
    devices = lax.axis_size("dp")
    columns = lax.axis_size("tensor")
    place, column = lax.axis_index("dp"), lax.axis_index("tensor")
    all_rows = tok_rows * devices
    part_rows = tok_rows // columns
    local_width = w_query.shape[1]
    experts = w_router.shape[1]
    top_count = routes.shape[1]
    capacity = 5 * tok_rows * top_count // 4
    score_scale = HEAD_DIM ** (-0.5)
    bf16, f32 = jnp.bfloat16, jnp.float32

    expert_units = expert_w_gate.shape[2]
    shared_units = shared_w_gate.shape[1] // devices
    shared_pad = -(-shared_units // 128) * 128
    units = shared_pad + expert_units
    units_pad = -(-(units + experts + 1) // 128) * 128

    def own_units(matrix):
        return lax.dynamic_slice_in_dim(matrix, place * shared_units, shared_units, 1)

    def pad_to(matrix, columns):
        return jnp.pad(matrix, ((0, 0), (0, columns - matrix.shape[1])))

    def side_by_side(shared, expert):
        joined = jnp.concatenate([pad_to(own_units(shared), shared_pad), expert[0]], 1)
        return joined

    w_pre = jnp.concatenate(
        [
            pad_to(
                jnp.concatenate(
                    [side_by_side(shared_w_gate, expert_w_gate), w_router, shared_gate[:, None]], 1
                ),
                units_pad,
            ),
            pad_to(side_by_side(shared_w_up, expert_w_up), units_pad),
        ],
        1,
    )
    w_down = pad_to(side_by_side(shared_w_down, expert_w_down), units_pad)

    out_all = gather_dp(out_grad)

    routes_all = lax.all_gather(routes, "dp", axis=0, tiled=True)
    pair_onehot = routes_all[:, :, None] == jnp.arange(experts, dtype=jnp.int32)[None, None, :]
    hits = jnp.any(pair_onehot, 1)
    hit_blocks = hits.astype(bf16).reshape(devices, tok_rows, experts)
    below = (
        jnp.arange(tok_rows)[None, :] < jnp.arange(tok_rows)[:, None]
    ).astype(bf16)
    within = jnp.einsum("ij,bje->bie", below, hit_blocks, preferred_element_type=f32)
    block_sums = jnp.sum(hit_blocks.astype(f32), 1)
    before = jnp.cumsum(block_sums, 0) - block_sums
    slots = (within + before[:, None, :]).reshape(all_rows, experts)
    kept = (hits & (slots < capacity)).astype(f32)

    path = path_of(parents, place * tok_rows // SEG)
    reachable = path >= 0
    path_rows = jnp.maximum(path, 0)
    row_ids = jnp.arange(tok_rows, dtype=jnp.int32)
    depth = jnp.sum(reachable.astype(f32)) - 1.0
    cosine, sine = rope_tables(depth * SEG + row_ids.astype(f32))
    allowed = jnp.concatenate(
        [
            row_ids[:, None] >= row_ids[None, :],
            jnp.broadcast_to(
                jnp.repeat(reachable[1:], tok_rows)[None, :], (tok_rows, (LEVELS - 1) * tok_rows)
            ),
        ],
        1,
    )
    hidden_f = hidden_in.astype(f32)
    attn_scale, attn_unit = norm_parts(hidden_f)
    attn_normed = (attn_unit * attn_gain).astype(bf16)
    query_rot = turn_heads(
        product(attn_normed, w_query) + b_query.reshape(-1), cosine, sine, 1.0
    ).astype(bf16)
    key_rot = turn_heads(
        product(attn_normed, w_key) + b_key.reshape(-1), cosine, sine, 1.0
    ).astype(bf16)
    value_rows = (product(attn_normed, w_value) + b_value.reshape(-1)).astype(bf16)
    gathered = gather_dp(jnp.concatenate([key_rot, value_rows], 1))
    kv_blocks = gathered.reshape(devices, tok_rows, 2 * local_width)
    kv_path = jnp.take(kv_blocks, path_rows, axis=0).reshape(LEVELS * tok_rows, 2 * local_width)
    key_path, value_path = kv_path[:, :local_width], kv_path[:, local_width:]
    attended, log_total = attend_forward(query_rot, key_path, value_path, allowed, score_scale)
    attended_low = attended.astype(bf16)
    attn_part = product_nt(attended_low, w_out).astype(bf16)

    hidden_own = lax.dynamic_slice_in_dim(hidden_in, column * part_rows, part_rows, 0)
    grad_own = lax.dynamic_slice_in_dim(out_grad, column * part_rows, part_rows, 0)
    layout = (shared_units, shared_pad, expert_units, experts, units_pad)
    cube = devices == 8 and columns == 4
    if cube and all_rows * model_width <= 2**22:
        kept_own = jnp.sum(jnp.where(jnp.arange(experts)[None, :] == place, kept, 0.0), 1)
        kept_own = kept_own.reshape(2, 2, 2, columns, part_rows).transpose(3, 2, 0, 1, 4)
        (
            residual,
            residual_grad,
            residual_low,
            ffn_part,
            grad_expert_gate,
            grad_expert_up,
            grad_expert_down,
            grad_shared,
            small,
        ) = ffn_layer(
            attn_part.reshape(columns, part_rows, model_width),
            hidden_own,
            grad_own,
            ffn_gain[None, :],
            kept_own.reshape(columns, 2, 4 * part_rows, 1),
            out_all.reshape(2, 2, 2, columns, part_rows, model_width),
            w_pre,
            w_down,
            layout,
        )
        spots = jnp.where(reachable[None, :], path[None, :], -1) == jnp.arange(devices)[:, None]
        level_mask = jnp.repeat(jnp.where(reachable, 0.0, -jnp.inf), tok_rows)[None, :]
        sign = jnp.where(jnp.arange(HEAD_DIM) < HEAD_DIM // 2, -1.0, 1.0)
        (
            hidden_out,
            hidden_in_grad,
            sum_query,
            sum_key,
            sum_value,
            sum_out,
            shared_grads,
            small,
            bias_sums,
        ) = back_layer(
            score_scale,
            experts + 2,
            (
                residual,
                residual_grad,
                residual_low,
                ffn_part,
                grad_shared,
                small,
                query_rot,
                key_path,
                value_path,
                level_mask,
                spots.astype(f32).reshape(-1),
                log_total,
                attended_low,
                attn_normed,
                hidden_in,
                attn_gain[None, :],
                cosine[:, 0],
                sine[:, 0] * sign[None, :],
                w_out,
                w_query,
                w_key,
                w_value,
            ),
        )
        hidden_out = hidden_out.reshape(tok_rows, model_width)
        hidden_in_grad = hidden_in_grad.reshape(tok_rows, model_width)
        small = small.T
        bias_sums = lax.dynamic_slice_in_dim(
            bias_sums[: 3 * b_query.shape[0]].reshape(3, *b_query.shape),
            place * (HEAD_DIM // devices),
            HEAD_DIM // devices,
            2,
        )
        return (
            hidden_out,
            hidden_in_grad,
            small[:, experts + 2],
            sum_query,
            sum_key,
            sum_value,
            bias_sums[0],
            bias_sums[1],
            bias_sums[2],
            sum_out,
            small[:, experts + 1],
            small[:, :experts],
            small[:, experts],
            shared_grads[0],
            shared_grads[1],
            shared_grads[2],
            grad_expert_gate[None],
            grad_expert_up[None],
            grad_expert_down[None],
        )

    (
        residual,
        residual_grad,
        residual_low,
        ffn_part,
        grad_expert_gate,
        grad_expert_up,
        grad_expert_down,
        grad_shared,
        grad_side,
        grad_ffn_gain,
    ) = ffn_plain(
        attn_part, hidden_own, grad_own, ffn_gain, kept, out_all, w_pre, w_down, layout
    )
    grad_shared = grad_shared[:, :, :shared_units]
    ffn_own = scatter_all(ffn_part).astype(f32)
    hidden_out = gather_tensor((residual + ffn_own).astype(bf16))
    residual_low = gather_tensor(residual_low)
    grad_out_proj = product_tn(residual_low, attended_low)
    attended_grad = product(residual_low, w_out).astype(bf16)

    query_grad, key_grad, value_grad = attend_backward(
        query_rot, key_path, value_path, allowed, log_total, attended_grad, score_scale
    )
    kv_grad = jnp.concatenate([key_grad, value_grad], 1).reshape(
        LEVELS, tok_rows, 2 * local_width
    )
    kv_all = jnp.zeros((devices, tok_rows, 2 * local_width), f32)
    for level in range(LEVELS):
        kv_all = kv_all.at[path_rows[level]].add(kv_grad[level])
    kv_own = scatter_dp(
        kv_all.reshape(all_rows, 2 * local_width).astype(bf16)
    ).astype(f32)
    query_pre_grad = turn_heads(query_grad, cosine, sine, -1.0).astype(bf16)
    key_pre_grad = turn_heads(kv_own[:, :local_width], cosine, sine, -1.0).astype(bf16)
    value_pre_grad = kv_own[:, local_width:].astype(bf16)
    qkv_pre_grad = jnp.concatenate([query_pre_grad, key_pre_grad, value_pre_grad], 1)
    grad_qkv = product_tn(attn_normed, qkv_pre_grad)
    bias_grads = jnp.sum(qkv_pre_grad.astype(f32), 0).reshape(3, -1, HEAD_DIM)
    attn_part_grad = (
        product_nt(query_pre_grad, w_query)
        + product_nt(key_pre_grad, w_key)
        + product_nt(value_pre_grad, w_value)
    )
    grad_attn_gain = jnp.sum(attn_part_grad * attn_unit, 0)
    attn_own_grad = scatter_tensor(attn_part_grad.astype(bf16)).astype(f32)
    own_rows = lambda array: lax.dynamic_slice_in_dim(
        array, column * part_rows, part_rows, 0
    )
    hidden_in_grad = gather_tensor(
        (
            residual_grad
            + norm_back(attn_own_grad, own_rows(attn_unit), own_rows(attn_scale), attn_gain)
        ).astype(bf16)
    )

    small = jnp.concatenate(
        [grad_side, grad_ffn_gain[:, None], grad_attn_gain[:, None]], 1
    )
    small = scatter_dp(lax.psum(small, "tensor"))
    bias_sums = lax.psum_scatter(bias_grads, "dp", scatter_dimension=2, tiled=True)
    grad_attn = scatter_dp(jnp.concatenate([grad_qkv, grad_out_proj], 1).astype(bf16)).astype(f32)
    shared_grads = lax.all_to_all(
        grad_shared, "dp", split_axis=1, concat_axis=2, tiled=True
    ).astype(f32)
    return (
        hidden_out,
        hidden_in_grad,
        small[:, experts + 2],
        grad_attn[:, :local_width],
        grad_attn[:, local_width : 2 * local_width],
        grad_attn[:, 2 * local_width : 3 * local_width],
        bias_sums[0],
        bias_sums[1],
        bias_sums[2],
        grad_attn[:, 3 * local_width :],
        small[:, experts + 1],
        small[:, :experts],
        small[:, experts],
        shared_grads[0],
        shared_grads[1],
        shared_grads[2],
        grad_expert_gate[None],
        grad_expert_up[None],
        grad_expert_down[None],
    )


def solution(mesh):
    return jax.shard_map(
        on_device,
        mesh=mesh,
        in_specs=(
            P("dp", None),
            P("dp", None),
            P(),
            P("dp", None),
            P(),
            P(None, "tensor"),
            P(None, "tensor"),
            P(None, "tensor"),
            P("tensor", None),
            P("tensor", None),
            P("tensor", None),
            P(None, "tensor"),
            P(),
            P(),
            P(),
            P(None, "tensor"),
            P(None, "tensor"),
            P(None, "tensor"),
            P("dp", None, "tensor"),
            P("dp", None, "tensor"),
            P("dp", None, "tensor"),
        ),
        out_specs=(
            P("dp", None),
            P("dp", None),
            P("dp"),
            P("dp", "tensor"),
            P("dp", "tensor"),
            P("dp", "tensor"),
            P("tensor", "dp"),
            P("tensor", "dp"),
            P("tensor", "dp"),
            P("dp", "tensor"),
            P("dp"),
            P("dp", None),
            P("dp"),
            P("dp", "tensor"),
            P("dp", "tensor"),
            P("dp", "tensor"),
            P("dp", None, "tensor"),
            P("dp", None, "tensor"),
            P("dp", None, "tensor"),
        ),
        check_vma=False,
    )
```

```python
import functools

import jax
import jax.numpy as jnp
from jax import lax
from jax.experimental import pallas as pl
from jax.experimental.pallas import tpu as pltpu
from jax.sharding import PartitionSpec as P

HEAD_DIM = 128
SEG = 256
MESH = pl.DeviceIdType.MESH


epsilon = 1e-06
rope_base = 1000000.0
highest = lax.Precision.HIGHEST


def product(left, right):
    return jnp.dot(left, right, preferred_element_type=jnp.float32)


def product_tn(left, right):
    return lax.dot_general(
        left, right, (((0,), (0,)), ((), ())), preferred_element_type=jnp.float32
    )


def product_nt(left, right):
    return lax.dot_general(
        left, right, (((1,), (1,)), ((), ())), preferred_element_type=jnp.float32
    )


def ancestry(parents):
    seg_count = parents.shape[0]
    labels = jnp.arange(seg_count, dtype=jnp.int32)

    def climb(level, carry):
        current, reach = carry
        upward = jnp.where(current >= 0, parents[jnp.maximum(current, 0)], -1)
        reach = jnp.maximum(reach, (upward[:, None] == labels[None, :]).astype(jnp.float32))
        return (upward, reach)

    start = (labels, jnp.eye(seg_count, dtype=jnp.float32))
    return lax.fori_loop(0, seg_count, climb, start)[1]


def rope_tables(positions):
    freqs = rope_base ** (-jnp.arange(0, HEAD_DIM, 2, dtype=jnp.float32) / HEAD_DIM)
    angles = positions[:, None] * freqs[None, :]
    angles = jnp.concatenate([angles, angles], 1)
    return (jnp.cos(angles)[:, None, :], jnp.sin(angles)[:, None, :])


def turn_heads(matrix, cosine, sine, sign_value):
    shaped = matrix.reshape(matrix.shape[0], matrix.shape[1] // HEAD_DIM, HEAD_DIM)
    half = HEAD_DIM // 2
    turned = jnp.concatenate([-shaped[..., half:], shaped[..., :half]], -1)
    return (shaped * cosine + sign_value * turned * sine).reshape(matrix.shape)


def norm_parts(values):
    scale_rows = lax.rsqrt(jnp.mean(values * values, 1, keepdims=True) + epsilon)
    return (scale_rows, values * scale_rows)


def norm_back(grad_rows, unit_rows, scale_rows, gain):
    unit_grad = grad_rows * gain
    return scale_rows * (unit_grad - unit_rows * jnp.mean(unit_grad * unit_rows, 1, keepdims=True))


LEVELS = 4


def gather_dp(rows):
    return lax.all_gather(rows, "dp", axis=0, tiled=True)


def gather_tensor(rows):
    return lax.all_gather(rows, "tensor", axis=0, tiled=True)


def gather_all(rows):
    return gather_dp(gather_tensor(rows))


def scatter_dp(rows):
    return lax.psum_scatter(rows, "dp", scatter_dimension=0, tiled=True)


def scatter_tensor(rows):
    return lax.psum_scatter(rows, "tensor", scatter_dimension=0, tiled=True)


def scatter_all(rows):
    return scatter_tensor(scatter_dp(rows))


def path_of(parents, segment):
    path = [segment]
    for _ in range(LEVELS - 1):
        last = path[-1]
        path.append(jnp.where(last >= 0, parents[jnp.maximum(last, 0)], -1))
    return jnp.stack(path)


def heads_of(matrix):
    return matrix.reshape(matrix.shape[0], -1, HEAD_DIM)


def attend_forward(query_rot, key_path, value_path, allowed, score_scale):
    scores = (
        jnp.einsum(
            "qhd,khd->hqk",
            heads_of(query_rot),
            heads_of(key_path),
            preferred_element_type=jnp.float32,
        )
        * score_scale
    )
    scores = jnp.where(allowed[None], scores, -jnp.inf)
    peak = jnp.max(scores, 2, keepdims=True)
    log_total = peak + jnp.log(jnp.sum(jnp.exp(scores - peak), 2, keepdims=True))
    weights = jnp.exp(scores - log_total).astype(jnp.bfloat16)
    attended = jnp.einsum(
        "hqk,khd->qhd", weights, heads_of(value_path), preferred_element_type=jnp.float32
    )
    return attended.reshape(query_rot.shape), log_total


def attend_backward(
    query_rot, key_path, value_path, allowed, log_total, attended_grad, score_scale
):
    query, key, value = heads_of(query_rot), heads_of(key_path), heads_of(value_path)
    grad = heads_of(attended_grad)
    scores = jnp.einsum("qhd,khd->hqk", query, key, preferred_element_type=jnp.float32)
    weights = jnp.exp(jnp.where(allowed[None], scores * score_scale, -jnp.inf) - log_total)
    weight_grad = jnp.einsum("qhd,khd->hqk", grad, value, preferred_element_type=jnp.float32)
    center = jnp.sum(weights * weight_grad, 2, keepdims=True)
    score_grad = (weights * (weight_grad - center)).astype(jnp.bfloat16)
    query_grad = (
        jnp.einsum("hqk,khd->qhd", score_grad, key, preferred_element_type=jnp.float32)
        * score_scale
    )
    key_grad = (
        jnp.einsum("hqk,qhd->khd", score_grad, query, preferred_element_type=jnp.float32)
        * score_scale
    )
    value_grad = jnp.einsum(
        "hqk,qhd->khd",
        weights.astype(jnp.bfloat16),
        grad,
        preferred_element_type=jnp.float32,
    )
    return (
        query_grad.reshape(query_rot.shape),
        key_grad.reshape(key_path.shape),
        value_grad.reshape(value_path.shape),
    )


def ffn_plain(attn_part, hidden_own, grad_own, ffn_gain, kept, out_all, w_pre, w_down, layout):
    _, shared_pad, expert_units, experts, units_pad = layout
    units = shared_pad + expert_units
    bf16, f32 = jnp.bfloat16, jnp.float32
    place, column = lax.axis_index("dp"), lax.axis_index("tensor")
    columns, part_rows = lax.axis_size("tensor"), hidden_own.shape[0]
    out_own = grad_own.astype(f32)
    residual = hidden_own.astype(f32) + scatter_tensor(attn_part).astype(f32)
    ffn_scale, ffn_unit = norm_parts(residual)
    ffn_normed = (ffn_unit * ffn_gain).astype(bf16)
    normed_all = gather_all(ffn_normed)

    pre = product(normed_all, w_pre)
    pre_gate, pre_up = pre[:, :units_pad], pre[:, units_pad:]
    logits = pre[:, units : units + experts]
    probs = jax.nn.softmax(logits, 1)
    shared_weight = jax.nn.sigmoid(pre[:, units + experts])
    own_expert = jnp.arange(experts, dtype=jnp.int32)[None, :] == place
    gate_own = jnp.sum(jnp.where(own_expert, probs * kept, 0.0), 1)
    lane = jnp.arange(units_pad)[None, :]
    weight = jnp.where(
        lane < shared_pad,
        shared_weight[:, None],
        jnp.where(lane < units, gate_own[:, None], 0.0),
    )
    down_back = product(out_all, w_down)
    sigmoid_gate = jax.nn.sigmoid(pre_gate)
    hidden = (pre_gate * sigmoid_gate * pre_up).astype(bf16).astype(f32)
    hidden_scaled = (hidden * weight).astype(bf16)
    hidden_grad = down_back * weight
    up_rows = (hidden_grad * pre_gate * sigmoid_gate).astype(bf16)
    gate_rows = (
        hidden_grad * pre_up * sigmoid_gate * (1.0 + pre_gate * (1.0 - sigmoid_gate))
    ).astype(bf16)
    both_rows = jnp.concatenate([gate_rows, up_rows], 1)
    dots = hidden * down_back
    gate_dot = jnp.sum(jnp.where((lane >= shared_pad) & (lane < units), dots, 0.0), 1)
    shared_dot = jnp.sum(jnp.where(lane < shared_pad, dots, 0.0), 1)
    dot_parts = jnp.concatenate(
        [jnp.where(own_expert, gate_dot[:, None] * kept, 0.0), shared_dot[:, None]], 1
    )
    ffn_part = product_nt(hidden_scaled, w_down).astype(bf16)
    normed_part = product_nt(both_rows, w_pre).astype(bf16)
    grad_pre = product_tn(normed_all, both_rows)
    grad_down = product_tn(out_all, hidden_scaled)

    dot_own = scatter_all(dot_parts)
    normed_own = scatter_all(normed_part).astype(f32)

    first = (place * columns + column) * part_rows
    own = lambda array: lax.dynamic_slice_in_dim(array, first, part_rows, 0)
    probs_own, shared_own = own(probs), own(shared_weight)
    prob_grad = dot_own[:, :experts]
    logit_grad = (
        probs_own * (prob_grad - jnp.sum(probs_own * prob_grad, 1, keepdims=True))
    ).astype(bf16)
    weight_logit_grad = (dot_own[:, experts] * shared_own * (1.0 - shared_own)).astype(bf16)
    side_grad = jnp.concatenate([logit_grad, weight_logit_grad[:, None]], 1)
    side_w = w_pre[:, units : units + experts + 1]
    normed_grad = normed_own + product_nt(side_grad, side_w)
    grad_side = product_tn(ffn_normed, side_grad)
    grad_ffn_gain = jnp.sum(normed_grad * ffn_unit, 0)
    residual_grad = out_own + norm_back(normed_grad, ffn_unit, ffn_scale, ffn_gain)
    expert = slice(shared_pad, units)
    expert_up = slice(units_pad + shared_pad, units_pad + units)
    grad_shared = jnp.stack(
        [
            grad_pre[:, : shared_pad],
            grad_pre[:, units_pad : units_pad + shared_pad],
            grad_down[:, : shared_pad],
        ]
    ).astype(bf16)
    return (
        residual,
        residual_grad,
        residual_grad.astype(bf16),
        ffn_part,
        grad_pre[:, expert],
        grad_pre[:, expert_up],
        grad_down[:, expert],
        grad_shared,
        grad_side,
        grad_ffn_gain,
    )


def flip(bit):
    return 1 - bit


def other(index, step):
    result, place = index, 1
    while place <= step:
        if step & place:
            result = result + place - 2 * place * ((index // place) % 2)
        place *= 2
    return result


def ffn_kernel(
    units,
    residual_ref,
    gain_ref,
    hits_ref,
    grad_all_ref,
    w_pre_ref,
    w_down_ref,
    res_grad_ref,
    res_low_ref,
    ffn_part_ref,
    e_gate_ref,
    e_up_ref,
    e_down_ref,
    shared_ref,
    small_ref,
    rows_all,
    dy_all,
    w_pre,
    w_down,
    both_all,
    scaled_all,
    sums,
    got_core,
    got_x1,
    got_y1,
    got_y2,
    got_x2,
    got_z,
    kept_ref,
    ffn_chunk,
    tile_gate,
    tile_up,
    tile_down,
    tile_shared,
    load_sems,
    store_sems,
    tile_sems,
    zs,
    links,
    cores,
    rs_core,
    rs_links,
    rs_z,
):
    shared_units, shared_pad, expert_units, experts, unit_pad, half, wide, capacity = units
    bf16, f32 = jnp.bfloat16, jnp.float32
    place, column = lax.axis_index("dp"), lax.axis_index("tensor")
    core, east, north = place % 2, (place // 2) % 2, place // 4
    rows, width = residual_ref.shape
    sibling = {"dp": other(place, 1)}
    x_side = {"dp": other(place, 2)}
    y_side = {"dp": other(place, 4)}
    levels = [{"tensor": other(column, k)} for k in range(4)]

    def level_of(k):
        low_i, high_i, low_k, high_k = column % 2, column // 2, k % 2, k // 2
        return (low_i + low_k - 2 * low_i * low_k) + 2 * (high_i + high_k - 2 * high_i * high_k)

    def remote(src, dst, sems, which, device):
        return pltpu.make_async_remote_copy(
            src_ref=src,
            dst_ref=dst,
            send_sem=sems.at[(0, *which)],
            recv_sem=sems.at[(1, *which)],
            device_id=device,
            device_id_type=MESH,
        )

    load_pre = pltpu.make_async_copy(w_pre_ref, w_pre, load_sems.at[0])
    load_down = pltpu.make_async_copy(w_down_ref, w_down, load_sems.at[1])
    load_pre.start()
    load_down.start()

    def load_grad(c, z):
        return pltpu.make_async_copy(
            grad_all_ref.at[:, :, c, z], dy_all.at[z, c], load_sems.at[2 + c * 4 + z]
        )

    for c in range(2):
        for z in range(4):
            load_grad(c, z).start()

    barrier = pltpu.get_barrier_semaphore()
    partners = [sibling, x_side, y_side] + levels[1:]
    for partner in partners:
        pl.semaphore_signal(barrier, inc=1, device_id=partner, device_id_type=MESH)
    pl.semaphore_wait(barrier, len(partners))

    residual = residual_ref[...]
    scale_rows = lax.rsqrt(jnp.mean(residual * residual, 1, keepdims=True) + epsilon)
    normed = (residual * scale_rows * gain_ref[...]).astype(bf16)
    rows_all[column, core, north, east] = normed

    own_slot = rows_all.at[column, core, north, east]

    def z_copy(k):
        return remote(own_slot, own_slot, zs, (k,), levels[k])

    def block(k, c, y, x, cols=slice(None)):
        return rows_all.at[level_of(k), c, y, x, :, cols]

    first_half, second_half = pl.ds(0, half), pl.ds(half, width - half)

    def direct_copies(k):
        own = block(k, core, north, east)
        return [
            remote(own, own, links, (0, k), x_side),
            remote(own, own, links, (1, k), y_side),
            remote(own, own, cores, (0, k), sibling),
        ]

    def forward_copies(k):
        from_x = block(k, core, north, flip(east), first_half)
        from_y = block(k, core, flip(north), east, second_half)
        all_x = block(k, core, north, flip(east))
        all_y = block(k, core, flip(north), east)
        return [
            remote(from_x, from_x, links, (2, k), y_side),
            remote(from_y, from_y, links, (3, k), x_side),
            remote(all_x, all_x, cores, (1, k), sibling),
            remote(all_y, all_y, cores, (2, k), sibling),
        ]

    def corner_copy(k):
        corner = block(k, core, flip(north), flip(east))
        return remote(corner, corner, cores, (3, k), sibling)

    def start_direct(k):
        for copy in direct_copies(k):
            copy.start()

    def start_forward(k):
        for copy in direct_copies(k)[:2]:
            copy.wait_recv()
        for copy in forward_copies(k):
            copy.start()

    def start_corner(k):
        for copy in forward_copies(k)[:2]:
            copy.wait_recv()
        corner_copy(k).start()

    def finish_gather(k):
        direct_copies(k)[2].wait_recv()
        for copy in forward_copies(k)[2:]:
            copy.wait_recv()
        corner_copy(k).wait_recv()

    def core_copy(k):
        return remote(sums.at[k, flip(core)], got_core.at[k], rs_core, (k,), sibling)

    left, right = pl.ds(0, half), pl.ds(half, wide - half)

    def first_copies(k):
        return [
            remote(
                sums.at[k, core, :, flip(east), :, left],
                got_x1.at[k],
                rs_links, (0, k),
                x_side,
            ),
            remote(
                sums.at[k, core, flip(north), :, :, right],
                got_y1.at[k],
                rs_links, (1, k),
                y_side,
            ),
        ]

    def second_copies(k):
        return [
            remote(
                sums.at[k, core, flip(north), east, :, left],
                got_y2.at[k],
                rs_links, (2, k),
                y_side,
            ),
            remote(
                sums.at[k, core, north, flip(east), :, right],
                got_x2.at[k],
                rs_links, (3, k),
                x_side,
            ),
        ]

    def level_copy(k, device):
        return remote(sums.at[k, core, north, east], got_z.at[k], rs_z, (k,), device)

    def add(ref, value):
        ref[...] = (ref[...].astype(f32) + value.astype(f32)).astype(bf16)

    def after_core(k):
        core_copy(k).wait_recv()
        for y in range(2):
            for x in range(2):
                add(sums.at[k, core, y, x], got_core[k, y, x])
        for copy in first_copies(k):
            copy.start()

    def after_first(k):
        x_copy, y_copy = first_copies(k)
        x_copy.wait_recv()
        for y in range(2):
            add(sums.at[k, core, y, east, :, left], got_x1[k, y])
        y_copy.wait_recv()
        for x in range(2):
            add(sums.at[k, core, north, x, :, right], got_y1[k, x])
        for copy in second_copies(k):
            copy.start()

    def after_second(k):
        y_copy, x_copy = second_copies(k)
        y_copy.wait_recv()
        add(sums.at[k, core, north, east, :, left], got_y2[k])
        x_copy.wait_recv()
        add(sums.at[k, core, north, east, :, right], got_x2[k])
        for level in range(1, 4):

            @pl.when(k == level)
            def _():
                level_copy(k, levels[level]).start()

    for k in (1, 2, 3):
        z_copy(k).start()
    start_direct(0)

    tokens_dev = 4 * rows
    expert_id = lax.broadcasted_iota(jnp.int32, hits_ref.shape, 1)
    hits = jnp.sum(jnp.where(expert_id == place, hits_ref[...], 0.0), 1)
    earlier = lax.broadcasted_iota(jnp.int32, (tokens_dev, tokens_dev), 0)
    later = lax.broadcasted_iota(jnp.int32, (tokens_dev, tokens_dev), 1)
    slots = product(hits.astype(bf16), (earlier < later).astype(bf16))
    counts = jnp.sum(hits, 1, keepdims=True)
    counts_wide = jnp.broadcast_to(counts, (8, 128))
    order_row = lax.broadcasted_iota(jnp.int32, (8, 8), 0)
    order_col = lax.broadcasted_iota(jnp.int32, (8, 8), 1)
    before = lax.dot_general(
        (order_col < order_row).astype(f32),
        counts_wide,
        (((1,), (0,)), ((), ())),
        precision=highest,
        preferred_element_type=f32,
    )
    kept = jnp.where(slots + before[:, :1] < capacity, hits, 0.0).astype(bf16)
    eye = (
        lax.broadcasted_iota(jnp.int32, (8, 128), 0)
        == lax.broadcasted_iota(jnp.int32, (8, 128), 1)
    ).astype(bf16)
    kept_columns = product_tn(kept, eye)
    for d in range(8):
        y, x, c = d // 4, (d // 2) % 2, d % 2
        for z in range(4):
            first = (2 * y + x) * rows
            kept_ref[z, c, first : first + rows, :] = kept_columns[
                z * rows : (z + 1) * rows, d : d + 1
            ]

    load_pre.wait()
    load_down.wait()
    for c in range(2):
        for z in range(4):
            load_grad(c, z).wait()
    start_forward(0)
    z_copy(1).wait_recv()
    start_direct(1)
    start_corner(0)

    last = unit_pad - 128
    lane = lax.broadcasted_iota(jnp.int32, (1, 128), 1)
    first_lane = shared_pad + expert_units - last
    in_router = (lane >= first_lane) & (lane < first_lane + experts)
    is_shared = lane == first_lane + experts

    def routing(logit_block):
        top = jnp.max(jnp.where(in_router, logit_block, -jnp.inf), 1, keepdims=True)
        powers = jnp.where(in_router, jnp.exp(jnp.where(in_router, logit_block - top, 0.0)), 0.0)
        probs = powers / jnp.sum(powers, 1, keepdims=True)
        shared_logit = jnp.sum(jnp.where(is_shared, logit_block, 0.0), 1, keepdims=True)
        return probs, jax.nn.sigmoid(shared_logit)

    def compute(k, c):
        z = level_of(k)
        row_block = rows_all[z, c].reshape(4 * rows, width)
        dy_block = dy_all[z, c].reshape(4 * rows, width)
        pre_gate = product(row_block, w_pre[:, :unit_pad])
        pre_up = product(row_block, w_pre[:, unit_pad:])
        down_back = product(dy_block, w_down[...])
        probs, shared_weight = routing(pre_gate[:, last:])
        kept = kept_ref[z, c]
        gate = (
            jnp.sum(jnp.where(lane == first_lane + place, probs, 0.0), 1, keepdims=True) * kept
        )
        dots = []
        for begin, end, weight in (
            (0, shared_pad, shared_weight),
            (shared_pad, unit_pad, gate),
        ):
            cols = slice(begin, end)
            a, b, back = pre_gate[:, cols], pre_up[:, cols], down_back[:, cols]
            sig = jax.nn.sigmoid(a)
            silu = a * sig
            hidden = (silu * b).astype(bf16).astype(f32)
            dots.append(jnp.sum(hidden * back, 1, keepdims=True))
            scaled_all[z, c, :, begin:end] = (hidden * weight).astype(bf16)
            grad = back * weight
            both_all[z, c, :, unit_pad + begin : unit_pad + end] = (grad * silu).astype(bf16)
            both_all[z, c, :, begin:end] = (
                grad * b * sig * (1.0 + a * (1.0 - sig))
            ).astype(bf16)
        dot_block = jnp.where(is_shared, dots[0], 0.0) + jnp.where(
            lane == first_lane + place, dots[1] * kept, 0.0
        )
        normed_grad = product_nt(both_all[z, c], w_pre[...]).astype(bf16)
        sums[k, c, :, :, :, 0:width] = normed_grad.reshape(2, 2, rows, width)
        sums[k, c, :, :, :, width:wide] = dot_block.astype(bf16).reshape(2, 2, rows, wide - width)

    def store_chunk(k, c):
        return pltpu.make_async_copy(
            ffn_chunk, ffn_part_ref.at[level_of(k), c], store_sems.at[c]
        )

    def chunk(k, carry):
        @pl.when(k < 3)
        def _():
            start_forward(k + 1)

        @pl.when(k < 2)
        def _():
            for level in (2, 3):

                @pl.when(k + 2 == level)
                def _():
                    z_copy(level).wait_recv()

            start_direct(k + 2)

        finish_gather(k)
        def rows_of(i, carry):
            compute(k, (i + 1 + core) % 2)

            @pl.when(i == 0)
            def _():
                core_copy(k).start()

            return carry

        lax.fori_loop(0, 2, rows_of, 0)

        @pl.when(k >= 1)
        def _():
            after_first(k - 1)
            store_chunk(k - 1, 1).wait()

        def outputs(c, carry):
            part = product_nt(scaled_all[level_of(k), c], w_down[...]).astype(bf16)

            @pl.when(c == 1)
            def _():
                store_chunk(k, 0).wait()

            ffn_chunk[...] = part.reshape(2, 2, rows, width)
            store_chunk(k, c).start()
            return carry

        lax.fori_loop(0, 2, outputs, 0)

        @pl.when(k < 3)
        def _():
            start_corner(k + 1)

        after_core(k)

        @pl.when(k >= 1)
        def _():
            after_second(k - 1)

        return carry

    lax.fori_loop(0, 4, chunk, 0)
    store_chunk(3, 1).wait()

    tile = tile_gate.shape[1]
    tiles = width // tile

    def tile_copies(i, slot):
        window = pl.ds(pl.multiple_of(i * tile, tile), tile)
        return [
            pltpu.make_async_copy(tile_gate.at[slot], e_gate_ref.at[window], tile_sems.at[slot, 0]),
            pltpu.make_async_copy(tile_up.at[slot], e_up_ref.at[window], tile_sems.at[slot, 1]),
            pltpu.make_async_copy(tile_down.at[slot], e_down_ref.at[window], tile_sems.at[slot, 2]),
            pltpu.make_async_copy(
                tile_shared.at[slot], shared_ref.at[i], tile_sems.at[slot, 3]
            ),
        ]

    tokens = rows * 32

    def weight_tile(i, carry):
        slot = i % 2

        @pl.when(i >= 2)
        def _():
            for copy in tile_copies(i - 2, slot):
                copy.wait()

        window = pl.ds(pl.multiple_of(i * tile, tile), tile)
        expert = slice(shared_pad, shared_pad + expert_units)
        lhs = rows_all[:, :, :, :, :, window].reshape(tokens, tile)
        grad = product_tn(lhs, both_all[...].reshape(tokens, 2 * unit_pad))
        tile_gate[slot] = grad[:, expert]
        tile_shared[slot, 0] = grad[:, :shared_pad].T[:shared_units].astype(bf16)
        tile_up[slot] = grad[:, unit_pad + shared_pad : unit_pad + shared_pad + expert_units]
        tile_shared[slot, 1] = grad[:, unit_pad : unit_pad + shared_pad].T[:shared_units].astype(bf16)
        lhs = dy_all[:, :, :, :, :, window].reshape(tokens, tile)
        grad = product_tn(lhs, scaled_all[...].reshape(tokens, unit_pad))
        tile_down[slot] = grad[:, expert]
        tile_shared[slot, 2] = grad[:, :shared_pad].T[:shared_units].astype(bf16)
        for copy in tile_copies(i, slot):
            copy.start()

        @pl.when(i == 1)
        def _():
            after_first(3)

        @pl.when(i == 3)
        def _():
            after_second(3)

        return carry

    lax.fori_loop(0, tiles, weight_tile, 0)
    for i in (tiles - 2, tiles - 1):
        for copy in tile_copies(i, i % 2):
            copy.wait()

    total = sums[0, core, north, east].astype(f32)
    for k in (1, 2, 3):
        level_copy(k, levels[k]).wait_recv()
        total = total + got_z[k].astype(f32)
    dots = total[:, width:]
    unit = residual_ref[...] * scale_rows
    own_normed = rows_all[column, core, north, east]
    side_w = w_pre[:, last:unit_pad]
    probs, shared_weight = routing(product(own_normed, side_w))
    router_dots = jnp.where(in_router, dots, 0.0)
    center = jnp.sum(probs * router_dots, 1, keepdims=True)
    side = jnp.where(in_router, probs * (router_dots - center), 0.0) + jnp.where(
        is_shared, dots * shared_weight * (1.0 - shared_weight), 0.0
    )
    side = side.astype(bf16)
    normed_grad = total[:, :width] + product_nt(side, side_w)
    side_rows = product_tn(side, own_normed)
    small_ref[...] = side_rows[first_lane : first_lane + small_ref.shape[0]]
    small_ref[experts + 1 : experts + 2, :] = jnp.sum(normed_grad * unit, 0, keepdims=True)
    own_grad = dy_all[column, core, north, east].astype(f32)
    grad_f = own_grad + norm_back(normed_grad, unit, scale_rows, gain_ref[...])
    res_grad_ref[...] = grad_f
    res_low_ref[...] = grad_f.astype(bf16)

    for k in (1, 2, 3):
        z_copy(k).wait_send()
        level_copy(k, levels[k]).wait_send()
    for k in range(4):
        for copy in direct_copies(k) + forward_copies(k) + [corner_copy(k), core_copy(k)]:
            copy.wait_send()
        for copy in first_copies(k) + second_copies(k):
            copy.wait_send()


def ffn_layer(residual, ffn_gain, hits, grad_all, w_pre, w_down, layout, capacity):
    shared_units, shared_pad, expert_units, experts, unit_pad = layout
    rows, width = residual.shape
    bf16, f32 = jnp.bfloat16, jnp.float32
    half = width // 2
    wide = width + 128
    tile = 256
    shape = jax.ShapeDtypeStruct
    vmem, anywhere = pl.BlockSpec(memory_space=pltpu.VMEM), pl.BlockSpec(memory_space=pl.ANY)
    dma = pltpu.SemaphoreType.DMA
    cost = pl.CostEstimate(
        flops=2 * 24 * 2048 * 2048 * 256, bytes_accessed=60 * 2**20, transcendentals=3 * 2**20
    )
    return pl.pallas_call(
        functools.partial(
            ffn_kernel,
            (shared_units, shared_pad, expert_units, experts, unit_pad, half, wide, capacity),
        ),
        out_shape=[
            shape((rows, width), f32),
            shape((rows, width), bf16),
            shape((4, 2, 2, 2, rows, width), bf16),
            shape((width, expert_units), f32),
            shape((width, expert_units), f32),
            shape((width, expert_units), f32),
            shape((width // tile, 3, shared_units, tile), bf16),
            shape((16, width), f32),
        ],
        in_specs=[vmem, vmem, vmem, anywhere, anywhere, anywhere],
        out_specs=[vmem, vmem] + [anywhere] * 5 + [vmem],
        scratch_shapes=[
            pltpu.VMEM((4, 2, 2, 2, rows, width), bf16),
            pltpu.VMEM((4, 2, 2, 2, rows, width), bf16),
            pltpu.VMEM(w_pre.shape, bf16),
            pltpu.VMEM(w_down.shape, bf16),
            pltpu.VMEM((4, 2, 4 * rows, 2 * unit_pad), bf16),
            pltpu.VMEM((4, 2, 4 * rows, unit_pad), bf16),
            pltpu.VMEM((4, 2, 2, 2, rows, wide), bf16),
            pltpu.VMEM((4, 2, 2, rows, wide), bf16),
            pltpu.VMEM((4, 2, rows, half), bf16),
            pltpu.VMEM((4, 2, rows, wide - half), bf16),
            pltpu.VMEM((4, rows, half), bf16),
            pltpu.VMEM((4, rows, wide - half), bf16),
            pltpu.VMEM((4, rows, wide), bf16),
            pltpu.VMEM((4, 2, 4 * rows, 1), f32),
            pltpu.VMEM((2, 2, rows, width), bf16),
            pltpu.VMEM((2, tile, expert_units), f32),
            pltpu.VMEM((2, tile, expert_units), f32),
            pltpu.VMEM((2, tile, expert_units), f32),
            pltpu.VMEM((2, 3, shared_units, tile), bf16),
            dma((10,)),
            dma((2,)),
            dma((2, 4)),
            dma((2, 4)),
            dma((2, 4, 4)),
            dma((2, 4, 4)),
            dma((2, 4)),
            dma((2, 4, 4)),
            dma((2, 4)),
        ],
        compiler_params=pltpu.CompilerParams(
            collective_id=0, has_side_effects=True, vmem_limit_bytes=63 * 2**20
        ),
        cost_estimate=cost,
    )(residual, ffn_gain, hits, grad_all, w_pre, w_down)


def path_scalars(parents_ref, segment):
    path = [segment]
    for _ in range(LEVELS - 1):
        last = path[-1]
        parent = parents_ref[jnp.maximum(last, 0)]
        path.append(jnp.where(last >= 0, parent, -1))
    return path


class PlaneGather:
    def __init__(self, block, width, link_sems, core_sems):
        self.block, self.link_sems, self.core_sems = block, link_sems, core_sems
        place = lax.axis_index("dp")
        self.x, self.y, self.corner = other(place, 2), other(place, 4), other(place, 6)
        self.place = place
        self.x_side, self.y_side = {"dp": self.x}, {"dp": self.y}
        self.sibling = {"dp": other(place, 1)}
        self.halves = (pl.ds(0, width // 2), pl.ds(width // 2, width - width // 2))

    def copy(self, ref, sems, which, device):
        return pltpu.make_async_remote_copy(
            src_ref=ref,
            dst_ref=ref,
            send_sem=sems.at[0, which],
            recv_sem=sems.at[1, which],
            device_id=device,
            device_id_type=MESH,
        )

    def direct(self):
        own = self.block(self.place)
        return [
            self.copy(own, self.link_sems, 0, self.x_side),
            self.copy(own, self.link_sems, 1, self.y_side),
            self.copy(own, self.core_sems, 0, self.sibling),
        ]

    def forward(self):
        return [
            self.copy(self.block(self.x, self.halves[0]), self.link_sems, 2, self.y_side),
            self.copy(self.block(self.y, self.halves[1]), self.link_sems, 3, self.x_side),
            self.copy(self.block(self.x), self.core_sems, 1, self.sibling),
            self.copy(self.block(self.y), self.core_sems, 2, self.sibling),
        ]

    def last(self):
        return self.copy(self.block(self.corner), self.core_sems, 3, self.sibling)

    def start(self):
        for copy in self.direct():
            copy.start()

    def start_forward(self):
        for copy in self.direct()[:2]:
            copy.wait_recv()
        for copy in self.forward():
            copy.start()

    def start_last(self):
        for copy in self.forward()[:2]:
            copy.wait_recv()
        self.last().start()

    def finish(self):
        self.direct()[2].wait_recv()
        for copy in self.forward()[2:]:
            copy.wait_recv()
        self.last().wait_recv()

    def wait_sends(self):
        for copy in self.direct() + self.forward() + [self.last()]:
            copy.wait_send()


def turn(values, cosine, sine):
    heads = []
    for begin in range(0, values.shape[1], HEAD_DIM):
        head = values[:, begin : begin + HEAD_DIM]
        heads.append(head * cosine + pltpu.roll(head, HEAD_DIM // 2, 1) * sine)
    return jnp.concatenate(heads, 1)


def front_kernel(
    score_scale,
    layout,
    parents_ref,
    hidden_ref,
    gain_ref,
    bias_ref,
    freqs_ref,
    hits_ref,
    side_ref,
    out_grad_ref,
    w_query_ref,
    w_key_ref,
    w_value_ref,
    w_out_ref,
    e_gate_ref,
    e_up_ref,
    e_down_ref,
    s_gate_ref,
    s_up_ref,
    s_down_ref,
    residual_ref,
    query_ref,
    key_ref,
    value_ref,
    log_total_ref,
    attended_ref,
    normed_ref,
    cosine_ref,
    sine_ref,
    hits_all_ref,
    grad_all_ref,
    w_pre_ref,
    w_down_ref,
    weights,
    kv_all,
    hits_all,
    part_send,
    part_z,
    e_tiles,
    s_tiles,
    pre_tiles,
    down_tiles,
    load_sems,
    tile_sems,
    store_sems,
    hit_sems,
    part_sems,
    kv_links,
    kv_cores,
    head_links,
    head_cores,
    tail_links,
    tail_cores,
):
    shared_units, shared_pad, expert_units, experts, unit_pad = layout
    bf16, f32 = jnp.bfloat16, jnp.float32
    place, column = lax.axis_index("dp"), lax.axis_index("tensor")
    tok_rows, width = hidden_ref.shape
    rows = tok_rows // 4
    local_width = w_query_ref.shape[1]
    levels = [{"tensor": other(column, k)} for k in range(4)]
    peers = [{"dp": other(place, j)} for j in range(8)]

    loads = [
        pltpu.make_async_copy(ref, weights.at[i], load_sems.at[i])
        for i, ref in enumerate((w_query_ref, w_key_ref, w_value_ref, w_out_ref))
    ]
    own_grad = pltpu.make_async_copy(out_grad_ref, grad_all_ref.at[place], load_sems.at[4])
    for copy in loads:
        copy.start()
    own_grad.start()
    hits_all[place] = hits_ref[...]

    barrier = pltpu.get_barrier_semaphore()
    partners = peers[1:] + levels[1:]
    for partner in partners:
        pl.semaphore_signal(barrier, inc=1, device_id=partner, device_id_type=MESH)
    pl.semaphore_wait(barrier, len(partners))

    def grad_block(first, count):
        def block(d, cols=slice(None)):
            return grad_all_ref.at[d, pl.ds(first, count), :, cols]

        return block

    head_gather = PlaneGather(grad_block(0, 1), width, head_links, head_cores)
    tail_gather = PlaneGather(grad_block(1, 3), width, tail_links, tail_cores)
    kv_gather = PlaneGather(
        lambda d, cols=slice(None): kv_all.at[d, :, cols], 2 * local_width, kv_links, kv_cores
    )
    own_grad.wait()
    head_gather.start()

    def hit_copy(j):
        return pltpu.make_async_remote_copy(
            src_ref=hits_all.at[place],
            dst_ref=hits_all.at[place],
            send_sem=hit_sems.at[0, j],
            recv_sem=hit_sems.at[1, j],
            device_id=peers[j],
            device_id_type=MESH,
        )

    for j in range(1, 8):
        hit_copy(j).start()

    path = path_scalars(parents_ref, place)
    depth = jnp.float32(-1.0)
    for segment in path:
        depth = depth + jnp.where(segment >= 0, 1.0, 0.0)
    row_ids = lax.broadcasted_iota(jnp.int32, (tok_rows, HEAD_DIM), 0).astype(f32)
    lane = lax.broadcasted_iota(jnp.int32, (tok_rows, HEAD_DIM), 1)
    angles = (depth * SEG + row_ids) * freqs_ref[...]
    cosine = jnp.cos(angles)
    sine = jnp.where(lane < HEAD_DIM // 2, -1.0, 1.0) * jnp.sin(angles)
    cosine_ref[...] = cosine
    sine_ref[...] = sine
    hidden_f = hidden_ref[...].astype(f32)
    scale_rows = lax.rsqrt(jnp.mean(hidden_f * hidden_f, 1, keepdims=True) + epsilon)
    normed_ref[...] = (hidden_f * scale_rows * gain_ref[...]).astype(bf16)
    for copy in loads[1:3]:
        copy.wait()
    key = product(normed_ref[...], weights[1]) + bias_ref[1:2, :]
    kv_all[place, :, :local_width] = turn(key, cosine, sine).astype(bf16)
    value = product(normed_ref[...], weights[2]) + bias_ref[2:3, :]
    kv_all[place, :, local_width:] = value.astype(bf16)
    kv_gather.start()
    loads[0].wait()
    query = product(normed_ref[...], weights[0]) + bias_ref[0:1, :]
    query_ref[...] = turn(query, cosine, sine).astype(bf16)

    tile = e_tiles.shape[2]
    shared_first = place * shared_units
    span = s_tiles.shape[3]
    shared_base = jnp.minimum(shared_first // 128 * 128, s_gate_ref.shape[1] - span)
    shift = (span - (shared_first - shared_base)) % span

    def tile_loads(i, slot):
        window = pl.ds(pl.multiple_of(i * tile, tile), tile)
        columns = pl.ds(pl.multiple_of(shared_base, 128), span)
        copies = []
        for j, ref in enumerate((e_gate_ref, e_up_ref, e_down_ref)):
            copies.append(
                pltpu.make_async_copy(ref.at[window], e_tiles.at[slot, j], tile_sems.at[slot, j])
            )
        for j, ref in enumerate((s_gate_ref, s_up_ref, s_down_ref)):
            copies.append(
                pltpu.make_async_copy(
                    ref.at[window, columns], s_tiles.at[slot, j], tile_sems.at[slot, 3 + j]
                )
            )
        return copies

    def tile_stores(i, slot):
        window = pl.ds(pl.multiple_of(i * tile, tile), tile)
        return [
            pltpu.make_async_copy(pre_tiles.at[slot], w_pre_ref.at[window], store_sems.at[slot, 0]),
            pltpu.make_async_copy(
                down_tiles.at[slot], w_down_ref.at[window], store_sems.at[slot, 1]
            ),
        ]

    tiles = width // tile
    whole = expert_units // 128 * 128
    tail = expert_units - whole
    shared_lane = lax.broadcasted_iota(jnp.int32, (tile, shared_pad), 1)
    end_first = shared_pad + whole

    def pack(i, carry):
        slot = i % 2

        @pl.when(i + 1 < tiles)
        def _():
            for copy in tile_loads(i + 1, (i + 1) % 2):
                copy.start()

        for copy in tile_loads(i, slot):
            copy.wait()

        @pl.when(i >= 2)
        def _():
            for copy in tile_stores(i - 2, slot):
                copy.wait()

        window = pl.ds(pl.multiple_of(i * tile, tile), tile)
        for j, (target, first) in enumerate(
            ((pre_tiles, 0), (pre_tiles, unit_pad), (down_tiles, 0))
        ):
            shared = pltpu.roll(s_tiles[slot, j].astype(f32), shift, 1)[:, :shared_pad]
            shared = jnp.where(shared_lane < shared_units, shared, 0.0)
            target[slot, :, first : first + shared_pad] = shared.astype(bf16)
            target[slot, :, first + shared_pad : first + end_first] = e_tiles[slot, j, :, :whole]
            end = e_tiles[slot, j, :, whole:].astype(f32)
            end = jnp.concatenate([end, jnp.zeros((tile, 128 - tail), f32)], 1)
            if j == 0:
                end = end + side_ref[window, :].astype(f32)
            target[slot, :, first + end_first : first + unit_pad] = end.astype(bf16)
        for copy in tile_stores(i, slot):
            copy.start()
        return carry

    for copy in tile_loads(0, 0):
        copy.start()
    lax.fori_loop(0, tiles // 2, pack, 0)
    kv_gather.start_forward()
    lax.fori_loop(tiles // 2, tiles, pack, 0)
    kv_gather.start_last()
    head_gather.start_forward()
    for i in (tiles - 2, tiles - 1):
        for copy in tile_stores(i, i % 2):
            copy.wait()
    kv_gather.finish()
    tail_gather.start()

    for level, segment in enumerate(path):
        block = kv_all[jnp.maximum(segment, 0)]
        key_ref[level * tok_rows : (level + 1) * tok_rows, :] = block[:, :local_width]
        value_ref[level * tok_rows : (level + 1) * tok_rows, :] = block[:, local_width:]
    key_rows = key_ref.shape[0]
    row_id = lax.broadcasted_iota(jnp.int32, (tok_rows, key_rows), 0)
    col_id = lax.broadcasted_iota(jnp.int32, (tok_rows, key_rows), 1)
    allowed = row_id >= col_id
    for level in range(1, LEVELS):
        barred = jnp.where(path[level] >= 0, key_rows, 0)
        inside = (col_id >= level * tok_rows) & (col_id < (level + 1) * tok_rows)
        allowed = allowed | (inside & (col_id < barred))

    def head(h, carry):
        cols = pl.ds(pl.multiple_of(h * HEAD_DIM, HEAD_DIM), HEAD_DIM)
        scores = product_nt(query_ref[:, cols], key_ref[:, cols]) * score_scale
        scores = jnp.where(allowed, scores, -jnp.inf)
        top = jnp.max(scores, 1, keepdims=True)
        powers = jnp.exp(scores - top)
        total = jnp.sum(powers, 1, keepdims=True)
        log_total_ref[h] = top + jnp.log(total)
        probs = (powers * (1.0 / total)).astype(bf16)
        attended_ref[:, cols] = product(probs, value_ref[:, cols]).astype(bf16)
        return carry

    lax.fori_loop(0, local_width // HEAD_DIM, head, 0)

    loads[3].wait()
    for quarter in range(4):
        mine = slice(quarter * rows, (quarter + 1) * rows)
        part_send[quarter] = product_nt(attended_ref[mine, :], weights[3]).astype(bf16)

    def part_copy(k):
        return pltpu.make_async_remote_copy(
            src_ref=part_send.at[other(column, k)],
            dst_ref=part_z.at[k],
            send_sem=part_sems.at[0, k],
            recv_sem=part_sems.at[1, k],
            device_id=levels[k],
            device_id_type=MESH,
        )

    for k in (3, 2, 1):
        part_copy(k).start()
    head_gather.start_last()
    tail_gather.start_forward()
    attn = part_send[column].astype(f32)
    for k in (1, 2, 3):
        part_copy(k).wait_recv()
        attn = attn + part_z[k].astype(f32)
    own_rows = pl.ds(pl.multiple_of(column * rows, rows), rows)
    residual_ref[...] = hidden_ref[own_rows, :].astype(f32) + attn
    tail_gather.start_last()
    head_gather.finish()
    for j in range(1, 8):
        hit_copy(j).wait_recv()
    hits_all_ref[...] = hits_all[...]
    tail_gather.finish()

    for gather in (kv_gather, head_gather, tail_gather):
        gather.wait_sends()
    for j in range(1, 8):
        hit_copy(j).wait_send()
    for k in (1, 2, 3):
        part_copy(k).wait_send()


def front_layer(score_scale, layout, operands):
    shared_units, shared_pad, expert_units, experts, unit_pad = layout
    hidden, w_query = operands[1], operands[8]
    tok_rows, width = hidden.shape
    rows, local_width = tok_rows // 4, w_query.shape[1]
    heads = local_width // HEAD_DIM
    tile, span = 256, 384
    bf16, f32 = jnp.bfloat16, jnp.float32
    shape = jax.ShapeDtypeStruct
    vmem, anywhere = pl.BlockSpec(memory_space=pltpu.VMEM), pl.BlockSpec(memory_space=pl.ANY)
    smem = pl.BlockSpec(memory_space=pltpu.SMEM)
    dma = pltpu.SemaphoreType.DMA
    return pl.pallas_call(
        functools.partial(front_kernel, score_scale, layout),
        out_shape=[
            shape((rows, width), f32),
            shape((tok_rows, local_width), bf16),
            shape((LEVELS * tok_rows, local_width), bf16),
            shape((LEVELS * tok_rows, local_width), bf16),
            shape((heads, tok_rows, 1), f32),
            shape((tok_rows, local_width), bf16),
            shape((tok_rows, width), bf16),
            shape((tok_rows, HEAD_DIM), f32),
            shape((tok_rows, HEAD_DIM), f32),
            shape((8, 16, tok_rows), f32),
            shape((8, 4, rows, width), bf16),
            shape((width, 2 * unit_pad), bf16),
            shape((width, unit_pad), bf16),
        ],
        in_specs=[smem] + [vmem] * 6 + [anywhere] * 11,
        out_specs=[vmem] * 10 + [anywhere] * 3,
        scratch_shapes=[
            pltpu.VMEM((4, width, local_width), bf16),
            pltpu.VMEM((8, tok_rows, 2 * local_width), bf16),
            pltpu.VMEM((8, 16, tok_rows), f32),
            pltpu.VMEM((4, rows, width), bf16),
            pltpu.VMEM((4, rows, width), bf16),
            pltpu.VMEM((2, 3, tile, expert_units), bf16),
            pltpu.VMEM((2, 3, tile, span), bf16),
            pltpu.VMEM((2, tile, 2 * unit_pad), bf16),
            pltpu.VMEM((2, tile, unit_pad), bf16),
            dma((5,)),
            dma((2, 6)),
            dma((2, 2)),
            dma((2, 8)),
            dma((2, 4)),
        ]
        + [dma((2, 4))] * 6,
        compiler_params=pltpu.CompilerParams(
            collective_id=2, has_side_effects=True, vmem_limit_bytes=56 * 2**20
        ),
        cost_estimate=pl.CostEstimate(
            flops=2 * 2**31, bytes_accessed=40 * 2**20, transcendentals=2**21
        ),
    )(*operands)


class PlaneSum:
    def __init__(self, mine, theirs, got_core, got_x1, got_y1, got_y2, got_x2, core_sems, sems):
        self.mine, self.theirs = mine, theirs
        self.got = (got_core, got_x1, got_y1, got_y2, got_x2)
        self.core_sems, self.sems = core_sems, sems
        self.wide = got_core.shape[-1]
        self.half = got_x1.shape[-1]
        self.left, self.right = pl.ds(0, self.half), pl.ds(self.half, self.wide - self.half)
        place = lax.axis_index("dp")
        self.core, self.east, self.north = place % 2, (place // 2) % 2, place // 4
        self.sibling = {"dp": other(place, 1)}
        self.x_side, self.y_side = {"dp": other(place, 2)}, {"dp": other(place, 4)}

    def remote(self, src, dst, sems, which, device):
        return pltpu.make_async_remote_copy(
            src_ref=src,
            dst_ref=dst,
            send_sem=sems.at[(0, *which)],
            recv_sem=sems.at[(1, *which)],
            device_id=device,
            device_id_type=MESH,
        )

    def core_copy(self, k):
        return self.remote(
            self.theirs(k), self.got[0].at[k], self.core_sems, (k,), self.sibling
        )

    def first_copies(self, k):
        mine = self.mine(k)
        return [
            self.remote(
                mine.at[:, flip(self.east), :, self.left],
                self.got[1].at[k],
                self.sems,
                (0, k),
                self.x_side,
            ),
            self.remote(
                mine.at[flip(self.north), :, :, self.right],
                self.got[2].at[k],
                self.sems,
                (1, k),
                self.y_side,
            ),
        ]

    def second_copies(self, k):
        mine = self.mine(k)
        return [
            self.remote(
                mine.at[flip(self.north), self.east, :, self.left],
                self.got[3].at[k],
                self.sems,
                (2, k),
                self.y_side,
            ),
            self.remote(
                mine.at[self.north, flip(self.east), :, self.right],
                self.got[4].at[k],
                self.sems,
                (3, k),
                self.x_side,
            ),
        ]

    def add(self, ref, value):
        ref[...] = (ref[...].astype(jnp.float32) + value.astype(jnp.float32)).astype(jnp.bfloat16)

    def start(self, k):
        self.core_copy(k).start()

    def after_core(self, k):
        self.core_copy(k).wait_recv()
        mine = self.mine(k)
        for y in range(2):
            for x in range(2):
                self.add(mine.at[y, x], self.got[0][k, y, x])
        for copy in self.first_copies(k):
            copy.start()

    def after_first(self, k):
        x_copy, y_copy = self.first_copies(k)
        mine = self.mine(k)
        x_copy.wait_recv()
        for y in range(2):
            self.add(mine.at[y, self.east, :, self.left], self.got[1][k, y])
        y_copy.wait_recv()
        for x in range(2):
            self.add(mine.at[self.north, x, :, self.right], self.got[2][k, x])
        for copy in self.second_copies(k):
            copy.start()

    def after_second(self, k):
        y_copy, x_copy = self.second_copies(k)
        own = self.mine(k).at[self.north, self.east]
        y_copy.wait_recv()
        self.add(own.at[:, self.left], self.got[3][k])
        x_copy.wait_recv()
        self.add(own.at[:, self.right], self.got[4][k])
        return own

    def wait_sends(self, k):
        self.core_copy(k).wait_send()
        for copy in self.first_copies(k) + self.second_copies(k):
            copy.wait_send()


def plane_scratch(count, rows, wide):
    half = wide // 2
    bf16, dma = jnp.bfloat16, pltpu.SemaphoreType.DMA
    return [
        pltpu.VMEM((count, 2, 2, rows, wide), bf16),
        pltpu.VMEM((count, 2, rows, half), bf16),
        pltpu.VMEM((count, 2, rows, wide - half), bf16),
        pltpu.VMEM((count, rows, half), bf16),
        pltpu.VMEM((count, rows, wide - half), bf16),
        dma((2, count)),
        dma((2, 4, count)),
    ]


def unturn(grad, cosine, sine):
    heads = []
    for begin in range(0, grad.shape[1], HEAD_DIM):
        head = grad[:, begin : begin + HEAD_DIM]
        heads.append(head * cosine - pltpu.roll(head, HEAD_DIM // 2, 1) * sine)
    return jnp.concatenate(heads, 1)


def back_kernel(
    score_scale,
    gain_row,
    residual_ref,
    res_grad_ref,
    res_low_ref,
    ffn_part_ref,
    shared_ref,
    small_ref,
    query_ref,
    key_ref,
    value_ref,
    parents_ref,
    log_total_ref,
    attended_ref,
    normed_ref,
    hidden_ref,
    gain_ref,
    cosine_ref,
    sine_ref,
    w_out_ref,
    w_query_ref,
    w_key_ref,
    w_value_ref,
    hidden_out_ref,
    hidden_grad_ref,
    grad_query_ref,
    grad_key_ref,
    grad_value_ref,
    grad_out_ref,
    grad_shared_ref,
    small_out_ref,
    bias_out_ref,
    low_all,
    w_qkv,
    out_mine,
    out_z,
    kv_sums,
    w_sums,
    kv_path,
    attended_grad,
    query_grad,
    pre_grads,
    part,
    part_send,
    part_z,
    hidden_stage,
    shared_got,
    shared_stage,
    small_send,
    small_got,
    small_z,
    *rest,
):
    bf16, f32 = jnp.bfloat16, jnp.float32
    out_scr, rest = rest[:7], rest[7:]
    kv_scr, rest = rest[:7], rest[7:]
    w_scr, rest = rest[:7], rest[7:]
    wkv_sems, rest = rest[:2], rest[2:]
    load_sems, low_sems, out_sems, part_sems, end_sems, shared_sems, small_sems, small_z_sems = rest
    place, column = lax.axis_index("dp"), lax.axis_index("tensor")
    core, east, north = place % 2, (place // 2) % 2, place // 4
    rows, width = residual_ref.shape
    tok_rows, local_width = query_ref.shape
    levels = [{"tensor": other(column, k)} for k in range(4)]
    peers = [{"dp": other(place, j)} for j in range(8)]

    def remote(src, dst, sems, which, device):
        return pltpu.make_async_remote_copy(
            src_ref=src,
            dst_ref=dst,
            send_sem=sems.at[(0, *which)],
            recv_sem=sems.at[(1, *which)],
            device_id=device,
            device_id_type=MESH,
        )

    def load_out(z):
        return pltpu.make_async_copy(ffn_part_ref.at[z, core], out_mine.at[z], load_sems.at[z])

    loads = [
        pltpu.make_async_copy(w_query_ref, w_qkv.at[0], load_sems.at[5]),
        pltpu.make_async_copy(w_key_ref, w_qkv.at[1], load_sems.at[6]),
        pltpu.make_async_copy(w_out_ref, w_qkv.at[2], load_sems.at[4]),
    ]
    load_value = pltpu.make_async_copy(w_value_ref, w_qkv.at[2], load_sems.at[7])
    for z in range(4):
        load_out(z).start()
    for copy in loads:
        copy.start()

    barrier = pltpu.get_barrier_semaphore()
    partners = peers[1:] + levels[1:]
    for partner in partners:
        pl.semaphore_signal(barrier, inc=1, device_id=partner, device_id_type=MESH)
    pl.semaphore_wait(barrier, len(partners))

    out_sum = PlaneSum(
        lambda k: out_mine.at[k], lambda k: ffn_part_ref.at[k, flip(core)], *out_scr
    )
    kv_sum = PlaneSum(
        lambda k: kv_sums.at[core], lambda k: kv_sums.at[flip(core)], *kv_scr
    )
    w_sum = PlaneSum(
        lambda k: w_sums.at[k, core], lambda k: w_sums.at[k, flip(core)], *w_scr
    )
    wkv_sum = PlaneSum(
        lambda k: kv_sums.at[core], lambda k: kv_sums.at[flip(core)], *kv_scr[:5], *wkv_sems
    )

    low_all[column] = res_low_ref[...]
    own_low = low_all.at[column]
    low_copies = [remote(own_low, own_low, low_sems, (k,), levels[k]) for k in (3, 2, 1)]
    for copy in low_copies:
        copy.start()
    for z in range(4):
        out_sum.start(z)
    for z in range(4):
        load_out(z).wait()
        out_sum.after_core(z)
    for copy in loads:
        copy.wait()
    for copy in low_copies:
        copy.wait_recv()

    low_rows = low_all[...].reshape(tok_rows, width)
    attended_grad[...] = product(low_rows, w_qkv[2]).astype(bf16)
    load_value.start()

    def block_index(place_of):
        return place_of % 2, place_of // 4, (place_of // 2) % 2

    def out_weights(i, carry):
        c, y, x = block_index(i)
        window = pl.ds(pl.multiple_of(i * tok_rows, tok_rows), tok_rows)
        lhs = low_all[:, :, window].reshape(tok_rows, tok_rows)
        w_sums[0, c, y, x] = product_tn(lhs, attended_ref[...]).astype(bf16)
        return carry

    lax.fori_loop(0, 8, out_weights, 0)
    w_sum.start(0)

    key_rows = key_ref.shape[0]
    row_id = lax.broadcasted_iota(jnp.int32, (tok_rows, key_rows), 0)
    col_id = lax.broadcasted_iota(jnp.int32, (tok_rows, key_rows), 1)
    path = path_scalars(parents_ref, place)
    allowed = row_id >= col_id
    for level in range(1, LEVELS):
        barred = jnp.where(path[level] >= 0, key_rows, 0)
        inside = (col_id >= level * tok_rows) & (col_id < (level + 1) * tok_rows)
        allowed = allowed | (inside & (col_id < barred))

    def head(h, carry):
        cols = pl.ds(pl.multiple_of(h * HEAD_DIM, HEAD_DIM), HEAD_DIM)
        value_cols = pl.ds(pl.multiple_of(local_width + h * HEAD_DIM, HEAD_DIM), HEAD_DIM)
        query, key, value = query_ref[:, cols], key_ref[:, cols], value_ref[:, cols]
        grad = attended_grad[:, cols]
        scores = jnp.where(allowed, product_nt(query, key) * score_scale, -jnp.inf)
        weights = jnp.exp(scores - log_total_ref[h])
        weight_grad = product_nt(grad, value)
        center = jnp.sum(weights * weight_grad, 1, keepdims=True)
        score_grad = (weights * (weight_grad - center)).astype(bf16)
        query_grad[:, cols] = product(score_grad, key) * score_scale
        kv_path[:, cols] = (product_tn(score_grad, query) * score_scale).astype(bf16)
        kv_path[:, value_cols] = product_tn(weights.astype(bf16), grad).astype(bf16)
        return carry

    lax.fori_loop(0, 2, head, 0)
    for z in range(4):
        out_sum.after_first(z)
    w_sum.after_core(0)
    lax.fori_loop(2, 4, head, 0)

    def kv_blocks(q, c):
        y, x = q // 2, q % 2
        segment = 4 * y + 2 * x + c
        total = jnp.zeros((tok_rows, 2 * local_width), f32)
        for level in range(1, LEVELS):
            spot = jnp.where(path[level] == segment, 1.0, 0.0)
            total = total + spot * kv_path[level * tok_rows : (level + 1) * tok_rows].astype(f32)
        kv_sums[c, y, x] = total.astype(bf16)
        return c

    lax.fori_loop(0, 4, kv_blocks, flip(core))
    kv_sum.start(0)
    lax.fori_loop(0, 4, kv_blocks, core)
    own_kv = kv_sums.at[core, north, east]
    own_kv[...] = (own_kv[...].astype(f32) + kv_path[0:tok_rows].astype(f32)).astype(bf16)
    kv_sum.after_core(0)

    def cast_pre(which, grad):
        low = grad.astype(bf16)
        pre_grads[which] = low
        bias = jnp.sum(low.astype(f32), 0, keepdims=True)
        for h in range(local_width // HEAD_DIM):
            small_send[0, 4 * which + h : 4 * which + h + 1, 2 * HEAD_DIM :] = bias[
                :, h * HEAD_DIM : (h + 1) * HEAD_DIM
            ]

    small_send[0, :, 2 * HEAD_DIM :] = jnp.zeros((16, HEAD_DIM), f32)
    cast_pre(0, unturn(query_grad[...], cosine_ref[...], sine_ref[...]))

    def query_weights(i, carry):
        c, y, x = block_index(i)
        window = pl.ds(pl.multiple_of(i * tok_rows, tok_rows), tok_rows)
        w_sums[1, c, y, x] = product_tn(normed_ref[:, window], pre_grads[0]).astype(bf16)
        return carry

    lax.fori_loop(0, 8, query_weights, 0)
    w_sum.start(1)
    part[...] = product_nt(pre_grads[0], w_qkv[0])
    kv_sum.after_first(0)

    def out_level(k):
        return remote(
            out_mine.at[other(column, k), north, east],
            out_z.at[k],
            out_sems,
            (0, k),
            levels[k],
        )

    w_sum.after_first(0)
    for z in range(4):
        out_sum.after_second(z)
    for k in (3, 2, 1):
        out_level(k).start()
    w_sum.after_core(1)

    own_kv = kv_sum.after_second(0)
    cast_pre(1, unturn(own_kv[:, :local_width].astype(f32), cosine_ref[...], sine_ref[...]))
    cast_pre(2, own_kv[:, local_width:].astype(f32))
    load_value.wait()
    for which in (1, 2):
        part[...] += product_nt(pre_grads[which], w_qkv[which])

    hidden_f = hidden_ref[...].astype(f32)
    unit_scale = lax.rsqrt(jnp.mean(hidden_f * hidden_f, 1, keepdims=True) + epsilon)
    part_send[...] = part[...].astype(bf16).reshape(4, rows, width)

    def part_copy(k):
        return remote(part_send.at[other(column, k)], part_z.at[k], part_sems, (k,), levels[k])

    for k in (3, 2, 1):
        part_copy(k).start()
    attn_gain_row = jnp.sum(part[...] * (hidden_f * unit_scale), 0, keepdims=True)

    kv_sum.wait_sends(0)

    def key_value_weights(i, carry):
        c, y, x = block_index(i)
        window = pl.ds(pl.multiple_of(i * tok_rows, tok_rows), tok_rows)
        lhs = normed_ref[:, window]
        kv_sums[c, y, x, :, :local_width] = product_tn(lhs, pre_grads[1]).astype(bf16)
        kv_sums[c, y, x, :, local_width:] = product_tn(lhs, pre_grads[2]).astype(bf16)
        return carry

    lax.fori_loop(0, 8, key_value_weights, 0)
    wkv_sum.start(0)

    bias_rows = small_send[0, :, 2 * HEAD_DIM :]
    for d in range(8):
        small_send[d, :, : 2 * HEAD_DIM] = small_ref[:, d * tok_rows : (d + 1) * tok_rows]
        small_send[d, gain_row : gain_row + 1, : 2 * HEAD_DIM] = attn_gain_row[
            :, d * tok_rows : (d + 1) * tok_rows
        ]
        small_send[d, :, 2 * HEAD_DIM :] = bias_rows

    def small_copy(j):
        return remote(
            small_send.at[other(place, j)], small_got.at[j], small_sems, (j,), peers[j]
        )

    for j in range(1, 8):
        small_copy(j).start()

    def shared_copy(j):
        return remote(
            shared_ref.at[other(place, j)], shared_got.at[place], shared_sems, (j,), peers[j]
        )

    w_sum.after_first(1)
    wkv_sum.after_core(0)
    grad_out_ref[...] = w_sum.after_second(0)[...].astype(f32)
    for j in (6, 7, 2, 3, 4, 5, 1):
        shared_copy(j).start()
    own_shared = pltpu.make_async_copy(shared_ref.at[place], shared_got.at[place], load_sems.at[8])
    own_shared.start()

    total = small_send[place]
    for j in range(1, 8):
        small_copy(j).wait_recv()
        total = total + small_got[j]
    bias_out_ref[...] = total[:, 2 * HEAD_DIM :]
    small_z[column] = total[:, : 2 * HEAD_DIM]
    own_small = small_z.at[column]
    small_levels = [
        remote(own_small, own_small, small_z_sems, (k,), levels[k]) for k in (1, 2, 3)
    ]
    for copy in small_levels:
        copy.start()

    mine = pl.ds(pl.multiple_of(column * rows, rows), rows)
    attn_grad = part_send[column].astype(f32)
    for k in (1, 2, 3):
        part_copy(k).wait_recv()
        attn_grad = attn_grad + part_z[k].astype(f32)
    own_hidden = hidden_ref[mine, :].astype(f32)
    own_scale = lax.rsqrt(jnp.mean(own_hidden * own_hidden, 1, keepdims=True) + epsilon)
    hidden_stage[0, column] = (
        res_grad_ref[...] + norm_back(attn_grad, own_hidden * own_scale, own_scale, gain_ref[...])
    ).astype(bf16)

    def end_copy(which, k):
        own = hidden_stage.at[which, column]
        return remote(own, own, end_sems, (which, k), levels[k])

    for k in (3, 2, 1):
        end_copy(0, k).start()

    out = residual_ref[...] + out_mine[column, north, east].astype(f32)
    for k in (1, 2, 3):
        out_level(k).wait_recv()
        out = out + out_z[k].astype(f32)
    hidden_stage[1, column] = out.astype(bf16)
    for k in (3, 2, 1):
        end_copy(1, k).start()

    wkv_sum.after_first(0)
    grad_query_ref[...] = w_sum.after_second(1)[...].astype(f32)
    for copy in small_levels:
        copy.wait_recv()
    small_out_ref[...] = (small_z[0] + small_z[1]) + (small_z[2] + small_z[3])
    own_wkv = wkv_sum.after_second(0)
    grad_key_ref[...] = own_wkv[:, :local_width].astype(f32)
    grad_value_ref[...] = own_wkv[:, local_width:].astype(f32)

    own_shared.wait()
    for j in range(1, 8):
        shared_copy(j).wait_recv()

    def store_shared(which):
        return pltpu.make_async_copy(
            shared_stage, grad_shared_ref.at[which], load_sems.at[9]
        )

    for which in range(3):
        units = shared_got[:, which].astype(f32)
        turned = units.reshape(-1, units.shape[-1]).T
        if which:
            store_shared(which - 1).wait()
        shared_stage[...] = turned
        store_shared(which).start()

    for k in (1, 2, 3):
        end_copy(0, k).wait_recv()
        end_copy(1, k).wait_recv()
    ends = [
        pltpu.make_async_copy(hidden_stage.at[0], hidden_grad_ref, load_sems.at[10]),
        pltpu.make_async_copy(hidden_stage.at[1], hidden_out_ref, load_sems.at[11]),
    ]
    for copy in ends:
        copy.start()
    store_shared(2).wait()
    for copy in ends:
        copy.wait()

    for copy in low_copies + small_levels:
        copy.wait_send()
    for z in range(4):
        out_sum.wait_sends(z)
    for k in (1, 2, 3):
        out_level(k).wait_send()
        part_copy(k).wait_send()
        end_copy(0, k).wait_send()
        end_copy(1, k).wait_send()
    for k in range(2):
        w_sum.wait_sends(k)
    wkv_sum.wait_sends(0)
    for j in range(1, 8):
        small_copy(j).wait_send()
        shared_copy(j).wait_send()


def back_layer(score_scale, gain_row, operands):
    (
        residual,
        res_grad,
        res_low,
        ffn_part,
        grad_shared,
        small,
        query,
        key,
        value,
        parents,
        log_total,
        attended,
        normed,
        hidden,
        gain,
        cosine,
        sine,
        w_out,
        w_query,
        w_key,
        w_value,
    ) = operands
    rows, width = residual.shape
    tok_rows, local_width = query.shape
    units = grad_shared.shape[2]
    bf16, f32 = jnp.bfloat16, jnp.float32
    shape = jax.ShapeDtypeStruct
    vmem, anywhere = pl.BlockSpec(memory_space=pltpu.VMEM), pl.BlockSpec(memory_space=pl.ANY)
    smem = pl.BlockSpec(memory_space=pltpu.SMEM)
    dma = pltpu.SemaphoreType.DMA
    return pl.pallas_call(
        functools.partial(back_kernel, score_scale, gain_row),
        out_shape=[
            shape((4, rows, width), bf16),
            shape((4, rows, width), bf16),
            shape((tok_rows, local_width), f32),
            shape((tok_rows, local_width), f32),
            shape((tok_rows, local_width), f32),
            shape((tok_rows, local_width), f32),
            shape((3, tok_rows, 8 * units), f32),
            shape((16, tok_rows), f32),
            shape((16, HEAD_DIM), f32),
        ],
        in_specs=[vmem, vmem, vmem, anywhere, anywhere, vmem]
        + [vmem] * 3
        + [smem]
        + [vmem] * 7
        + [anywhere] * 4,
        out_specs=[anywhere] * 2 + [vmem] * 4 + [anywhere, vmem, vmem],
        scratch_shapes=[
            pltpu.VMEM((4, rows, width), bf16),
            pltpu.VMEM((3, width, local_width), bf16),
            pltpu.VMEM((4, 2, 2, rows, width), bf16),
            pltpu.VMEM((4, rows, width), bf16),
            pltpu.VMEM((2, 2, 2, tok_rows, 2 * local_width), bf16),
            pltpu.VMEM((2, 2, 2, 2, tok_rows, local_width), bf16),
            pltpu.VMEM((LEVELS * tok_rows, 2 * local_width), bf16),
            pltpu.VMEM((tok_rows, local_width), bf16),
            pltpu.VMEM((tok_rows, local_width), f32),
            pltpu.VMEM((3, tok_rows, local_width), bf16),
            pltpu.VMEM((tok_rows, width), f32),
            pltpu.VMEM((4, rows, width), bf16),
            pltpu.VMEM((4, rows, width), bf16),
            pltpu.VMEM((2, 4, rows, width), bf16),
            pltpu.VMEM((8, 3, units, tok_rows), bf16),
            pltpu.VMEM((tok_rows, 8 * units), f32),
            pltpu.VMEM((8, 16, 2 * HEAD_DIM + HEAD_DIM), f32),
            pltpu.VMEM((8, 16, 2 * HEAD_DIM + HEAD_DIM), f32),
            pltpu.VMEM((4, 16, 2 * HEAD_DIM), f32),
        ]
        + plane_scratch(4, rows, width)
        + plane_scratch(1, tok_rows, 2 * local_width)
        + plane_scratch(2, tok_rows, local_width)
        + plane_scratch(1, tok_rows, 2 * local_width)[5:]
        + [
            dma((12,)),
            dma((2, 4)),
            dma((2, 1, 4)),
            dma((2, 4)),
            dma((2, 2, 4)),
            dma((2, 8)),
            dma((2, 8)),
            dma((2, 4)),
        ],
        compiler_params=pltpu.CompilerParams(
            collective_id=1, has_side_effects=True, vmem_limit_bytes=63 * 2**20
        ),
        cost_estimate=pl.CostEstimate(
            flops=2 * 12 * 2**30, bytes_accessed=40 * 2**20, transcendentals=2**20
        ),
    )(*operands)


def on_slice(
    hidden_in,
    out_grad,
    parents,
    routes,
    attn_gain,
    w_query,
    w_key,
    w_value,
    b_query,
    b_key,
    b_value,
    w_out,
    ffn_gain,
    w_router,
    shared_gate,
    shared_w_gate,
    shared_w_up,
    shared_w_down,
    expert_w_gate,
    expert_w_up,
    expert_w_down,
):
    tok_rows, model_width = hidden_in.shape
    devices = lax.axis_size("dp")
    columns = lax.axis_size("tensor")
    place, column = lax.axis_index("dp"), lax.axis_index("tensor")
    all_rows = tok_rows * devices
    part_rows = tok_rows // columns
    local_width = w_query.shape[1]
    experts = w_router.shape[1]
    top_count = routes.shape[1]
    capacity = 5 * tok_rows * top_count // 4
    score_scale = HEAD_DIM ** (-0.5)
    bf16, f32 = jnp.bfloat16, jnp.float32

    expert_units = expert_w_gate.shape[2]
    shared_units = shared_w_gate.shape[1] // devices
    shared_pad = -(-shared_units // 128) * 128
    units = shared_pad + expert_units
    units_pad = -(-(units + experts + 1) // 128) * 128

    def own_units(matrix):
        return lax.dynamic_slice_in_dim(matrix, place * shared_units, shared_units, 1)

    def pad_to(matrix, columns):
        return jnp.pad(matrix, ((0, 0), (0, columns - matrix.shape[1])))

    def side_by_side(shared, expert):
        joined = jnp.concatenate([pad_to(own_units(shared), shared_pad), expert[0]], 1)
        return joined

    w_pre = jnp.concatenate(
        [
            pad_to(
                jnp.concatenate(
                    [side_by_side(shared_w_gate, expert_w_gate), w_router, shared_gate[:, None]], 1
                ),
                units_pad,
            ),
            pad_to(side_by_side(shared_w_up, expert_w_up), units_pad),
        ],
        1,
    )
    w_down = pad_to(side_by_side(shared_w_down, expert_w_down), units_pad)

    out_all = gather_dp(out_grad)

    routes_all = lax.all_gather(routes, "dp", axis=0, tiled=True)
    pair_onehot = routes_all[:, :, None] == jnp.arange(experts, dtype=jnp.int32)[None, None, :]
    hits = jnp.any(pair_onehot, 1)
    hit_blocks = hits.astype(bf16).reshape(devices, tok_rows, experts)
    below = (
        jnp.arange(tok_rows)[None, :] < jnp.arange(tok_rows)[:, None]
    ).astype(bf16)
    within = jnp.einsum("ij,bje->bie", below, hit_blocks, preferred_element_type=f32)
    block_sums = jnp.sum(hit_blocks.astype(f32), 1)
    before = jnp.cumsum(block_sums, 0) - block_sums
    slots = (within + before[:, None, :]).reshape(all_rows, experts)
    kept = (hits & (slots < capacity)).astype(f32)

    path = path_of(parents, place * tok_rows // SEG)
    reachable = path >= 0
    path_rows = jnp.maximum(path, 0)
    row_ids = jnp.arange(tok_rows, dtype=jnp.int32)
    depth = jnp.sum(reachable.astype(f32)) - 1.0
    cosine, sine = rope_tables(depth * SEG + row_ids.astype(f32))
    allowed = jnp.concatenate(
        [
            row_ids[:, None] >= row_ids[None, :],
            jnp.broadcast_to(
                jnp.repeat(reachable[1:], tok_rows)[None, :], (tok_rows, (LEVELS - 1) * tok_rows)
            ),
        ],
        1,
    )
    hidden_f = hidden_in.astype(f32)
    attn_scale, attn_unit = norm_parts(hidden_f)
    attn_normed = (attn_unit * attn_gain).astype(bf16)
    query_rot = turn_heads(
        product(attn_normed, w_query) + b_query.reshape(-1), cosine, sine, 1.0
    ).astype(bf16)
    key_rot = turn_heads(
        product(attn_normed, w_key) + b_key.reshape(-1), cosine, sine, 1.0
    ).astype(bf16)
    value_rows = (product(attn_normed, w_value) + b_value.reshape(-1)).astype(bf16)
    gathered = gather_dp(jnp.concatenate([key_rot, value_rows], 1))
    kv_blocks = gathered.reshape(devices, tok_rows, 2 * local_width)
    kv_path = jnp.take(kv_blocks, path_rows, axis=0).reshape(LEVELS * tok_rows, 2 * local_width)
    key_path, value_path = kv_path[:, :local_width], kv_path[:, local_width:]
    attended, log_total = attend_forward(query_rot, key_path, value_path, allowed, score_scale)
    attended_low = attended.astype(bf16)
    attn_part = product_nt(attended_low, w_out).astype(bf16)

    hidden_own = lax.dynamic_slice_in_dim(hidden_in, column * part_rows, part_rows, 0)
    grad_own = lax.dynamic_slice_in_dim(out_grad, column * part_rows, part_rows, 0)
    layout = (shared_units, shared_pad, expert_units, experts, units_pad)
    (
        residual,
        residual_grad,
        residual_low,
        ffn_part,
        grad_expert_gate,
        grad_expert_up,
        grad_expert_down,
        grad_shared,
        grad_side,
        grad_ffn_gain,
    ) = ffn_plain(
        attn_part, hidden_own, grad_own, ffn_gain, kept, out_all, w_pre, w_down, layout
    )
    grad_shared = grad_shared[:, :, :shared_units]
    ffn_own = scatter_all(ffn_part).astype(f32)
    hidden_out = gather_tensor((residual + ffn_own).astype(bf16))
    residual_low = gather_tensor(residual_low)
    grad_out_proj = product_tn(residual_low, attended_low)
    attended_grad = product(residual_low, w_out).astype(bf16)

    query_grad, key_grad, value_grad = attend_backward(
        query_rot, key_path, value_path, allowed, log_total, attended_grad, score_scale
    )
    kv_grad = jnp.concatenate([key_grad, value_grad], 1).reshape(
        LEVELS, tok_rows, 2 * local_width
    )
    kv_all = jnp.zeros((devices, tok_rows, 2 * local_width), f32)
    for level in range(LEVELS):
        kv_all = kv_all.at[path_rows[level]].add(kv_grad[level])
    kv_own = scatter_dp(
        kv_all.reshape(all_rows, 2 * local_width).astype(bf16)
    ).astype(f32)
    query_pre_grad = turn_heads(query_grad, cosine, sine, -1.0).astype(bf16)
    key_pre_grad = turn_heads(kv_own[:, :local_width], cosine, sine, -1.0).astype(bf16)
    value_pre_grad = kv_own[:, local_width:].astype(bf16)
    qkv_pre_grad = jnp.concatenate([query_pre_grad, key_pre_grad, value_pre_grad], 1)
    grad_qkv = product_tn(attn_normed, qkv_pre_grad)
    bias_grads = jnp.sum(qkv_pre_grad.astype(f32), 0).reshape(3, -1, HEAD_DIM)
    attn_part_grad = (
        product_nt(query_pre_grad, w_query)
        + product_nt(key_pre_grad, w_key)
        + product_nt(value_pre_grad, w_value)
    )
    grad_attn_gain = jnp.sum(attn_part_grad * attn_unit, 0)
    attn_own_grad = scatter_tensor(attn_part_grad.astype(bf16)).astype(f32)
    own_rows = lambda array: lax.dynamic_slice_in_dim(
        array, column * part_rows, part_rows, 0
    )
    hidden_in_grad = gather_tensor(
        (
            residual_grad
            + norm_back(attn_own_grad, own_rows(attn_unit), own_rows(attn_scale), attn_gain)
        ).astype(bf16)
    )

    small = jnp.concatenate(
        [grad_side, grad_ffn_gain[:, None], grad_attn_gain[:, None]], 1
    )
    small = scatter_dp(lax.psum(small, "tensor"))
    bias_sums = lax.psum_scatter(bias_grads, "dp", scatter_dimension=2, tiled=True)
    grad_attn = scatter_dp(jnp.concatenate([grad_qkv, grad_out_proj], 1).astype(bf16)).astype(f32)
    shared_grads = lax.all_to_all(
        grad_shared, "dp", split_axis=1, concat_axis=2, tiled=True
    ).astype(f32)
    return (
        hidden_out,
        hidden_in_grad,
        small[:, experts + 2],
        grad_attn[:, :local_width],
        grad_attn[:, local_width : 2 * local_width],
        grad_attn[:, 2 * local_width : 3 * local_width],
        bias_sums[0],
        bias_sums[1],
        bias_sums[2],
        grad_attn[:, 3 * local_width :],
        small[:, experts + 1],
        small[:, :experts],
        small[:, experts],
        shared_grads[0],
        shared_grads[1],
        shared_grads[2],
        grad_expert_gate[None],
        grad_expert_up[None],
        grad_expert_down[None],
    )


def on_cube(
    hidden_in,
    out_grad,
    parents,
    routes,
    attn_gain,
    w_query,
    w_key,
    w_value,
    b_query,
    b_key,
    b_value,
    w_out,
    ffn_gain,
    w_router,
    shared_gate,
    shared_w_gate,
    shared_w_up,
    shared_w_down,
    expert_w_gate,
    expert_w_up,
    expert_w_down,
):
    tok_rows, model_width = hidden_in.shape
    devices, columns = lax.axis_size("dp"), lax.axis_size("tensor")
    place = lax.axis_index("dp")
    experts, top_count = w_router.shape[1], routes.shape[1]
    capacity = 5 * tok_rows * top_count // 4
    score_scale = HEAD_DIM ** (-0.5)
    bf16, f32 = jnp.bfloat16, jnp.float32
    expert_units = expert_w_gate.shape[2]
    shared_units = shared_w_gate.shape[1] // devices
    shared_pad = -(-shared_units // 128) * 128
    units = shared_pad + expert_units
    units_pad = -(-(units + experts + 1) // 128) * 128
    layout = (shared_units, shared_pad, expert_units, experts, units_pad)
    part_rows = tok_rows // columns

    side_first = units - (units_pad - 128)
    side = jnp.pad(
        jnp.concatenate([w_router, shared_gate[:, None]], 1),
        ((0, 0), (side_first, 128 - side_first - experts - 1)),
    )
    hits = jnp.any(
        routes.T[:, None, :] == jnp.arange(16, dtype=jnp.int32)[None, :, None], 0
    ).astype(f32)
    freqs = rope_base ** (-jnp.arange(0, HEAD_DIM, 2, dtype=f32) / HEAD_DIM)
    biases = jnp.stack([b_query.reshape(-1), b_key.reshape(-1), b_value.reshape(-1)])
    (
        residual,
        query_rot,
        key_path,
        value_path,
        log_total,
        attended,
        attn_normed,
        cosine,
        sine,
        hits_all,
        grad_all,
        w_pre,
        w_down,
    ) = front_layer(
        score_scale,
        layout,
        (
            parents,
            hidden_in,
            attn_gain[None, :],
            biases,
            jnp.concatenate([freqs, freqs])[None, :],
            hits,
            side,
            out_grad.reshape(columns, part_rows, model_width),
            w_query,
            w_key,
            w_value,
            w_out,
            expert_w_gate[0],
            expert_w_up[0],
            expert_w_down[0],
            shared_w_gate,
            shared_w_up,
            shared_w_down,
        ),
    )
    (
        residual_grad,
        residual_low,
        ffn_part,
        grad_expert_gate,
        grad_expert_up,
        grad_expert_down,
        grad_shared,
        small,
    ) = ffn_layer(
        residual,
        ffn_gain[None, :],
        hits_all,
        grad_all.reshape(2, 2, 2, columns, part_rows, model_width),
        w_pre,
        w_down,
        layout,
        capacity,
    )
    (
        hidden_out,
        hidden_in_grad,
        sum_query,
        sum_key,
        sum_value,
        sum_out,
        shared_grads,
        small,
        bias_sums,
    ) = back_layer(
        score_scale,
        experts + 2,
        (
            residual,
            residual_grad,
            residual_low,
            ffn_part,
            grad_shared,
            small,
            query_rot,
            key_path,
            value_path,
            parents,
            log_total,
            attended,
            attn_normed,
            hidden_in,
            attn_gain[None, :],
            cosine,
            sine,
            w_out,
            w_query,
            w_key,
            w_value,
        ),
    )
    small = small.T
    bias_sums = lax.dynamic_slice_in_dim(
        bias_sums[: 3 * b_query.shape[0]].reshape(3, *b_query.shape),
        place * (HEAD_DIM // devices),
        HEAD_DIM // devices,
        2,
    )
    return (
        hidden_out.reshape(tok_rows, model_width),
        hidden_in_grad.reshape(tok_rows, model_width),
        small[:, experts + 2],
        sum_query,
        sum_key,
        sum_value,
        bias_sums[0],
        bias_sums[1],
        bias_sums[2],
        sum_out,
        small[:, experts + 1],
        small[:, :experts],
        small[:, experts],
        shared_grads[0],
        shared_grads[1],
        shared_grads[2],
        grad_expert_gate[None],
        grad_expert_up[None],
        grad_expert_down[None],
    )


def on_device(*arrays):
    devices, columns = lax.axis_size("dp"), lax.axis_size("tensor")
    tok_rows, model_width = arrays[0].shape
    cube = devices == 8 and columns == 4 and tok_rows == SEG
    if cube and tok_rows * devices * model_width <= 2**22:
        return on_cube(*arrays)
    return on_slice(*arrays)


def solution(mesh):
    return jax.shard_map(
        on_device,
        mesh=mesh,
        in_specs=(
            P("dp", None),
            P("dp", None),
            P(),
            P("dp", None),
            P(),
            P(None, "tensor"),
            P(None, "tensor"),
            P(None, "tensor"),
            P("tensor", None),
            P("tensor", None),
            P("tensor", None),
            P(None, "tensor"),
            P(),
            P(),
            P(),
            P(None, "tensor"),
            P(None, "tensor"),
            P(None, "tensor"),
            P("dp", None, "tensor"),
            P("dp", None, "tensor"),
            P("dp", None, "tensor"),
        ),
        out_specs=(
            P("dp", None),
            P("dp", None),
            P("dp"),
            P("dp", "tensor"),
            P("dp", "tensor"),
            P("dp", "tensor"),
            P("tensor", "dp"),
            P("tensor", "dp"),
            P("tensor", "dp"),
            P("dp", "tensor"),
            P("dp"),
            P("dp", None),
            P("dp"),
            P("dp", "tensor"),
            P("dp", "tensor"),
            P("dp", "tensor"),
            P("dp", None, "tensor"),
            P("dp", None, "tensor"),
            P("dp", None, "tensor"),
        ),
        check_vma=False,
    )
```

```python
import functools

import jax
import jax.numpy as jnp
from jax import lax
from jax.experimental import pallas as pl
from jax.experimental.pallas import tpu as pltpu
from jax.sharding import PartitionSpec as P

HEAD_DIM = 128
SEG = 256
MESH = pl.DeviceIdType.MESH


epsilon = 1e-06
rope_base = 1000000.0
highest = lax.Precision.HIGHEST


def product(left, right):
    return jnp.dot(left, right, preferred_element_type=jnp.float32)


def product_tn(left, right):
    return lax.dot_general(
        left, right, (((0,), (0,)), ((), ())), preferred_element_type=jnp.float32
    )


def product_nt(left, right):
    return lax.dot_general(
        left, right, (((1,), (1,)), ((), ())), preferred_element_type=jnp.float32
    )


def ancestry(parents):
    seg_count = parents.shape[0]
    labels = jnp.arange(seg_count, dtype=jnp.int32)

    def climb(level, carry):
        current, reach = carry
        upward = jnp.where(current >= 0, parents[jnp.maximum(current, 0)], -1)
        reach = jnp.maximum(reach, (upward[:, None] == labels[None, :]).astype(jnp.float32))
        return (upward, reach)

    start = (labels, jnp.eye(seg_count, dtype=jnp.float32))
    return lax.fori_loop(0, seg_count, climb, start)[1]


def rope_tables(positions):
    freqs = rope_base ** (-jnp.arange(0, HEAD_DIM, 2, dtype=jnp.float32) / HEAD_DIM)
    angles = positions[:, None] * freqs[None, :]
    angles = jnp.concatenate([angles, angles], 1)
    return (jnp.cos(angles)[:, None, :], jnp.sin(angles)[:, None, :])


def turn_heads(matrix, cosine, sine, sign_value):
    shaped = matrix.reshape(matrix.shape[0], matrix.shape[1] // HEAD_DIM, HEAD_DIM)
    half = HEAD_DIM // 2
    turned = jnp.concatenate([-shaped[..., half:], shaped[..., :half]], -1)
    return (shaped * cosine + sign_value * turned * sine).reshape(matrix.shape)


def norm_parts(values):
    scale_rows = lax.rsqrt(jnp.mean(values * values, 1, keepdims=True) + epsilon)
    return (scale_rows, values * scale_rows)


def norm_back(grad_rows, unit_rows, scale_rows, gain):
    unit_grad = grad_rows * gain
    return scale_rows * (unit_grad - unit_rows * jnp.mean(unit_grad * unit_rows, 1, keepdims=True))


LEVELS = 4


def gather_dp(rows):
    return lax.all_gather(rows, "dp", axis=0, tiled=True)


def gather_tensor(rows):
    return lax.all_gather(rows, "tensor", axis=0, tiled=True)


def gather_all(rows):
    return gather_dp(gather_tensor(rows))


def scatter_dp(rows):
    return lax.psum_scatter(rows, "dp", scatter_dimension=0, tiled=True)


def scatter_tensor(rows):
    return lax.psum_scatter(rows, "tensor", scatter_dimension=0, tiled=True)


def scatter_all(rows):
    return scatter_tensor(scatter_dp(rows))


def path_of(parents, segment):
    path = [segment]
    for _ in range(LEVELS - 1):
        last = path[-1]
        path.append(jnp.where(last >= 0, parents[jnp.maximum(last, 0)], -1))
    return jnp.stack(path)


def heads_of(matrix):
    return matrix.reshape(matrix.shape[0], -1, HEAD_DIM)


def attend_forward(query_rot, key_path, value_path, allowed, score_scale):
    scores = (
        jnp.einsum(
            "qhd,khd->hqk",
            heads_of(query_rot),
            heads_of(key_path),
            preferred_element_type=jnp.float32,
        )
        * score_scale
    )
    scores = jnp.where(allowed[None], scores, -jnp.inf)
    peak = jnp.max(scores, 2, keepdims=True)
    log_total = peak + jnp.log(jnp.sum(jnp.exp(scores - peak), 2, keepdims=True))
    weights = jnp.exp(scores - log_total).astype(jnp.bfloat16)
    attended = jnp.einsum(
        "hqk,khd->qhd", weights, heads_of(value_path), preferred_element_type=jnp.float32
    )
    return attended.reshape(query_rot.shape), log_total


def attend_backward(
    query_rot, key_path, value_path, allowed, log_total, attended_grad, score_scale
):
    query, key, value = heads_of(query_rot), heads_of(key_path), heads_of(value_path)
    grad = heads_of(attended_grad)
    scores = jnp.einsum("qhd,khd->hqk", query, key, preferred_element_type=jnp.float32)
    weights = jnp.exp(jnp.where(allowed[None], scores * score_scale, -jnp.inf) - log_total)
    weight_grad = jnp.einsum("qhd,khd->hqk", grad, value, preferred_element_type=jnp.float32)
    center = jnp.sum(weights * weight_grad, 2, keepdims=True)
    score_grad = (weights * (weight_grad - center)).astype(jnp.bfloat16)
    query_grad = (
        jnp.einsum("hqk,khd->qhd", score_grad, key, preferred_element_type=jnp.float32)
        * score_scale
    )
    key_grad = (
        jnp.einsum("hqk,qhd->khd", score_grad, query, preferred_element_type=jnp.float32)
        * score_scale
    )
    value_grad = jnp.einsum(
        "hqk,qhd->khd",
        weights.astype(jnp.bfloat16),
        grad,
        preferred_element_type=jnp.float32,
    )
    return (
        query_grad.reshape(query_rot.shape),
        key_grad.reshape(key_path.shape),
        value_grad.reshape(value_path.shape),
    )


def ffn_plain(attn_part, hidden_own, grad_own, ffn_gain, kept, out_all, w_pre, w_down, layout):
    _, shared_pad, expert_units, experts, units_pad = layout
    units = shared_pad + expert_units
    bf16, f32 = jnp.bfloat16, jnp.float32
    place, column = lax.axis_index("dp"), lax.axis_index("tensor")
    columns, part_rows = lax.axis_size("tensor"), hidden_own.shape[0]
    out_own = grad_own.astype(f32)
    residual = hidden_own.astype(f32) + scatter_tensor(attn_part).astype(f32)
    ffn_scale, ffn_unit = norm_parts(residual)
    ffn_normed = (ffn_unit * ffn_gain).astype(bf16)
    normed_all = gather_all(ffn_normed)

    pre = product(normed_all, w_pre)
    pre_gate, pre_up = pre[:, :units_pad], pre[:, units_pad:]
    logits = pre[:, units : units + experts]
    probs = jax.nn.softmax(logits, 1)
    shared_weight = jax.nn.sigmoid(pre[:, units + experts])
    own_expert = jnp.arange(experts, dtype=jnp.int32)[None, :] == place
    gate_own = jnp.sum(jnp.where(own_expert, probs * kept, 0.0), 1)
    lane = jnp.arange(units_pad)[None, :]
    weight = jnp.where(
        lane < shared_pad,
        shared_weight[:, None],
        jnp.where(lane < units, gate_own[:, None], 0.0),
    )
    down_back = product(out_all, w_down)
    sigmoid_gate = jax.nn.sigmoid(pre_gate)
    hidden = (pre_gate * sigmoid_gate * pre_up).astype(bf16).astype(f32)
    hidden_scaled = (hidden * weight).astype(bf16)
    hidden_grad = down_back * weight
    up_rows = (hidden_grad * pre_gate * sigmoid_gate).astype(bf16)
    gate_rows = (
        hidden_grad * pre_up * sigmoid_gate * (1.0 + pre_gate * (1.0 - sigmoid_gate))
    ).astype(bf16)
    both_rows = jnp.concatenate([gate_rows, up_rows], 1)
    dots = hidden * down_back
    gate_dot = jnp.sum(jnp.where((lane >= shared_pad) & (lane < units), dots, 0.0), 1)
    shared_dot = jnp.sum(jnp.where(lane < shared_pad, dots, 0.0), 1)
    dot_parts = jnp.concatenate(
        [jnp.where(own_expert, gate_dot[:, None] * kept, 0.0), shared_dot[:, None]], 1
    )
    ffn_part = product_nt(hidden_scaled, w_down).astype(bf16)
    normed_part = product_nt(both_rows, w_pre).astype(bf16)
    grad_pre = product_tn(normed_all, both_rows)
    grad_down = product_tn(out_all, hidden_scaled)

    dot_own = scatter_all(dot_parts)
    normed_own = scatter_all(normed_part).astype(f32)

    first = (place * columns + column) * part_rows
    own = lambda array: lax.dynamic_slice_in_dim(array, first, part_rows, 0)
    probs_own, shared_own = own(probs), own(shared_weight)
    prob_grad = dot_own[:, :experts]
    logit_grad = (
        probs_own * (prob_grad - jnp.sum(probs_own * prob_grad, 1, keepdims=True))
    ).astype(bf16)
    weight_logit_grad = (dot_own[:, experts] * shared_own * (1.0 - shared_own)).astype(bf16)
    side_grad = jnp.concatenate([logit_grad, weight_logit_grad[:, None]], 1)
    side_w = w_pre[:, units : units + experts + 1]
    normed_grad = normed_own + product_nt(side_grad, side_w)
    grad_side = product_tn(ffn_normed, side_grad)
    grad_ffn_gain = jnp.sum(normed_grad * ffn_unit, 0)
    residual_grad = out_own + norm_back(normed_grad, ffn_unit, ffn_scale, ffn_gain)
    expert = slice(shared_pad, units)
    expert_up = slice(units_pad + shared_pad, units_pad + units)
    grad_shared = jnp.stack(
        [
            grad_pre[:, : shared_pad],
            grad_pre[:, units_pad : units_pad + shared_pad],
            grad_down[:, : shared_pad],
        ]
    ).astype(bf16)
    return (
        residual,
        residual_grad,
        residual_grad.astype(bf16),
        ffn_part,
        grad_pre[:, expert],
        grad_pre[:, expert_up],
        grad_down[:, expert],
        grad_shared,
        grad_side,
        grad_ffn_gain,
    )


def flip(bit):
    return 1 - bit


def other(index, step):
    result, place = index, 1
    while place <= step:
        if step & place:
            result = result + place - 2 * place * ((index // place) % 2)
        place *= 2
    return result


def ffn_kernel(
    units,
    residual_ref,
    gain_ref,
    hits_ref,
    grad_all_ref,
    side_ref,
    shared_w_ref,
    e_gate_w_ref,
    e_up_w_ref,
    e_down_w_ref,
    res_grad_ref,
    res_low_ref,
    ffn_part_ref,
    e_gate_ref,
    e_up_ref,
    e_down_ref,
    shared_ref,
    small_ref,
    rows_all,
    dy_all,
    w_pre,
    w_down,
    both_all,
    scaled_all,
    scaled_now,
    sums,
    got_core,
    got_x1,
    got_y1,
    got_y2,
    got_x2,
    got_z,
    kept_ref,
    ffn_chunk,
    tile_gate,
    tile_up,
    tile_down,
    tile_shared,
    load_sems,
    store_sems,
    tile_sems,
    zs,
    links,
    cores,
    rs_core,
    rs_links,
    rs_z,
):
    shared_units, shared_pad, expert_units, experts, unit_pad, half, wide, capacity = units
    bf16, f32 = jnp.bfloat16, jnp.float32
    place, column = lax.axis_index("dp"), lax.axis_index("tensor")
    core, east, north = place % 2, (place // 2) % 2, place // 4
    rows, width = residual_ref.shape
    sibling = {"dp": other(place, 1)}
    x_side = {"dp": other(place, 2)}
    y_side = {"dp": other(place, 4)}
    levels = [{"tensor": other(column, k)} for k in range(4)]

    def level_of(k):
        low_i, high_i, low_k, high_k = column % 2, column // 2, k % 2, k // 2
        return (low_i + low_k - 2 * low_i * low_k) + 2 * (high_i + high_k - 2 * high_i * high_k)

    def remote(src, dst, sems, which, device):
        return pltpu.make_async_remote_copy(
            src_ref=src,
            dst_ref=dst,
            send_sem=sems.at[(0, *which)],
            recv_sem=sems.at[(1, *which)],
            device_id=device,
            device_id_type=MESH,
        )

    expert_first, side_first = shared_pad, shared_pad + expert_units
    loads = []
    for j, (target, first, ref) in enumerate(
        ((w_pre, 0, e_gate_w_ref), (w_pre, unit_pad, e_up_w_ref), (w_down, 0, e_down_w_ref))
    ):
        own_rows = pl.ds(first + expert_first, expert_units)
        shared_rows = pl.ds(first, shared_units)
        loads += [
            pltpu.make_async_copy(ref, target.at[own_rows], load_sems.at[8 + 2 * j]),
            pltpu.make_async_copy(
                shared_w_ref.at[j], target.at[shared_rows], load_sems.at[9 + 2 * j]
            ),
        ]
    for copy in loads:
        copy.start()
    for target, first in ((w_pre, 0), (w_pre, unit_pad), (w_down, 0)):
        gap = shared_pad - shared_units
        target[first + shared_units : first + shared_pad, :] = jnp.zeros((gap, width), bf16)
        rest = unit_pad - side_first
        target[first + side_first : first + unit_pad, :] = jnp.zeros((rest, width), bf16)
    w_pre[side_first : side_first + side_ref.shape[0], :] = side_ref[...]

    def load_grad(c, z):
        return pltpu.make_async_copy(
            grad_all_ref.at[:, :, c, z], dy_all.at[z, c], load_sems.at[c * 4 + z]
        )

    for c in range(2):
        for z in range(4):
            load_grad(c, z).start()

    barrier = pltpu.get_barrier_semaphore()
    partners = [sibling, x_side, y_side] + levels[1:]
    for partner in partners:
        pl.semaphore_signal(barrier, inc=1, device_id=partner, device_id_type=MESH)
    pl.semaphore_wait(barrier, len(partners))

    residual = residual_ref[...]
    scale_rows = lax.rsqrt(jnp.mean(residual * residual, 1, keepdims=True) + epsilon)
    normed = (residual * scale_rows * gain_ref[...]).astype(bf16)
    rows_all[column, core, north, east] = normed

    own_slot = rows_all.at[column, core, north, east]

    def z_copy(k):
        return remote(own_slot, own_slot, zs, (k,), levels[k])

    def block(k, c, y, x, cols=slice(None)):
        return rows_all.at[level_of(k), c, y, x, :, cols]

    first_half, second_half = pl.ds(0, half), pl.ds(half, width - half)

    def direct_copies(k):
        own = block(k, core, north, east)
        return [
            remote(own, own, links, (0, k), x_side),
            remote(own, own, links, (1, k), y_side),
            remote(own, own, cores, (0, k), sibling),
        ]

    def forward_copies(k):
        from_x = block(k, core, north, flip(east), first_half)
        from_y = block(k, core, flip(north), east, second_half)
        all_x = block(k, core, north, flip(east))
        all_y = block(k, core, flip(north), east)
        return [
            remote(from_x, from_x, links, (2, k), y_side),
            remote(from_y, from_y, links, (3, k), x_side),
            remote(all_x, all_x, cores, (1, k), sibling),
            remote(all_y, all_y, cores, (2, k), sibling),
        ]

    def corner_copy(k):
        corner = block(k, core, flip(north), flip(east))
        return remote(corner, corner, cores, (3, k), sibling)

    def start_direct(k):
        for copy in direct_copies(k):
            copy.start()

    def start_forward(k):
        for copy in direct_copies(k)[:2]:
            copy.wait_recv()
        for copy in forward_copies(k):
            copy.start()

    def start_corner(k):
        for copy in forward_copies(k)[:2]:
            copy.wait_recv()
        corner_copy(k).start()

    def finish_gather(k):
        direct_copies(k)[2].wait_recv()
        for copy in forward_copies(k)[2:]:
            copy.wait_recv()
        corner_copy(k).wait_recv()

    def core_copy(k):
        return remote(sums.at[k, flip(core)], got_core.at[k], rs_core, (k,), sibling)

    left, right = pl.ds(0, half), pl.ds(half, wide - half)

    def first_copies(k):
        return [
            remote(
                sums.at[k, core, :, flip(east), :, left],
                got_x1.at[k],
                rs_links, (0, k),
                x_side,
            ),
            remote(
                sums.at[k, core, flip(north), :, :, right],
                got_y1.at[k],
                rs_links, (1, k),
                y_side,
            ),
        ]

    def second_copies(k):
        return [
            remote(
                sums.at[k, core, flip(north), east, :, left],
                got_y2.at[k],
                rs_links, (2, k),
                y_side,
            ),
            remote(
                sums.at[k, core, north, flip(east), :, right],
                got_x2.at[k],
                rs_links, (3, k),
                x_side,
            ),
        ]

    def level_copy(k, device):
        return remote(sums.at[k, core, north, east], got_z.at[k], rs_z, (k,), device)

    def add(ref, value):
        ref[...] = (ref[...].astype(f32) + value.astype(f32)).astype(bf16)

    def after_core(k):
        core_copy(k).wait_recv()
        for y in range(2):
            for x in range(2):
                add(sums.at[k, core, y, x], got_core[k, y, x])
        for copy in first_copies(k):
            copy.start()

    def after_first(k):
        x_copy, y_copy = first_copies(k)
        x_copy.wait_recv()
        for y in range(2):
            add(sums.at[k, core, y, east, :, left], got_x1[k, y])
        y_copy.wait_recv()
        for x in range(2):
            add(sums.at[k, core, north, x, :, right], got_y1[k, x])
        for copy in second_copies(k):
            copy.start()

    def after_second(k):
        y_copy, x_copy = second_copies(k)
        y_copy.wait_recv()
        add(sums.at[k, core, north, east, :, left], got_y2[k])
        x_copy.wait_recv()
        add(sums.at[k, core, north, east, :, right], got_x2[k])
        for level in range(1, 4):

            @pl.when(k == level)
            def _():
                level_copy(k, levels[level]).start()

    for k in (1, 2, 3):
        z_copy(k).start()
    start_direct(0)

    tokens_dev = 4 * rows
    expert_id = lax.broadcasted_iota(jnp.int32, hits_ref.shape, 1)
    hits = jnp.sum(jnp.where(expert_id == place, hits_ref[...], 0.0), 1)
    earlier = lax.broadcasted_iota(jnp.int32, (tokens_dev, tokens_dev), 0)
    later = lax.broadcasted_iota(jnp.int32, (tokens_dev, tokens_dev), 1)
    slots = product(hits.astype(bf16), (earlier < later).astype(bf16))
    counts = jnp.sum(hits, 1, keepdims=True)
    counts_wide = jnp.broadcast_to(counts, (8, 128))
    order_row = lax.broadcasted_iota(jnp.int32, (8, 8), 0)
    order_col = lax.broadcasted_iota(jnp.int32, (8, 8), 1)
    before = lax.dot_general(
        (order_col < order_row).astype(f32),
        counts_wide,
        (((1,), (0,)), ((), ())),
        precision=highest,
        preferred_element_type=f32,
    )
    kept = jnp.where(slots + before[:, :1] < capacity, hits, 0.0).astype(bf16)
    eye = (
        lax.broadcasted_iota(jnp.int32, (8, 128), 0)
        == lax.broadcasted_iota(jnp.int32, (8, 128), 1)
    ).astype(bf16)
    kept_columns = product_tn(kept, eye)
    for d in range(8):
        y, x, c = d // 4, (d // 2) % 2, d % 2
        for z in range(4):
            first = (2 * y + x) * rows
            kept_ref[z, c, first : first + rows, :] = kept_columns[
                z * rows : (z + 1) * rows, d : d + 1
            ]

    for copy in loads:
        copy.wait()
    for c in range(2):
        for z in range(4):
            load_grad(c, z).wait()
    start_forward(0)
    z_copy(1).wait_recv()
    start_direct(1)
    start_corner(0)

    last = unit_pad - 128
    lane = lax.broadcasted_iota(jnp.int32, (1, 128), 1)
    first_lane = shared_pad + expert_units - last
    in_router = (lane >= first_lane) & (lane < first_lane + experts)
    is_shared = lane == first_lane + experts

    def routing(logit_block):
        top = jnp.max(jnp.where(in_router, logit_block, -jnp.inf), 1, keepdims=True)
        powers = jnp.where(in_router, jnp.exp(jnp.where(in_router, logit_block - top, 0.0)), 0.0)
        probs = powers / jnp.sum(powers, 1, keepdims=True)
        shared_logit = jnp.sum(jnp.where(is_shared, logit_block, 0.0), 1, keepdims=True)
        return probs, jax.nn.sigmoid(shared_logit)

    def compute(k, c):
        z = level_of(k)
        row_block = rows_all[z, c].reshape(4 * rows, width)
        dy_block = dy_all[z, c].reshape(4 * rows, width)
        pre_gate = product_nt(row_block, w_pre[:unit_pad])
        pre_up = product_nt(row_block, w_pre[unit_pad:])
        down_back = product_nt(dy_block, w_down[...])
        probs, shared_weight = routing(pre_gate[:, last:])
        kept = kept_ref[z, c]
        gate = (
            jnp.sum(jnp.where(lane == first_lane + place, probs, 0.0), 1, keepdims=True) * kept
        )
        dots, scaled, gate_rows, up_rows = [], [], [], []
        for begin, end, weight in (
            (0, shared_pad, shared_weight),
            (shared_pad, unit_pad, gate),
        ):
            cols = slice(begin, end)
            a, b, back = pre_gate[:, cols], pre_up[:, cols], down_back[:, cols]
            sig = jax.nn.sigmoid(a)
            silu = a * sig
            hidden = (silu * b).astype(bf16).astype(f32)
            dots.append(jnp.sum(hidden * back, 1, keepdims=True))
            scaled.append((hidden * weight).astype(bf16))
            grad = back * weight
            up_rows.append((grad * silu).astype(bf16))
            gate_rows.append((grad * b * sig * (1.0 + a * (1.0 - sig))).astype(bf16))
        both = jnp.concatenate(gate_rows + up_rows, 1)
        own_scaled = jnp.concatenate(scaled, 1)
        first_token = pl.multiple_of((2 * z + c) * 4 * rows, 4 * rows)
        both_all[:, pl.ds(first_token, 4 * rows)] = both.T
        scaled_all[:, pl.ds(first_token, 4 * rows)] = own_scaled.T
        scaled_now[c] = own_scaled
        dot_block = jnp.where(is_shared, dots[0], 0.0) + jnp.where(
            lane == first_lane + place, dots[1] * kept, 0.0
        )
        normed_grad = product(both, w_pre[...]).astype(bf16)
        sums[k, c, :, :, :, 0:width] = normed_grad.reshape(2, 2, rows, width)
        sums[k, c, :, :, :, width:wide] = dot_block.astype(bf16).reshape(2, 2, rows, wide - width)

    def store_chunk(k, c):
        return pltpu.make_async_copy(
            ffn_chunk, ffn_part_ref.at[level_of(k), c], store_sems.at[c]
        )

    def chunk(k, carry):
        @pl.when(k < 3)
        def _():
            start_forward(k + 1)

        @pl.when(k < 2)
        def _():
            for level in (2, 3):

                @pl.when(k + 2 == level)
                def _():
                    z_copy(level).wait_recv()

            start_direct(k + 2)

        finish_gather(k)
        def rows_of(i, carry):
            compute(k, (i + 1 + core) % 2)

            @pl.when(i == 0)
            def _():
                core_copy(k).start()

            return carry

        lax.fori_loop(0, 2, rows_of, 0)

        @pl.when(k >= 1)
        def _():
            after_first(k - 1)
            store_chunk(k - 1, 1).wait()

        def outputs(c, carry):
            part = product(scaled_now[c], w_down[...]).astype(bf16)

            @pl.when(c == 1)
            def _():
                store_chunk(k, 0).wait()

            ffn_chunk[...] = part.reshape(2, 2, rows, width)
            store_chunk(k, c).start()
            return carry

        lax.fori_loop(0, 2, outputs, 0)

        @pl.when(k < 3)
        def _():
            start_corner(k + 1)

        after_core(k)

        @pl.when(k >= 1)
        def _():
            after_second(k - 1)

        return carry

    lax.fori_loop(0, 4, chunk, 0)
    store_chunk(3, 1).wait()

    tile = tile_gate.shape[2]
    tiles = width // tile

    def tile_copies(i, slot):
        window = pl.ds(pl.multiple_of(i * tile, tile), tile)
        return [
            pltpu.make_async_copy(tile_gate.at[slot], e_gate_ref.at[:, window], tile_sems.at[slot, 0]),
            pltpu.make_async_copy(tile_up.at[slot], e_up_ref.at[:, window], tile_sems.at[slot, 1]),
            pltpu.make_async_copy(tile_down.at[slot], e_down_ref.at[:, window], tile_sems.at[slot, 2]),
            pltpu.make_async_copy(
                tile_shared.at[slot], shared_ref.at[i], tile_sems.at[slot, 3]
            ),
        ]

    tokens = rows * 32

    def weight_tile(i, carry):
        slot = i % 2

        @pl.when(i >= 2)
        def _():
            for copy in tile_copies(i - 2, slot):
                copy.wait()

        window = pl.ds(pl.multiple_of(i * tile, tile), tile)
        expert = slice(shared_pad, shared_pad + expert_units)
        row_tile = rows_all[:, :, :, :, :, window].reshape(tokens, tile)
        for j, (first, target) in enumerate(((0, tile_gate), (unit_pad, tile_up))):
            grad = product(both_all[first : first + unit_pad], row_tile).astype(bf16)
            target[slot] = grad[expert]
            tile_shared[slot, j] = grad[:shared_units]
        dy_tile = dy_all[:, :, :, :, :, window].reshape(tokens, tile)
        grad = product(scaled_all[...], dy_tile).astype(bf16)
        tile_down[slot] = grad[expert]
        tile_shared[slot, 2] = grad[:shared_units]
        for copy in tile_copies(i, slot):
            copy.start()

        @pl.when(i == 1)
        def _():
            after_first(3)

        @pl.when(i == 3)
        def _():
            after_second(3)

        return carry

    lax.fori_loop(0, tiles, weight_tile, 0)
    for i in (tiles - 2, tiles - 1):
        for copy in tile_copies(i, i % 2):
            copy.wait()

    total = sums[0, core, north, east].astype(f32)
    for k in (1, 2, 3):
        level_copy(k, levels[k]).wait_recv()
        total = total + got_z[k].astype(f32)
    dots = total[:, width:]
    unit = residual_ref[...] * scale_rows
    own_normed = rows_all[column, core, north, east]
    side_w = w_pre[last:unit_pad]
    probs, shared_weight = routing(product_nt(own_normed, side_w))
    router_dots = jnp.where(in_router, dots, 0.0)
    center = jnp.sum(probs * router_dots, 1, keepdims=True)
    side = jnp.where(in_router, probs * (router_dots - center), 0.0) + jnp.where(
        is_shared, dots * shared_weight * (1.0 - shared_weight), 0.0
    )
    side = side.astype(bf16)
    normed_grad = total[:, :width] + product(side, side_w)
    side_rows = product_tn(side, own_normed)
    small_ref[...] = side_rows[first_lane : first_lane + small_ref.shape[0]]
    small_ref[experts + 1 : experts + 2, :] = jnp.sum(normed_grad * unit, 0, keepdims=True)
    own_grad = dy_all[column, core, north, east].astype(f32)
    grad_f = own_grad + norm_back(normed_grad, unit, scale_rows, gain_ref[...])
    res_grad_ref[...] = grad_f
    res_low_ref[...] = grad_f.astype(bf16)

    for k in (1, 2, 3):
        z_copy(k).wait_send()
        level_copy(k, levels[k]).wait_send()
    for k in range(4):
        for copy in direct_copies(k) + forward_copies(k) + [corner_copy(k), core_copy(k)]:
            copy.wait_send()
        for copy in first_copies(k) + second_copies(k):
            copy.wait_send()


def ffn_layer(residual, ffn_gain, hits, grad_all, side, shared_w, expert_w, layout, capacity):
    shared_units, shared_pad, expert_units, experts, unit_pad = layout
    rows, width = residual.shape
    bf16, f32 = jnp.bfloat16, jnp.float32
    half = width // 2
    wide = width + 128
    tile = 256
    shape = jax.ShapeDtypeStruct
    vmem, anywhere = pl.BlockSpec(memory_space=pltpu.VMEM), pl.BlockSpec(memory_space=pl.ANY)
    dma = pltpu.SemaphoreType.DMA
    cost = pl.CostEstimate(
        flops=2 * 24 * 2048 * 2048 * 256, bytes_accessed=60 * 2**20, transcendentals=3 * 2**20
    )
    return pl.pallas_call(
        functools.partial(
            ffn_kernel,
            (shared_units, shared_pad, expert_units, experts, unit_pad, half, wide, capacity),
        ),
        out_shape=[
            shape((rows, width), f32),
            shape((rows, width), bf16),
            shape((4, 2, 2, 2, rows, width), bf16),
            shape((expert_units, width), bf16),
            shape((expert_units, width), bf16),
            shape((expert_units, width), bf16),
            shape((width // tile, 3, shared_units, tile), bf16),
            shape((16, width), f32),
        ],
        in_specs=[vmem, vmem, vmem, anywhere, vmem] + [anywhere] * 4,
        out_specs=[vmem, vmem] + [anywhere] * 5 + [vmem],
        scratch_shapes=[
            pltpu.VMEM((4, 2, 2, 2, rows, width), bf16),
            pltpu.VMEM((4, 2, 2, 2, rows, width), bf16),
            pltpu.VMEM((2 * unit_pad, width), bf16),
            pltpu.VMEM((unit_pad, width), bf16),
            pltpu.VMEM((2 * unit_pad, 32 * rows), bf16),
            pltpu.VMEM((unit_pad, 32 * rows), bf16),
            pltpu.VMEM((2, 4 * rows, unit_pad), bf16),
            pltpu.VMEM((4, 2, 2, 2, rows, wide), bf16),
            pltpu.VMEM((4, 2, 2, rows, wide), bf16),
            pltpu.VMEM((4, 2, rows, half), bf16),
            pltpu.VMEM((4, 2, rows, wide - half), bf16),
            pltpu.VMEM((4, rows, half), bf16),
            pltpu.VMEM((4, rows, wide - half), bf16),
            pltpu.VMEM((4, rows, wide), bf16),
            pltpu.VMEM((4, 2, 4 * rows, 1), f32),
            pltpu.VMEM((2, 2, rows, width), bf16),
            pltpu.VMEM((2, expert_units, tile), bf16),
            pltpu.VMEM((2, expert_units, tile), bf16),
            pltpu.VMEM((2, expert_units, tile), bf16),
            pltpu.VMEM((2, 3, shared_units, tile), bf16),
            dma((14,)),
            dma((2,)),
            dma((2, 4)),
            dma((2, 4)),
            dma((2, 4, 4)),
            dma((2, 4, 4)),
            dma((2, 4)),
            dma((2, 4, 4)),
            dma((2, 4)),
        ],
        compiler_params=pltpu.CompilerParams(
            collective_id=0, has_side_effects=True, vmem_limit_bytes=63 * 2**20
        ),
        cost_estimate=cost,
    )(residual, ffn_gain, hits, grad_all, side, shared_w, *expert_w)


def path_scalars(parents_ref, segment):
    path = [segment]
    for _ in range(LEVELS - 1):
        last = path[-1]
        parent = parents_ref[jnp.maximum(last, 0)]
        path.append(jnp.where(last >= 0, parent, -1))
    return path


class Line:
    def __init__(self, sems):
        self.sems = sems
        self.column = lax.axis_index("tensor")
        self.levels = [{"tensor": other(self.column, k)} for k in range(4)]
        self.outer = (self.column % 3) == 0
        self.inner = (self.column % 3) != 0

    def remote(self, src, dst, send, receive, device):
        return pltpu.make_async_remote_copy(
            src_ref=src,
            dst_ref=dst,
            send_sem=self.sems.at[0, send],
            recv_sem=self.sems.at[1, receive],
            device_id=device,
            device_id_type=MESH,
        )


class LineGather(Line):
    def __init__(self, slot, sems):
        super().__init__(sems)
        self.slot = slot

    def own(self, k):
        ref = self.slot(self.column)
        return self.remote(ref, ref, k, k, self.levels[k])

    def passed(self):
        ref = self.slot(other(self.column, 2))
        return self.remote(ref, ref, 0, 3, self.levels[1])

    def start(self):
        self.own(2).start()
        self.own(1).start()

        @pl.when(self.inner)
        def _():
            self.own(3).start()

    def forward(self):
        self.own(2).wait_recv()

        @pl.when(self.inner)
        def _():
            self.passed().start()

    def finish(self):
        self.own(1).wait_recv()
        self.own(3).wait_recv()

    def wait_sends(self):
        self.own(1).wait_send()
        self.own(2).wait_send()

        @pl.when(self.inner)
        def _():
            self.own(3).wait_send()
            self.passed().wait_send()


class LineSum(Line):
    def __init__(self, part, got, sems):
        super().__init__(sems)
        self.part, self.got = part, got

    def own(self, k):
        part = self.part(other(self.column, k))
        return self.remote(part, self.got.at[k], k, k, self.levels[k])

    def passed(self):
        part = self.part(other(self.column, 3))
        return self.remote(part, self.got.at[0], 0, 0, self.levels[1])

    def start(self):
        @pl.when(self.outer)
        def _():
            self.passed().start()
            self.own(2).start()
            self.got[3] = jnp.zeros(self.got.shape[1:], self.got.dtype)

        @pl.when(self.inner)
        def _():
            self.own(3).start()

        self.own(1).start()

    def forward(self):
        @pl.when(self.inner)
        def _():
            self.passed().wait_recv()
            part = self.part(other(self.column, 2))
            total = part[...].astype(jnp.float32) + self.got[0].astype(jnp.float32)
            part[...] = total.astype(part.dtype)
            self.own(2).start()

    def finish(self):
        self.own(1).wait_recv()
        self.own(2).wait_recv()

        @pl.when(self.inner)
        def _():
            self.own(3).wait_recv()

        total = self.part(self.column)[...].astype(jnp.float32)
        for k in (1, 2, 3):
            total = total + self.got[k].astype(jnp.float32)
        return total

    def wait_sends(self):
        self.own(1).wait_send()
        self.own(2).wait_send()

        @pl.when(self.outer)
        def _():
            self.passed().wait_send()

        @pl.when(self.inner)
        def _():
            self.own(3).wait_send()


class PlaneGather:
    def __init__(self, block, width, link_sems, core_sems):
        self.block, self.link_sems, self.core_sems = block, link_sems, core_sems
        place = lax.axis_index("dp")
        self.x, self.y, self.corner = other(place, 2), other(place, 4), other(place, 6)
        self.place = place
        self.x_side, self.y_side = {"dp": self.x}, {"dp": self.y}
        self.sibling = {"dp": other(place, 1)}
        self.halves = (pl.ds(0, width // 2), pl.ds(width // 2, width - width // 2))

    def copy(self, ref, sems, which, device):
        return pltpu.make_async_remote_copy(
            src_ref=ref,
            dst_ref=ref,
            send_sem=sems.at[0, which],
            recv_sem=sems.at[1, which],
            device_id=device,
            device_id_type=MESH,
        )

    def direct(self):
        own = self.block(self.place)
        return [
            self.copy(own, self.link_sems, 0, self.x_side),
            self.copy(own, self.link_sems, 1, self.y_side),
            self.copy(own, self.core_sems, 0, self.sibling),
        ]

    def forward(self):
        return [
            self.copy(self.block(self.x, self.halves[0]), self.link_sems, 2, self.y_side),
            self.copy(self.block(self.y, self.halves[1]), self.link_sems, 3, self.x_side),
            self.copy(self.block(self.x), self.core_sems, 1, self.sibling),
            self.copy(self.block(self.y), self.core_sems, 2, self.sibling),
        ]

    def last(self):
        return self.copy(self.block(self.corner), self.core_sems, 3, self.sibling)

    def start(self):
        for copy in self.direct():
            copy.start()

    def start_forward(self):
        for copy in self.direct()[:2]:
            copy.wait_recv()
        for copy in self.forward():
            copy.start()

    def start_last(self):
        for copy in self.forward()[:2]:
            copy.wait_recv()
        self.last().start()

    def finish(self):
        self.direct()[2].wait_recv()
        for copy in self.forward()[2:]:
            copy.wait_recv()
        self.last().wait_recv()

    def wait_sends(self):
        for copy in self.direct() + self.forward() + [self.last()]:
            copy.wait_send()


def turn(values, cosine, sine):
    heads = []
    for begin in range(0, values.shape[1], HEAD_DIM):
        head = values[:, begin : begin + HEAD_DIM]
        heads.append(head * cosine + pltpu.roll(head, HEAD_DIM // 2, 1) * sine)
    return jnp.concatenate(heads, 1)


def front_kernel(
    score_scale,
    shared_units,
    parents_ref,
    hidden_ref,
    gain_ref,
    bias_ref,
    freqs_ref,
    hits_ref,
    out_grad_ref,
    w_query_ref,
    w_key_ref,
    w_value_ref,
    w_out_ref,
    s_gate_ref,
    s_up_ref,
    s_down_ref,
    residual_ref,
    query_ref,
    key_ref,
    value_ref,
    log_total_ref,
    attended_ref,
    normed_ref,
    cosine_ref,
    sine_ref,
    hits_all_ref,
    grad_all_ref,
    shared_ref,
    weights,
    kv_all,
    hits_all,
    part_send,
    part_z,
    s_tiles,
    t_tiles,
    load_sems,
    tile_sems,
    store_sems,
    hit_sems,
    part_sems,
    kv_links,
    kv_cores,
    head_links,
    head_cores,
    tail_links,
    tail_cores,
):
    bf16, f32 = jnp.bfloat16, jnp.float32
    place, column = lax.axis_index("dp"), lax.axis_index("tensor")
    tok_rows, width = hidden_ref.shape
    rows = tok_rows // 4
    local_width = w_query_ref.shape[1]
    levels = [{"tensor": other(column, k)} for k in range(4)]
    peers = [{"dp": other(place, j)} for j in range(8)]

    loads = [
        pltpu.make_async_copy(ref, weights.at[i], load_sems.at[i])
        for i, ref in enumerate((w_query_ref, w_key_ref, w_value_ref, w_out_ref))
    ]
    own_grad = pltpu.make_async_copy(out_grad_ref, grad_all_ref.at[place], load_sems.at[4])
    for copy in loads:
        copy.start()
    own_grad.start()
    hits_all[place] = hits_ref[...]

    barrier = pltpu.get_barrier_semaphore()
    partners = peers[1:] + levels[1:]
    for partner in partners:
        pl.semaphore_signal(barrier, inc=1, device_id=partner, device_id_type=MESH)
    pl.semaphore_wait(barrier, len(partners))

    def grad_block(first, count):
        def block(d, cols=slice(None)):
            return grad_all_ref.at[d, pl.ds(first, count), :, cols]

        return block

    head_gather = PlaneGather(grad_block(0, 1), width, head_links, head_cores)
    tail_gather = PlaneGather(grad_block(1, 3), width, tail_links, tail_cores)
    kv_gather = PlaneGather(
        lambda d, cols=slice(None): kv_all.at[d, :, cols], 2 * local_width, kv_links, kv_cores
    )
    own_grad.wait()
    head_gather.start()

    def hit_copy(j):
        return pltpu.make_async_remote_copy(
            src_ref=hits_all.at[place],
            dst_ref=hits_all.at[place],
            send_sem=hit_sems.at[0, j],
            recv_sem=hit_sems.at[1, j],
            device_id=peers[j],
            device_id_type=MESH,
        )

    for j in range(1, 8):
        hit_copy(j).start()

    path = path_scalars(parents_ref, place)
    depth = jnp.float32(-1.0)
    for segment in path:
        depth = depth + jnp.where(segment >= 0, 1.0, 0.0)
    row_ids = lax.broadcasted_iota(jnp.int32, (tok_rows, HEAD_DIM), 0).astype(f32)
    lane = lax.broadcasted_iota(jnp.int32, (tok_rows, HEAD_DIM), 1)
    angles = (depth * SEG + row_ids) * freqs_ref[...]
    cosine = jnp.cos(angles)
    sine = jnp.where(lane < HEAD_DIM // 2, -1.0, 1.0) * jnp.sin(angles)
    cosine_ref[...] = cosine
    sine_ref[...] = sine
    hidden_f = hidden_ref[...].astype(f32)
    scale_rows = lax.rsqrt(jnp.mean(hidden_f * hidden_f, 1, keepdims=True) + epsilon)
    normed_ref[...] = (hidden_f * scale_rows * gain_ref[...]).astype(bf16)
    for copy in loads[1:3]:
        copy.wait()
    key = product(normed_ref[...], weights[1]) + bias_ref[1:2, :]
    kv_all[place, :, :local_width] = turn(key, cosine, sine).astype(bf16)
    value = product(normed_ref[...], weights[2]) + bias_ref[2:3, :]
    kv_all[place, :, local_width:] = value.astype(bf16)
    kv_gather.start()
    loads[0].wait()
    query = product(normed_ref[...], weights[0]) + bias_ref[0:1, :]
    query_ref[...] = turn(query, cosine, sine).astype(bf16)

    tile, span = s_tiles.shape[2:]
    shared_first = place * shared_units
    shared_base = jnp.minimum(shared_first // 128 * 128, s_gate_ref.shape[1] - span)
    shared_skip = shared_first - shared_base

    def tile_loads(i, slot):
        window = pl.ds(pl.multiple_of(i * tile, tile), tile)
        columns = pl.ds(pl.multiple_of(shared_base, 128), span)
        return [
            pltpu.make_async_copy(
                ref.at[window, columns], s_tiles.at[slot, j], tile_sems.at[slot, j]
            )
            for j, ref in enumerate((s_gate_ref, s_up_ref, s_down_ref))
        ]

    def tile_stores(i, slot):
        window = pl.ds(pl.multiple_of(i * tile, tile), tile)
        units = pl.ds(pl.multiple_of(shared_skip, 16), shared_units)
        return [
            pltpu.make_async_copy(
                t_tiles.at[slot, j, units], shared_ref.at[j, :, window], store_sems.at[slot, j]
            )
            for j in range(3)
        ]

    tiles = width // tile

    def pack(i, carry):
        slot = i % 2

        @pl.when(i + 1 < tiles)
        def _():
            for copy in tile_loads(i + 1, (i + 1) % 2):
                copy.start()

        for copy in tile_loads(i, slot):
            copy.wait()

        @pl.when(i >= 2)
        def _():
            for copy in tile_stores(i - 2, slot):
                copy.wait()

        for j in range(3):
            t_tiles[slot, j] = s_tiles[slot, j].T
        for copy in tile_stores(i, slot):
            copy.start()
        return carry

    for copy in tile_loads(0, 0):
        copy.start()
    lax.fori_loop(0, tiles // 2, pack, 0)
    kv_gather.start_forward()
    lax.fori_loop(tiles // 2, tiles, pack, 0)
    kv_gather.start_last()
    head_gather.start_forward()
    for i in (tiles - 2, tiles - 1):
        for copy in tile_stores(i, i % 2):
            copy.wait()
    kv_gather.finish()
    tail_gather.start()

    for level, segment in enumerate(path):
        block = kv_all[jnp.maximum(segment, 0)]
        key_ref[level * tok_rows : (level + 1) * tok_rows, :] = block[:, :local_width]
        value_ref[level * tok_rows : (level + 1) * tok_rows, :] = block[:, local_width:]
    key_rows = key_ref.shape[0]
    row_id = lax.broadcasted_iota(jnp.int32, (tok_rows, key_rows), 0)
    col_id = lax.broadcasted_iota(jnp.int32, (tok_rows, key_rows), 1)
    allowed = row_id >= col_id
    for level in range(1, LEVELS):
        barred = jnp.where(path[level] >= 0, key_rows, 0)
        inside = (col_id >= level * tok_rows) & (col_id < (level + 1) * tok_rows)
        allowed = allowed | (inside & (col_id < barred))

    def head(h, carry):
        cols = pl.ds(pl.multiple_of(h * HEAD_DIM, HEAD_DIM), HEAD_DIM)
        scores = product_nt(query_ref[:, cols], key_ref[:, cols]) * score_scale
        scores = jnp.where(allowed, scores, -jnp.inf)
        top = jnp.max(scores, 1, keepdims=True)
        powers = jnp.exp(scores - top)
        total = jnp.sum(powers, 1, keepdims=True)
        log_total_ref[h] = top + jnp.log(total)
        probs = (powers * (1.0 / total)).astype(bf16)
        attended_ref[:, cols] = product(probs, value_ref[:, cols]).astype(bf16)
        return carry

    lax.fori_loop(0, local_width // HEAD_DIM, head, 0)

    loads[3].wait()
    for quarter in range(4):
        mine = slice(quarter * rows, (quarter + 1) * rows)
        part_send[quarter] = product_nt(attended_ref[mine, :], weights[3]).astype(bf16)

    line = LineSum(lambda z: part_send.at[z], part_z, part_sems)
    line.start()
    head_gather.start_last()
    line.forward()
    tail_gather.start_forward()
    attn = line.finish()
    own_rows = pl.ds(pl.multiple_of(column * rows, rows), rows)
    residual_ref[...] = hidden_ref[own_rows, :].astype(f32) + attn
    tail_gather.start_last()
    head_gather.finish()
    for j in range(1, 8):
        hit_copy(j).wait_recv()
    hits_all_ref[...] = hits_all[...]
    tail_gather.finish()

    for gather in (kv_gather, head_gather, tail_gather):
        gather.wait_sends()
    for j in range(1, 8):
        hit_copy(j).wait_send()
    line.wait_sends()


def front_layer(score_scale, shared_units, operands):
    hidden, w_query = operands[1], operands[7]
    tok_rows, width = hidden.shape
    rows, local_width = tok_rows // 4, w_query.shape[1]
    heads = local_width // HEAD_DIM
    tile, span = 256, 384
    bf16, f32 = jnp.bfloat16, jnp.float32
    shape = jax.ShapeDtypeStruct
    vmem, anywhere = pl.BlockSpec(memory_space=pltpu.VMEM), pl.BlockSpec(memory_space=pl.ANY)
    smem = pl.BlockSpec(memory_space=pltpu.SMEM)
    dma = pltpu.SemaphoreType.DMA
    return pl.pallas_call(
        functools.partial(front_kernel, score_scale, shared_units),
        out_shape=[
            shape((rows, width), f32),
            shape((tok_rows, local_width), bf16),
            shape((LEVELS * tok_rows, local_width), bf16),
            shape((LEVELS * tok_rows, local_width), bf16),
            shape((heads, tok_rows, 1), f32),
            shape((tok_rows, local_width), bf16),
            shape((tok_rows, width), bf16),
            shape((tok_rows, HEAD_DIM), f32),
            shape((tok_rows, HEAD_DIM), f32),
            shape((8, 16, tok_rows), f32),
            shape((8, 4, rows, width), bf16),
            shape((3, shared_units, width), bf16),
        ],
        in_specs=[smem] + [vmem] * 6 + [anywhere] * 7,
        out_specs=[vmem] * 10 + [anywhere] * 2,
        scratch_shapes=[
            pltpu.VMEM((4, width, local_width), bf16),
            pltpu.VMEM((8, tok_rows, 2 * local_width), bf16),
            pltpu.VMEM((8, 16, tok_rows), f32),
            pltpu.VMEM((4, rows, width), bf16),
            pltpu.VMEM((4, rows, width), bf16),
            pltpu.VMEM((2, 3, tile, span), bf16),
            pltpu.VMEM((2, 3, span, tile), bf16),
            dma((5,)),
            dma((2, 3)),
            dma((2, 3)),
            dma((2, 8)),
            dma((2, 4)),
        ]
        + [dma((2, 4))] * 6,
        compiler_params=pltpu.CompilerParams(
            collective_id=2, has_side_effects=True, vmem_limit_bytes=56 * 2**20
        ),
        cost_estimate=pl.CostEstimate(
            flops=2 * 2**31, bytes_accessed=40 * 2**20, transcendentals=2**21
        ),
    )(*operands)


class PlaneSum:
    def __init__(self, mine, theirs, got_core, got_x1, got_y1, got_y2, got_x2, core_sems, sems):
        self.mine, self.theirs = mine, theirs
        self.got = (got_core, got_x1, got_y1, got_y2, got_x2)
        self.core_sems, self.sems = core_sems, sems
        self.wide = got_core.shape[-1]
        self.half = got_x1.shape[-1]
        self.left, self.right = pl.ds(0, self.half), pl.ds(self.half, self.wide - self.half)
        place = lax.axis_index("dp")
        self.core, self.east, self.north = place % 2, (place // 2) % 2, place // 4
        self.sibling = {"dp": other(place, 1)}
        self.x_side, self.y_side = {"dp": other(place, 2)}, {"dp": other(place, 4)}

    def remote(self, src, dst, sems, which, device):
        return pltpu.make_async_remote_copy(
            src_ref=src,
            dst_ref=dst,
            send_sem=sems.at[(0, *which)],
            recv_sem=sems.at[(1, *which)],
            device_id=device,
            device_id_type=MESH,
        )

    def core_copy(self, k):
        return self.remote(
            self.theirs(k), self.got[0].at[k], self.core_sems, (k,), self.sibling
        )

    def first_copies(self, k):
        mine = self.mine(k)
        return [
            self.remote(
                mine.at[:, flip(self.east), :, self.left],
                self.got[1].at[k],
                self.sems,
                (0, k),
                self.x_side,
            ),
            self.remote(
                mine.at[flip(self.north), :, :, self.right],
                self.got[2].at[k],
                self.sems,
                (1, k),
                self.y_side,
            ),
        ]

    def second_copies(self, k):
        mine = self.mine(k)
        return [
            self.remote(
                mine.at[flip(self.north), self.east, :, self.left],
                self.got[3].at[k],
                self.sems,
                (2, k),
                self.y_side,
            ),
            self.remote(
                mine.at[self.north, flip(self.east), :, self.right],
                self.got[4].at[k],
                self.sems,
                (3, k),
                self.x_side,
            ),
        ]

    def add(self, ref, value):
        ref[...] = (ref[...].astype(jnp.float32) + value.astype(jnp.float32)).astype(jnp.bfloat16)

    def start(self, k):
        self.core_copy(k).start()

    def after_core(self, k):
        self.core_copy(k).wait_recv()
        mine = self.mine(k)
        for y in range(2):
            for x in range(2):
                self.add(mine.at[y, x], self.got[0][k, y, x])
        for copy in self.first_copies(k):
            copy.start()

    def after_first(self, k):
        x_copy, y_copy = self.first_copies(k)
        mine = self.mine(k)
        x_copy.wait_recv()
        for y in range(2):
            self.add(mine.at[y, self.east, :, self.left], self.got[1][k, y])
        y_copy.wait_recv()
        for x in range(2):
            self.add(mine.at[self.north, x, :, self.right], self.got[2][k, x])
        for copy in self.second_copies(k):
            copy.start()

    def after_second(self, k):
        y_copy, x_copy = self.second_copies(k)
        own = self.mine(k).at[self.north, self.east]
        y_copy.wait_recv()
        self.add(own.at[:, self.left], self.got[3][k])
        x_copy.wait_recv()
        self.add(own.at[:, self.right], self.got[4][k])
        return own

    def wait_sends(self, k):
        self.core_copy(k).wait_send()
        for copy in self.first_copies(k) + self.second_copies(k):
            copy.wait_send()


def plane_scratch(count, rows, wide):
    half = wide // 2
    bf16, dma = jnp.bfloat16, pltpu.SemaphoreType.DMA
    return [
        pltpu.VMEM((count, 2, 2, rows, wide), bf16),
        pltpu.VMEM((count, 2, rows, half), bf16),
        pltpu.VMEM((count, 2, rows, wide - half), bf16),
        pltpu.VMEM((count, rows, half), bf16),
        pltpu.VMEM((count, rows, wide - half), bf16),
        dma((2, count)),
        dma((2, 4, count)),
    ]


def unturn(grad, cosine, sine):
    heads = []
    for begin in range(0, grad.shape[1], HEAD_DIM):
        head = grad[:, begin : begin + HEAD_DIM]
        heads.append(head * cosine - pltpu.roll(head, HEAD_DIM // 2, 1) * sine)
    return jnp.concatenate(heads, 1)


def back_kernel(
    score_scale,
    gain_row,
    residual_ref,
    res_grad_ref,
    res_low_ref,
    ffn_part_ref,
    shared_ref,
    small_ref,
    query_ref,
    key_ref,
    value_ref,
    parents_ref,
    log_total_ref,
    attended_ref,
    normed_ref,
    hidden_ref,
    gain_ref,
    cosine_ref,
    sine_ref,
    w_out_ref,
    w_query_ref,
    w_key_ref,
    w_value_ref,
    hidden_out_ref,
    hidden_grad_ref,
    grad_query_ref,
    grad_key_ref,
    grad_value_ref,
    grad_out_ref,
    shared_got,
    small_out_ref,
    bias_out_ref,
    low_all,
    w_qkv,
    out_mine,
    out_z,
    kv_sums,
    w_sums,
    kv_path,
    attended_grad,
    query_grad,
    pre_grads,
    part,
    part_send,
    part_z,
    hidden_stage,
    shared_stage,
    small_send,
    small_got,
    small_z,
    *rest,
):
    bf16, f32 = jnp.bfloat16, jnp.float32
    out_scr, rest = rest[:7], rest[7:]
    kv_scr, rest = rest[:7], rest[7:]
    w_scr, rest = rest[:7], rest[7:]
    wkv_sems, rest = rest[:2], rest[2:]
    load_sems, low_sems, out_sems, part_sems, end_sems, shared_sems, small_sems, small_z_sems = rest
    place, column = lax.axis_index("dp"), lax.axis_index("tensor")
    core, east, north = place % 2, (place // 2) % 2, place // 4
    rows, width = residual_ref.shape
    tok_rows, local_width = query_ref.shape
    levels = [{"tensor": other(column, k)} for k in range(4)]
    peers = [{"dp": other(place, j)} for j in range(8)]

    def remote(src, dst, sems, which, device):
        return pltpu.make_async_remote_copy(
            src_ref=src,
            dst_ref=dst,
            send_sem=sems.at[(0, *which)],
            recv_sem=sems.at[(1, *which)],
            device_id=device,
            device_id_type=MESH,
        )

    def load_out(z):
        return pltpu.make_async_copy(ffn_part_ref.at[z, core], out_mine.at[z], load_sems.at[z])

    loads = [
        pltpu.make_async_copy(w_query_ref, w_qkv.at[0], load_sems.at[5]),
        pltpu.make_async_copy(w_key_ref, w_qkv.at[1], load_sems.at[6]),
        pltpu.make_async_copy(w_out_ref, w_qkv.at[2], load_sems.at[4]),
    ]
    load_value = pltpu.make_async_copy(w_value_ref, w_qkv.at[2], load_sems.at[7])
    load_shared = pltpu.make_async_copy(shared_ref.at[place], shared_stage, load_sems.at[9])
    load_shared.start()
    for z in range(4):
        load_out(z).start()
    for copy in loads:
        copy.start()

    barrier = pltpu.get_barrier_semaphore()
    partners = peers[1:] + levels[1:]
    for partner in partners:
        pl.semaphore_signal(barrier, inc=1, device_id=partner, device_id_type=MESH)
    pl.semaphore_wait(barrier, len(partners))

    out_sum = PlaneSum(
        lambda k: out_mine.at[k], lambda k: ffn_part_ref.at[k, flip(core)], *out_scr
    )
    kv_sum = PlaneSum(
        lambda k: kv_sums.at[k, core], lambda k: kv_sums.at[k, flip(core)], *kv_scr
    )
    w_sum = PlaneSum(
        lambda k: w_sums.at[k, core], lambda k: w_sums.at[k, flip(core)], *w_scr
    )
    wkv_sum = PlaneSum(
        lambda k: kv_sums.at[k, core],
        lambda k: kv_sums.at[k, flip(core)],
        *kv_scr[:5],
        *wkv_sems,
    )

    low_all[column] = res_low_ref[...]
    low_line = LineGather(lambda z: low_all.at[z], low_sems)
    low_line.start()
    order = [other(column, k) for k in (1, 3, 2, 0)]
    for z in order:
        out_sum.start(z)
    kv_path[...] = jnp.zeros(kv_path.shape, f32)
    for z in range(4):
        load_out(z).wait()
    for z in order:
        out_sum.after_core(z)
    for copy in loads:
        copy.wait()

    out_line = LineSum(lambda z: out_mine.at[z, north, east], out_z, out_sems)
    low_line.forward()

    half_rows = tok_rows // 2
    key_rows = key_ref.shape[0]
    row_id = lax.broadcasted_iota(jnp.int32, (half_rows, key_rows), 0)
    col_id = lax.broadcasted_iota(jnp.int32, (half_rows, key_rows), 1)
    path = path_scalars(parents_ref, place)
    reached = col_id < 0
    for level in range(1, LEVELS):
        barred = jnp.where(path[level] >= 0, key_rows, 0)
        inside = (col_id >= level * tok_rows) & (col_id < (level + 1) * tok_rows)
        reached = reached | (inside & (col_id < barred))

    def half(i, carry):
        pair = (column // 2 + i) % 2
        first = pl.multiple_of(pair * half_rows, half_rows)
        window = pl.ds(first, half_rows)

        @pl.when(i == 0)
        def _():
            low_line.own(1).wait_recv()

        @pl.when(i == 1)
        def _():
            low_line.own(3).wait_recv()

        low_rows = low_all[pl.ds(2 * pair, 2)].reshape(half_rows, width)
        attended_grad[window, :] = product(low_rows, w_qkv[2]).astype(bf16)
        allowed = (row_id + first >= col_id) | reached

        def head(h, carry):
            cols = pl.ds(pl.multiple_of(h * HEAD_DIM, HEAD_DIM), HEAD_DIM)
            value_cols = pl.ds(pl.multiple_of(local_width + h * HEAD_DIM, HEAD_DIM), HEAD_DIM)
            query, key, value = query_ref[window, cols], key_ref[:, cols], value_ref[:, cols]
            grad = attended_grad[window, cols]
            scores = jnp.where(allowed, product_nt(query, key) * score_scale, -jnp.inf)
            weights = jnp.exp(scores - log_total_ref[h, window])
            weight_grad = product_nt(grad, value)
            center = jnp.sum(weights * weight_grad, 1, keepdims=True)
            score_grad = (weights * (weight_grad - center)).astype(bf16)
            query_grad[window, cols] = product(score_grad, key) * score_scale
            kv_path[:, cols] += product_tn(score_grad, query) * score_scale
            kv_path[:, value_cols] += product_tn(weights.astype(bf16), grad)
            return carry

        lax.fori_loop(0, local_width // HEAD_DIM, head, 0)

        @pl.when(i == 0)
        def _():
            out_sum.after_first(order[0])

        return carry

    lax.fori_loop(0, 2, half, 0)
    for z in order[1:]:
        out_sum.after_first(z)
    load_value.start()

    part_rows = rows // 2

    def kv_blocks(i, c):
        which, y, x = i // 4, (i // 2) % 2, i % 2
        segment = 4 * y + 2 * x + c
        total = jnp.zeros((4, part_rows, 2 * local_width), f32)
        for level in range(1, LEVELS):
            spot = jnp.where(path[level] == segment, 1.0, 0.0)
            total = total + spot * kv_rows(level, which)
        kv_sums[which, c, y, x] = total.reshape(4 * part_rows, 2 * local_width).astype(bf16)
        return c

    def kv_rows(level, which):
        rows_view = kv_path.at[level * tok_rows : (level + 1) * tok_rows]
        pieces = []
        for z in range(4):
            start = pl.multiple_of(z * rows + which * part_rows, part_rows)
            pieces.append(rows_view[pl.ds(start, part_rows), :])
        return jnp.stack(pieces)

    lax.fori_loop(0, 4, kv_blocks, flip(core))
    kv_sum.start(0)
    lax.fori_loop(4, 8, kv_blocks, flip(core))
    kv_sum.start(1)
    lax.fori_loop(0, 8, kv_blocks, core)
    for which in range(2):
        own_kv = kv_sums.at[which, core, north, east]
        added = own_kv[...].astype(f32) + kv_rows(0, which).reshape(4 * part_rows, -1)
        own_kv[...] = added.astype(bf16)
        kv_sum.after_core(which)

    def bias_of(which, grad, begin):
        bias = jnp.sum(grad.astype(f32), 0, keepdims=True)
        for h in range(local_width // HEAD_DIM):
            spot = slice(4 * which + h, 4 * which + h + 1)
            added = bias[:, h * HEAD_DIM : (h + 1) * HEAD_DIM]
            if not begin:
                added = added + small_send[0, spot, 2 * HEAD_DIM :]
            small_send[0, spot, 2 * HEAD_DIM :] = added

    small_send[0, :, 2 * HEAD_DIM :] = jnp.zeros((16, HEAD_DIM), f32)
    query_pre = unturn(query_grad[...], cosine_ref[...], sine_ref[...]).astype(bf16)
    pre_grads[0] = query_pre.reshape(4, 2, part_rows, local_width)
    bias_of(0, query_pre, True)
    part[...] = product_nt(query_pre, w_qkv[0]).reshape(4, 2, part_rows, width)
    def block_index(place_of):
        return place_of % 2, place_of // 4, (place_of // 2) % 2

    def out_weights(i, carry):
        c, y, x = block_index(i)
        window = pl.ds(pl.multiple_of(i * tok_rows, tok_rows), tok_rows)
        lhs = low_all[:, :, window].reshape(tok_rows, tok_rows)
        w_sums[0, c, y, x] = product_tn(lhs, attended_ref[...]).astype(bf16)
        return carry

    def query_weights(i, carry):
        c, y, x = block_index(i)
        window = pl.ds(pl.multiple_of(i * tok_rows, tok_rows), tok_rows)
        rows_pre = pre_grads[0].reshape(tok_rows, local_width)
        w_sums[1, c, y, x] = product_tn(normed_ref[:, window], rows_pre).astype(bf16)
        return carry

    lax.fori_loop(0, 8, out_weights, 0)
    w_sum.start(0)
    lax.fori_loop(0, 8, query_weights, 0)
    w_sum.start(1)
    kv_sum.after_first(0)
    kv_sum.after_first(1)
    for z in order:
        out_sum.after_second(z)
    out_line.start()

    load_value.wait()
    hidden_f = hidden_ref[...].astype(f32)
    unit_scale = lax.rsqrt(jnp.mean(hidden_f * hidden_f, 1, keepdims=True) + epsilon)

    part_lines = [
        LineSum(
            lambda z, which=which: part_send.at[which, z],
            part_z.at[which],
            part_sems.at[which],
        )
        for which in range(2)
    ]

    for which in range(2):
        own_kv = kv_sum.after_second(which)
        cos_rows = cosine_ref[...].reshape(4, 2, part_rows, HEAD_DIM)[:, which]
        sin_rows = sine_ref[...].reshape(4, 2, part_rows, HEAD_DIM)[:, which]
        key_pre = unturn(
            own_kv[:, :local_width].astype(f32),
            cos_rows.reshape(4 * part_rows, HEAD_DIM),
            sin_rows.reshape(4 * part_rows, HEAD_DIM),
        ).astype(bf16)
        value_pre = own_kv[:, local_width:]
        pre_grads[1, :, which] = key_pre.reshape(4, part_rows, local_width)
        pre_grads[2, :, which] = value_pre.reshape(4, part_rows, local_width)
        bias_of(1, key_pre, which == 0)
        bias_of(2, value_pre, which == 0)
        added = product_nt(key_pre, w_qkv[1]) + product_nt(value_pre, w_qkv[2])
        whole = part[:, which] + added.reshape(4, part_rows, width)
        part[:, which] = whole
        part_send[which] = whole.astype(bf16)
        part_lines[which].start()
        if which == 0:
            out_line.forward()


    def shared_copy(j):
        return remote(
            shared_ref.at[other(place, j)], shared_got.at[place], shared_sems, (j,), peers[j]
        )

    for k in range(2):
        w_sum.after_core(k)
    part_lines[0].forward()
    attn_gain_row = jnp.sum(
        part[...].reshape(tok_rows, width) * (hidden_f * unit_scale), 0, keepdims=True
    )
    def key_value_weights(i, carry):
        c, y, x = block_index(i)
        window = pl.ds(pl.multiple_of(i * tok_rows, tok_rows), tok_rows)
        lhs = normed_ref[:, window]
        for which, cols in ((1, slice(0, local_width)), (2, slice(local_width, None))):
            rows_pre = pre_grads[which].reshape(tok_rows, local_width)
            grad = product_tn(lhs, rows_pre).astype(bf16)
            for k in range(2):
                piece = slice(k * half_rows, (k + 1) * half_rows)
                kv_sums[k, c, y, x, :, cols] = grad[piece]
        return carry

    for k in range(2):
        kv_sum.wait_sends(k)
    lax.fori_loop(0, 8, key_value_weights, 0)
    for k in range(2):
        wkv_sum.start(k)
    part_lines[1].forward()

    bias_rows = small_send[0, :, 2 * HEAD_DIM :]
    for d in range(8):
        small_send[d, :, : 2 * HEAD_DIM] = small_ref[:, d * tok_rows : (d + 1) * tok_rows]
        small_send[d, gain_row : gain_row + 1, : 2 * HEAD_DIM] = attn_gain_row[
            :, d * tok_rows : (d + 1) * tok_rows
        ]
        small_send[d, :, 2 * HEAD_DIM :] = bias_rows

    def small_copy(j):
        return remote(
            small_send.at[other(place, j)], small_got.at[j], small_sems, (j,), peers[j]
        )

    for j in range(1, 8):
        small_copy(j).start()

    w_sum.after_first(0)
    for k in range(2):
        wkv_sum.after_core(k)
    w_sum.after_first(1)
    own_shared = pltpu.make_async_copy(shared_stage, shared_got.at[place], load_sems.at[8])
    load_shared.wait()
    own_shared.start()

    total = small_send[place]
    for j in range(1, 8):
        small_copy(j).wait_recv()
        total = total + small_got[j]
    bias_out_ref[...] = total[:, 2 * HEAD_DIM :]
    small_z[column] = total[:, : 2 * HEAD_DIM]
    own_small = small_z.at[column]
    small_levels = [
        remote(own_small, own_small, small_z_sems, (k,), levels[k]) for k in (1, 2, 3)
    ]
    for copy in small_levels:
        copy.start()

    end_lines = [
        LineGather(
            lambda z, which=which, piece=piece: hidden_stage.at[which, z, piece],
            end_sems.at[which, piece],
        )
        for which in range(2)
        for piece in range(2)
    ]

    for which in range(2):
        attn_grad = part_lines[which].finish()
        start = pl.multiple_of(column * rows + which * part_rows, part_rows)
        own_hidden = hidden_ref[pl.ds(start, part_rows), :].astype(f32)
        own_scale = lax.rsqrt(jnp.mean(own_hidden * own_hidden, 1, keepdims=True) + epsilon)
        own_grad = res_grad_ref[which * part_rows : (which + 1) * part_rows, :]
        hidden_stage[0, column, which] = (
            own_grad + norm_back(attn_grad, own_hidden * own_scale, own_scale, gain_ref[...])
        ).astype(bf16)
        end_lines[which].start()
        if which == 0:
            grad_out_ref[...] = w_sum.after_second(0)[...]
            for k in range(2):
                wkv_sum.after_first(k)
            for j in (6, 7, 2, 3, 4, 5, 1):
                shared_copy(j).start()

    end_lines[0].forward()
    out = residual_ref[...] + out_line.finish()
    hidden_stage[1, column] = out.astype(bf16).reshape(2, part_rows, width)
    end_lines[1].forward()
    end_lines[2].start()
    end_lines[3].start()

    grad_query_ref[...] = w_sum.after_second(1)[...]
    for copy in small_levels:
        copy.wait_recv()
    small_out_ref[...] = (small_z[0] + small_z[1]) + (small_z[2] + small_z[3])
    for k in range(2):
        own_wkv = wkv_sum.after_second(k)
        piece = slice(k * half_rows, (k + 1) * half_rows)
        grad_key_ref[piece, :] = own_wkv[:, :local_width]
        grad_value_ref[piece, :] = own_wkv[:, local_width:]

    end_lines[2].forward()
    end_lines[3].forward()
    own_shared.wait()
    for j in range(1, 8):
        shared_copy(j).wait_recv()
    for line in end_lines:
        line.finish()
    ends = [
        pltpu.make_async_copy(hidden_stage.at[0], hidden_grad_ref, load_sems.at[10]),
        pltpu.make_async_copy(hidden_stage.at[1], hidden_out_ref, load_sems.at[11]),
    ]
    for copy in ends:
        copy.start()
    for copy in ends:
        copy.wait()

    for copy in small_levels:
        copy.wait_send()
    for line in [low_line, out_line] + part_lines + end_lines:
        line.wait_sends()
    for z in range(4):
        out_sum.wait_sends(z)
    for k in range(2):
        w_sum.wait_sends(k)
        wkv_sum.wait_sends(k)
    for j in range(1, 8):
        small_copy(j).wait_send()
        shared_copy(j).wait_send()


def back_layer(score_scale, gain_row, operands):
    (
        residual,
        res_grad,
        res_low,
        ffn_part,
        grad_shared,
        small,
        query,
        key,
        value,
        parents,
        log_total,
        attended,
        normed,
        hidden,
        gain,
        cosine,
        sine,
        w_out,
        w_query,
        w_key,
        w_value,
    ) = operands
    rows, width = residual.shape
    tok_rows, local_width = query.shape
    units = grad_shared.shape[2]
    bf16, f32 = jnp.bfloat16, jnp.float32
    shape = jax.ShapeDtypeStruct
    vmem, anywhere = pl.BlockSpec(memory_space=pltpu.VMEM), pl.BlockSpec(memory_space=pl.ANY)
    smem = pl.BlockSpec(memory_space=pltpu.SMEM)
    dma = pltpu.SemaphoreType.DMA
    return pl.pallas_call(
        functools.partial(back_kernel, score_scale, gain_row),
        out_shape=[
            shape((4, 2, rows // 2, width), bf16),
            shape((4, 2, rows // 2, width), bf16),
            shape((tok_rows, local_width), bf16),
            shape((tok_rows, local_width), bf16),
            shape((tok_rows, local_width), bf16),
            shape((tok_rows, local_width), bf16),
            shape((8, 3, units, tok_rows), bf16),
            shape((16, tok_rows), f32),
            shape((16, HEAD_DIM), f32),
        ],
        in_specs=[vmem, vmem, vmem, anywhere, anywhere, vmem]
        + [vmem] * 3
        + [smem]
        + [vmem] * 7
        + [anywhere] * 4,
        out_specs=[anywhere] * 2 + [vmem] * 4 + [anywhere] + [vmem] * 2,
        scratch_shapes=[
            pltpu.VMEM((4, rows, width), bf16),
            pltpu.VMEM((3, width, local_width), bf16),
            pltpu.VMEM((4, 2, 2, rows, width), bf16),
            pltpu.VMEM((4, rows, width), bf16),
            pltpu.VMEM((2, 2, 2, 2, tok_rows // 2, 2 * local_width), bf16),
            pltpu.VMEM((2, 2, 2, 2, tok_rows, local_width), bf16),
            pltpu.VMEM((LEVELS * tok_rows, 2 * local_width), f32),
            pltpu.VMEM((tok_rows, local_width), bf16),
            pltpu.VMEM((tok_rows, local_width), f32),
            pltpu.VMEM((3, 4, 2, rows // 2, local_width), bf16),
            pltpu.VMEM((4, 2, rows // 2, width), f32),
            pltpu.VMEM((2, 4, rows // 2, width), bf16),
            pltpu.VMEM((2, 4, rows // 2, width), bf16),
            pltpu.VMEM((2, 4, 2, rows // 2, width), bf16),
            pltpu.VMEM((3, units, tok_rows), bf16),
            pltpu.VMEM((8, 16, 2 * HEAD_DIM + HEAD_DIM), f32),
            pltpu.VMEM((8, 16, 2 * HEAD_DIM + HEAD_DIM), f32),
            pltpu.VMEM((4, 16, 2 * HEAD_DIM), f32),
        ]
        + plane_scratch(4, rows, width)
        + plane_scratch(2, tok_rows // 2, 2 * local_width)
        + plane_scratch(2, tok_rows, local_width)
        + plane_scratch(2, tok_rows // 2, 2 * local_width)[5:]
        + [
            dma((12,)),
            dma((2, 4)),
            dma((2, 4)),
            dma((2, 2, 4)),
            dma((2, 2, 2, 4)),
            dma((2, 8)),
            dma((2, 8)),
            dma((2, 4)),
        ],
        compiler_params=pltpu.CompilerParams(
            collective_id=1, has_side_effects=True, vmem_limit_bytes=63 * 2**20
        ),
        cost_estimate=pl.CostEstimate(
            flops=2 * 12 * 2**30, bytes_accessed=40 * 2**20, transcendentals=2**20
        ),
    )(*operands)


def on_slice(
    hidden_in,
    out_grad,
    parents,
    routes,
    attn_gain,
    w_query,
    w_key,
    w_value,
    b_query,
    b_key,
    b_value,
    w_out,
    ffn_gain,
    w_router,
    shared_gate,
    shared_w_gate,
    shared_w_up,
    shared_w_down,
    expert_w_gate,
    expert_w_up,
    expert_w_down,
):
    tok_rows, model_width = hidden_in.shape
    devices = lax.axis_size("dp")
    columns = lax.axis_size("tensor")
    place, column = lax.axis_index("dp"), lax.axis_index("tensor")
    all_rows = tok_rows * devices
    part_rows = tok_rows // columns
    local_width = w_query.shape[1]
    experts = w_router.shape[1]
    top_count = routes.shape[1]
    capacity = 5 * tok_rows * top_count // 4
    score_scale = HEAD_DIM ** (-0.5)
    bf16, f32 = jnp.bfloat16, jnp.float32

    expert_units = expert_w_gate.shape[2]
    shared_units = shared_w_gate.shape[1] // devices
    shared_pad = -(-shared_units // 128) * 128
    units = shared_pad + expert_units
    units_pad = -(-(units + experts + 1) // 128) * 128

    def own_units(matrix):
        return lax.dynamic_slice_in_dim(matrix, place * shared_units, shared_units, 1)

    def pad_to(matrix, columns):
        return jnp.pad(matrix, ((0, 0), (0, columns - matrix.shape[1])))

    def side_by_side(shared, expert):
        joined = jnp.concatenate([pad_to(own_units(shared), shared_pad), expert[0]], 1)
        return joined

    w_pre = jnp.concatenate(
        [
            pad_to(
                jnp.concatenate(
                    [side_by_side(shared_w_gate, expert_w_gate), w_router, shared_gate[:, None]], 1
                ),
                units_pad,
            ),
            pad_to(side_by_side(shared_w_up, expert_w_up), units_pad),
        ],
        1,
    )
    w_down = pad_to(side_by_side(shared_w_down, expert_w_down), units_pad)

    out_all = gather_dp(out_grad)

    routes_all = lax.all_gather(routes, "dp", axis=0, tiled=True)
    pair_onehot = routes_all[:, :, None] == jnp.arange(experts, dtype=jnp.int32)[None, None, :]
    hits = jnp.any(pair_onehot, 1)
    hit_blocks = hits.astype(bf16).reshape(devices, tok_rows, experts)
    below = (
        jnp.arange(tok_rows)[None, :] < jnp.arange(tok_rows)[:, None]
    ).astype(bf16)
    within = jnp.einsum("ij,bje->bie", below, hit_blocks, preferred_element_type=f32)
    block_sums = jnp.sum(hit_blocks.astype(f32), 1)
    before = jnp.cumsum(block_sums, 0) - block_sums
    slots = (within + before[:, None, :]).reshape(all_rows, experts)
    kept = (hits & (slots < capacity)).astype(f32)

    path = path_of(parents, place * tok_rows // SEG)
    reachable = path >= 0
    path_rows = jnp.maximum(path, 0)
    row_ids = jnp.arange(tok_rows, dtype=jnp.int32)
    depth = jnp.sum(reachable.astype(f32)) - 1.0
    cosine, sine = rope_tables(depth * SEG + row_ids.astype(f32))
    allowed = jnp.concatenate(
        [
            row_ids[:, None] >= row_ids[None, :],
            jnp.broadcast_to(
                jnp.repeat(reachable[1:], tok_rows)[None, :], (tok_rows, (LEVELS - 1) * tok_rows)
            ),
        ],
        1,
    )
    hidden_f = hidden_in.astype(f32)
    attn_scale, attn_unit = norm_parts(hidden_f)
    attn_normed = (attn_unit * attn_gain).astype(bf16)
    query_rot = turn_heads(
        product(attn_normed, w_query) + b_query.reshape(-1), cosine, sine, 1.0
    ).astype(bf16)
    key_rot = turn_heads(
        product(attn_normed, w_key) + b_key.reshape(-1), cosine, sine, 1.0
    ).astype(bf16)
    value_rows = (product(attn_normed, w_value) + b_value.reshape(-1)).astype(bf16)
    gathered = gather_dp(jnp.concatenate([key_rot, value_rows], 1))
    kv_blocks = gathered.reshape(devices, tok_rows, 2 * local_width)
    kv_path = jnp.take(kv_blocks, path_rows, axis=0).reshape(LEVELS * tok_rows, 2 * local_width)
    key_path, value_path = kv_path[:, :local_width], kv_path[:, local_width:]
    attended, log_total = attend_forward(query_rot, key_path, value_path, allowed, score_scale)
    attended_low = attended.astype(bf16)
    attn_part = product_nt(attended_low, w_out).astype(bf16)

    hidden_own = lax.dynamic_slice_in_dim(hidden_in, column * part_rows, part_rows, 0)
    grad_own = lax.dynamic_slice_in_dim(out_grad, column * part_rows, part_rows, 0)
    layout = (shared_units, shared_pad, expert_units, experts, units_pad)
    (
        residual,
        residual_grad,
        residual_low,
        ffn_part,
        grad_expert_gate,
        grad_expert_up,
        grad_expert_down,
        grad_shared,
        grad_side,
        grad_ffn_gain,
    ) = ffn_plain(
        attn_part, hidden_own, grad_own, ffn_gain, kept, out_all, w_pre, w_down, layout
    )
    grad_shared = grad_shared[:, :, :shared_units]
    ffn_own = scatter_all(ffn_part).astype(f32)
    hidden_out = gather_tensor((residual + ffn_own).astype(bf16))
    residual_low = gather_tensor(residual_low)
    grad_out_proj = product_tn(residual_low, attended_low)
    attended_grad = product(residual_low, w_out).astype(bf16)

    query_grad, key_grad, value_grad = attend_backward(
        query_rot, key_path, value_path, allowed, log_total, attended_grad, score_scale
    )
    kv_grad = jnp.concatenate([key_grad, value_grad], 1).reshape(
        LEVELS, tok_rows, 2 * local_width
    )
    kv_all = jnp.zeros((devices, tok_rows, 2 * local_width), f32)
    for level in range(LEVELS):
        kv_all = kv_all.at[path_rows[level]].add(kv_grad[level])
    kv_own = scatter_dp(
        kv_all.reshape(all_rows, 2 * local_width).astype(bf16)
    ).astype(f32)
    query_pre_grad = turn_heads(query_grad, cosine, sine, -1.0).astype(bf16)
    key_pre_grad = turn_heads(kv_own[:, :local_width], cosine, sine, -1.0).astype(bf16)
    value_pre_grad = kv_own[:, local_width:].astype(bf16)
    qkv_pre_grad = jnp.concatenate([query_pre_grad, key_pre_grad, value_pre_grad], 1)
    grad_qkv = product_tn(attn_normed, qkv_pre_grad)
    bias_grads = jnp.sum(qkv_pre_grad.astype(f32), 0).reshape(3, -1, HEAD_DIM)
    attn_part_grad = (
        product_nt(query_pre_grad, w_query)
        + product_nt(key_pre_grad, w_key)
        + product_nt(value_pre_grad, w_value)
    )
    grad_attn_gain = jnp.sum(attn_part_grad * attn_unit, 0)
    attn_own_grad = scatter_tensor(attn_part_grad.astype(bf16)).astype(f32)
    own_rows = lambda array: lax.dynamic_slice_in_dim(
        array, column * part_rows, part_rows, 0
    )
    hidden_in_grad = gather_tensor(
        (
            residual_grad
            + norm_back(attn_own_grad, own_rows(attn_unit), own_rows(attn_scale), attn_gain)
        ).astype(bf16)
    )

    small = jnp.concatenate(
        [grad_side, grad_ffn_gain[:, None], grad_attn_gain[:, None]], 1
    )
    small = scatter_dp(lax.psum(small, "tensor"))
    bias_sums = lax.psum_scatter(bias_grads, "dp", scatter_dimension=2, tiled=True)
    grad_attn = scatter_dp(jnp.concatenate([grad_qkv, grad_out_proj], 1).astype(bf16)).astype(f32)
    shared_grads = lax.all_to_all(
        grad_shared, "dp", split_axis=1, concat_axis=2, tiled=True
    ).astype(f32)
    return (
        hidden_out,
        hidden_in_grad,
        small[:, experts + 2],
        grad_attn[:, :local_width],
        grad_attn[:, local_width : 2 * local_width],
        grad_attn[:, 2 * local_width : 3 * local_width],
        bias_sums[0],
        bias_sums[1],
        bias_sums[2],
        grad_attn[:, 3 * local_width :],
        small[:, experts + 1],
        small[:, :experts],
        small[:, experts],
        shared_grads[0],
        shared_grads[1],
        shared_grads[2],
        grad_expert_gate[None],
        grad_expert_up[None],
        grad_expert_down[None],
    )


def finish_kernel(
    hidden_out_in,
    hidden_grad_in,
    query_in,
    key_in,
    value_in,
    out_in,
    shared_in,
    gate_in,
    up_in,
    down_in,
    small_in,
    hidden_out,
    hidden_grad,
    query_out,
    key_out,
    value_out,
    out_out,
    s_gate_out,
    s_up_out,
    s_down_out,
    gate_out,
    up_out,
    down_out,
    router_out,
    shared_gate_out,
    ffn_gain_out,
    attn_gain_out,
):
    f32 = jnp.float32
    experts = router_out.shape[0]
    hidden_out[...] = hidden_out_in[...]
    hidden_grad[...] = hidden_grad_in[...]
    for source, target in (
        (query_in, query_out),
        (key_in, key_out),
        (value_in, value_out),
        (out_in, out_out),
        (gate_in, gate_out),
        (up_in, up_out),
        (down_in, down_out),
    ):
        target[...] = source[...].astype(f32)

    @pl.when(pl.program_id(0) % 4 == 0)
    def _():
        for which, target in enumerate((s_gate_out, s_up_out, s_down_out)):
            units = shared_in[:, which]
            target[...] = units.reshape(-1, units.shape[-1]).T.astype(f32)

    router_out[...] = small_in[0:experts]
    shared_gate_out[...] = small_in[experts : experts + 1]
    ffn_gain_out[...] = small_in[experts + 1 : experts + 2]
    attn_gain_out[...] = small_in[experts + 2 : experts + 3]


def finish_layer(hidden_out, hidden_grad, grads, shared, expert_grads, small, experts):
    steps = 8
    tok_rows, width = hidden_out.shape
    local_width = grads[0].shape[1]
    units = shared.shape[2]
    expert_units = expert_grads[0].shape[0]
    f32, bf16 = jnp.float32, jnp.bfloat16
    shape = jax.ShapeDtypeStruct
    row = lambda wide: pl.BlockSpec((tok_rows // steps, wide), lambda i: (i, 0))
    column = pl.BlockSpec((expert_units, width // steps), lambda i: (0, i))
    whole = lambda *dims: pl.BlockSpec(dims, lambda i: (0,) * len(dims))
    return pl.pallas_call(
        finish_kernel,
        grid=(steps,),
        in_specs=[row(width)] * 2
        + [row(local_width)] * 4
        + [pl.BlockSpec((8, 3, units, tok_rows // 2), lambda i: (0, 0, 0, i // 4))]
        + [column] * 3
        + [whole(16, tok_rows)],
        out_specs=[row(width)] * 2
        + [row(local_width)] * 4
        + [pl.BlockSpec((tok_rows // 2, 8 * units), lambda i: (i // 4, 0))] * 3
        + [column] * 3
        + [whole(experts, tok_rows)]
        + [whole(1, tok_rows)] * 3,
        out_shape=[shape((tok_rows, width), bf16)] * 2
        + [shape((tok_rows, local_width), f32)] * 4
        + [shape((tok_rows, 8 * units), f32)] * 3
        + [shape((expert_units, width), f32)] * 3
        + [shape((experts, tok_rows), f32)]
        + [shape((1, tok_rows), f32)] * 3,
        compiler_params=pltpu.CompilerParams(vmem_limit_bytes=63 * 2**20),
        cost_estimate=pl.CostEstimate(flops=0, bytes_accessed=26 * 2**20, transcendentals=0),
    )(hidden_out, hidden_grad, *grads, shared, *expert_grads, small)


def on_cube(
    hidden_in,
    out_grad,
    parents,
    routes,
    attn_gain,
    w_query,
    w_key,
    w_value,
    b_query,
    b_key,
    b_value,
    w_out,
    ffn_gain,
    w_router,
    shared_gate,
    shared_w_gate,
    shared_w_up,
    shared_w_down,
    expert_w_gate,
    expert_w_up,
    expert_w_down,
):
    tok_rows, model_width = hidden_in.shape
    devices, columns = lax.axis_size("dp"), lax.axis_size("tensor")
    place = lax.axis_index("dp")
    experts, top_count = w_router.shape[1], routes.shape[1]
    capacity = 5 * tok_rows * top_count // 4
    score_scale = HEAD_DIM ** (-0.5)
    bf16, f32 = jnp.bfloat16, jnp.float32
    expert_units = expert_w_gate.shape[2]
    shared_units = shared_w_gate.shape[1] // devices
    shared_pad = -(-shared_units // 128) * 128
    units = shared_pad + expert_units
    units_pad = -(-(units + experts + 1) // 128) * 128
    layout = (shared_units, shared_pad, expert_units, experts, units_pad)
    part_rows = tok_rows // columns

    side = jnp.pad(
        jnp.concatenate([w_router.T, shared_gate[None, :]], 0), ((0, 16 - experts - 1), (0, 0))
    )
    hits = jnp.any(
        routes.T[:, None, :] == jnp.arange(16, dtype=jnp.int32)[None, :, None], 0
    ).astype(f32)
    freqs = rope_base ** (-jnp.arange(0, HEAD_DIM, 2, dtype=f32) / HEAD_DIM)
    biases = jnp.stack([b_query.reshape(-1), b_key.reshape(-1), b_value.reshape(-1)])
    (
        residual,
        query_rot,
        key_path,
        value_path,
        log_total,
        attended,
        attn_normed,
        cosine,
        sine,
        hits_all,
        grad_all,
        shared_w,
    ) = front_layer(
        score_scale,
        shared_units,
        (
            parents,
            hidden_in,
            attn_gain[None, :],
            biases,
            jnp.concatenate([freqs, freqs])[None, :],
            hits,
            out_grad.reshape(columns, part_rows, model_width),
            w_query,
            w_key,
            w_value,
            w_out,
            shared_w_gate,
            shared_w_up,
            shared_w_down,
        ),
    )
    (
        residual_grad,
        residual_low,
        ffn_part,
        grad_expert_gate,
        grad_expert_up,
        grad_expert_down,
        grad_shared,
        small,
    ) = ffn_layer(
        residual,
        ffn_gain[None, :],
        hits_all,
        grad_all.reshape(2, 2, 2, columns, part_rows, model_width),
        side,
        shared_w,
        (expert_w_gate[0].T, expert_w_up[0].T, expert_w_down[0].T),
        layout,
        capacity,
    )
    (
        hidden_out,
        hidden_in_grad,
        sum_query,
        sum_key,
        sum_value,
        sum_out,
        grad_shared,
        small,
        bias_sums,
    ) = back_layer(
        score_scale,
        experts + 2,
        (
            residual,
            residual_grad,
            residual_low,
            ffn_part,
            grad_shared,
            small,
            query_rot,
            key_path,
            value_path,
            parents,
            log_total,
            attended,
            attn_normed,
            hidden_in,
            attn_gain[None, :],
            cosine,
            sine,
            w_out,
            w_query,
            w_key,
            w_value,
        ),
    )
    bias_sums = lax.dynamic_slice_in_dim(
        bias_sums[: 3 * b_query.shape[0]].reshape(3, *b_query.shape),
        place * (HEAD_DIM // devices),
        HEAD_DIM // devices,
        2,
    )
    (
        hidden_out,
        hidden_in_grad,
        sum_query,
        sum_key,
        sum_value,
        sum_out,
        sum_s_gate,
        sum_s_up,
        sum_s_down,
        grad_expert_gate,
        grad_expert_up,
        grad_expert_down,
        sum_router,
        sum_shared_gate,
        sum_ffn_gain,
        sum_attn_gain,
    ) = finish_layer(
        hidden_out.reshape(tok_rows, model_width),
        hidden_in_grad.reshape(tok_rows, model_width),
        (sum_query, sum_key, sum_value, sum_out),
        grad_shared,
        (grad_expert_gate, grad_expert_up, grad_expert_down),
        small,
        experts,
    )
    return (
        hidden_out,
        hidden_in_grad,
        sum_attn_gain[0],
        sum_query,
        sum_key,
        sum_value,
        bias_sums[0],
        bias_sums[1],
        bias_sums[2],
        sum_out,
        sum_ffn_gain[0],
        sum_router.T,
        sum_shared_gate[0],
        sum_s_gate,
        sum_s_up,
        sum_s_down,
        grad_expert_gate.T[None],
        grad_expert_up.T[None],
        grad_expert_down.T[None],
    )


def on_device(*arrays):
    devices, columns = lax.axis_size("dp"), lax.axis_size("tensor")
    tok_rows, model_width = arrays[0].shape
    cube = devices == 8 and columns == 4 and tok_rows == SEG
    if cube and tok_rows * devices * model_width <= 2**22:
        return on_cube(*arrays)
    return on_slice(*arrays)


def solution(mesh):
    return jax.shard_map(
        on_device,
        mesh=mesh,
        in_specs=(
            P("dp", None),
            P("dp", None),
            P(),
            P("dp", None),
            P(),
            P(None, "tensor"),
            P(None, "tensor"),
            P(None, "tensor"),
            P("tensor", None),
            P("tensor", None),
            P("tensor", None),
            P(None, "tensor"),
            P(),
            P(),
            P(),
            P(None, "tensor"),
            P(None, "tensor"),
            P(None, "tensor"),
            P("dp", None, "tensor"),
            P("dp", None, "tensor"),
            P("dp", None, "tensor"),
        ),
        out_specs=(
            P("dp", None),
            P("dp", None),
            P("dp"),
            P("dp", "tensor"),
            P("dp", "tensor"),
            P("dp", "tensor"),
            P("tensor", "dp"),
            P("tensor", "dp"),
            P("tensor", "dp"),
            P("dp", "tensor"),
            P("dp"),
            P("dp", None),
            P("dp"),
            P("dp", "tensor"),
            P("dp", "tensor"),
            P("dp", "tensor"),
            P("dp", None, "tensor"),
            P("dp", None, "tensor"),
            P("dp", None, "tensor"),
        ),
        check_vma=False,
    )
```

```python
import functools

import jax
import jax.numpy as jnp
from jax import lax
from jax.experimental import pallas as pl
from jax.experimental.pallas import tpu as pltpu
from jax.sharding import PartitionSpec as P

HEAD_DIM = 128
SEG = 256
MESH = pl.DeviceIdType.MESH


epsilon = 1e-06
rope_base = 1000000.0
highest = lax.Precision.HIGHEST


def product(left, right):
    return jnp.dot(left, right, preferred_element_type=jnp.float32)


def product_tn(left, right):
    return lax.dot_general(
        left, right, (((0,), (0,)), ((), ())), preferred_element_type=jnp.float32
    )


def product_nt(left, right):
    return lax.dot_general(
        left, right, (((1,), (1,)), ((), ())), preferred_element_type=jnp.float32
    )


def ancestry(parents):
    seg_count = parents.shape[0]
    labels = jnp.arange(seg_count, dtype=jnp.int32)

    def climb(level, carry):
        current, reach = carry
        upward = jnp.where(current >= 0, parents[jnp.maximum(current, 0)], -1)
        reach = jnp.maximum(reach, (upward[:, None] == labels[None, :]).astype(jnp.float32))
        return (upward, reach)

    start = (labels, jnp.eye(seg_count, dtype=jnp.float32))
    return lax.fori_loop(0, seg_count, climb, start)[1]


def rope_tables(positions):
    freqs = rope_base ** (-jnp.arange(0, HEAD_DIM, 2, dtype=jnp.float32) / HEAD_DIM)
    angles = positions[:, None] * freqs[None, :]
    angles = jnp.concatenate([angles, angles], 1)
    return (jnp.cos(angles)[:, None, :], jnp.sin(angles)[:, None, :])


def turn_heads(matrix, cosine, sine, sign_value):
    shaped = matrix.reshape(matrix.shape[0], matrix.shape[1] // HEAD_DIM, HEAD_DIM)
    half = HEAD_DIM // 2
    turned = jnp.concatenate([-shaped[..., half:], shaped[..., :half]], -1)
    return (shaped * cosine + sign_value * turned * sine).reshape(matrix.shape)


def norm_parts(values):
    scale_rows = lax.rsqrt(jnp.mean(values * values, 1, keepdims=True) + epsilon)
    return (scale_rows, values * scale_rows)


def norm_back(grad_rows, unit_rows, scale_rows, gain):
    unit_grad = grad_rows * gain
    return scale_rows * (unit_grad - unit_rows * jnp.mean(unit_grad * unit_rows, 1, keepdims=True))


LEVELS = 4


def gather_dp(rows):
    return lax.all_gather(rows, "dp", axis=0, tiled=True)


def gather_tensor(rows):
    return lax.all_gather(rows, "tensor", axis=0, tiled=True)


def gather_all(rows):
    return gather_dp(gather_tensor(rows))


def scatter_dp(rows):
    return lax.psum_scatter(rows, "dp", scatter_dimension=0, tiled=True)


def scatter_tensor(rows):
    return lax.psum_scatter(rows, "tensor", scatter_dimension=0, tiled=True)


def scatter_all(rows):
    return scatter_tensor(scatter_dp(rows))


def path_of(parents, segment):
    path = [segment]
    for _ in range(LEVELS - 1):
        last = path[-1]
        path.append(jnp.where(last >= 0, parents[jnp.maximum(last, 0)], -1))
    return jnp.stack(path)


def heads_of(matrix):
    return matrix.reshape(matrix.shape[0], -1, HEAD_DIM)


def attend_forward(query_rot, key_path, value_path, allowed, score_scale):
    scores = (
        jnp.einsum(
            "qhd,khd->hqk",
            heads_of(query_rot),
            heads_of(key_path),
            preferred_element_type=jnp.float32,
        )
        * score_scale
    )
    scores = jnp.where(allowed[None], scores, -jnp.inf)
    peak = jnp.max(scores, 2, keepdims=True)
    log_total = peak + jnp.log(jnp.sum(jnp.exp(scores - peak), 2, keepdims=True))
    weights = jnp.exp(scores - log_total).astype(jnp.bfloat16)
    attended = jnp.einsum(
        "hqk,khd->qhd", weights, heads_of(value_path), preferred_element_type=jnp.float32
    )
    return attended.reshape(query_rot.shape), log_total


def attend_backward(
    query_rot, key_path, value_path, allowed, log_total, attended_grad, score_scale
):
    query, key, value = heads_of(query_rot), heads_of(key_path), heads_of(value_path)
    grad = heads_of(attended_grad)
    scores = jnp.einsum("qhd,khd->hqk", query, key, preferred_element_type=jnp.float32)
    weights = jnp.exp(jnp.where(allowed[None], scores * score_scale, -jnp.inf) - log_total)
    weight_grad = jnp.einsum("qhd,khd->hqk", grad, value, preferred_element_type=jnp.float32)
    center = jnp.sum(weights * weight_grad, 2, keepdims=True)
    score_grad = (weights * (weight_grad - center)).astype(jnp.bfloat16)
    query_grad = (
        jnp.einsum("hqk,khd->qhd", score_grad, key, preferred_element_type=jnp.float32)
        * score_scale
    )
    key_grad = (
        jnp.einsum("hqk,qhd->khd", score_grad, query, preferred_element_type=jnp.float32)
        * score_scale
    )
    value_grad = jnp.einsum(
        "hqk,qhd->khd",
        weights.astype(jnp.bfloat16),
        grad,
        preferred_element_type=jnp.float32,
    )
    return (
        query_grad.reshape(query_rot.shape),
        key_grad.reshape(key_path.shape),
        value_grad.reshape(value_path.shape),
    )


def ffn_plain(attn_part, hidden_own, grad_own, ffn_gain, kept, out_all, w_pre, w_down, layout):
    _, shared_pad, expert_units, experts, units_pad = layout
    units = shared_pad + expert_units
    bf16, f32 = jnp.bfloat16, jnp.float32
    place, column = lax.axis_index("dp"), lax.axis_index("tensor")
    columns, part_rows = lax.axis_size("tensor"), hidden_own.shape[0]
    out_own = grad_own.astype(f32)
    residual = hidden_own.astype(f32) + scatter_tensor(attn_part).astype(f32)
    ffn_scale, ffn_unit = norm_parts(residual)
    ffn_normed = (ffn_unit * ffn_gain).astype(bf16)
    normed_all = gather_all(ffn_normed)

    pre = product(normed_all, w_pre)
    pre_gate, pre_up = pre[:, :units_pad], pre[:, units_pad:]
    logits = pre[:, units : units + experts]
    probs = jax.nn.softmax(logits, 1)
    shared_weight = jax.nn.sigmoid(pre[:, units + experts])
    own_expert = jnp.arange(experts, dtype=jnp.int32)[None, :] == place
    gate_own = jnp.sum(jnp.where(own_expert, probs * kept, 0.0), 1)
    lane = jnp.arange(units_pad)[None, :]
    weight = jnp.where(
        lane < shared_pad,
        shared_weight[:, None],
        jnp.where(lane < units, gate_own[:, None], 0.0),
    )
    down_back = product(out_all, w_down)
    sigmoid_gate = jax.nn.sigmoid(pre_gate)
    hidden = (pre_gate * sigmoid_gate * pre_up).astype(bf16).astype(f32)
    hidden_scaled = (hidden * weight).astype(bf16)
    hidden_grad = down_back * weight
    up_rows = (hidden_grad * pre_gate * sigmoid_gate).astype(bf16)
    gate_rows = (
        hidden_grad * pre_up * sigmoid_gate * (1.0 + pre_gate * (1.0 - sigmoid_gate))
    ).astype(bf16)
    both_rows = jnp.concatenate([gate_rows, up_rows], 1)
    dots = hidden * down_back
    gate_dot = jnp.sum(jnp.where((lane >= shared_pad) & (lane < units), dots, 0.0), 1)
    shared_dot = jnp.sum(jnp.where(lane < shared_pad, dots, 0.0), 1)
    dot_parts = jnp.concatenate(
        [jnp.where(own_expert, gate_dot[:, None] * kept, 0.0), shared_dot[:, None]], 1
    )
    ffn_part = product_nt(hidden_scaled, w_down).astype(bf16)
    normed_part = product_nt(both_rows, w_pre).astype(bf16)
    grad_pre = product_tn(normed_all, both_rows)
    grad_down = product_tn(out_all, hidden_scaled)

    dot_own = scatter_all(dot_parts)
    normed_own = scatter_all(normed_part).astype(f32)

    first = (place * columns + column) * part_rows
    own = lambda array: lax.dynamic_slice_in_dim(array, first, part_rows, 0)
    probs_own, shared_own = own(probs), own(shared_weight)
    prob_grad = dot_own[:, :experts]
    logit_grad = (
        probs_own * (prob_grad - jnp.sum(probs_own * prob_grad, 1, keepdims=True))
    ).astype(bf16)
    weight_logit_grad = (dot_own[:, experts] * shared_own * (1.0 - shared_own)).astype(bf16)
    side_grad = jnp.concatenate([logit_grad, weight_logit_grad[:, None]], 1)
    side_w = w_pre[:, units : units + experts + 1]
    normed_grad = normed_own + product_nt(side_grad, side_w)
    grad_side = product_tn(ffn_normed, side_grad)
    grad_ffn_gain = jnp.sum(normed_grad * ffn_unit, 0)
    residual_grad = out_own + norm_back(normed_grad, ffn_unit, ffn_scale, ffn_gain)
    expert = slice(shared_pad, units)
    expert_up = slice(units_pad + shared_pad, units_pad + units)
    grad_shared = jnp.stack(
        [
            grad_pre[:, : shared_pad],
            grad_pre[:, units_pad : units_pad + shared_pad],
            grad_down[:, : shared_pad],
        ]
    ).astype(bf16)
    return (
        residual,
        residual_grad,
        residual_grad.astype(bf16),
        ffn_part,
        grad_pre[:, expert],
        grad_pre[:, expert_up],
        grad_down[:, expert],
        grad_shared,
        grad_side,
        grad_ffn_gain,
    )


def flip(bit):
    return 1 - bit


def other(index, step):
    result, place = index, 1
    while place <= step:
        if step & place:
            result = result + place - 2 * place * ((index // place) % 2)
        place *= 2
    return result


def ffn_kernel(
    units,
    residual_ref,
    gain_ref,
    hits_ref,
    grad_all_ref,
    side_ref,
    shared_w_ref,
    e_gate_w_ref,
    e_up_w_ref,
    e_down_w_ref,
    res_grad_ref,
    res_low_ref,
    ffn_part_ref,
    e_gate_ref,
    e_up_ref,
    e_down_ref,
    shared_ref,
    small_ref,
    rows_all,
    dy_all,
    w_pre,
    w_down,
    both_all,
    scaled_all,
    scaled_now,
    down_back_all,
    sums,
    got_core,
    got_x1,
    got_y1,
    got_y2,
    got_x2,
    got_z,
    kept_ref,
    out_send,
    out_own,
    got_out,
    tile_gate,
    tile_up,
    tile_down,
    tile_shared,
    load_sems,
    store_sems,
    tile_sems,
    zs,
    links,
    cores,
    rs_core,
    rs_links,
    rs_z,
    rs_out,
):
    shared_units, shared_pad, expert_units, experts, unit_pad, half, wide, capacity = units
    bf16, f32 = jnp.bfloat16, jnp.float32
    place, column = lax.axis_index("dp"), lax.axis_index("tensor")
    core, east, north = place % 2, (place // 2) % 2, place // 4
    rows, width = residual_ref.shape
    sibling = {"dp": other(place, 1)}
    x_side = {"dp": other(place, 2)}
    y_side = {"dp": other(place, 4)}
    levels = [{"tensor": other(column, k)} for k in range(4)]

    def level_of(k):
        low_i, high_i, low_k, high_k = column % 2, column // 2, k % 2, k // 2
        return (low_i + low_k - 2 * low_i * low_k) + 2 * (high_i + high_k - 2 * high_i * high_k)

    def remote(src, dst, sems, which, device):
        return pltpu.make_async_remote_copy(
            src_ref=src,
            dst_ref=dst,
            send_sem=sems.at[(0, *which)],
            recv_sem=sems.at[(1, *which)],
            device_id=device,
            device_id_type=MESH,
        )

    expert_first, side_first = shared_pad, shared_pad + expert_units
    loads = []
    for j, (target, first, ref) in enumerate(
        ((w_pre, 0, e_gate_w_ref), (w_pre, unit_pad, e_up_w_ref), (w_down, 0, e_down_w_ref))
    ):
        own_rows = pl.ds(first + expert_first, expert_units)
        shared_rows = pl.ds(first, shared_units)
        loads += [
            pltpu.make_async_copy(ref, target.at[own_rows], load_sems.at[8 + 2 * j]),
            pltpu.make_async_copy(
                shared_w_ref.at[j], target.at[shared_rows], load_sems.at[9 + 2 * j]
            ),
        ]
    for copy in loads:
        copy.start()
    for target, first in ((w_pre, 0), (w_pre, unit_pad), (w_down, 0)):
        gap = shared_pad - shared_units
        target[first + shared_units : first + shared_pad, :] = jnp.zeros((gap, width), bf16)
        rest = unit_pad - side_first
        target[first + side_first : first + unit_pad, :] = jnp.zeros((rest, width), bf16)
    w_pre[side_first : side_first + side_ref.shape[0], :] = side_ref[...]

    def load_grad(c, z):
        return pltpu.make_async_copy(
            grad_all_ref.at[:, :, c, z], dy_all.at[z, c], load_sems.at[c * 4 + z]
        )

    for c in range(2):
        for z in range(4):
            load_grad(c, z).start()

    barrier = pltpu.get_barrier_semaphore()
    partners = [sibling, x_side, y_side] + levels[1:]
    for partner in partners:
        pl.semaphore_signal(barrier, inc=1, device_id=partner, device_id_type=MESH)
    pl.semaphore_wait(barrier, len(partners))

    residual = residual_ref[...]
    scale_rows = lax.rsqrt(jnp.mean(residual * residual, 1, keepdims=True) + epsilon)
    normed = (residual * scale_rows * gain_ref[...]).astype(bf16)
    rows_all[column, core, north, east] = normed

    own_slot = rows_all.at[column, core, north, east]

    def z_copy(k):
        return remote(own_slot, own_slot, zs, (k,), levels[k])

    def block(k, c, y, x, cols=slice(None)):
        return rows_all.at[level_of(k), c, y, x, :, cols]

    first_half, second_half = pl.ds(0, half), pl.ds(half, width - half)

    def direct_copies(k):
        own = block(k, core, north, east)
        return [
            remote(own, own, links, (0, k), x_side),
            remote(own, own, links, (1, k), y_side),
            remote(own, own, cores, (0, k), sibling),
        ]

    def forward_copies(k):
        from_x = block(k, core, north, flip(east), first_half)
        from_y = block(k, core, flip(north), east, second_half)
        all_x = block(k, core, north, flip(east))
        all_y = block(k, core, flip(north), east)
        return [
            remote(from_x, from_x, links, (2, k), y_side),
            remote(from_y, from_y, links, (3, k), x_side),
            remote(all_x, all_x, cores, (1, k), sibling),
            remote(all_y, all_y, cores, (2, k), sibling),
        ]

    def corner_copy(k):
        corner = block(k, core, flip(north), flip(east))
        return remote(corner, corner, cores, (3, k), sibling)

    def start_direct(k):
        for copy in direct_copies(k):
            copy.start()

    def start_forward(k):
        for copy in direct_copies(k)[:2]:
            copy.wait_recv()
        for copy in forward_copies(k):
            copy.start()

    def start_corner(k):
        for copy in forward_copies(k)[:2]:
            copy.wait_recv()
        corner_copy(k).start()

    def finish_gather(k):
        direct_copies(k)[2].wait_recv()
        for copy in forward_copies(k)[2:]:
            copy.wait_recv()
        corner_copy(k).wait_recv()

    def core_copy(k):
        return remote(sums.at[k, flip(core)], got_core.at[k % 2], rs_core, (k,), sibling)

    left, right = pl.ds(0, half), pl.ds(half, wide - half)

    def first_copies(k):
        return [
            remote(
                sums.at[k, core, :, flip(east), :, left],
                got_x1.at[k % 2],
                rs_links, (0, k),
                x_side,
            ),
            remote(
                sums.at[k, core, flip(north), :, :, right],
                got_y1.at[k % 2],
                rs_links, (1, k),
                y_side,
            ),
        ]

    def second_copies(k):
        return [
            remote(
                sums.at[k, core, flip(north), east, :, left],
                got_y2.at[k % 2],
                rs_links, (2, k),
                y_side,
            ),
            remote(
                sums.at[k, core, north, flip(east), :, right],
                got_x2.at[k % 2],
                rs_links, (3, k),
                x_side,
            ),
        ]

    def level_copy(k, device):
        return remote(sums.at[k, core, north, east], got_z.at[k], rs_z, (k,), device)

    def add(ref, value):
        ref[...] = (ref[...].astype(f32) + value.astype(f32)).astype(bf16)

    def after_core(k):
        core_copy(k).wait_recv()
        for y in range(2):
            for x in range(2):
                add(sums.at[k, core, y, x], got_core[k % 2, y, x])
        for copy in first_copies(k):
            copy.start()

    def after_first(k):
        x_copy, y_copy = first_copies(k)
        x_copy.wait_recv()
        for y in range(2):
            add(sums.at[k, core, y, east, :, left], got_x1[k % 2, y])
        y_copy.wait_recv()
        for x in range(2):
            add(sums.at[k, core, north, x, :, right], got_y1[k % 2, x])
        for copy in second_copies(k):
            copy.start()

    def after_second(k):
        y_copy, x_copy = second_copies(k)
        y_copy.wait_recv()
        add(sums.at[k, core, north, east, :, left], got_y2[k % 2])
        x_copy.wait_recv()
        add(sums.at[k, core, north, east, :, right], got_x2[k % 2])
        for level in range(1, 4):

            @pl.when(k == level)
            def _():
                level_copy(k, levels[level]).start()

    for k in (1, 2, 3):
        z_copy(k).start()
    start_direct(0)

    tokens_dev = 4 * rows
    expert_id = lax.broadcasted_iota(jnp.int32, hits_ref.shape, 1)
    hits = jnp.sum(jnp.where(expert_id == place, hits_ref[...], 0.0), 1)
    earlier = lax.broadcasted_iota(jnp.int32, (tokens_dev, tokens_dev), 0)
    later = lax.broadcasted_iota(jnp.int32, (tokens_dev, tokens_dev), 1)
    slots = product(hits.astype(bf16), (earlier < later).astype(bf16))
    counts = jnp.sum(hits, 1, keepdims=True)
    counts_wide = jnp.broadcast_to(counts, (8, 128))
    order_row = lax.broadcasted_iota(jnp.int32, (8, 8), 0)
    order_col = lax.broadcasted_iota(jnp.int32, (8, 8), 1)
    before = lax.dot_general(
        (order_col < order_row).astype(f32),
        counts_wide,
        (((1,), (0,)), ((), ())),
        precision=highest,
        preferred_element_type=f32,
    )
    kept = jnp.where(slots + before[:, :1] < capacity, hits, 0.0).astype(bf16)
    eye = (
        lax.broadcasted_iota(jnp.int32, (8, 128), 0)
        == lax.broadcasted_iota(jnp.int32, (8, 128), 1)
    ).astype(bf16)
    kept_columns = product_tn(kept, eye)
    for d in range(8):
        y, x, c = d // 4, (d // 2) % 2, d % 2
        for z in range(4):
            first = (2 * y + x) * rows
            kept_ref[z, c, first : first + rows, :] = kept_columns[
                z * rows : (z + 1) * rows, d : d + 1
            ]

    for copy in loads:
        copy.wait()
    for c in range(2):
        for z in range(4):
            load_grad(c, z).wait()

    def back_down(i, carry):
        z, c = i // 2, i % 2
        dy_block = dy_all[z, c].reshape(4 * rows, width)
        down_back_all[z, c] = product_nt(dy_block, w_down[...]).astype(bf16)
        return carry

    lax.fori_loop(0, 3, back_down, 0)
    start_forward(0)
    z_copy(1).wait_recv()
    start_direct(1)
    lax.fori_loop(3, 5, back_down, 0)
    start_corner(0)
    lax.fori_loop(5, 8, back_down, 0)

    last = unit_pad - 128
    lane = lax.broadcasted_iota(jnp.int32, (1, 128), 1)
    first_lane = shared_pad + expert_units - last
    in_router = (lane >= first_lane) & (lane < first_lane + experts)
    is_shared = lane == first_lane + experts

    def routing(logit_block):
        top = jnp.max(jnp.where(in_router, logit_block, -jnp.inf), 1, keepdims=True)
        powers = jnp.where(in_router, jnp.exp(jnp.where(in_router, logit_block - top, 0.0)), 0.0)
        probs = powers / jnp.sum(powers, 1, keepdims=True)
        shared_logit = jnp.sum(jnp.where(is_shared, logit_block, 0.0), 1, keepdims=True)
        return probs, jax.nn.sigmoid(shared_logit)

    def compute(k, c):
        z = level_of(k)
        row_block = rows_all[z, c].reshape(4 * rows, width)
        pre_gate = product_nt(row_block, w_pre[:unit_pad])
        pre_up = product_nt(row_block, w_pre[unit_pad:])
        down_back = down_back_all[z, c].astype(f32)
        probs, shared_weight = routing(pre_gate[:, last:])
        kept = kept_ref[z, c]
        gate = (
            jnp.sum(jnp.where(lane == first_lane + place, probs, 0.0), 1, keepdims=True) * kept
        )
        dots, scaled, gate_rows, up_rows = [], [], [], []
        for begin, end, weight in (
            (0, shared_pad, shared_weight),
            (shared_pad, unit_pad, gate),
        ):
            cols = slice(begin, end)
            a, b, back = pre_gate[:, cols], pre_up[:, cols], down_back[:, cols]
            sig = jax.nn.sigmoid(a)
            silu = a * sig
            hidden = (silu * b).astype(bf16).astype(f32)
            dots.append(jnp.sum(hidden * back, 1, keepdims=True))
            scaled.append((hidden * weight).astype(bf16))
            grad = back * weight
            up_rows.append((grad * silu).astype(bf16))
            gate_rows.append((grad * b * sig * (1.0 + a * (1.0 - sig))).astype(bf16))
        both = jnp.concatenate(gate_rows + up_rows, 1)
        own_scaled = jnp.concatenate(scaled, 1)
        first_token = pl.multiple_of((2 * z + c) * 4 * rows, 4 * rows)
        both_all[:, pl.ds(first_token, 4 * rows)] = both.T
        scaled_all[:, pl.ds(first_token, 4 * rows)] = own_scaled.T
        scaled_now[c] = own_scaled
        dot_block = jnp.where(is_shared, dots[0], 0.0) + jnp.where(
            lane == first_lane + place, dots[1] * kept, 0.0
        )
        normed_grad = product(both, w_pre[...]).astype(bf16)
        sums[k, c, :, :, :, 0:width] = normed_grad.reshape(2, 2, rows, width)
        sums[k, c, :, :, :, width:wide] = dot_block.astype(bf16).reshape(2, 2, rows, wide - width)

    def store_chunk(k):
        return pltpu.make_async_copy(out_own, ffn_part_ref.at[level_of(k)], store_sems.at[0])

    def out_core_copy(k):
        return remote(out_send, got_out.at[k % 2], rs_out, (k,), sibling)

    def chunk(k, carry):
        @pl.when(k < 3)
        def _():
            start_forward(k + 1)

        @pl.when(k < 2)
        def _():
            for level in (2, 3):

                @pl.when(k + 2 == level)
                def _():
                    z_copy(level).wait_recv()

            start_direct(k + 2)

        finish_gather(k)
        def rows_of(i, carry):
            compute(k, (i + 1 + core) % 2)

            @pl.when(i == 0)
            def _():
                core_copy(k).start()

            return carry

        lax.fori_loop(0, 2, rows_of, 0)

        @pl.when(k >= 1)
        def _():
            after_first(k - 1)
            store_chunk(k - 1).wait()
            out_core_copy(k - 1).wait_send()

        def outputs(i, carry):
            part = product(scaled_now[(i + 1 + core) % 2], w_down[...]).astype(bf16)

            @pl.when(i == 0)
            def _():
                out_send[...] = part.reshape(2, 2, rows, width)
                out_core_copy(k).start()

            @pl.when(i == 1)
            def _():
                out_own[...] = part.reshape(2, 2, rows, width)

            return carry

        lax.fori_loop(0, 2, outputs, 0)

        @pl.when(k < 3)
        def _():
            start_corner(k + 1)

        after_core(k)
        out_core_copy(k).wait_recv()
        for y in range(2):
            for x in range(2):
                add(out_own.at[y, x], got_out[k % 2, y, x])
        store_chunk(k).start()

        @pl.when(k >= 1)
        def _():
            after_second(k - 1)

        return carry

    lax.fori_loop(0, 4, chunk, 0)
    store_chunk(3).wait()
    out_core_copy(3).wait_send()

    tile = tile_gate.shape[2]
    tiles = width // tile

    def tile_copies(i, slot):
        window = pl.ds(pl.multiple_of(i * tile, tile), tile)
        return [
            pltpu.make_async_copy(tile_gate.at[slot], e_gate_ref.at[:, window], tile_sems.at[slot, 0]),
            pltpu.make_async_copy(tile_up.at[slot], e_up_ref.at[:, window], tile_sems.at[slot, 1]),
            pltpu.make_async_copy(tile_down.at[slot], e_down_ref.at[:, window], tile_sems.at[slot, 2]),
            pltpu.make_async_copy(
                tile_shared.at[slot], shared_ref.at[i], tile_sems.at[slot, 3]
            ),
        ]

    tokens = rows * 32

    def weight_tile(i, carry):
        slot = i % 2

        @pl.when(i >= 2)
        def _():
            for copy in tile_copies(i - 2, slot):
                copy.wait()

        window = pl.ds(pl.multiple_of(i * tile, tile), tile)
        expert = slice(shared_pad, shared_pad + expert_units)
        row_tile = rows_all[:, :, :, :, :, window].reshape(tokens, tile)
        for j, (first, target) in enumerate(((0, tile_gate), (unit_pad, tile_up))):
            grad = product(both_all[first : first + unit_pad], row_tile).astype(bf16)
            target[slot] = grad[expert]
            tile_shared[slot, j] = grad[:shared_units]
        dy_tile = dy_all[:, :, :, :, :, window].reshape(tokens, tile)
        grad = product(scaled_all[...], dy_tile).astype(bf16)
        tile_down[slot] = grad[expert]
        tile_shared[slot, 2] = grad[:shared_units]
        for copy in tile_copies(i, slot):
            copy.start()

        @pl.when(i == 1)
        def _():
            after_first(3)

        @pl.when(i == 3)
        def _():
            after_second(3)

        return carry

    lax.fori_loop(0, tiles, weight_tile, 0)
    for i in (tiles - 2, tiles - 1):
        for copy in tile_copies(i, i % 2):
            copy.wait()

    total = sums[0, core, north, east].astype(f32)
    for k in (1, 2, 3):
        level_copy(k, levels[k]).wait_recv()
        total = total + got_z[k].astype(f32)
    dots = total[:, width:]
    unit = residual_ref[...] * scale_rows
    own_normed = rows_all[column, core, north, east]
    side_w = w_pre[last:unit_pad]
    probs, shared_weight = routing(product_nt(own_normed, side_w))
    router_dots = jnp.where(in_router, dots, 0.0)
    center = jnp.sum(probs * router_dots, 1, keepdims=True)
    side = jnp.where(in_router, probs * (router_dots - center), 0.0) + jnp.where(
        is_shared, dots * shared_weight * (1.0 - shared_weight), 0.0
    )
    side = side.astype(bf16)
    normed_grad = total[:, :width] + product(side, side_w)
    side_rows = product_tn(side, own_normed)
    small_ref[...] = side_rows[first_lane : first_lane + small_ref.shape[0]]
    small_ref[experts + 1 : experts + 2, :] = jnp.sum(normed_grad * unit, 0, keepdims=True)
    own_grad = dy_all[column, core, north, east].astype(f32)
    grad_f = own_grad + norm_back(normed_grad, unit, scale_rows, gain_ref[...])
    res_grad_ref[...] = grad_f
    res_low_ref[...] = grad_f.astype(bf16)

    for k in (1, 2, 3):
        z_copy(k).wait_send()
        level_copy(k, levels[k]).wait_send()
    for k in range(4):
        for copy in direct_copies(k) + forward_copies(k) + [corner_copy(k), core_copy(k)]:
            copy.wait_send()
        for copy in first_copies(k) + second_copies(k):
            copy.wait_send()


def ffn_layer(residual, ffn_gain, hits, grad_all, side, shared_w, expert_w, layout, capacity):
    shared_units, shared_pad, expert_units, experts, unit_pad = layout
    rows, width = residual.shape
    bf16, f32 = jnp.bfloat16, jnp.float32
    half = width // 2
    wide = width + 128
    tile = 256
    shape = jax.ShapeDtypeStruct
    vmem, anywhere = pl.BlockSpec(memory_space=pltpu.VMEM), pl.BlockSpec(memory_space=pl.ANY)
    dma = pltpu.SemaphoreType.DMA
    cost = pl.CostEstimate(
        flops=2 * 24 * 2048 * 2048 * 256, bytes_accessed=60 * 2**20, transcendentals=3 * 2**20
    )
    return pl.pallas_call(
        functools.partial(
            ffn_kernel,
            (shared_units, shared_pad, expert_units, experts, unit_pad, half, wide, capacity),
        ),
        out_shape=[
            shape((rows, width), f32),
            shape((rows, width), bf16),
            shape((4, 2, 2, rows, width), bf16),
            shape((expert_units, width), bf16),
            shape((expert_units, width), bf16),
            shape((expert_units, width), bf16),
            shape((width // tile, 3, shared_units, tile), bf16),
            shape((16, width), f32),
        ],
        in_specs=[vmem, vmem, vmem, anywhere, vmem] + [anywhere] * 4,
        out_specs=[vmem, vmem] + [anywhere] * 5 + [vmem],
        scratch_shapes=[
            pltpu.VMEM((4, 2, 2, 2, rows, width), bf16),
            pltpu.VMEM((4, 2, 2, 2, rows, width), bf16),
            pltpu.VMEM((2 * unit_pad, width), bf16),
            pltpu.VMEM((unit_pad, width), bf16),
            pltpu.VMEM((2 * unit_pad, 32 * rows), bf16),
            pltpu.VMEM((unit_pad, 32 * rows), bf16),
            pltpu.VMEM((2, 4 * rows, unit_pad), bf16),
            pltpu.VMEM((4, 2, 4 * rows, unit_pad), bf16),
            pltpu.VMEM((4, 2, 2, 2, rows, wide), bf16),
            pltpu.VMEM((2, 2, 2, rows, wide), bf16),
            pltpu.VMEM((2, 2, rows, half), bf16),
            pltpu.VMEM((2, 2, rows, wide - half), bf16),
            pltpu.VMEM((2, rows, half), bf16),
            pltpu.VMEM((2, rows, wide - half), bf16),
            pltpu.VMEM((4, rows, wide), bf16),
            pltpu.VMEM((4, 2, 4 * rows, 1), f32),
            pltpu.VMEM((2, 2, rows, width), bf16),
            pltpu.VMEM((2, 2, rows, width), bf16),
            pltpu.VMEM((2, 2, 2, rows, width), bf16),
            pltpu.VMEM((2, expert_units, tile), bf16),
            pltpu.VMEM((2, expert_units, tile), bf16),
            pltpu.VMEM((2, expert_units, tile), bf16),
            pltpu.VMEM((2, 3, shared_units, tile), bf16),
            dma((14,)),
            dma((2,)),
            dma((2, 4)),
            dma((2, 4)),
            dma((2, 4, 4)),
            dma((2, 4, 4)),
            dma((2, 4)),
            dma((2, 4, 4)),
            dma((2, 4)),
            dma((2, 4)),
        ],
        compiler_params=pltpu.CompilerParams(
            collective_id=0, has_side_effects=True, vmem_limit_bytes=63 * 2**20
        ),
        cost_estimate=cost,
    )(residual, ffn_gain, hits, grad_all, side, shared_w, *expert_w)


def path_scalars(parents_ref, segment):
    path = [segment]
    for _ in range(LEVELS - 1):
        last = path[-1]
        parent = parents_ref[jnp.maximum(last, 0)]
        path.append(jnp.where(last >= 0, parent, -1))
    return path


class Line:
    def __init__(self, sems):
        self.sems = sems
        self.column = lax.axis_index("tensor")
        self.levels = [{"tensor": other(self.column, k)} for k in range(4)]
        self.outer = (self.column % 3) == 0
        self.inner = (self.column % 3) != 0

    def remote(self, src, dst, send, receive, device):
        return pltpu.make_async_remote_copy(
            src_ref=src,
            dst_ref=dst,
            send_sem=self.sems.at[0, send],
            recv_sem=self.sems.at[1, receive],
            device_id=device,
            device_id_type=MESH,
        )


class LineGather(Line):
    def __init__(self, slot, sems):
        super().__init__(sems)
        self.slot = slot

    def own(self, k):
        ref = self.slot(self.column)
        return self.remote(ref, ref, k, k, self.levels[k])

    def passed(self):
        ref = self.slot(other(self.column, 2))
        return self.remote(ref, ref, 0, 3, self.levels[1])

    def start(self):
        self.own(2).start()
        self.own(1).start()

        @pl.when(self.inner)
        def _():
            self.own(3).start()

    def forward(self):
        self.own(2).wait_recv()

        @pl.when(self.inner)
        def _():
            self.passed().start()

    def finish(self):
        self.own(1).wait_recv()
        self.own(3).wait_recv()

    def wait_sends(self):
        self.own(1).wait_send()
        self.own(2).wait_send()

        @pl.when(self.inner)
        def _():
            self.own(3).wait_send()
            self.passed().wait_send()


class LineSum(Line):
    def __init__(self, part, got, sems):
        super().__init__(sems)
        self.part, self.got = part, got

    def own(self, k):
        part = self.part(other(self.column, k))
        return self.remote(part, self.got.at[k], k, k, self.levels[k])

    def passed(self):
        part = self.part(other(self.column, 3))
        return self.remote(part, self.got.at[0], 0, 0, self.levels[1])

    def start(self):
        @pl.when(self.outer)
        def _():
            self.passed().start()
            self.own(2).start()
            self.got[3] = jnp.zeros(self.got.shape[1:], self.got.dtype)

        @pl.when(self.inner)
        def _():
            self.own(3).start()

        self.own(1).start()

    def forward(self):
        @pl.when(self.inner)
        def _():
            self.passed().wait_recv()
            part = self.part(other(self.column, 2))
            total = part[...].astype(jnp.float32) + self.got[0].astype(jnp.float32)
            part[...] = total.astype(part.dtype)
            self.own(2).start()

    def finish(self):
        self.own(1).wait_recv()
        self.own(2).wait_recv()

        @pl.when(self.inner)
        def _():
            self.own(3).wait_recv()

        total = self.part(self.column)[...].astype(jnp.float32)
        for k in (1, 2, 3):
            total = total + self.got[k].astype(jnp.float32)
        return total

    def wait_sends(self):
        self.own(1).wait_send()
        self.own(2).wait_send()

        @pl.when(self.outer)
        def _():
            self.passed().wait_send()

        @pl.when(self.inner)
        def _():
            self.own(3).wait_send()


class PlaneGather:
    def __init__(self, block, width, link_sems, core_sems):
        self.block, self.link_sems, self.core_sems = block, link_sems, core_sems
        place = lax.axis_index("dp")
        self.x, self.y, self.corner = other(place, 2), other(place, 4), other(place, 6)
        self.place = place
        self.x_side, self.y_side = {"dp": self.x}, {"dp": self.y}
        self.sibling = {"dp": other(place, 1)}
        self.halves = (pl.ds(0, width // 2), pl.ds(width // 2, width - width // 2))

    def copy(self, ref, sems, which, device):
        return pltpu.make_async_remote_copy(
            src_ref=ref,
            dst_ref=ref,
            send_sem=sems.at[0, which],
            recv_sem=sems.at[1, which],
            device_id=device,
            device_id_type=MESH,
        )

    def direct(self):
        own = self.block(self.place)
        return [
            self.copy(own, self.link_sems, 0, self.x_side),
            self.copy(own, self.link_sems, 1, self.y_side),
            self.copy(own, self.core_sems, 0, self.sibling),
        ]

    def forward(self):
        return [
            self.copy(self.block(self.x, self.halves[0]), self.link_sems, 2, self.y_side),
            self.copy(self.block(self.y, self.halves[1]), self.link_sems, 3, self.x_side),
            self.copy(self.block(self.x), self.core_sems, 1, self.sibling),
            self.copy(self.block(self.y), self.core_sems, 2, self.sibling),
        ]

    def last(self):
        return self.copy(self.block(self.corner), self.core_sems, 3, self.sibling)

    def start(self):
        for copy in self.direct():
            copy.start()

    def start_forward(self):
        for copy in self.direct()[:2]:
            copy.wait_recv()
        for copy in self.forward():
            copy.start()

    def start_last(self):
        for copy in self.forward()[:2]:
            copy.wait_recv()
        self.last().start()

    def finish(self):
        self.direct()[2].wait_recv()
        for copy in self.forward()[2:]:
            copy.wait_recv()
        self.last().wait_recv()

    def wait_sends(self):
        for copy in self.direct() + self.forward() + [self.last()]:
            copy.wait_send()


def turn(values, cosine, sine):
    heads = []
    for begin in range(0, values.shape[1], HEAD_DIM):
        head = values[:, begin : begin + HEAD_DIM]
        heads.append(head * cosine + pltpu.roll(head, HEAD_DIM // 2, 1) * sine)
    return jnp.concatenate(heads, 1)


def front_kernel(
    score_scale,
    shared_units,
    parents_ref,
    hidden_ref,
    gain_ref,
    bias_ref,
    freqs_ref,
    hits_ref,
    out_grad_ref,
    w_query_ref,
    w_key_ref,
    w_value_ref,
    w_out_ref,
    s_gate_ref,
    s_up_ref,
    s_down_ref,
    residual_ref,
    query_ref,
    key_ref,
    value_ref,
    log_total_ref,
    attended_ref,
    normed_ref,
    cosine_ref,
    sine_ref,
    hits_all_ref,
    grad_all_ref,
    shared_ref,
    weights,
    kv_all,
    hits_all,
    part_send,
    part_z,
    s_tiles,
    t_tiles,
    load_sems,
    tile_sems,
    store_sems,
    hit_sems,
    part_sems,
    kv_links,
    kv_cores,
    head_links,
    head_cores,
    tail_links,
    tail_cores,
):
    bf16, f32 = jnp.bfloat16, jnp.float32
    place, column = lax.axis_index("dp"), lax.axis_index("tensor")
    tok_rows, width = hidden_ref.shape
    rows = tok_rows // 4
    local_width = w_query_ref.shape[1]
    levels = [{"tensor": other(column, k)} for k in range(4)]
    peers = [{"dp": other(place, j)} for j in range(8)]

    loads = [
        pltpu.make_async_copy(ref, weights.at[i], load_sems.at[i])
        for i, ref in enumerate((w_query_ref, w_key_ref, w_value_ref, w_out_ref))
    ]
    own_grad = pltpu.make_async_copy(out_grad_ref, grad_all_ref.at[place], load_sems.at[4])
    for copy in loads:
        copy.start()
    own_grad.start()
    hits_all[place] = hits_ref[...]

    barrier = pltpu.get_barrier_semaphore()
    partners = peers[1:] + levels[1:]
    for partner in partners:
        pl.semaphore_signal(barrier, inc=1, device_id=partner, device_id_type=MESH)
    pl.semaphore_wait(barrier, len(partners))

    def grad_block(first, count):
        def block(d, cols=slice(None)):
            return grad_all_ref.at[d, pl.ds(first, count), :, cols]

        return block

    head_gather = PlaneGather(grad_block(0, 1), width, head_links, head_cores)
    tail_gather = PlaneGather(grad_block(1, 3), width, tail_links, tail_cores)
    kv_gather = PlaneGather(
        lambda d, cols=slice(None): kv_all.at[d, :, cols], 2 * local_width, kv_links, kv_cores
    )
    own_grad.wait()
    head_gather.start()

    def hit_copy(j):
        return pltpu.make_async_remote_copy(
            src_ref=hits_all.at[place],
            dst_ref=hits_all.at[place],
            send_sem=hit_sems.at[0, j],
            recv_sem=hit_sems.at[1, j],
            device_id=peers[j],
            device_id_type=MESH,
        )

    for j in range(1, 8):
        hit_copy(j).start()

    path = path_scalars(parents_ref, place)
    depth = jnp.float32(-1.0)
    for segment in path:
        depth = depth + jnp.where(segment >= 0, 1.0, 0.0)
    row_ids = lax.broadcasted_iota(jnp.int32, (tok_rows, HEAD_DIM), 0).astype(f32)
    lane = lax.broadcasted_iota(jnp.int32, (tok_rows, HEAD_DIM), 1)
    angles = (depth * SEG + row_ids) * freqs_ref[...]
    cosine = jnp.cos(angles)
    sine = jnp.where(lane < HEAD_DIM // 2, -1.0, 1.0) * jnp.sin(angles)
    cosine_ref[...] = cosine
    sine_ref[...] = sine
    hidden_f = hidden_ref[...].astype(f32)
    scale_rows = lax.rsqrt(jnp.mean(hidden_f * hidden_f, 1, keepdims=True) + epsilon)
    normed_ref[...] = (hidden_f * scale_rows * gain_ref[...]).astype(bf16)
    for copy in loads[1:3]:
        copy.wait()
    key = product(normed_ref[...], weights[1]) + bias_ref[1:2, :]
    kv_all[place, :, :local_width] = turn(key, cosine, sine).astype(bf16)
    value = product(normed_ref[...], weights[2]) + bias_ref[2:3, :]
    kv_all[place, :, local_width:] = value.astype(bf16)
    kv_gather.start()
    loads[0].wait()
    query = product(normed_ref[...], weights[0]) + bias_ref[0:1, :]
    query_ref[...] = turn(query, cosine, sine).astype(bf16)

    tile, span = s_tiles.shape[2:]
    shared_first = place * shared_units
    shared_base = jnp.minimum(shared_first // 128 * 128, s_gate_ref.shape[1] - span)
    shared_skip = shared_first - shared_base

    def tile_loads(i, slot):
        window = pl.ds(pl.multiple_of(i * tile, tile), tile)
        columns = pl.ds(pl.multiple_of(shared_base, 128), span)
        return [
            pltpu.make_async_copy(
                ref.at[window, columns], s_tiles.at[slot, j], tile_sems.at[slot, j]
            )
            for j, ref in enumerate((s_gate_ref, s_up_ref, s_down_ref))
        ]

    def tile_stores(i, slot):
        window = pl.ds(pl.multiple_of(i * tile, tile), tile)
        units = pl.ds(pl.multiple_of(shared_skip, 16), shared_units)
        return [
            pltpu.make_async_copy(
                t_tiles.at[slot, j, units], shared_ref.at[j, :, window], store_sems.at[slot, j]
            )
            for j in range(3)
        ]

    tiles = width // tile

    def pack(i, carry):
        slot = i % 2

        @pl.when(i + 1 < tiles)
        def _():
            for copy in tile_loads(i + 1, (i + 1) % 2):
                copy.start()

        for copy in tile_loads(i, slot):
            copy.wait()

        @pl.when(i >= 2)
        def _():
            for copy in tile_stores(i - 2, slot):
                copy.wait()

        for j in range(3):
            t_tiles[slot, j] = s_tiles[slot, j].T
        for copy in tile_stores(i, slot):
            copy.start()
        return carry

    for copy in tile_loads(0, 0):
        copy.start()
    lax.fori_loop(0, tiles // 2, pack, 0)
    kv_gather.start_forward()
    lax.fori_loop(tiles // 2, tiles, pack, 0)
    kv_gather.start_last()
    tail_gather.start()
    head_gather.start_forward()
    for i in (tiles - 2, tiles - 1):
        for copy in tile_stores(i, i % 2):
            copy.wait()
    kv_gather.finish()

    for level, segment in enumerate(path):
        block = kv_all[jnp.maximum(segment, 0)]
        key_ref[level * tok_rows : (level + 1) * tok_rows, :] = block[:, :local_width]
        value_ref[level * tok_rows : (level + 1) * tok_rows, :] = block[:, local_width:]
    key_rows = key_ref.shape[0]
    row_id = lax.broadcasted_iota(jnp.int32, (tok_rows, key_rows), 0)
    col_id = lax.broadcasted_iota(jnp.int32, (tok_rows, key_rows), 1)
    allowed = row_id >= col_id
    for level in range(1, LEVELS):
        barred = jnp.where(path[level] >= 0, key_rows, 0)
        inside = (col_id >= level * tok_rows) & (col_id < (level + 1) * tok_rows)
        allowed = allowed | (inside & (col_id < barred))

    def head(h, carry):
        cols = pl.ds(pl.multiple_of(h * HEAD_DIM, HEAD_DIM), HEAD_DIM)
        scores = product_nt(query_ref[:, cols], key_ref[:, cols]) * score_scale
        scores = jnp.where(allowed, scores, -jnp.inf)
        top = jnp.max(scores, 1, keepdims=True)
        powers = jnp.exp(scores - top)
        total = jnp.sum(powers, 1, keepdims=True)
        log_total_ref[h] = top + jnp.log(total)
        probs = (powers * (1.0 / total)).astype(bf16)
        attended_ref[:, cols] = product(probs, value_ref[:, cols]).astype(bf16)
        return carry

    lax.fori_loop(0, local_width // HEAD_DIM, head, 0)

    loads[3].wait()
    for quarter in range(4):
        mine = slice(quarter * rows, (quarter + 1) * rows)
        part_send[quarter] = product_nt(attended_ref[mine, :], weights[3]).astype(bf16)

    line = LineSum(lambda z: part_send.at[z], part_z, part_sems)
    line.start()
    head_gather.start_last()
    tail_gather.start_forward()
    line.forward()
    attn = line.finish()
    own_rows = pl.ds(pl.multiple_of(column * rows, rows), rows)
    residual_ref[...] = hidden_ref[own_rows, :].astype(f32) + attn
    tail_gather.start_last()
    head_gather.finish()
    for j in range(1, 8):
        hit_copy(j).wait_recv()
    hits_all_ref[...] = hits_all[...]
    tail_gather.finish()

    for gather in (kv_gather, head_gather, tail_gather):
        gather.wait_sends()
    for j in range(1, 8):
        hit_copy(j).wait_send()
    line.wait_sends()


def front_layer(score_scale, shared_units, operands):
    hidden, w_query = operands[1], operands[7]
    tok_rows, width = hidden.shape
    rows, local_width = tok_rows // 4, w_query.shape[1]
    heads = local_width // HEAD_DIM
    tile, span = 256, 384
    bf16, f32 = jnp.bfloat16, jnp.float32
    shape = jax.ShapeDtypeStruct
    vmem, anywhere = pl.BlockSpec(memory_space=pltpu.VMEM), pl.BlockSpec(memory_space=pl.ANY)
    smem = pl.BlockSpec(memory_space=pltpu.SMEM)
    dma = pltpu.SemaphoreType.DMA
    return pl.pallas_call(
        functools.partial(front_kernel, score_scale, shared_units),
        out_shape=[
            shape((rows, width), f32),
            shape((tok_rows, local_width), bf16),
            shape((LEVELS * tok_rows, local_width), bf16),
            shape((LEVELS * tok_rows, local_width), bf16),
            shape((heads, tok_rows, 1), f32),
            shape((tok_rows, local_width), bf16),
            shape((tok_rows, width), bf16),
            shape((tok_rows, HEAD_DIM), f32),
            shape((tok_rows, HEAD_DIM), f32),
            shape((8, 16, tok_rows), f32),
            shape((8, 4, rows, width), bf16),
            shape((3, shared_units, width), bf16),
        ],
        in_specs=[smem] + [vmem] * 6 + [anywhere] * 7,
        out_specs=[vmem] * 10 + [anywhere] * 2,
        scratch_shapes=[
            pltpu.VMEM((4, width, local_width), bf16),
            pltpu.VMEM((8, tok_rows, 2 * local_width), bf16),
            pltpu.VMEM((8, 16, tok_rows), f32),
            pltpu.VMEM((4, rows, width), bf16),
            pltpu.VMEM((4, rows, width), bf16),
            pltpu.VMEM((2, 3, tile, span), bf16),
            pltpu.VMEM((2, 3, span, tile), bf16),
            dma((5,)),
            dma((2, 3)),
            dma((2, 3)),
            dma((2, 8)),
            dma((2, 4)),
        ]
        + [dma((2, 4))] * 6,
        compiler_params=pltpu.CompilerParams(
            collective_id=2, has_side_effects=True, vmem_limit_bytes=56 * 2**20
        ),
        cost_estimate=pl.CostEstimate(
            flops=2 * 2**31, bytes_accessed=40 * 2**20, transcendentals=2**21
        ),
    )(*operands)


class PlaneSum:
    def __init__(self, mine, theirs, got_core, got_x1, got_y1, got_y2, got_x2, core_sems, sems):
        self.mine, self.theirs = mine, theirs
        self.got = (got_core, got_x1, got_y1, got_y2, got_x2)
        self.core_sems, self.sems = core_sems, sems
        self.half = got_x1.shape[-1]
        self.wide = self.half + got_y1.shape[-1]
        self.left, self.right = pl.ds(0, self.half), pl.ds(self.half, self.wide - self.half)
        place = lax.axis_index("dp")
        self.core, self.east, self.north = place % 2, (place // 2) % 2, place // 4
        self.sibling = {"dp": other(place, 1)}
        self.x_side, self.y_side = {"dp": other(place, 2)}, {"dp": other(place, 4)}

    def remote(self, src, dst, sems, which, device):
        return pltpu.make_async_remote_copy(
            src_ref=src,
            dst_ref=dst,
            send_sem=sems.at[(0, *which)],
            recv_sem=sems.at[(1, *which)],
            device_id=device,
            device_id_type=MESH,
        )

    def core_copy(self, k):
        return self.remote(
            self.theirs(k), self.got[0].at[k], self.core_sems, (k,), self.sibling
        )

    def first_copies(self, k):
        mine = self.mine(k)
        return [
            self.remote(
                mine.at[:, flip(self.east), :, self.left],
                self.got[1].at[k],
                self.sems,
                (0, k),
                self.x_side,
            ),
            self.remote(
                mine.at[flip(self.north), :, :, self.right],
                self.got[2].at[k],
                self.sems,
                (1, k),
                self.y_side,
            ),
        ]

    def second_copies(self, k):
        mine = self.mine(k)
        return [
            self.remote(
                mine.at[flip(self.north), self.east, :, self.left],
                self.got[3].at[k],
                self.sems,
                (2, k),
                self.y_side,
            ),
            self.remote(
                mine.at[self.north, flip(self.east), :, self.right],
                self.got[4].at[k],
                self.sems,
                (3, k),
                self.x_side,
            ),
        ]

    def add(self, ref, value):
        ref[...] = (ref[...].astype(jnp.float32) + value.astype(jnp.float32)).astype(jnp.bfloat16)

    def start(self, k):
        self.core_copy(k).start()

    def after_core(self, k):
        self.core_copy(k).wait_recv()
        mine = self.mine(k)
        for y in range(2):
            for x in range(2):
                self.add(mine.at[y, x], self.got[0][k, y, x])
        self.start_first(k)

    def start_first(self, k):
        for copy in self.first_copies(k):
            copy.start()

    def after_first(self, k):
        x_copy, y_copy = self.first_copies(k)
        mine = self.mine(k)
        x_copy.wait_recv()
        for y in range(2):
            self.add(mine.at[y, self.east, :, self.left], self.got[1][k, y])
        y_copy.wait_recv()
        for x in range(2):
            self.add(mine.at[self.north, x, :, self.right], self.got[2][k, x])
        for copy in self.second_copies(k):
            copy.start()

    def after_second(self, k):
        y_copy, x_copy = self.second_copies(k)
        own = self.mine(k).at[self.north, self.east]
        y_copy.wait_recv()
        self.add(own.at[:, self.left], self.got[3][k])
        x_copy.wait_recv()
        self.add(own.at[:, self.right], self.got[4][k])
        return own

    def wait_sends(self, k):
        if self.theirs is not None:
            self.core_copy(k).wait_send()
        for copy in self.first_copies(k) + self.second_copies(k):
            copy.wait_send()


def plane_scratch(count, rows, wide):
    half = wide // 2
    bf16, dma = jnp.bfloat16, pltpu.SemaphoreType.DMA
    return [
        pltpu.VMEM((count, 2, 2, rows, wide), bf16),
        pltpu.VMEM((count, 2, rows, half), bf16),
        pltpu.VMEM((count, 2, rows, wide - half), bf16),
        pltpu.VMEM((count, rows, half), bf16),
        pltpu.VMEM((count, rows, wide - half), bf16),
        dma((2, count)),
        dma((2, 4, count)),
    ]


def unturn(grad, cosine, sine):
    heads = []
    for begin in range(0, grad.shape[1], HEAD_DIM):
        head = grad[:, begin : begin + HEAD_DIM]
        heads.append(head * cosine - pltpu.roll(head, HEAD_DIM // 2, 1) * sine)
    return jnp.concatenate(heads, 1)


def back_kernel(
    score_scale,
    gain_row,
    residual_ref,
    res_grad_ref,
    res_low_ref,
    ffn_part_ref,
    shared_ref,
    small_ref,
    query_ref,
    key_ref,
    value_ref,
    parents_ref,
    log_total_ref,
    attended_ref,
    normed_ref,
    hidden_ref,
    gain_ref,
    cosine_ref,
    sine_ref,
    w_out_ref,
    w_query_ref,
    w_key_ref,
    w_value_ref,
    hidden_out_ref,
    hidden_grad_ref,
    grad_query_ref,
    grad_key_ref,
    grad_value_ref,
    grad_out_ref,
    shared_got,
    small_out_ref,
    bias_out_ref,
    low_all,
    w_qkv,
    out_mine,
    out_z,
    kv_sums,
    w_sums,
    kv_path,
    attended_grad,
    query_grad,
    pre_grads,
    part,
    part_send,
    part_z,
    hidden_stage,
    shared_stage,
    small_send,
    small_got,
    small_z,
    *rest,
):
    bf16, f32 = jnp.bfloat16, jnp.float32
    out_scr, rest = rest[:5], rest[5:]
    kv_scr, rest = rest[:7], rest[7:]
    w_scr, rest = rest[:7], rest[7:]
    wkv_sems, rest = rest[:2], rest[2:]
    load_sems, low_sems, out_sems, part_sems, end_sems, shared_sems, small_sems, small_z_sems = rest
    place, column = lax.axis_index("dp"), lax.axis_index("tensor")
    core, east, north = place % 2, (place // 2) % 2, place // 4
    rows, width = residual_ref.shape
    tok_rows, local_width = query_ref.shape
    levels = [{"tensor": other(column, k)} for k in range(4)]
    peers = [{"dp": other(place, j)} for j in range(8)]

    def remote(src, dst, sems, which, device):
        return pltpu.make_async_remote_copy(
            src_ref=src,
            dst_ref=dst,
            send_sem=sems.at[(0, *which)],
            recv_sem=sems.at[(1, *which)],
            device_id=device,
            device_id_type=MESH,
        )

    def load_out(z):
        return pltpu.make_async_copy(ffn_part_ref.at[z], out_mine.at[z], load_sems.at[z])

    loads = [
        pltpu.make_async_copy(w_query_ref, w_qkv.at[0], load_sems.at[5]),
        pltpu.make_async_copy(w_key_ref, w_qkv.at[1], load_sems.at[6]),
        pltpu.make_async_copy(w_out_ref, w_qkv.at[2], load_sems.at[4]),
    ]
    load_value = pltpu.make_async_copy(w_value_ref, w_qkv.at[2], load_sems.at[7])
    load_shared = pltpu.make_async_copy(shared_ref.at[place], shared_stage, load_sems.at[9])
    load_shared.start()
    for z in range(4):
        load_out(z).start()
    for copy in loads:
        copy.start()

    barrier = pltpu.get_barrier_semaphore()
    partners = peers[1:] + levels[1:]
    for partner in partners:
        pl.semaphore_signal(barrier, inc=1, device_id=partner, device_id_type=MESH)
    pl.semaphore_wait(barrier, len(partners))

    out_sum = PlaneSum(lambda k: out_mine.at[k], None, None, *out_scr[:4], None, out_scr[4])
    kv_sum = PlaneSum(
        lambda k: kv_sums.at[k, core], lambda k: kv_sums.at[k, flip(core)], *kv_scr
    )
    w_sum = PlaneSum(
        lambda k: w_sums.at[k, core], lambda k: w_sums.at[k, flip(core)], *w_scr
    )
    wkv_sum = PlaneSum(
        lambda k: kv_sums.at[k, core],
        lambda k: kv_sums.at[k, flip(core)],
        *kv_scr[:5],
        *wkv_sems,
    )

    low_all[column] = res_low_ref[...]
    low_line = LineGather(lambda z: low_all.at[z], low_sems)
    low_line.start()
    order = [other(column, k) for k in (1, 3, 2, 0)]
    for z in range(4):
        load_out(z).wait()
    for z in order:
        out_sum.start_first(z)
    kv_path[...] = jnp.zeros(kv_path.shape, f32)
    for copy in loads:
        copy.wait()

    out_line = LineSum(lambda z: out_mine.at[z, north, east], out_z, out_sems)
    low_line.forward()

    half_rows = tok_rows // 2
    key_rows = key_ref.shape[0]
    row_id = lax.broadcasted_iota(jnp.int32, (half_rows, key_rows), 0)
    col_id = lax.broadcasted_iota(jnp.int32, (half_rows, key_rows), 1)
    path = path_scalars(parents_ref, place)
    reached = col_id < 0
    for level in range(1, LEVELS):
        barred = jnp.where(path[level] >= 0, key_rows, 0)
        inside = (col_id >= level * tok_rows) & (col_id < (level + 1) * tok_rows)
        reached = reached | (inside & (col_id < barred))

    def half(i, carry):
        pair = (column // 2 + i) % 2
        first = pl.multiple_of(pair * half_rows, half_rows)
        window = pl.ds(first, half_rows)

        @pl.when(i == 0)
        def _():
            low_line.own(1).wait_recv()

        @pl.when(i == 1)
        def _():
            low_line.own(3).wait_recv()

        low_rows = low_all[pl.ds(2 * pair, 2)].reshape(half_rows, width)
        attended_grad[window, :] = product(low_rows, w_qkv[2]).astype(bf16)
        allowed = (row_id + first >= col_id) | reached

        def head(h, carry):
            cols = pl.ds(pl.multiple_of(h * HEAD_DIM, HEAD_DIM), HEAD_DIM)
            value_cols = pl.ds(pl.multiple_of(local_width + h * HEAD_DIM, HEAD_DIM), HEAD_DIM)
            query, key, value = query_ref[window, cols], key_ref[:, cols], value_ref[:, cols]
            grad = attended_grad[window, cols]
            scores = jnp.where(allowed, product_nt(query, key) * score_scale, -jnp.inf)
            weights = jnp.exp(scores - log_total_ref[h, window])
            weight_grad = product_nt(grad, value)
            center = jnp.sum(weights * weight_grad, 1, keepdims=True)
            score_grad = (weights * (weight_grad - center)).astype(bf16)
            query_grad[window, cols] = product(score_grad, key) * score_scale
            kv_path[:, cols] += product_tn(score_grad, query) * score_scale
            kv_path[:, value_cols] += product_tn(weights.astype(bf16), grad)
            return carry

        lax.fori_loop(0, local_width // HEAD_DIM, head, 0)

        @pl.when(i == 0)
        def _():
            out_sum.after_first(order[0])
            out_sum.after_first(order[1])

        return carry

    lax.fori_loop(0, 2, half, 0)
    for z in order[2:]:
        out_sum.after_first(z)
    load_value.start()

    part_rows = rows // 2

    def kv_blocks(i, c):
        which, y, x = i // 4, (i // 2) % 2, i % 2
        segment = 4 * y + 2 * x + c
        total = jnp.zeros((4, part_rows, 2 * local_width), f32)
        for level in range(1, LEVELS):
            spot = jnp.where(path[level] == segment, 1.0, 0.0)
            total = total + spot * kv_rows(level, which)
        kv_sums[which, c, y, x] = total.reshape(4 * part_rows, 2 * local_width).astype(bf16)
        return c

    def kv_rows(level, which):
        rows_view = kv_path.at[level * tok_rows : (level + 1) * tok_rows]
        pieces = []
        for z in range(4):
            start = pl.multiple_of(z * rows + which * part_rows, part_rows)
            pieces.append(rows_view[pl.ds(start, part_rows), :])
        return jnp.stack(pieces)

    lax.fori_loop(0, 4, kv_blocks, flip(core))
    kv_sum.start(0)
    lax.fori_loop(4, 8, kv_blocks, flip(core))
    kv_sum.start(1)
    lax.fori_loop(0, 8, kv_blocks, core)
    for which in range(2):
        own_kv = kv_sums.at[which, core, north, east]
        added = own_kv[...].astype(f32) + kv_rows(0, which).reshape(4 * part_rows, -1)
        own_kv[...] = added.astype(bf16)
        kv_sum.after_core(which)
    for z in order:
        out_sum.after_second(z)
    out_line.start()

    def bias_of(which, grad, begin):
        bias = jnp.sum(grad.astype(f32), 0, keepdims=True)
        for h in range(local_width // HEAD_DIM):
            spot = slice(4 * which + h, 4 * which + h + 1)
            added = bias[:, h * HEAD_DIM : (h + 1) * HEAD_DIM]
            if not begin:
                added = added + small_send[0, spot, 2 * HEAD_DIM :]
            small_send[0, spot, 2 * HEAD_DIM :] = added

    small_send[0, :, 2 * HEAD_DIM :] = jnp.zeros((16, HEAD_DIM), f32)
    query_pre = unturn(query_grad[...], cosine_ref[...], sine_ref[...]).astype(bf16)
    pre_grads[0] = query_pre.reshape(4, 2, part_rows, local_width)
    bias_of(0, query_pre, True)
    part[...] = product_nt(query_pre, w_qkv[0]).reshape(4, 2, part_rows, width)
    def block_index(place_of):
        return place_of % 2, place_of // 4, (place_of // 2) % 2

    def out_weights(i, carry):
        c, y, x = block_index(i)
        window = pl.ds(pl.multiple_of(i * tok_rows, tok_rows), tok_rows)
        lhs = low_all[:, :, window].reshape(tok_rows, tok_rows)
        w_sums[0, c, y, x] = product_tn(lhs, attended_ref[...]).astype(bf16)
        return carry

    def query_weights(i, carry):
        c, y, x = block_index(i)
        window = pl.ds(pl.multiple_of(i * tok_rows, tok_rows), tok_rows)
        rows_pre = pre_grads[0].reshape(tok_rows, local_width)
        w_sums[1, c, y, x] = product_tn(normed_ref[:, window], rows_pre).astype(bf16)
        return carry

    lax.fori_loop(0, 8, out_weights, 0)
    w_sum.start(0)
    lax.fori_loop(0, 8, query_weights, 0)
    w_sum.start(1)
    kv_sum.after_first(0)
    kv_sum.after_first(1)

    load_value.wait()
    hidden_f = hidden_ref[...].astype(f32)
    unit_scale = lax.rsqrt(jnp.mean(hidden_f * hidden_f, 1, keepdims=True) + epsilon)

    part_lines = [
        LineSum(
            lambda z, which=which: part_send.at[which, z],
            part_z.at[which],
            part_sems.at[which],
        )
        for which in range(2)
    ]

    for which in range(2):
        own_kv = kv_sum.after_second(which)
        cos_rows = cosine_ref[...].reshape(4, 2, part_rows, HEAD_DIM)[:, which]
        sin_rows = sine_ref[...].reshape(4, 2, part_rows, HEAD_DIM)[:, which]
        key_pre = unturn(
            own_kv[:, :local_width].astype(f32),
            cos_rows.reshape(4 * part_rows, HEAD_DIM),
            sin_rows.reshape(4 * part_rows, HEAD_DIM),
        ).astype(bf16)
        value_pre = own_kv[:, local_width:]
        pre_grads[1, :, which] = key_pre.reshape(4, part_rows, local_width)
        pre_grads[2, :, which] = value_pre.reshape(4, part_rows, local_width)
        bias_of(1, key_pre, which == 0)
        bias_of(2, value_pre, which == 0)
        added = product_nt(key_pre, w_qkv[1]) + product_nt(value_pre, w_qkv[2])
        whole = part[:, which] + added.reshape(4, part_rows, width)
        part[:, which] = whole
        part_send[which] = whole.astype(bf16)
        part_lines[which].start()
        if which == 0:
            out_line.forward()


    def shared_copy(j):
        return remote(
            shared_ref.at[other(place, j)], shared_got.at[place], shared_sems, (j,), peers[j]
        )

    for k in range(2):
        w_sum.after_core(k)
    part_lines[0].forward()
    attn_gain_row = jnp.sum(
        part[...].reshape(tok_rows, width) * (hidden_f * unit_scale), 0, keepdims=True
    )
    def key_value_weights(i, carry):
        c, y, x = block_index(i)
        window = pl.ds(pl.multiple_of(i * tok_rows, tok_rows), tok_rows)
        lhs = normed_ref[:, window]
        for which, cols in ((1, slice(0, local_width)), (2, slice(local_width, None))):
            rows_pre = pre_grads[which].reshape(tok_rows, local_width)
            grad = product_tn(lhs, rows_pre).astype(bf16)
            for k in range(2):
                piece = slice(k * half_rows, (k + 1) * half_rows)
                kv_sums[k, c, y, x, :, cols] = grad[piece]
        return carry

    for k in range(2):
        kv_sum.wait_sends(k)
    lax.fori_loop(0, 8, key_value_weights, 0)
    for k in range(2):
        wkv_sum.start(k)
    part_lines[1].forward()

    bias_rows = small_send[0, :, 2 * HEAD_DIM :]
    for d in range(8):
        small_send[d, :, : 2 * HEAD_DIM] = small_ref[:, d * tok_rows : (d + 1) * tok_rows]
        small_send[d, gain_row : gain_row + 1, : 2 * HEAD_DIM] = attn_gain_row[
            :, d * tok_rows : (d + 1) * tok_rows
        ]
        small_send[d, :, 2 * HEAD_DIM :] = bias_rows

    def small_copy(j):
        return remote(
            small_send.at[other(place, j)], small_got.at[j], small_sems, (j,), peers[j]
        )

    for j in range(1, 8):
        small_copy(j).start()

    w_sum.after_first(0)
    for k in range(2):
        wkv_sum.after_core(k)
    w_sum.after_first(1)
    own_shared = pltpu.make_async_copy(shared_stage, shared_got.at[place], load_sems.at[8])
    load_shared.wait()
    own_shared.start()

    total = small_send[place]
    for j in range(1, 8):
        small_copy(j).wait_recv()
        total = total + small_got[j]
    bias_out_ref[...] = total[:, 2 * HEAD_DIM :]
    small_z[column] = total[:, : 2 * HEAD_DIM]
    own_small = small_z.at[column]
    small_levels = [
        remote(own_small, own_small, small_z_sems, (k,), levels[k]) for k in (1, 2, 3)
    ]
    for copy in small_levels:
        copy.start()

    end_lines = [
        LineGather(
            lambda z, which=which, piece=piece: hidden_stage.at[which, z, piece],
            end_sems.at[which, piece],
        )
        for which in range(2)
        for piece in range(2)
    ]

    for which in range(2):
        attn_grad = part_lines[which].finish()
        start = pl.multiple_of(column * rows + which * part_rows, part_rows)
        own_hidden = hidden_ref[pl.ds(start, part_rows), :].astype(f32)
        own_scale = lax.rsqrt(jnp.mean(own_hidden * own_hidden, 1, keepdims=True) + epsilon)
        own_grad = res_grad_ref[which * part_rows : (which + 1) * part_rows, :]
        hidden_stage[0, column, which] = (
            own_grad + norm_back(attn_grad, own_hidden * own_scale, own_scale, gain_ref[...])
        ).astype(bf16)
        end_lines[which].start()
        if which == 0:
            grad_out_ref[...] = w_sum.after_second(0)[...]
            for k in range(2):
                wkv_sum.after_first(k)
            for j in (6, 7, 2, 3, 4, 5, 1):
                shared_copy(j).start()

    end_lines[0].forward()
    out = residual_ref[...] + out_line.finish()
    hidden_stage[1, column] = out.astype(bf16).reshape(2, part_rows, width)
    end_lines[1].forward()
    end_lines[2].start()
    end_lines[3].start()

    grad_query_ref[...] = w_sum.after_second(1)[...]
    for copy in small_levels:
        copy.wait_recv()
    small_out_ref[...] = (small_z[0] + small_z[1]) + (small_z[2] + small_z[3])
    for k in range(2):
        own_wkv = wkv_sum.after_second(k)
        piece = slice(k * half_rows, (k + 1) * half_rows)
        grad_key_ref[piece, :] = own_wkv[:, :local_width]
        grad_value_ref[piece, :] = own_wkv[:, local_width:]

    end_lines[2].forward()
    end_lines[3].forward()
    own_shared.wait()
    for j in range(1, 8):
        shared_copy(j).wait_recv()
    for line in end_lines:
        line.finish()
    ends = [
        pltpu.make_async_copy(hidden_stage.at[0], hidden_grad_ref, load_sems.at[10]),
        pltpu.make_async_copy(hidden_stage.at[1], hidden_out_ref, load_sems.at[11]),
    ]
    for copy in ends:
        copy.start()
    for copy in ends:
        copy.wait()

    for copy in small_levels:
        copy.wait_send()
    for line in [low_line, out_line] + part_lines + end_lines:
        line.wait_sends()
    for z in range(4):
        out_sum.wait_sends(z)
    for k in range(2):
        w_sum.wait_sends(k)
        wkv_sum.wait_sends(k)
    for j in range(1, 8):
        small_copy(j).wait_send()
        shared_copy(j).wait_send()


def back_layer(score_scale, gain_row, operands):
    (
        residual,
        res_grad,
        res_low,
        ffn_part,
        grad_shared,
        small,
        query,
        key,
        value,
        parents,
        log_total,
        attended,
        normed,
        hidden,
        gain,
        cosine,
        sine,
        w_out,
        w_query,
        w_key,
        w_value,
    ) = operands
    rows, width = residual.shape
    tok_rows, local_width = query.shape
    units = grad_shared.shape[2]
    bf16, f32 = jnp.bfloat16, jnp.float32
    shape = jax.ShapeDtypeStruct
    vmem, anywhere = pl.BlockSpec(memory_space=pltpu.VMEM), pl.BlockSpec(memory_space=pl.ANY)
    smem = pl.BlockSpec(memory_space=pltpu.SMEM)
    dma = pltpu.SemaphoreType.DMA
    return pl.pallas_call(
        functools.partial(back_kernel, score_scale, gain_row),
        out_shape=[
            shape((4, 2, rows // 2, width), bf16),
            shape((4, 2, rows // 2, width), bf16),
            shape((tok_rows, local_width), bf16),
            shape((tok_rows, local_width), bf16),
            shape((tok_rows, local_width), bf16),
            shape((tok_rows, local_width), bf16),
            shape((8, 3, units, tok_rows), bf16),
            shape((16, tok_rows), f32),
            shape((16, HEAD_DIM), f32),
        ],
        in_specs=[vmem, vmem, vmem, anywhere, anywhere, vmem]
        + [vmem] * 3
        + [smem]
        + [vmem] * 7
        + [anywhere] * 4,
        out_specs=[anywhere] * 2 + [vmem] * 4 + [anywhere] + [vmem] * 2,
        scratch_shapes=[
            pltpu.VMEM((4, rows, width), bf16),
            pltpu.VMEM((3, width, local_width), bf16),
            pltpu.VMEM((4, 2, 2, rows, width), bf16),
            pltpu.VMEM((4, rows, width), bf16),
            pltpu.VMEM((2, 2, 2, 2, tok_rows // 2, 2 * local_width), bf16),
            pltpu.VMEM((2, 2, 2, 2, tok_rows, local_width), bf16),
            pltpu.VMEM((LEVELS * tok_rows, 2 * local_width), f32),
            pltpu.VMEM((tok_rows, local_width), bf16),
            pltpu.VMEM((tok_rows, local_width), f32),
            pltpu.VMEM((3, 4, 2, rows // 2, local_width), bf16),
            pltpu.VMEM((4, 2, rows // 2, width), f32),
            pltpu.VMEM((2, 4, rows // 2, width), bf16),
            pltpu.VMEM((2, 4, rows // 2, width), bf16),
            pltpu.VMEM((2, 4, 2, rows // 2, width), bf16),
            pltpu.VMEM((3, units, tok_rows), bf16),
            pltpu.VMEM((8, 16, 2 * HEAD_DIM + HEAD_DIM), f32),
            pltpu.VMEM((8, 16, 2 * HEAD_DIM + HEAD_DIM), f32),
            pltpu.VMEM((4, 16, 2 * HEAD_DIM), f32),
        ]
        + plane_scratch(4, rows, width)[1:5]
        + plane_scratch(4, rows, width)[6:]
        + plane_scratch(2, tok_rows // 2, 2 * local_width)
        + plane_scratch(2, tok_rows, local_width)
        + plane_scratch(2, tok_rows // 2, 2 * local_width)[5:]
        + [
            dma((12,)),
            dma((2, 4)),
            dma((2, 4)),
            dma((2, 2, 4)),
            dma((2, 2, 2, 4)),
            dma((2, 8)),
            dma((2, 8)),
            dma((2, 4)),
        ],
        compiler_params=pltpu.CompilerParams(
            collective_id=1, has_side_effects=True, vmem_limit_bytes=63 * 2**20
        ),
        cost_estimate=pl.CostEstimate(
            flops=2 * 12 * 2**30, bytes_accessed=40 * 2**20, transcendentals=2**20
        ),
    )(*operands)


def on_slice(
    hidden_in,
    out_grad,
    parents,
    routes,
    attn_gain,
    w_query,
    w_key,
    w_value,
    b_query,
    b_key,
    b_value,
    w_out,
    ffn_gain,
    w_router,
    shared_gate,
    shared_w_gate,
    shared_w_up,
    shared_w_down,
    expert_w_gate,
    expert_w_up,
    expert_w_down,
):
    tok_rows, model_width = hidden_in.shape
    devices = lax.axis_size("dp")
    columns = lax.axis_size("tensor")
    place, column = lax.axis_index("dp"), lax.axis_index("tensor")
    all_rows = tok_rows * devices
    part_rows = tok_rows // columns
    local_width = w_query.shape[1]
    experts = w_router.shape[1]
    top_count = routes.shape[1]
    capacity = 5 * tok_rows * top_count // 4
    score_scale = HEAD_DIM ** (-0.5)
    bf16, f32 = jnp.bfloat16, jnp.float32

    expert_units = expert_w_gate.shape[2]
    shared_units = shared_w_gate.shape[1] // devices
    shared_pad = -(-shared_units // 128) * 128
    units = shared_pad + expert_units
    units_pad = -(-(units + experts + 1) // 128) * 128

    def own_units(matrix):
        return lax.dynamic_slice_in_dim(matrix, place * shared_units, shared_units, 1)

    def pad_to(matrix, columns):
        return jnp.pad(matrix, ((0, 0), (0, columns - matrix.shape[1])))

    def side_by_side(shared, expert):
        joined = jnp.concatenate([pad_to(own_units(shared), shared_pad), expert[0]], 1)
        return joined

    w_pre = jnp.concatenate(
        [
            pad_to(
                jnp.concatenate(
                    [side_by_side(shared_w_gate, expert_w_gate), w_router, shared_gate[:, None]], 1
                ),
                units_pad,
            ),
            pad_to(side_by_side(shared_w_up, expert_w_up), units_pad),
        ],
        1,
    )
    w_down = pad_to(side_by_side(shared_w_down, expert_w_down), units_pad)

    out_all = gather_dp(out_grad)

    routes_all = lax.all_gather(routes, "dp", axis=0, tiled=True)
    pair_onehot = routes_all[:, :, None] == jnp.arange(experts, dtype=jnp.int32)[None, None, :]
    hits = jnp.any(pair_onehot, 1)
    hit_blocks = hits.astype(bf16).reshape(devices, tok_rows, experts)
    below = (
        jnp.arange(tok_rows)[None, :] < jnp.arange(tok_rows)[:, None]
    ).astype(bf16)
    within = jnp.einsum("ij,bje->bie", below, hit_blocks, preferred_element_type=f32)
    block_sums = jnp.sum(hit_blocks.astype(f32), 1)
    before = jnp.cumsum(block_sums, 0) - block_sums
    slots = (within + before[:, None, :]).reshape(all_rows, experts)
    kept = (hits & (slots < capacity)).astype(f32)

    path = path_of(parents, place * tok_rows // SEG)
    reachable = path >= 0
    path_rows = jnp.maximum(path, 0)
    row_ids = jnp.arange(tok_rows, dtype=jnp.int32)
    depth = jnp.sum(reachable.astype(f32)) - 1.0
    cosine, sine = rope_tables(depth * SEG + row_ids.astype(f32))
    allowed = jnp.concatenate(
        [
            row_ids[:, None] >= row_ids[None, :],
            jnp.broadcast_to(
                jnp.repeat(reachable[1:], tok_rows)[None, :], (tok_rows, (LEVELS - 1) * tok_rows)
            ),
        ],
        1,
    )
    hidden_f = hidden_in.astype(f32)
    attn_scale, attn_unit = norm_parts(hidden_f)
    attn_normed = (attn_unit * attn_gain).astype(bf16)
    query_rot = turn_heads(
        product(attn_normed, w_query) + b_query.reshape(-1), cosine, sine, 1.0
    ).astype(bf16)
    key_rot = turn_heads(
        product(attn_normed, w_key) + b_key.reshape(-1), cosine, sine, 1.0
    ).astype(bf16)
    value_rows = (product(attn_normed, w_value) + b_value.reshape(-1)).astype(bf16)
    gathered = gather_dp(jnp.concatenate([key_rot, value_rows], 1))
    kv_blocks = gathered.reshape(devices, tok_rows, 2 * local_width)
    kv_path = jnp.take(kv_blocks, path_rows, axis=0).reshape(LEVELS * tok_rows, 2 * local_width)
    key_path, value_path = kv_path[:, :local_width], kv_path[:, local_width:]
    attended, log_total = attend_forward(query_rot, key_path, value_path, allowed, score_scale)
    attended_low = attended.astype(bf16)
    attn_part = product_nt(attended_low, w_out).astype(bf16)

    hidden_own = lax.dynamic_slice_in_dim(hidden_in, column * part_rows, part_rows, 0)
    grad_own = lax.dynamic_slice_in_dim(out_grad, column * part_rows, part_rows, 0)
    layout = (shared_units, shared_pad, expert_units, experts, units_pad)
    (
        residual,
        residual_grad,
        residual_low,
        ffn_part,
        grad_expert_gate,
        grad_expert_up,
        grad_expert_down,
        grad_shared,
        grad_side,
        grad_ffn_gain,
    ) = ffn_plain(
        attn_part, hidden_own, grad_own, ffn_gain, kept, out_all, w_pre, w_down, layout
    )
    grad_shared = grad_shared[:, :, :shared_units]
    ffn_own = scatter_all(ffn_part).astype(f32)
    hidden_out = gather_tensor((residual + ffn_own).astype(bf16))
    residual_low = gather_tensor(residual_low)
    grad_out_proj = product_tn(residual_low, attended_low)
    attended_grad = product(residual_low, w_out).astype(bf16)

    query_grad, key_grad, value_grad = attend_backward(
        query_rot, key_path, value_path, allowed, log_total, attended_grad, score_scale
    )
    kv_grad = jnp.concatenate([key_grad, value_grad], 1).reshape(
        LEVELS, tok_rows, 2 * local_width
    )
    kv_all = jnp.zeros((devices, tok_rows, 2 * local_width), f32)
    for level in range(LEVELS):
        kv_all = kv_all.at[path_rows[level]].add(kv_grad[level])
    kv_own = scatter_dp(
        kv_all.reshape(all_rows, 2 * local_width).astype(bf16)
    ).astype(f32)
    query_pre_grad = turn_heads(query_grad, cosine, sine, -1.0).astype(bf16)
    key_pre_grad = turn_heads(kv_own[:, :local_width], cosine, sine, -1.0).astype(bf16)
    value_pre_grad = kv_own[:, local_width:].astype(bf16)
    qkv_pre_grad = jnp.concatenate([query_pre_grad, key_pre_grad, value_pre_grad], 1)
    grad_qkv = product_tn(attn_normed, qkv_pre_grad)
    bias_grads = jnp.sum(qkv_pre_grad.astype(f32), 0).reshape(3, -1, HEAD_DIM)
    attn_part_grad = (
        product_nt(query_pre_grad, w_query)
        + product_nt(key_pre_grad, w_key)
        + product_nt(value_pre_grad, w_value)
    )
    grad_attn_gain = jnp.sum(attn_part_grad * attn_unit, 0)
    attn_own_grad = scatter_tensor(attn_part_grad.astype(bf16)).astype(f32)
    own_rows = lambda array: lax.dynamic_slice_in_dim(
        array, column * part_rows, part_rows, 0
    )
    hidden_in_grad = gather_tensor(
        (
            residual_grad
            + norm_back(attn_own_grad, own_rows(attn_unit), own_rows(attn_scale), attn_gain)
        ).astype(bf16)
    )

    small = jnp.concatenate(
        [grad_side, grad_ffn_gain[:, None], grad_attn_gain[:, None]], 1
    )
    small = scatter_dp(lax.psum(small, "tensor"))
    bias_sums = lax.psum_scatter(bias_grads, "dp", scatter_dimension=2, tiled=True)
    grad_attn = scatter_dp(jnp.concatenate([grad_qkv, grad_out_proj], 1).astype(bf16)).astype(f32)
    shared_grads = lax.all_to_all(
        grad_shared, "dp", split_axis=1, concat_axis=2, tiled=True
    ).astype(f32)
    return (
        hidden_out,
        hidden_in_grad,
        small[:, experts + 2],
        grad_attn[:, :local_width],
        grad_attn[:, local_width : 2 * local_width],
        grad_attn[:, 2 * local_width : 3 * local_width],
        bias_sums[0],
        bias_sums[1],
        bias_sums[2],
        grad_attn[:, 3 * local_width :],
        small[:, experts + 1],
        small[:, :experts],
        small[:, experts],
        shared_grads[0],
        shared_grads[1],
        shared_grads[2],
        grad_expert_gate[None],
        grad_expert_up[None],
        grad_expert_down[None],
    )


def finish_kernel(
    hidden_out_in,
    hidden_grad_in,
    query_in,
    key_in,
    value_in,
    out_in,
    shared_in,
    gate_in,
    up_in,
    down_in,
    small_in,
    hidden_out,
    hidden_grad,
    query_out,
    key_out,
    value_out,
    out_out,
    s_gate_out,
    s_up_out,
    s_down_out,
    gate_out,
    up_out,
    down_out,
    router_out,
    shared_gate_out,
    ffn_gain_out,
    attn_gain_out,
):
    f32 = jnp.float32
    experts = router_out.shape[0]
    hidden_out[...] = hidden_out_in[...]
    hidden_grad[...] = hidden_grad_in[...]
    for source, target in (
        (query_in, query_out),
        (key_in, key_out),
        (value_in, value_out),
        (out_in, out_out),
        (gate_in, gate_out),
        (up_in, up_out),
        (down_in, down_out),
    ):
        target[...] = source[...].astype(f32)

    for which, target in enumerate((s_gate_out, s_up_out, s_down_out)):
        units = shared_in[:, which]
        target[...] = units.reshape(-1, units.shape[-1]).T.astype(f32)

    router_out[...] = small_in[0:experts]
    shared_gate_out[...] = small_in[experts : experts + 1]
    ffn_gain_out[...] = small_in[experts + 1 : experts + 2]
    attn_gain_out[...] = small_in[experts + 2 : experts + 3]


def finish_layer(hidden_out, hidden_grad, grads, shared, expert_grads, small, experts):
    steps = 2
    tok_rows, width = hidden_out.shape
    local_width = grads[0].shape[1]
    units = shared.shape[2]
    expert_units = expert_grads[0].shape[0]
    f32, bf16 = jnp.float32, jnp.bfloat16
    shape = jax.ShapeDtypeStruct
    row = lambda wide: pl.BlockSpec((tok_rows // steps, wide), lambda i: (i, 0))
    column = pl.BlockSpec((expert_units, width // steps), lambda i: (0, i))
    whole = lambda *dims: pl.BlockSpec(dims, lambda i: (0,) * len(dims))
    return pl.pallas_call(
        finish_kernel,
        grid=(steps,),
        in_specs=[row(width)] * 2
        + [row(local_width)] * 4
        + [pl.BlockSpec((8, 3, units, tok_rows // steps), lambda i: (0, 0, 0, i))]
        + [column] * 3
        + [whole(16, tok_rows)],
        out_specs=[row(width)] * 2
        + [row(local_width)] * 4
        + [pl.BlockSpec((tok_rows // steps, 8 * units), lambda i: (i, 0))] * 3
        + [column] * 3
        + [whole(experts, tok_rows)]
        + [whole(1, tok_rows)] * 3,
        out_shape=[shape((tok_rows, width), bf16)] * 2
        + [shape((tok_rows, local_width), f32)] * 4
        + [shape((tok_rows, 8 * units), f32)] * 3
        + [shape((expert_units, width), f32)] * 3
        + [shape((experts, tok_rows), f32)]
        + [shape((1, tok_rows), f32)] * 3,
        compiler_params=pltpu.CompilerParams(vmem_limit_bytes=63 * 2**20),
        cost_estimate=pl.CostEstimate(flops=0, bytes_accessed=26 * 2**20, transcendentals=0),
    )(hidden_out, hidden_grad, *grads, shared, *expert_grads, small)


def on_cube(
    hidden_in,
    out_grad,
    parents,
    routes,
    attn_gain,
    w_query,
    w_key,
    w_value,
    b_query,
    b_key,
    b_value,
    w_out,
    ffn_gain,
    w_router,
    shared_gate,
    shared_w_gate,
    shared_w_up,
    shared_w_down,
    expert_w_gate,
    expert_w_up,
    expert_w_down,
):
    tok_rows, model_width = hidden_in.shape
    devices, columns = lax.axis_size("dp"), lax.axis_size("tensor")
    place = lax.axis_index("dp")
    experts, top_count = w_router.shape[1], routes.shape[1]
    capacity = 5 * tok_rows * top_count // 4
    score_scale = HEAD_DIM ** (-0.5)
    bf16, f32 = jnp.bfloat16, jnp.float32
    expert_units = expert_w_gate.shape[2]
    shared_units = shared_w_gate.shape[1] // devices
    shared_pad = -(-shared_units // 128) * 128
    units = shared_pad + expert_units
    units_pad = -(-(units + experts + 1) // 128) * 128
    layout = (shared_units, shared_pad, expert_units, experts, units_pad)
    part_rows = tok_rows // columns

    side = jnp.pad(
        jnp.concatenate([w_router.T, shared_gate[None, :]], 0), ((0, 16 - experts - 1), (0, 0))
    )
    hits = jnp.any(
        routes.T[:, None, :] == jnp.arange(16, dtype=jnp.int32)[None, :, None], 0
    ).astype(f32)
    freqs = rope_base ** (-jnp.arange(0, HEAD_DIM, 2, dtype=f32) / HEAD_DIM)
    biases = jnp.stack([b_query.reshape(-1), b_key.reshape(-1), b_value.reshape(-1)])
    (
        residual,
        query_rot,
        key_path,
        value_path,
        log_total,
        attended,
        attn_normed,
        cosine,
        sine,
        hits_all,
        grad_all,
        shared_w,
    ) = front_layer(
        score_scale,
        shared_units,
        (
            parents,
            hidden_in,
            attn_gain[None, :],
            biases,
            jnp.concatenate([freqs, freqs])[None, :],
            hits,
            out_grad.reshape(columns, part_rows, model_width),
            w_query,
            w_key,
            w_value,
            w_out,
            shared_w_gate,
            shared_w_up,
            shared_w_down,
        ),
    )
    (
        residual_grad,
        residual_low,
        ffn_part,
        grad_expert_gate,
        grad_expert_up,
        grad_expert_down,
        grad_shared,
        small,
    ) = ffn_layer(
        residual,
        ffn_gain[None, :],
        hits_all,
        grad_all.reshape(2, 2, 2, columns, part_rows, model_width),
        side,
        shared_w,
        (expert_w_gate[0].T, expert_w_up[0].T, expert_w_down[0].T),
        layout,
        capacity,
    )
    (
        hidden_out,
        hidden_in_grad,
        sum_query,
        sum_key,
        sum_value,
        sum_out,
        grad_shared,
        small,
        bias_sums,
    ) = back_layer(
        score_scale,
        experts + 2,
        (
            residual,
            residual_grad,
            residual_low,
            ffn_part,
            grad_shared,
            small,
            query_rot,
            key_path,
            value_path,
            parents,
            log_total,
            attended,
            attn_normed,
            hidden_in,
            attn_gain[None, :],
            cosine,
            sine,
            w_out,
            w_query,
            w_key,
            w_value,
        ),
    )
    bias_sums = lax.dynamic_slice_in_dim(
        bias_sums[: 3 * b_query.shape[0]].reshape(3, *b_query.shape),
        place * (HEAD_DIM // devices),
        HEAD_DIM // devices,
        2,
    )
    (
        hidden_out,
        hidden_in_grad,
        sum_query,
        sum_key,
        sum_value,
        sum_out,
        sum_s_gate,
        sum_s_up,
        sum_s_down,
        grad_expert_gate,
        grad_expert_up,
        grad_expert_down,
        sum_router,
        sum_shared_gate,
        sum_ffn_gain,
        sum_attn_gain,
    ) = finish_layer(
        hidden_out.reshape(tok_rows, model_width),
        hidden_in_grad.reshape(tok_rows, model_width),
        (sum_query, sum_key, sum_value, sum_out),
        grad_shared,
        (grad_expert_gate, grad_expert_up, grad_expert_down),
        small,
        experts,
    )
    return (
        hidden_out,
        hidden_in_grad,
        sum_attn_gain[0],
        sum_query,
        sum_key,
        sum_value,
        bias_sums[0],
        bias_sums[1],
        bias_sums[2],
        sum_out,
        sum_ffn_gain[0],
        sum_router.T,
        sum_shared_gate[0],
        sum_s_gate,
        sum_s_up,
        sum_s_down,
        grad_expert_gate.T[None],
        grad_expert_up.T[None],
        grad_expert_down.T[None],
    )


def on_device(*arrays):
    devices, columns = lax.axis_size("dp"), lax.axis_size("tensor")
    tok_rows, model_width = arrays[0].shape
    cube = devices == 8 and columns == 4 and tok_rows == SEG
    if cube and tok_rows * devices * model_width <= 2**22:
        return on_cube(*arrays)
    return on_slice(*arrays)


def solution(mesh):
    return jax.shard_map(
        on_device,
        mesh=mesh,
        in_specs=(
            P("dp", None),
            P("dp", None),
            P(),
            P("dp", None),
            P(),
            P(None, "tensor"),
            P(None, "tensor"),
            P(None, "tensor"),
            P("tensor", None),
            P("tensor", None),
            P("tensor", None),
            P(None, "tensor"),
            P(),
            P(),
            P(),
            P(None, "tensor"),
            P(None, "tensor"),
            P(None, "tensor"),
            P("dp", None, "tensor"),
            P("dp", None, "tensor"),
            P("dp", None, "tensor"),
        ),
        out_specs=(
            P("dp", None),
            P("dp", None),
            P("dp"),
            P("dp", "tensor"),
            P("dp", "tensor"),
            P("dp", "tensor"),
            P("tensor", "dp"),
            P("tensor", "dp"),
            P("tensor", "dp"),
            P("dp", "tensor"),
            P("dp"),
            P("dp", None),
            P("dp"),
            P("dp", "tensor"),
            P("dp", "tensor"),
            P("dp", "tensor"),
            P("dp", None, "tensor"),
            P("dp", None, "tensor"),
            P("dp", None, "tensor"),
        ),
        check_vma=False,
    )
```

```python
import functools

import jax
import jax.numpy as jnp
import numpy as np
from jax import lax
from jax.experimental import pallas as pl
from jax.experimental.pallas import tpu as pltpu
from jax.sharding import PartitionSpec as P

HEAD_DIM = 128
SEG = 256
MESH = pl.DeviceIdType.MESH


epsilon = 1e-06
rope_base = 1000000.0
highest = lax.Precision.HIGHEST


def product(left, right):
    return jnp.dot(left, right, preferred_element_type=jnp.float32)


def product_tn(left, right):
    return lax.dot_general(
        left, right, (((0,), (0,)), ((), ())), preferred_element_type=jnp.float32
    )


def product_nt(left, right):
    return lax.dot_general(
        left, right, (((1,), (1,)), ((), ())), preferred_element_type=jnp.float32
    )


def ancestry(parents):
    seg_count = parents.shape[0]
    labels = jnp.arange(seg_count, dtype=jnp.int32)

    def climb(level, carry):
        current, reach = carry
        upward = jnp.where(current >= 0, parents[jnp.maximum(current, 0)], -1)
        reach = jnp.maximum(reach, (upward[:, None] == labels[None, :]).astype(jnp.float32))
        return (upward, reach)

    start = (labels, jnp.eye(seg_count, dtype=jnp.float32))
    return lax.fori_loop(0, seg_count, climb, start)[1]


def rope_tables(positions):
    freqs = rope_base ** (-jnp.arange(0, HEAD_DIM, 2, dtype=jnp.float32) / HEAD_DIM)
    angles = positions[:, None] * freqs[None, :]
    angles = jnp.concatenate([angles, angles], 1)
    return (jnp.cos(angles)[:, None, :], jnp.sin(angles)[:, None, :])


def turn_heads(matrix, cosine, sine, sign_value):
    shaped = matrix.reshape(matrix.shape[0], matrix.shape[1] // HEAD_DIM, HEAD_DIM)
    half = HEAD_DIM // 2
    turned = jnp.concatenate([-shaped[..., half:], shaped[..., :half]], -1)
    return (shaped * cosine + sign_value * turned * sine).reshape(matrix.shape)


def norm_parts(values):
    scale_rows = lax.rsqrt(jnp.mean(values * values, 1, keepdims=True) + epsilon)
    return (scale_rows, values * scale_rows)


def norm_back(grad_rows, unit_rows, scale_rows, gain):
    unit_grad = grad_rows * gain
    return scale_rows * (unit_grad - unit_rows * jnp.mean(unit_grad * unit_rows, 1, keepdims=True))


LEVELS = 4


def gather_dp(rows):
    return lax.all_gather(rows, "dp", axis=0, tiled=True)


def gather_tensor(rows):
    return lax.all_gather(rows, "tensor", axis=0, tiled=True)


def gather_all(rows):
    return gather_dp(gather_tensor(rows))


def scatter_dp(rows):
    return lax.psum_scatter(rows, "dp", scatter_dimension=0, tiled=True)


def scatter_tensor(rows):
    return lax.psum_scatter(rows, "tensor", scatter_dimension=0, tiled=True)


def scatter_all(rows):
    return scatter_tensor(scatter_dp(rows))


def path_of(parents, segment):
    path = [segment]
    for _ in range(LEVELS - 1):
        last = path[-1]
        path.append(jnp.where(last >= 0, parents[jnp.maximum(last, 0)], -1))
    return jnp.stack(path)


def heads_of(matrix):
    return matrix.reshape(matrix.shape[0], -1, HEAD_DIM)


def attend_forward(query_rot, key_path, value_path, allowed, score_scale):
    scores = (
        jnp.einsum(
            "qhd,khd->hqk",
            heads_of(query_rot),
            heads_of(key_path),
            preferred_element_type=jnp.float32,
        )
        * score_scale
    )
    scores = jnp.where(allowed[None], scores, -jnp.inf)
    peak = jnp.max(scores, 2, keepdims=True)
    log_total = peak + jnp.log(jnp.sum(jnp.exp(scores - peak), 2, keepdims=True))
    weights = jnp.exp(scores - log_total).astype(jnp.bfloat16)
    attended = jnp.einsum(
        "hqk,khd->qhd", weights, heads_of(value_path), preferred_element_type=jnp.float32
    )
    return attended.reshape(query_rot.shape), log_total


def attend_backward(
    query_rot, key_path, value_path, allowed, log_total, attended_grad, score_scale
):
    query, key, value = heads_of(query_rot), heads_of(key_path), heads_of(value_path)
    grad = heads_of(attended_grad)
    scores = jnp.einsum("qhd,khd->hqk", query, key, preferred_element_type=jnp.float32)
    weights = jnp.exp(jnp.where(allowed[None], scores * score_scale, -jnp.inf) - log_total)
    weight_grad = jnp.einsum("qhd,khd->hqk", grad, value, preferred_element_type=jnp.float32)
    center = jnp.sum(weights * weight_grad, 2, keepdims=True)
    score_grad = (weights * (weight_grad - center)).astype(jnp.bfloat16)
    query_grad = (
        jnp.einsum("hqk,khd->qhd", score_grad, key, preferred_element_type=jnp.float32)
        * score_scale
    )
    key_grad = (
        jnp.einsum("hqk,qhd->khd", score_grad, query, preferred_element_type=jnp.float32)
        * score_scale
    )
    value_grad = jnp.einsum(
        "hqk,qhd->khd",
        weights.astype(jnp.bfloat16),
        grad,
        preferred_element_type=jnp.float32,
    )
    return (
        query_grad.reshape(query_rot.shape),
        key_grad.reshape(key_path.shape),
        value_grad.reshape(value_path.shape),
    )


def ffn_plain(attn_part, hidden_own, grad_own, ffn_gain, kept, out_all, w_pre, w_down, layout):
    _, shared_pad, expert_units, experts, units_pad = layout
    units = shared_pad + expert_units
    bf16, f32 = jnp.bfloat16, jnp.float32
    place, column = lax.axis_index("dp"), lax.axis_index("tensor")
    columns, part_rows = lax.axis_size("tensor"), hidden_own.shape[0]
    out_own = grad_own.astype(f32)
    residual = hidden_own.astype(f32) + scatter_tensor(attn_part).astype(f32)
    ffn_scale, ffn_unit = norm_parts(residual)
    ffn_normed = (ffn_unit * ffn_gain).astype(bf16)
    normed_all = gather_all(ffn_normed)

    pre = product(normed_all, w_pre)
    pre_gate, pre_up = pre[:, :units_pad], pre[:, units_pad:]
    logits = pre[:, units : units + experts]
    probs = jax.nn.softmax(logits, 1)
    shared_weight = jax.nn.sigmoid(pre[:, units + experts])
    own_expert = jnp.arange(experts, dtype=jnp.int32)[None, :] == place
    gate_own = jnp.sum(jnp.where(own_expert, probs * kept, 0.0), 1)
    lane = jnp.arange(units_pad)[None, :]
    weight = jnp.where(
        lane < shared_pad,
        shared_weight[:, None],
        jnp.where(lane < units, gate_own[:, None], 0.0),
    )
    down_back = product(out_all, w_down)
    sigmoid_gate = jax.nn.sigmoid(pre_gate)
    hidden = (pre_gate * sigmoid_gate * pre_up).astype(bf16).astype(f32)
    hidden_scaled = (hidden * weight).astype(bf16)
    hidden_grad = down_back * weight
    up_rows = (hidden_grad * pre_gate * sigmoid_gate).astype(bf16)
    gate_rows = (
        hidden_grad * pre_up * sigmoid_gate * (1.0 + pre_gate * (1.0 - sigmoid_gate))
    ).astype(bf16)
    both_rows = jnp.concatenate([gate_rows, up_rows], 1)
    dots = hidden * down_back
    gate_dot = jnp.sum(jnp.where((lane >= shared_pad) & (lane < units), dots, 0.0), 1)
    shared_dot = jnp.sum(jnp.where(lane < shared_pad, dots, 0.0), 1)
    dot_parts = jnp.concatenate(
        [jnp.where(own_expert, gate_dot[:, None] * kept, 0.0), shared_dot[:, None]], 1
    )
    ffn_part = product_nt(hidden_scaled, w_down).astype(bf16)
    normed_part = product_nt(both_rows, w_pre).astype(bf16)
    grad_pre = product_tn(normed_all, both_rows)
    grad_down = product_tn(out_all, hidden_scaled)

    dot_own = scatter_all(dot_parts)
    normed_own = scatter_all(normed_part).astype(f32)

    first = (place * columns + column) * part_rows
    own = lambda array: lax.dynamic_slice_in_dim(array, first, part_rows, 0)
    probs_own, shared_own = own(probs), own(shared_weight)
    prob_grad = dot_own[:, :experts]
    logit_grad = (
        probs_own * (prob_grad - jnp.sum(probs_own * prob_grad, 1, keepdims=True))
    ).astype(bf16)
    weight_logit_grad = (dot_own[:, experts] * shared_own * (1.0 - shared_own)).astype(bf16)
    side_grad = jnp.concatenate([logit_grad, weight_logit_grad[:, None]], 1)
    side_w = w_pre[:, units : units + experts + 1]
    normed_grad = normed_own + product_nt(side_grad, side_w)
    grad_side = product_tn(ffn_normed, side_grad)
    grad_ffn_gain = jnp.sum(normed_grad * ffn_unit, 0)
    residual_grad = out_own + norm_back(normed_grad, ffn_unit, ffn_scale, ffn_gain)
    expert = slice(shared_pad, units)
    expert_up = slice(units_pad + shared_pad, units_pad + units)
    grad_shared = jnp.stack(
        [
            grad_pre[:, : shared_pad],
            grad_pre[:, units_pad : units_pad + shared_pad],
            grad_down[:, : shared_pad],
        ]
    ).astype(bf16)
    return (
        residual,
        residual_grad,
        residual_grad.astype(bf16),
        ffn_part,
        grad_pre[:, expert],
        grad_pre[:, expert_up],
        grad_down[:, expert],
        grad_shared,
        grad_side,
        grad_ffn_gain,
    )


def flip(bit):
    return 1 - bit


def other(index, step):
    result, place = index, 1
    while place <= step:
        if step & place:
            result = result + place - 2 * place * ((index // place) % 2)
        place *= 2
    return result


def ffn_kernel(
    units,
    residual_ref,
    gain_ref,
    hits_ref,
    grad_all_ref,
    router_ref,
    shared_gate_ref,
    shared_w_ref,
    e_gate_w_ref,
    e_up_w_ref,
    e_down_w_ref,
    res_grad_ref,
    res_low_ref,
    ffn_part_ref,
    e_gate_ref,
    e_up_ref,
    e_down_ref,
    shared_ref,
    small_ref,
    rows_all,
    dy_all,
    w_pre,
    w_down,
    both_all,
    scaled_all,
    scaled_now,
    down_back_all,
    sums,
    got_core,
    got_x1,
    got_y1,
    got_y2,
    got_x2,
    got_z,
    kept_ref,
    out_send,
    out_own,
    got_out,
    tile_gate,
    tile_up,
    tile_down,
    tile_shared,
    load_sems,
    store_sems,
    tile_sems,
    zs,
    links,
    cores,
    rs_core,
    rs_links,
    rs_z,
    rs_out,
):
    shared_units, shared_pad, expert_units, experts, unit_pad, half, wide, capacity = units
    bf16, f32 = jnp.bfloat16, jnp.float32
    place, column = lax.axis_index("dp"), lax.axis_index("tensor")
    core, east, north = place % 2, (place // 2) % 2, place // 4
    rows, width = residual_ref.shape
    sibling = {"dp": other(place, 1)}
    x_side = {"dp": other(place, 2)}
    y_side = {"dp": other(place, 4)}
    levels = [{"tensor": other(column, k)} for k in range(4)]

    def level_of(k):
        low_i, high_i, low_k, high_k = column % 2, column // 2, k % 2, k // 2
        return (low_i + low_k - 2 * low_i * low_k) + 2 * (high_i + high_k - 2 * high_i * high_k)

    def remote(src, dst, sems, which, device):
        return pltpu.make_async_remote_copy(
            src_ref=src,
            dst_ref=dst,
            send_sem=sems.at[(0, *which)],
            recv_sem=sems.at[(1, *which)],
            device_id=device,
            device_id_type=MESH,
        )

    expert_first, side_first = shared_pad, shared_pad + expert_units
    loads = []
    for j, (target, first, ref) in enumerate(
        ((w_pre, 0, e_gate_w_ref), (w_pre, unit_pad, e_up_w_ref), (w_down, 0, e_down_w_ref))
    ):
        own_rows = pl.ds(first + expert_first, expert_units)
        shared_rows = pl.ds(first, shared_units)
        loads += [
            pltpu.make_async_copy(ref, target.at[own_rows], load_sems.at[8 + 2 * j]),
            pltpu.make_async_copy(
                shared_w_ref.at[j], target.at[shared_rows], load_sems.at[9 + 2 * j]
            ),
        ]
    for copy in loads:
        copy.start()
    for target, first in ((w_pre, 0), (w_pre, unit_pad), (w_down, 0)):
        gap = shared_pad - shared_units
        target[first + shared_units : first + shared_pad, :] = jnp.zeros((gap, width), bf16)
        rest = unit_pad - side_first
        target[first + side_first : first + unit_pad, :] = jnp.zeros((rest, width), bf16)
    side_rows = [router_ref[...].astype(f32), shared_gate_ref[...].astype(f32)]
    side_rows.append(jnp.zeros((16 - experts - 1, width), f32))
    w_pre[side_first : side_first + 16, :] = jnp.concatenate(side_rows, 0).astype(bf16)

    def load_grad(c, z):
        return pltpu.make_async_copy(
            grad_all_ref.at[:, :, c, z], dy_all.at[z, c], load_sems.at[c * 4 + z]
        )

    for c in range(2):
        for z in range(4):
            load_grad(c, z).start()

    barrier = pltpu.get_barrier_semaphore()
    partners = [sibling, x_side, y_side] + levels[1:]
    for partner in partners:
        pl.semaphore_signal(barrier, inc=1, device_id=partner, device_id_type=MESH)
    pl.semaphore_wait(barrier, len(partners))

    residual = residual_ref[...]
    scale_rows = lax.rsqrt(jnp.mean(residual * residual, 1, keepdims=True) + epsilon)
    normed = (residual * scale_rows * gain_ref[...]).astype(bf16)
    rows_all[column, core, north, east] = normed

    own_slot = rows_all.at[column, core, north, east]

    def z_copy(k):
        return remote(own_slot, own_slot, zs, (k,), levels[k])

    def block(k, c, y, x, cols=slice(None)):
        return rows_all.at[level_of(k), c, y, x, :, cols]

    first_half, second_half = pl.ds(0, half), pl.ds(half, width - half)

    def direct_copies(k):
        own = block(k, core, north, east)
        return [
            remote(own, own, links, (0, k), x_side),
            remote(own, own, links, (1, k), y_side),
            remote(own, own, cores, (0, k), sibling),
        ]

    def forward_copies(k):
        from_x = block(k, core, north, flip(east), first_half)
        from_y = block(k, core, flip(north), east, second_half)
        all_x = block(k, core, north, flip(east))
        all_y = block(k, core, flip(north), east)
        return [
            remote(from_x, from_x, links, (2, k), y_side),
            remote(from_y, from_y, links, (3, k), x_side),
            remote(all_x, all_x, cores, (1, k), sibling),
            remote(all_y, all_y, cores, (2, k), sibling),
        ]

    def corner_copy(k):
        corner = block(k, core, flip(north), flip(east))
        return remote(corner, corner, cores, (3, k), sibling)

    def start_direct(k):
        for copy in direct_copies(k):
            copy.start()

    def start_forward(k):
        for copy in direct_copies(k)[:2]:
            copy.wait_recv()
        for copy in forward_copies(k):
            copy.start()

    def start_corner(k):
        for copy in forward_copies(k)[:2]:
            copy.wait_recv()
        corner_copy(k).start()

    def finish_gather(k):
        direct_copies(k)[2].wait_recv()
        for copy in forward_copies(k)[2:]:
            copy.wait_recv()
        corner_copy(k).wait_recv()

    def core_copy(k):
        return remote(sums.at[k, flip(core)], got_core.at[k % 2], rs_core, (k,), sibling)

    left, right = pl.ds(0, half), pl.ds(half, wide - half)

    def first_copies(k):
        return [
            remote(
                sums.at[k, core, :, flip(east), :, left],
                got_x1.at[k % 2],
                rs_links, (0, k),
                x_side,
            ),
            remote(
                sums.at[k, core, flip(north), :, :, right],
                got_y1.at[k % 2],
                rs_links, (1, k),
                y_side,
            ),
        ]

    def second_copies(k):
        return [
            remote(
                sums.at[k, core, flip(north), east, :, left],
                got_y2.at[k % 2],
                rs_links, (2, k),
                y_side,
            ),
            remote(
                sums.at[k, core, north, flip(east), :, right],
                got_x2.at[k % 2],
                rs_links, (3, k),
                x_side,
            ),
        ]

    def level_copy(k, device):
        return remote(sums.at[k, core, north, east], got_z.at[k], rs_z, (k,), device)

    def add(ref, value):
        ref[...] = (ref[...].astype(f32) + value.astype(f32)).astype(bf16)

    def after_core(k):
        core_copy(k).wait_recv()
        for y in range(2):
            for x in range(2):
                add(sums.at[k, core, y, x], got_core[k % 2, y, x])
        for copy in first_copies(k):
            copy.start()

    def after_first(k):
        x_copy, y_copy = first_copies(k)
        x_copy.wait_recv()
        for y in range(2):
            add(sums.at[k, core, y, east, :, left], got_x1[k % 2, y])
        y_copy.wait_recv()
        for x in range(2):
            add(sums.at[k, core, north, x, :, right], got_y1[k % 2, x])
        for copy in second_copies(k):
            copy.start()

    def after_second(k):
        y_copy, x_copy = second_copies(k)
        y_copy.wait_recv()
        add(sums.at[k, core, north, east, :, left], got_y2[k % 2])
        x_copy.wait_recv()
        add(sums.at[k, core, north, east, :, right], got_x2[k % 2])
        for level in range(1, 4):

            @pl.when(k == level)
            def _():
                level_copy(k, levels[level]).start()

    for k in (1, 2, 3):
        z_copy(k).start()
    start_direct(0)

    tokens_dev = 4 * rows
    expert_id = lax.broadcasted_iota(jnp.int32, hits_ref.shape, 1)
    hits = jnp.sum(jnp.where(expert_id == place, hits_ref[...], 0.0), 1)
    earlier = lax.broadcasted_iota(jnp.int32, (tokens_dev, tokens_dev), 0)
    later = lax.broadcasted_iota(jnp.int32, (tokens_dev, tokens_dev), 1)
    slots = product(hits.astype(bf16), (earlier < later).astype(bf16))
    counts = jnp.sum(hits, 1, keepdims=True)
    counts_wide = jnp.broadcast_to(counts, (8, 128))
    order_row = lax.broadcasted_iota(jnp.int32, (8, 8), 0)
    order_col = lax.broadcasted_iota(jnp.int32, (8, 8), 1)
    before = lax.dot_general(
        (order_col < order_row).astype(f32),
        counts_wide,
        (((1,), (0,)), ((), ())),
        precision=highest,
        preferred_element_type=f32,
    )
    kept = jnp.where(slots + before[:, :1] < capacity, hits, 0.0).astype(bf16)
    eye = (
        lax.broadcasted_iota(jnp.int32, (8, 128), 0)
        == lax.broadcasted_iota(jnp.int32, (8, 128), 1)
    ).astype(bf16)
    kept_columns = product_tn(kept, eye)
    for d in range(8):
        y, x, c = d // 4, (d // 2) % 2, d % 2
        for z in range(4):
            first = (2 * y + x) * rows
            kept_ref[z, c, first : first + rows, :] = kept_columns[
                z * rows : (z + 1) * rows, d : d + 1
            ]

    for copy in loads:
        copy.wait()
    for c in range(2):
        for z in range(4):
            load_grad(c, z).wait()

    def back_down(i, carry):
        z, c = i // 2, i % 2
        dy_block = dy_all[z, c].reshape(4 * rows, width)
        down_back_all[z, c] = product_nt(dy_block, w_down[...]).astype(bf16)
        return carry

    lax.fori_loop(0, 3, back_down, 0)
    start_forward(0)
    z_copy(1).wait_recv()
    start_direct(1)
    lax.fori_loop(3, 5, back_down, 0)
    start_corner(0)
    lax.fori_loop(5, 8, back_down, 0)

    last = unit_pad - 128
    lane = lax.broadcasted_iota(jnp.int32, (1, 128), 1)
    first_lane = shared_pad + expert_units - last
    in_router = (lane >= first_lane) & (lane < first_lane + experts)
    is_shared = lane == first_lane + experts

    def routing(logit_block):
        top = jnp.max(jnp.where(in_router, logit_block, -jnp.inf), 1, keepdims=True)
        powers = jnp.where(in_router, jnp.exp(jnp.where(in_router, logit_block - top, 0.0)), 0.0)
        probs = powers / jnp.sum(powers, 1, keepdims=True)
        shared_logit = jnp.sum(jnp.where(is_shared, logit_block, 0.0), 1, keepdims=True)
        return probs, jax.nn.sigmoid(shared_logit)

    def compute(k, c):
        z = level_of(k)
        row_block = rows_all[z, c].reshape(4 * rows, width)
        pre_gate = product_nt(row_block, w_pre[:unit_pad])
        pre_up = product_nt(row_block, w_pre[unit_pad:])
        down_back = down_back_all[z, c].astype(f32)
        probs, shared_weight = routing(pre_gate[:, last:])
        kept = kept_ref[z, c]
        gate = (
            jnp.sum(jnp.where(lane == first_lane + place, probs, 0.0), 1, keepdims=True) * kept
        )
        dots, scaled, gate_rows, up_rows = [], [], [], []
        for begin, end, weight in (
            (0, shared_pad, shared_weight),
            (shared_pad, unit_pad, gate),
        ):
            cols = slice(begin, end)
            a, b, back = pre_gate[:, cols], pre_up[:, cols], down_back[:, cols]
            sig = jax.nn.sigmoid(a)
            silu = a * sig
            hidden = (silu * b).astype(bf16).astype(f32)
            dots.append(jnp.sum(hidden * back, 1, keepdims=True))
            scaled.append((hidden * weight).astype(bf16))
            grad = back * weight
            up_rows.append((grad * silu).astype(bf16))
            gate_rows.append((grad * b * sig * (1.0 + a * (1.0 - sig))).astype(bf16))
        both = jnp.concatenate(gate_rows + up_rows, 1)
        own_scaled = jnp.concatenate(scaled, 1)
        first_token = pl.multiple_of((2 * z + c) * 4 * rows, 4 * rows)
        both_all[:, pl.ds(first_token, 4 * rows)] = both.T
        scaled_all[:, pl.ds(first_token, 4 * rows)] = own_scaled.T
        scaled_now[c] = own_scaled
        dot_block = jnp.where(is_shared, dots[0], 0.0) + jnp.where(
            lane == first_lane + place, dots[1] * kept, 0.0
        )
        normed_grad = product(both, w_pre[...]).astype(bf16)
        sums[k, c, :, :, :, 0:width] = normed_grad.reshape(2, 2, rows, width)
        sums[k, c, :, :, :, width:wide] = dot_block.astype(bf16).reshape(2, 2, rows, wide - width)

    def store_chunk(k):
        return pltpu.make_async_copy(out_own, ffn_part_ref.at[level_of(k)], store_sems.at[0])

    def out_core_copy(k):
        return remote(out_send, got_out.at[k % 2], rs_out, (k,), sibling)

    def chunk(k, carry):
        @pl.when(k < 3)
        def _():
            start_forward(k + 1)

        @pl.when(k < 2)
        def _():
            for level in (2, 3):

                @pl.when(k + 2 == level)
                def _():
                    z_copy(level).wait_recv()

            start_direct(k + 2)

        finish_gather(k)
        def rows_of(i, carry):
            compute(k, (i + 1 + core) % 2)

            @pl.when(i == 0)
            def _():
                core_copy(k).start()

            return carry

        lax.fori_loop(0, 2, rows_of, 0)

        @pl.when(k >= 1)
        def _():
            after_first(k - 1)
            store_chunk(k - 1).wait()
            out_core_copy(k - 1).wait_send()

        def outputs(i, carry):
            part = product(scaled_now[(i + 1 + core) % 2], w_down[...]).astype(bf16)

            @pl.when(i == 0)
            def _():
                out_send[...] = part.reshape(2, 2, rows, width)
                out_core_copy(k).start()

            @pl.when(i == 1)
            def _():
                out_own[...] = part.reshape(2, 2, rows, width)

            return carry

        lax.fori_loop(0, 2, outputs, 0)

        @pl.when(k < 3)
        def _():
            start_corner(k + 1)

        after_core(k)
        out_core_copy(k).wait_recv()
        for y in range(2):
            for x in range(2):
                add(out_own.at[y, x], got_out[k % 2, y, x])
        store_chunk(k).start()

        @pl.when(k >= 1)
        def _():
            after_second(k - 1)

        return carry

    lax.fori_loop(0, 4, chunk, 0)
    store_chunk(3).wait()
    out_core_copy(3).wait_send()

    tile = tile_gate.shape[2]
    tiles = width // tile

    def tile_copies(i, slot):
        window = pl.ds(pl.multiple_of(i * tile, tile), tile)
        return [
            pltpu.make_async_copy(tile_gate.at[slot], e_gate_ref.at[:, window], tile_sems.at[slot, 0]),
            pltpu.make_async_copy(tile_up.at[slot], e_up_ref.at[:, window], tile_sems.at[slot, 1]),
            pltpu.make_async_copy(tile_down.at[slot], e_down_ref.at[:, window], tile_sems.at[slot, 2]),
            pltpu.make_async_copy(
                tile_shared.at[slot], shared_ref.at[i], tile_sems.at[slot, 3]
            ),
        ]

    tokens = rows * 32

    def weight_tile(i, carry):
        slot = i % 2

        @pl.when(i >= 2)
        def _():
            for copy in tile_copies(i - 2, slot):
                copy.wait()

        window = pl.ds(pl.multiple_of(i * tile, tile), tile)
        expert = slice(shared_pad, shared_pad + expert_units)
        row_tile = rows_all[:, :, :, :, :, window].reshape(tokens, tile)
        for j, (first, target) in enumerate(((0, tile_gate), (unit_pad, tile_up))):
            grad = product(both_all[first : first + unit_pad], row_tile).astype(bf16)
            target[slot] = grad[expert]
            tile_shared[slot, j] = grad[:shared_units]
        dy_tile = dy_all[:, :, :, :, :, window].reshape(tokens, tile)
        grad = product(scaled_all[...], dy_tile).astype(bf16)
        tile_down[slot] = grad[expert]
        tile_shared[slot, 2] = grad[:shared_units]
        for copy in tile_copies(i, slot):
            copy.start()

        @pl.when(i == 1)
        def _():
            after_first(3)

        @pl.when(i == 3)
        def _():
            after_second(3)

        return carry

    lax.fori_loop(0, tiles, weight_tile, 0)
    for i in (tiles - 2, tiles - 1):
        for copy in tile_copies(i, i % 2):
            copy.wait()

    total = sums[0, core, north, east].astype(f32)
    for k in (1, 2, 3):
        level_copy(k, levels[k]).wait_recv()
        total = total + got_z[k].astype(f32)
    dots = total[:, width:]
    unit = residual_ref[...] * scale_rows
    own_normed = rows_all[column, core, north, east]
    side_w = w_pre[last:unit_pad]
    probs, shared_weight = routing(product_nt(own_normed, side_w))
    router_dots = jnp.where(in_router, dots, 0.0)
    center = jnp.sum(probs * router_dots, 1, keepdims=True)
    side = jnp.where(in_router, probs * (router_dots - center), 0.0) + jnp.where(
        is_shared, dots * shared_weight * (1.0 - shared_weight), 0.0
    )
    side = side.astype(bf16)
    normed_grad = total[:, :width] + product(side, side_w)
    side_rows = product_tn(side, own_normed)
    small_ref[...] = side_rows[first_lane : first_lane + small_ref.shape[0]]
    small_ref[experts + 1 : experts + 2, :] = jnp.sum(normed_grad * unit, 0, keepdims=True)
    own_grad = dy_all[column, core, north, east].astype(f32)
    grad_f = own_grad + norm_back(normed_grad, unit, scale_rows, gain_ref[...])
    res_grad_ref[...] = grad_f
    res_low_ref[...] = grad_f.astype(bf16)

    for k in (1, 2, 3):
        z_copy(k).wait_send()
        level_copy(k, levels[k]).wait_send()
    for k in range(4):
        for copy in direct_copies(k) + forward_copies(k) + [corner_copy(k), core_copy(k)]:
            copy.wait_send()
        for copy in first_copies(k) + second_copies(k):
            copy.wait_send()


def ffn_layer(
    residual, ffn_gain, hits, grad_all, router, shared_gate, shared_w, expert_w, layout, capacity
):
    shared_units, shared_pad, expert_units, experts, unit_pad = layout
    rows, width = residual.shape
    bf16, f32 = jnp.bfloat16, jnp.float32
    half = width // 2
    wide = width + 128
    tile = 256
    shape = jax.ShapeDtypeStruct
    vmem, anywhere = pl.BlockSpec(memory_space=pltpu.VMEM), pl.BlockSpec(memory_space=pl.ANY)
    dma = pltpu.SemaphoreType.DMA
    cost = pl.CostEstimate(
        flops=2 * 24 * 2048 * 2048 * 256, bytes_accessed=60 * 2**20, transcendentals=3 * 2**20
    )
    return pl.pallas_call(
        functools.partial(
            ffn_kernel,
            (shared_units, shared_pad, expert_units, experts, unit_pad, half, wide, capacity),
        ),
        out_shape=[
            shape((rows, width), f32),
            shape((rows, width), bf16),
            shape((4, 2, 2, rows, width), bf16),
            shape((expert_units, width), bf16),
            shape((expert_units, width), bf16),
            shape((expert_units, width), bf16),
            shape((width // tile, 3, shared_units, tile), bf16),
            shape((16, width), f32),
        ],
        in_specs=[vmem, vmem, vmem, anywhere, vmem, vmem] + [anywhere] * 4,
        out_specs=[vmem, vmem] + [anywhere] * 5 + [vmem],
        scratch_shapes=[
            pltpu.VMEM((4, 2, 2, 2, rows, width), bf16),
            pltpu.VMEM((4, 2, 2, 2, rows, width), bf16),
            pltpu.VMEM((2 * unit_pad, width), bf16),
            pltpu.VMEM((unit_pad, width), bf16),
            pltpu.VMEM((2 * unit_pad, 32 * rows), bf16),
            pltpu.VMEM((unit_pad, 32 * rows), bf16),
            pltpu.VMEM((2, 4 * rows, unit_pad), bf16),
            pltpu.VMEM((4, 2, 4 * rows, unit_pad), bf16),
            pltpu.VMEM((4, 2, 2, 2, rows, wide), bf16),
            pltpu.VMEM((2, 2, 2, rows, wide), bf16),
            pltpu.VMEM((2, 2, rows, half), bf16),
            pltpu.VMEM((2, 2, rows, wide - half), bf16),
            pltpu.VMEM((2, rows, half), bf16),
            pltpu.VMEM((2, rows, wide - half), bf16),
            pltpu.VMEM((4, rows, wide), bf16),
            pltpu.VMEM((4, 2, 4 * rows, 1), f32),
            pltpu.VMEM((2, 2, rows, width), bf16),
            pltpu.VMEM((2, 2, rows, width), bf16),
            pltpu.VMEM((2, 2, 2, rows, width), bf16),
            pltpu.VMEM((2, expert_units, tile), bf16),
            pltpu.VMEM((2, expert_units, tile), bf16),
            pltpu.VMEM((2, expert_units, tile), bf16),
            pltpu.VMEM((2, 3, shared_units, tile), bf16),
            dma((14,)),
            dma((2,)),
            dma((2, 4)),
            dma((2, 4)),
            dma((2, 4, 4)),
            dma((2, 4, 4)),
            dma((2, 4)),
            dma((2, 4, 4)),
            dma((2, 4)),
            dma((2, 4)),
        ],
        compiler_params=pltpu.CompilerParams(
            collective_id=0, has_side_effects=True, vmem_limit_bytes=63 * 2**20
        ),
        cost_estimate=cost,
    )(residual, ffn_gain, hits, grad_all, router, shared_gate, shared_w, *expert_w)


def path_scalars(parents_ref, segment):
    path = [segment]
    for _ in range(LEVELS - 1):
        last = path[-1]
        parent = parents_ref[jnp.maximum(last, 0)]
        path.append(jnp.where(last >= 0, parent, -1))
    return path


class Line:
    def __init__(self, sems):
        self.sems = sems
        self.column = lax.axis_index("tensor")
        self.levels = [{"tensor": other(self.column, k)} for k in range(4)]
        self.outer = (self.column % 3) == 0
        self.inner = (self.column % 3) != 0

    def remote(self, src, dst, send, receive, device):
        return pltpu.make_async_remote_copy(
            src_ref=src,
            dst_ref=dst,
            send_sem=self.sems.at[0, send],
            recv_sem=self.sems.at[1, receive],
            device_id=device,
            device_id_type=MESH,
        )


class LineGather(Line):
    def __init__(self, slot, sems):
        super().__init__(sems)
        self.slot = slot

    def own(self, k):
        ref = self.slot(self.column)
        return self.remote(ref, ref, k, k, self.levels[k])

    def passed(self):
        ref = self.slot(other(self.column, 2))
        return self.remote(ref, ref, 0, 3, self.levels[1])

    def start(self):
        self.own(2).start()
        self.own(1).start()

        @pl.when(self.inner)
        def _():
            self.own(3).start()

    def forward(self):
        self.own(2).wait_recv()

        @pl.when(self.inner)
        def _():
            self.passed().start()

    def finish(self):
        self.own(1).wait_recv()
        self.own(3).wait_recv()

    def wait_sends(self):
        self.own(1).wait_send()
        self.own(2).wait_send()

        @pl.when(self.inner)
        def _():
            self.own(3).wait_send()
            self.passed().wait_send()


class LineSum(Line):
    def __init__(self, part, got, sems):
        super().__init__(sems)
        self.part, self.got = part, got

    def own(self, k):
        part = self.part(other(self.column, k))
        return self.remote(part, self.got.at[k], k, k, self.levels[k])

    def passed(self):
        part = self.part(other(self.column, 3))
        return self.remote(part, self.got.at[0], 0, 0, self.levels[1])

    def start(self):
        @pl.when(self.outer)
        def _():
            self.passed().start()
            self.own(2).start()
            self.got[3] = jnp.zeros(self.got.shape[1:], self.got.dtype)

        @pl.when(self.inner)
        def _():
            self.own(3).start()

        self.own(1).start()

    def forward(self):
        @pl.when(self.inner)
        def _():
            self.passed().wait_recv()
            part = self.part(other(self.column, 2))
            total = part[...].astype(jnp.float32) + self.got[0].astype(jnp.float32)
            part[...] = total.astype(part.dtype)
            self.own(2).start()

    def finish(self):
        self.own(1).wait_recv()
        self.own(2).wait_recv()

        @pl.when(self.inner)
        def _():
            self.own(3).wait_recv()

        total = self.part(self.column)[...].astype(jnp.float32)
        for k in (1, 2, 3):
            total = total + self.got[k].astype(jnp.float32)
        return total

    def wait_sends(self):
        self.own(1).wait_send()
        self.own(2).wait_send()

        @pl.when(self.outer)
        def _():
            self.passed().wait_send()

        @pl.when(self.inner)
        def _():
            self.own(3).wait_send()


class PlaneGather:
    def __init__(self, block, width, link_sems, core_sems):
        self.block, self.link_sems, self.core_sems = block, link_sems, core_sems
        place = lax.axis_index("dp")
        self.x, self.y, self.corner = other(place, 2), other(place, 4), other(place, 6)
        self.place = place
        self.x_side, self.y_side = {"dp": self.x}, {"dp": self.y}
        self.sibling = {"dp": other(place, 1)}
        self.halves = (pl.ds(0, width // 2), pl.ds(width // 2, width - width // 2))

    def copy(self, ref, sems, which, device):
        return pltpu.make_async_remote_copy(
            src_ref=ref,
            dst_ref=ref,
            send_sem=sems.at[0, which],
            recv_sem=sems.at[1, which],
            device_id=device,
            device_id_type=MESH,
        )

    def direct(self):
        own = self.block(self.place)
        return [
            self.copy(own, self.link_sems, 0, self.x_side),
            self.copy(own, self.link_sems, 1, self.y_side),
            self.copy(own, self.core_sems, 0, self.sibling),
        ]

    def forward(self):
        return [
            self.copy(self.block(self.x, self.halves[0]), self.link_sems, 2, self.y_side),
            self.copy(self.block(self.y, self.halves[1]), self.link_sems, 3, self.x_side),
            self.copy(self.block(self.x), self.core_sems, 1, self.sibling),
            self.copy(self.block(self.y), self.core_sems, 2, self.sibling),
        ]

    def last(self):
        return self.copy(self.block(self.corner), self.core_sems, 3, self.sibling)

    def start(self):
        for copy in self.direct():
            copy.start()

    def start_forward(self):
        for copy in self.direct()[:2]:
            copy.wait_recv()
        for copy in self.forward():
            copy.start()

    def start_last(self):
        for copy in self.forward()[:2]:
            copy.wait_recv()
        self.last().start()

    def finish(self):
        self.direct()[2].wait_recv()
        for copy in self.forward()[2:]:
            copy.wait_recv()
        self.last().wait_recv()

    def wait_sends(self):
        for copy in self.direct() + self.forward() + [self.last()]:
            copy.wait_send()


def turn(values, cosine, sine):
    heads = []
    for begin in range(0, values.shape[1], HEAD_DIM):
        head = values[:, begin : begin + HEAD_DIM]
        heads.append(head * cosine + pltpu.roll(head, HEAD_DIM // 2, 1) * sine)
    return jnp.concatenate(heads, 1)


def front_kernel(
    score_scale,
    shared_units,
    parents_ref,
    hidden_ref,
    gain_ref,
    b_query_ref,
    b_key_ref,
    b_value_ref,
    freqs_ref,
    routes_ref,
    out_grad_ref,
    w_query_ref,
    w_key_ref,
    w_value_ref,
    w_out_ref,
    s_gate_ref,
    s_up_ref,
    s_down_ref,
    residual_ref,
    query_ref,
    key_out,
    value_out,
    log_total_ref,
    attended_ref,
    normed_out,
    cosine_ref,
    sine_ref,
    hits_all_ref,
    grad_all_ref,
    shared_ref,
    weights,
    kv_all,
    hits_all,
    part_send,
    part_z,
    s_tiles,
    t_tiles,
    key_ref,
    value_ref,
    normed_ref,
    load_sems,
    tile_sems,
    store_sems,
    hit_sems,
    part_sems,
    kv_links,
    kv_cores,
    head_links,
    head_cores,
    tail_links,
    tail_cores,
):
    bf16, f32 = jnp.bfloat16, jnp.float32
    place, column = lax.axis_index("dp"), lax.axis_index("tensor")
    tok_rows, width = hidden_ref.shape
    rows = tok_rows // 4
    local_width = w_query_ref.shape[1]
    levels = [{"tensor": other(column, k)} for k in range(4)]
    peers = [{"dp": other(place, j)} for j in range(8)]

    loads = [
        pltpu.make_async_copy(ref, weights.at[i], load_sems.at[i])
        for i, ref in enumerate((w_query_ref, w_key_ref, w_value_ref, w_out_ref))
    ]
    own_grad = pltpu.make_async_copy(out_grad_ref, grad_all_ref.at[place], load_sems.at[4])
    for copy in loads:
        copy.start()
    own_grad.start()
    expert_id = lax.broadcasted_iota(jnp.int32, hits_all.shape[1:], 0)
    hits = jnp.zeros(hits_all.shape[1:], f32)
    for choice in range(routes_ref.shape[0]):
        hits = hits + jnp.where(expert_id == routes_ref[choice : choice + 1, :], 1.0, 0.0)
    hits_all[place] = hits

    barrier = pltpu.get_barrier_semaphore()
    partners = peers[1:] + levels[1:]
    for partner in partners:
        pl.semaphore_signal(barrier, inc=1, device_id=partner, device_id_type=MESH)
    pl.semaphore_wait(barrier, len(partners))

    def grad_block(first, count):
        def block(d, cols=slice(None)):
            return grad_all_ref.at[d, pl.ds(first, count), :, cols]

        return block

    head_gather = PlaneGather(grad_block(0, 1), width, head_links, head_cores)
    tail_gather = PlaneGather(grad_block(1, 3), width, tail_links, tail_cores)
    kv_gather = PlaneGather(
        lambda d, cols=slice(None): kv_all.at[d, :, cols], 2 * local_width, kv_links, kv_cores
    )
    own_grad.wait()
    head_gather.start()

    def hit_copy(j):
        return pltpu.make_async_remote_copy(
            src_ref=hits_all.at[place],
            dst_ref=hits_all.at[place],
            send_sem=hit_sems.at[0, j],
            recv_sem=hit_sems.at[1, j],
            device_id=peers[j],
            device_id_type=MESH,
        )

    for j in range(1, 8):
        hit_copy(j).start()

    def row_of(ref):
        return jnp.concatenate([ref[h : h + 1, :] for h in range(ref.shape[0])], 1)

    path = path_scalars(parents_ref, place)
    depth = jnp.float32(-1.0)
    for segment in path:
        depth = depth + jnp.where(segment >= 0, 1.0, 0.0)
    row_ids = lax.broadcasted_iota(jnp.int32, (tok_rows, HEAD_DIM), 0).astype(f32)
    lane = lax.broadcasted_iota(jnp.int32, (tok_rows, HEAD_DIM), 1)
    angles = (depth * SEG + row_ids) * freqs_ref[...]
    cosine = jnp.cos(angles)
    sine = jnp.where(lane < HEAD_DIM // 2, -1.0, 1.0) * jnp.sin(angles)
    cosine_ref[...] = cosine
    sine_ref[...] = sine
    hidden_f = hidden_ref[...].astype(f32)
    scale_rows = lax.rsqrt(jnp.mean(hidden_f * hidden_f, 1, keepdims=True) + epsilon)
    normed_ref[...] = (hidden_f * scale_rows * gain_ref[...]).astype(bf16)
    results = [
        pltpu.make_async_copy(source, target, load_sems.at[5 + i])
        for i, (source, target) in enumerate(
            ((normed_ref, normed_out), (key_ref, key_out), (value_ref, value_out))
        )
    ]
    results[0].start()
    for copy in loads[1:3]:
        copy.wait()
    key = product(normed_ref[...], weights[1]) + row_of(b_key_ref)
    kv_all[place, :, :local_width] = turn(key, cosine, sine).astype(bf16)
    value = product(normed_ref[...], weights[2]) + row_of(b_value_ref)
    kv_all[place, :, local_width:] = value.astype(bf16)
    kv_gather.start()
    loads[0].wait()
    query = product(normed_ref[...], weights[0]) + row_of(b_query_ref)
    query_ref[...] = turn(query, cosine, sine).astype(bf16)

    tile, span = s_tiles.shape[2:]
    shared_first = place * shared_units
    shared_base = jnp.minimum(shared_first // 128 * 128, s_gate_ref.shape[1] - span)
    shared_skip = shared_first - shared_base

    def tile_loads(i, slot):
        window = pl.ds(pl.multiple_of(i * tile, tile), tile)
        columns = pl.ds(pl.multiple_of(shared_base, 128), span)
        return [
            pltpu.make_async_copy(
                ref.at[window, columns], s_tiles.at[slot, j], tile_sems.at[slot, j]
            )
            for j, ref in enumerate((s_gate_ref, s_up_ref, s_down_ref))
        ]

    def tile_stores(i, slot):
        window = pl.ds(pl.multiple_of(i * tile, tile), tile)
        units = pl.ds(pl.multiple_of(shared_skip, 16), shared_units)
        return [
            pltpu.make_async_copy(
                t_tiles.at[slot, j, units], shared_ref.at[j, :, window], store_sems.at[slot, j]
            )
            for j in range(3)
        ]

    tiles = width // tile

    def pack(i, carry):
        slot = i % 2

        @pl.when(i + 1 < tiles)
        def _():
            for copy in tile_loads(i + 1, (i + 1) % 2):
                copy.start()

        for copy in tile_loads(i, slot):
            copy.wait()

        @pl.when(i >= 2)
        def _():
            for copy in tile_stores(i - 2, slot):
                copy.wait()

        for j in range(3):
            t_tiles[slot, j] = s_tiles[slot, j].T
        for copy in tile_stores(i, slot):
            copy.start()
        return carry

    for copy in tile_loads(0, 0):
        copy.start()
    lax.fori_loop(0, tiles // 2, pack, 0)
    kv_gather.start_forward()
    lax.fori_loop(tiles // 2, tiles, pack, 0)
    kv_gather.start_last()
    tail_gather.start()
    head_gather.start_forward()
    for i in (tiles - 2, tiles - 1):
        for copy in tile_stores(i, i % 2):
            copy.wait()
    kv_gather.finish()

    for level, segment in enumerate(path):
        block = kv_all[jnp.maximum(segment, 0)]
        key_ref[level * tok_rows : (level + 1) * tok_rows, :] = block[:, :local_width]
        value_ref[level * tok_rows : (level + 1) * tok_rows, :] = block[:, local_width:]
    for copy in results[1:]:
        copy.start()
    key_rows = key_ref.shape[0]
    row_id = lax.broadcasted_iota(jnp.int32, (tok_rows, key_rows), 0)
    col_id = lax.broadcasted_iota(jnp.int32, (tok_rows, key_rows), 1)
    allowed = row_id >= col_id
    for level in range(1, LEVELS):
        barred = jnp.where(path[level] >= 0, key_rows, 0)
        inside = (col_id >= level * tok_rows) & (col_id < (level + 1) * tok_rows)
        allowed = allowed | (inside & (col_id < barred))

    def head(h, carry):
        cols = pl.ds(pl.multiple_of(h * HEAD_DIM, HEAD_DIM), HEAD_DIM)
        scores = product_nt(query_ref[:, cols], key_ref[:, cols]) * score_scale
        scores = jnp.where(allowed, scores, -jnp.inf)
        top = jnp.max(scores, 1, keepdims=True)
        powers = jnp.exp(scores - top)
        total = jnp.sum(powers, 1, keepdims=True)
        log_total_ref[h] = top + jnp.log(total)
        probs = (powers * (1.0 / total)).astype(bf16)
        attended_ref[:, cols] = product(probs, value_ref[:, cols]).astype(bf16)
        return carry

    lax.fori_loop(0, local_width // HEAD_DIM, head, 0)

    loads[3].wait()
    for quarter in range(4):
        mine = slice(quarter * rows, (quarter + 1) * rows)
        part_send[quarter] = product_nt(attended_ref[mine, :], weights[3]).astype(bf16)

    line = LineSum(lambda z: part_send.at[z], part_z, part_sems)
    line.start()
    head_gather.start_last()
    tail_gather.start_forward()
    line.forward()
    attn = line.finish()
    own_rows = pl.ds(pl.multiple_of(column * rows, rows), rows)
    residual_ref[...] = hidden_ref[own_rows, :].astype(f32) + attn
    tail_gather.start_last()
    head_gather.finish()
    for j in range(1, 8):
        hit_copy(j).wait_recv()
    hits_all_ref[...] = hits_all[...]
    tail_gather.finish()

    for copy in results:
        copy.wait()

    for gather in (kv_gather, head_gather, tail_gather):
        gather.wait_sends()
    for j in range(1, 8):
        hit_copy(j).wait_send()
    line.wait_sends()


def front_layer(score_scale, shared_units, operands):
    hidden, w_query = operands[1], operands[9]
    tok_rows, width = hidden.shape
    rows, local_width = tok_rows // 4, w_query.shape[1]
    heads = local_width // HEAD_DIM
    tile, span = 256, 384
    bf16, f32 = jnp.bfloat16, jnp.float32
    shape = jax.ShapeDtypeStruct
    vmem, anywhere = pl.BlockSpec(memory_space=pltpu.VMEM), pl.BlockSpec(memory_space=pl.ANY)
    smem = pl.BlockSpec(memory_space=pltpu.SMEM)
    dma = pltpu.SemaphoreType.DMA
    return pl.pallas_call(
        functools.partial(front_kernel, score_scale, shared_units),
        out_shape=[
            shape((rows, width), f32),
            shape((tok_rows, local_width), bf16),
            shape((LEVELS * tok_rows, local_width), bf16),
            shape((LEVELS * tok_rows, local_width), bf16),
            shape((heads, tok_rows, 1), f32),
            shape((tok_rows, local_width), bf16),
            shape((tok_rows, width), bf16),
            shape((tok_rows, HEAD_DIM), f32),
            shape((tok_rows, HEAD_DIM), f32),
            shape((8, 16, tok_rows), f32),
            shape((8, 4, rows, width), bf16),
            shape((3, shared_units, width), bf16),
        ],
        in_specs=[smem] + [vmem] * 8 + [anywhere] * 7,
        out_specs=[vmem, vmem, anywhere, anywhere, vmem, vmem, anywhere]
        + [vmem] * 3
        + [anywhere] * 2,
        scratch_shapes=[
            pltpu.VMEM((4, width, local_width), bf16),
            pltpu.VMEM((8, tok_rows, 2 * local_width), bf16),
            pltpu.VMEM((8, 16, tok_rows), f32),
            pltpu.VMEM((4, rows, width), bf16),
            pltpu.VMEM((4, rows, width), bf16),
            pltpu.VMEM((2, 3, tile, span), bf16),
            pltpu.VMEM((2, 3, span, tile), bf16),
            pltpu.VMEM((LEVELS * tok_rows, local_width), bf16),
            pltpu.VMEM((LEVELS * tok_rows, local_width), bf16),
            pltpu.VMEM((tok_rows, width), bf16),
            dma((8,)),
            dma((2, 3)),
            dma((2, 3)),
            dma((2, 8)),
            dma((2, 4)),
        ]
        + [dma((2, 4))] * 6,
        compiler_params=pltpu.CompilerParams(
            collective_id=2, has_side_effects=True, vmem_limit_bytes=56 * 2**20
        ),
        cost_estimate=pl.CostEstimate(
            flops=2 * 2**31, bytes_accessed=40 * 2**20, transcendentals=2**21
        ),
    )(*operands)


class PlaneSum:
    def __init__(self, mine, theirs, got_core, got_x1, got_y1, got_y2, got_x2, core_sems, sems):
        self.mine, self.theirs = mine, theirs
        self.got = (got_core, got_x1, got_y1, got_y2, got_x2)
        self.core_sems, self.sems = core_sems, sems
        self.half = got_x1.shape[-1]
        self.wide = self.half + got_y1.shape[-1]
        self.left, self.right = pl.ds(0, self.half), pl.ds(self.half, self.wide - self.half)
        place = lax.axis_index("dp")
        self.core, self.east, self.north = place % 2, (place // 2) % 2, place // 4
        self.sibling = {"dp": other(place, 1)}
        self.x_side, self.y_side = {"dp": other(place, 2)}, {"dp": other(place, 4)}

    def remote(self, src, dst, sems, which, device):
        return pltpu.make_async_remote_copy(
            src_ref=src,
            dst_ref=dst,
            send_sem=sems.at[(0, *which)],
            recv_sem=sems.at[(1, *which)],
            device_id=device,
            device_id_type=MESH,
        )

    def core_copy(self, k):
        return self.remote(
            self.theirs(k), self.got[0].at[k], self.core_sems, (k,), self.sibling
        )

    def first_copies(self, k):
        mine = self.mine(k)
        return [
            self.remote(
                mine.at[:, flip(self.east), :, self.left],
                self.got[1].at[k],
                self.sems,
                (0, k),
                self.x_side,
            ),
            self.remote(
                mine.at[flip(self.north), :, :, self.right],
                self.got[2].at[k],
                self.sems,
                (1, k),
                self.y_side,
            ),
        ]

    def second_copies(self, k):
        mine = self.mine(k)
        return [
            self.remote(
                mine.at[flip(self.north), self.east, :, self.left],
                self.got[3].at[k],
                self.sems,
                (2, k),
                self.y_side,
            ),
            self.remote(
                mine.at[self.north, flip(self.east), :, self.right],
                self.got[4].at[k],
                self.sems,
                (3, k),
                self.x_side,
            ),
        ]

    def add(self, ref, value):
        ref[...] = (ref[...].astype(jnp.float32) + value.astype(jnp.float32)).astype(jnp.bfloat16)

    def start(self, k):
        self.core_copy(k).start()

    def after_core(self, k):
        self.core_copy(k).wait_recv()
        mine = self.mine(k)
        for y in range(2):
            for x in range(2):
                self.add(mine.at[y, x], self.got[0][k, y, x])
        self.start_first(k)

    def start_first(self, k):
        for copy in self.first_copies(k):
            copy.start()

    def after_first(self, k):
        x_copy, y_copy = self.first_copies(k)
        mine = self.mine(k)
        x_copy.wait_recv()
        for y in range(2):
            self.add(mine.at[y, self.east, :, self.left], self.got[1][k, y])
        y_copy.wait_recv()
        for x in range(2):
            self.add(mine.at[self.north, x, :, self.right], self.got[2][k, x])
        for copy in self.second_copies(k):
            copy.start()

    def after_second(self, k):
        y_copy, x_copy = self.second_copies(k)
        own = self.mine(k).at[self.north, self.east]
        y_copy.wait_recv()
        self.add(own.at[:, self.left], self.got[3][k])
        x_copy.wait_recv()
        self.add(own.at[:, self.right], self.got[4][k])
        return own

    def wait_sends(self, k):
        if self.theirs is not None:
            self.core_copy(k).wait_send()
        for copy in self.first_copies(k) + self.second_copies(k):
            copy.wait_send()


def plane_scratch(count, rows, wide):
    half = wide // 2
    bf16, dma = jnp.bfloat16, pltpu.SemaphoreType.DMA
    return [
        pltpu.VMEM((count, 2, 2, rows, wide), bf16),
        pltpu.VMEM((count, 2, rows, half), bf16),
        pltpu.VMEM((count, 2, rows, wide - half), bf16),
        pltpu.VMEM((count, rows, half), bf16),
        pltpu.VMEM((count, rows, wide - half), bf16),
        dma((2, count)),
        dma((2, 4, count)),
    ]


def unturn(grad, cosine, sine):
    heads = []
    for begin in range(0, grad.shape[1], HEAD_DIM):
        head = grad[:, begin : begin + HEAD_DIM]
        heads.append(head * cosine - pltpu.roll(head, HEAD_DIM // 2, 1) * sine)
    return jnp.concatenate(heads, 1)


def back_kernel(
    score_scale,
    gain_row,
    residual_in,
    res_grad_in,
    res_low_ref,
    ffn_part_ref,
    shared_ref,
    small_ref,
    query_ref,
    key_in,
    value_in,
    parents_ref,
    log_total_ref,
    attended_ref,
    normed_in,
    hidden_in,
    gain_ref,
    cosine_ref,
    sine_ref,
    w_out_ref,
    w_query_ref,
    w_key_ref,
    w_value_ref,
    hidden_out_ref,
    hidden_grad_ref,
    grad_query_ref,
    grad_key_ref,
    grad_value_ref,
    grad_out_ref,
    shared_got,
    small_out_ref,
    bias_out_ref,
    low_all,
    w_qkv,
    out_mine,
    out_z,
    kv_sums,
    w_sums,
    kv_path,
    attended_grad,
    query_grad,
    pre_grads,
    part,
    part_send,
    part_z,
    hidden_stage,
    shared_stage,
    small_send,
    small_got,
    small_z,
    residual_ref,
    res_grad_ref,
    key_ref,
    value_ref,
    normed_ref,
    hidden_ref,
    *rest,
):
    bf16, f32 = jnp.bfloat16, jnp.float32
    out_scr, rest = rest[:5], rest[5:]
    kv_scr, rest = rest[:7], rest[7:]
    w_scr, rest = rest[:7], rest[7:]
    wkv_sems, rest = rest[:2], rest[2:]
    load_sems, low_sems, out_sems, part_sems, end_sems, shared_sems, small_sems, small_z_sems = rest
    place, column = lax.axis_index("dp"), lax.axis_index("tensor")
    core, east, north = place % 2, (place // 2) % 2, place // 4
    rows, width = residual_ref.shape
    tok_rows, local_width = query_ref.shape
    levels = [{"tensor": other(column, k)} for k in range(4)]
    peers = [{"dp": other(place, j)} for j in range(8)]

    def remote(src, dst, sems, which, device):
        return pltpu.make_async_remote_copy(
            src_ref=src,
            dst_ref=dst,
            send_sem=sems.at[(0, *which)],
            recv_sem=sems.at[(1, *which)],
            device_id=device,
            device_id_type=MESH,
        )

    def load_out(z):
        return pltpu.make_async_copy(ffn_part_ref.at[z], out_mine.at[z], load_sems.at[z])

    loads = [
        pltpu.make_async_copy(w_query_ref, w_qkv.at[0], load_sems.at[5]),
        pltpu.make_async_copy(w_key_ref, w_qkv.at[1], load_sems.at[6]),
        pltpu.make_async_copy(w_out_ref, w_qkv.at[2], load_sems.at[4]),
    ]
    fetches = [
        pltpu.make_async_copy(source, target, load_sems.at[12 + i])
        for i, (source, target) in enumerate(
            (
                (key_in, key_ref),
                (value_in, value_ref),
                (normed_in, normed_ref),
                (hidden_in, hidden_ref),
                (residual_in, residual_ref),
                (res_grad_in, res_grad_ref),
            )
        )
    ]
    for copy in fetches:
        copy.start()
    load_value = pltpu.make_async_copy(w_value_ref, w_qkv.at[2], load_sems.at[7])
    load_shared = pltpu.make_async_copy(shared_ref.at[place], shared_stage, load_sems.at[9])
    load_shared.start()
    for z in range(4):
        load_out(z).start()
    for copy in loads:
        copy.start()

    barrier = pltpu.get_barrier_semaphore()
    partners = peers[1:] + levels[1:]
    for partner in partners:
        pl.semaphore_signal(barrier, inc=1, device_id=partner, device_id_type=MESH)
    pl.semaphore_wait(barrier, len(partners))

    out_sum = PlaneSum(lambda k: out_mine.at[k], None, None, *out_scr[:4], None, out_scr[4])
    kv_sum = PlaneSum(
        lambda k: kv_sums.at[k, core], lambda k: kv_sums.at[k, flip(core)], *kv_scr
    )
    w_sum = PlaneSum(
        lambda k: w_sums.at[k, core], lambda k: w_sums.at[k, flip(core)], *w_scr
    )
    wkv_sum = PlaneSum(
        lambda k: kv_sums.at[k, core],
        lambda k: kv_sums.at[k, flip(core)],
        *kv_scr[:5],
        *wkv_sems,
    )

    low_all[column] = res_low_ref[...]
    low_line = LineGather(lambda z: low_all.at[z], low_sems)
    low_line.start()
    order = [other(column, k) for k in (1, 3, 2, 0)]
    for z in range(4):
        load_out(z).wait()
    for z in order:
        out_sum.start_first(z)
    kv_path[...] = jnp.zeros(kv_path.shape, f32)
    for copy in loads + fetches:
        copy.wait()

    out_line = LineSum(lambda z: out_mine.at[z, north, east], out_z, out_sems)
    low_line.forward()

    half_rows = tok_rows // 2
    key_rows = key_ref.shape[0]
    row_id = lax.broadcasted_iota(jnp.int32, (half_rows, key_rows), 0)
    col_id = lax.broadcasted_iota(jnp.int32, (half_rows, key_rows), 1)
    path = path_scalars(parents_ref, place)
    reached = col_id < 0
    for level in range(1, LEVELS):
        barred = jnp.where(path[level] >= 0, key_rows, 0)
        inside = (col_id >= level * tok_rows) & (col_id < (level + 1) * tok_rows)
        reached = reached | (inside & (col_id < barred))

    def half(i, carry):
        pair = (column // 2 + i) % 2
        first = pl.multiple_of(pair * half_rows, half_rows)
        window = pl.ds(first, half_rows)

        @pl.when(i == 0)
        def _():
            low_line.own(1).wait_recv()

        @pl.when(i == 1)
        def _():
            low_line.own(3).wait_recv()

        low_rows = low_all[pl.ds(2 * pair, 2)].reshape(half_rows, width)
        attended_grad[window, :] = product(low_rows, w_qkv[2]).astype(bf16)
        allowed = (row_id + first >= col_id) | reached

        def head(h, carry):
            cols = pl.ds(pl.multiple_of(h * HEAD_DIM, HEAD_DIM), HEAD_DIM)
            value_cols = pl.ds(pl.multiple_of(local_width + h * HEAD_DIM, HEAD_DIM), HEAD_DIM)
            query, key, value = query_ref[window, cols], key_ref[:, cols], value_ref[:, cols]
            grad = attended_grad[window, cols]
            scores = jnp.where(allowed, product_nt(query, key) * score_scale, -jnp.inf)
            weights = jnp.exp(scores - log_total_ref[h, window])
            weight_grad = product_nt(grad, value)
            center = jnp.sum(weights * weight_grad, 1, keepdims=True)
            score_grad = (weights * (weight_grad - center)).astype(bf16)
            query_grad[window, cols] = product(score_grad, key) * score_scale
            kv_path[:, cols] += product_tn(score_grad, query) * score_scale
            kv_path[:, value_cols] += product_tn(weights.astype(bf16), grad)
            return carry

        lax.fori_loop(0, local_width // HEAD_DIM, head, 0)

        @pl.when(i == 0)
        def _():
            out_sum.after_first(order[0])
            out_sum.after_first(order[1])

        return carry

    lax.fori_loop(0, 2, half, 0)
    for z in order[2:]:
        out_sum.after_first(z)
    load_value.start()

    part_rows = rows // 2

    def kv_blocks(i, c):
        which, y, x = i // 4, (i // 2) % 2, i % 2
        segment = 4 * y + 2 * x + c
        total = jnp.zeros((4, part_rows, 2 * local_width), f32)
        for level in range(1, LEVELS):
            spot = jnp.where(path[level] == segment, 1.0, 0.0)
            total = total + spot * kv_rows(level, which)
        kv_sums[which, c, y, x] = total.reshape(4 * part_rows, 2 * local_width).astype(bf16)
        return c

    def kv_rows(level, which):
        rows_view = kv_path.at[level * tok_rows : (level + 1) * tok_rows]
        pieces = []
        for z in range(4):
            start = pl.multiple_of(z * rows + which * part_rows, part_rows)
            pieces.append(rows_view[pl.ds(start, part_rows), :])
        return jnp.stack(pieces)

    lax.fori_loop(0, 4, kv_blocks, flip(core))
    kv_sum.start(0)
    lax.fori_loop(4, 8, kv_blocks, flip(core))
    kv_sum.start(1)
    lax.fori_loop(0, 8, kv_blocks, core)
    for which in range(2):
        own_kv = kv_sums.at[which, core, north, east]
        added = own_kv[...].astype(f32) + kv_rows(0, which).reshape(4 * part_rows, -1)
        own_kv[...] = added.astype(bf16)
        kv_sum.after_core(which)
    for z in order:
        out_sum.after_second(z)
    out_line.start()

    def bias_of(which, grad, begin):
        bias = jnp.sum(grad.astype(f32), 0, keepdims=True)
        for h in range(local_width // HEAD_DIM):
            spot = slice(4 * which + h, 4 * which + h + 1)
            added = bias[:, h * HEAD_DIM : (h + 1) * HEAD_DIM]
            if not begin:
                added = added + small_send[0, spot, 2 * HEAD_DIM :]
            small_send[0, spot, 2 * HEAD_DIM :] = added

    small_send[0, :, 2 * HEAD_DIM :] = jnp.zeros((16, HEAD_DIM), f32)
    query_pre = unturn(query_grad[...], cosine_ref[...], sine_ref[...]).astype(bf16)
    pre_grads[0] = query_pre.reshape(4, 2, part_rows, local_width)
    bias_of(0, query_pre, True)
    part[...] = product_nt(query_pre, w_qkv[0]).reshape(4, 2, part_rows, width)
    def block_index(place_of):
        return place_of % 2, place_of // 4, (place_of // 2) % 2

    def out_weights(i, carry):
        c, y, x = block_index(i)
        window = pl.ds(pl.multiple_of(i * tok_rows, tok_rows), tok_rows)
        lhs = low_all[:, :, window].reshape(tok_rows, tok_rows)
        w_sums[0, c, y, x] = product_tn(lhs, attended_ref[...]).astype(bf16)
        return carry

    def query_weights(i, carry):
        c, y, x = block_index(i)
        window = pl.ds(pl.multiple_of(i * tok_rows, tok_rows), tok_rows)
        rows_pre = pre_grads[0].reshape(tok_rows, local_width)
        w_sums[1, c, y, x] = product_tn(normed_ref[:, window], rows_pre).astype(bf16)
        return carry

    lax.fori_loop(0, 8, out_weights, 0)
    w_sum.start(0)
    lax.fori_loop(0, 8, query_weights, 0)
    w_sum.start(1)
    kv_sum.after_first(0)
    kv_sum.after_first(1)

    load_value.wait()
    hidden_f = hidden_ref[...].astype(f32)
    unit_scale = lax.rsqrt(jnp.mean(hidden_f * hidden_f, 1, keepdims=True) + epsilon)

    part_lines = [
        LineSum(
            lambda z, which=which: part_send.at[which, z],
            part_z.at[which],
            part_sems.at[which],
        )
        for which in range(2)
    ]

    for which in range(2):
        own_kv = kv_sum.after_second(which)
        cos_rows = cosine_ref[...].reshape(4, 2, part_rows, HEAD_DIM)[:, which]
        sin_rows = sine_ref[...].reshape(4, 2, part_rows, HEAD_DIM)[:, which]
        key_pre = unturn(
            own_kv[:, :local_width].astype(f32),
            cos_rows.reshape(4 * part_rows, HEAD_DIM),
            sin_rows.reshape(4 * part_rows, HEAD_DIM),
        ).astype(bf16)
        value_pre = own_kv[:, local_width:]
        pre_grads[1, :, which] = key_pre.reshape(4, part_rows, local_width)
        pre_grads[2, :, which] = value_pre.reshape(4, part_rows, local_width)
        bias_of(1, key_pre, which == 0)
        bias_of(2, value_pre, which == 0)
        added = product_nt(key_pre, w_qkv[1]) + product_nt(value_pre, w_qkv[2])
        whole = part[:, which] + added.reshape(4, part_rows, width)
        part[:, which] = whole
        part_send[which] = whole.astype(bf16)
        part_lines[which].start()
        if which == 0:
            out_line.forward()


    def shared_copy(j):
        return remote(
            shared_ref.at[other(place, j)], shared_got.at[place], shared_sems, (j,), peers[j]
        )

    for k in range(2):
        w_sum.after_core(k)
    part_lines[0].forward()
    attn_gain_row = jnp.sum(
        part[...].reshape(tok_rows, width) * (hidden_f * unit_scale), 0, keepdims=True
    )
    def key_value_weights(i, carry):
        c, y, x = block_index(i)
        window = pl.ds(pl.multiple_of(i * tok_rows, tok_rows), tok_rows)
        lhs = normed_ref[:, window]
        for which, cols in ((1, slice(0, local_width)), (2, slice(local_width, None))):
            rows_pre = pre_grads[which].reshape(tok_rows, local_width)
            grad = product_tn(lhs, rows_pre).astype(bf16)
            for k in range(2):
                piece = slice(k * half_rows, (k + 1) * half_rows)
                kv_sums[k, c, y, x, :, cols] = grad[piece]
        return carry

    for k in range(2):
        kv_sum.wait_sends(k)
    lax.fori_loop(0, 8, key_value_weights, 0)
    for k in range(2):
        wkv_sum.start(k)
    part_lines[1].forward()

    bias_rows = small_send[0, :, 2 * HEAD_DIM :]
    for d in range(8):
        small_send[d, :, : 2 * HEAD_DIM] = small_ref[:, d * tok_rows : (d + 1) * tok_rows]
        small_send[d, gain_row : gain_row + 1, : 2 * HEAD_DIM] = attn_gain_row[
            :, d * tok_rows : (d + 1) * tok_rows
        ]
        small_send[d, :, 2 * HEAD_DIM :] = bias_rows

    def small_copy(j):
        return remote(
            small_send.at[other(place, j)], small_got.at[j], small_sems, (j,), peers[j]
        )

    for j in range(1, 8):
        small_copy(j).start()

    w_sum.after_first(0)
    for k in range(2):
        wkv_sum.after_core(k)
    w_sum.after_first(1)
    own_shared = pltpu.make_async_copy(shared_stage, shared_got.at[place], load_sems.at[8])
    load_shared.wait()
    own_shared.start()

    total = small_send[place]
    for j in range(1, 8):
        small_copy(j).wait_recv()
        total = total + small_got[j]
    bias_out_ref[...] = total[:, 2 * HEAD_DIM :]
    small_z[column] = total[:, : 2 * HEAD_DIM]
    own_small = small_z.at[column]
    small_levels = [
        remote(own_small, own_small, small_z_sems, (k,), levels[k]) for k in (1, 2, 3)
    ]
    for copy in small_levels:
        copy.start()

    end_lines = [
        LineGather(
            lambda z, which=which, piece=piece: hidden_stage.at[which, z, piece],
            end_sems.at[which, piece],
        )
        for which in range(2)
        for piece in range(2)
    ]

    for which in range(2):
        attn_grad = part_lines[which].finish()
        start = pl.multiple_of(column * rows + which * part_rows, part_rows)
        own_hidden = hidden_ref[pl.ds(start, part_rows), :].astype(f32)
        own_scale = lax.rsqrt(jnp.mean(own_hidden * own_hidden, 1, keepdims=True) + epsilon)
        own_grad = res_grad_ref[which * part_rows : (which + 1) * part_rows, :]
        hidden_stage[0, column, which] = (
            own_grad + norm_back(attn_grad, own_hidden * own_scale, own_scale, gain_ref[...])
        ).astype(bf16)
        end_lines[which].start()
        if which == 0:
            grad_out_ref[...] = w_sum.after_second(0)[...]
            for k in range(2):
                wkv_sum.after_first(k)
            for j in (6, 7, 2, 3, 4, 5, 1):
                shared_copy(j).start()

    end_lines[0].forward()
    out = residual_ref[...] + out_line.finish()
    hidden_stage[1, column] = out.astype(bf16).reshape(2, part_rows, width)
    end_lines[1].forward()
    end_lines[2].start()
    end_lines[3].start()

    grad_query_ref[...] = w_sum.after_second(1)[...]
    for copy in small_levels:
        copy.wait_recv()
    small_out_ref[...] = (small_z[0] + small_z[1]) + (small_z[2] + small_z[3])
    for k in range(2):
        own_wkv = wkv_sum.after_second(k)
        piece = slice(k * half_rows, (k + 1) * half_rows)
        grad_key_ref[piece, :] = own_wkv[:, :local_width]
        grad_value_ref[piece, :] = own_wkv[:, local_width:]

    end_lines[2].forward()
    end_lines[3].forward()
    own_shared.wait()
    for j in range(1, 8):
        shared_copy(j).wait_recv()
    for line in end_lines:
        line.finish()
    ends = [
        pltpu.make_async_copy(hidden_stage.at[0], hidden_grad_ref, load_sems.at[10]),
        pltpu.make_async_copy(hidden_stage.at[1], hidden_out_ref, load_sems.at[11]),
    ]
    for copy in ends:
        copy.start()
    for copy in ends:
        copy.wait()

    for copy in small_levels:
        copy.wait_send()
    for line in [low_line, out_line] + part_lines + end_lines:
        line.wait_sends()
    for z in range(4):
        out_sum.wait_sends(z)
    for k in range(2):
        w_sum.wait_sends(k)
        wkv_sum.wait_sends(k)
    for j in range(1, 8):
        small_copy(j).wait_send()
        shared_copy(j).wait_send()


def back_layer(score_scale, gain_row, operands):
    (
        residual,
        res_grad,
        res_low,
        ffn_part,
        grad_shared,
        small,
        query,
        key,
        value,
        parents,
        log_total,
        attended,
        normed,
        hidden,
        gain,
        cosine,
        sine,
        w_out,
        w_query,
        w_key,
        w_value,
    ) = operands
    rows, width = residual.shape
    tok_rows, local_width = query.shape
    units = grad_shared.shape[2]
    bf16, f32 = jnp.bfloat16, jnp.float32
    shape = jax.ShapeDtypeStruct
    vmem, anywhere = pl.BlockSpec(memory_space=pltpu.VMEM), pl.BlockSpec(memory_space=pl.ANY)
    smem = pl.BlockSpec(memory_space=pltpu.SMEM)
    dma = pltpu.SemaphoreType.DMA
    return pl.pallas_call(
        functools.partial(back_kernel, score_scale, gain_row),
        out_shape=[
            shape((4, 2, rows // 2, width), bf16),
            shape((4, 2, rows // 2, width), bf16),
            shape((tok_rows, local_width), bf16),
            shape((tok_rows, local_width), bf16),
            shape((tok_rows, local_width), bf16),
            shape((tok_rows, local_width), bf16),
            shape((8, 3, units, tok_rows), bf16),
            shape((16, tok_rows), f32),
            shape((16, HEAD_DIM), f32),
        ],
        in_specs=[anywhere, anywhere, vmem, anywhere, anywhere, vmem]
        + [vmem, anywhere, anywhere]
        + [smem]
        + [vmem, vmem, anywhere, anywhere, vmem, vmem, vmem]
        + [anywhere] * 4,
        out_specs=[anywhere] * 2 + [vmem] * 4 + [anywhere] + [vmem] * 2,
        scratch_shapes=[
            pltpu.VMEM((4, rows, width), bf16),
            pltpu.VMEM((3, width, local_width), bf16),
            pltpu.VMEM((4, 2, 2, rows, width), bf16),
            pltpu.VMEM((4, rows, width), bf16),
            pltpu.VMEM((2, 2, 2, 2, tok_rows // 2, 2 * local_width), bf16),
            pltpu.VMEM((2, 2, 2, 2, tok_rows, local_width), bf16),
            pltpu.VMEM((LEVELS * tok_rows, 2 * local_width), f32),
            pltpu.VMEM((tok_rows, local_width), bf16),
            pltpu.VMEM((tok_rows, local_width), f32),
            pltpu.VMEM((3, 4, 2, rows // 2, local_width), bf16),
            pltpu.VMEM((4, 2, rows // 2, width), f32),
            pltpu.VMEM((2, 4, rows // 2, width), bf16),
            pltpu.VMEM((2, 4, rows // 2, width), bf16),
            pltpu.VMEM((2, 4, 2, rows // 2, width), bf16),
            pltpu.VMEM((3, units, tok_rows), bf16),
            pltpu.VMEM((8, 16, 2 * HEAD_DIM + HEAD_DIM), f32),
            pltpu.VMEM((8, 16, 2 * HEAD_DIM + HEAD_DIM), f32),
            pltpu.VMEM((4, 16, 2 * HEAD_DIM), f32),
            pltpu.VMEM(residual.shape, f32),
            pltpu.VMEM(res_grad.shape, f32),
            pltpu.VMEM(key.shape, bf16),
            pltpu.VMEM(value.shape, bf16),
            pltpu.VMEM(normed.shape, bf16),
            pltpu.VMEM(hidden.shape, bf16),
        ]
        + plane_scratch(4, rows, width)[1:5]
        + plane_scratch(4, rows, width)[6:]
        + plane_scratch(2, tok_rows // 2, 2 * local_width)
        + plane_scratch(2, tok_rows, local_width)
        + plane_scratch(2, tok_rows // 2, 2 * local_width)[5:]
        + [
            dma((18,)),
            dma((2, 4)),
            dma((2, 4)),
            dma((2, 2, 4)),
            dma((2, 2, 2, 4)),
            dma((2, 8)),
            dma((2, 8)),
            dma((2, 4)),
        ],
        compiler_params=pltpu.CompilerParams(
            collective_id=1, has_side_effects=True, vmem_limit_bytes=63 * 2**20
        ),
        cost_estimate=pl.CostEstimate(
            flops=2 * 12 * 2**30, bytes_accessed=40 * 2**20, transcendentals=2**20
        ),
    )(*operands)


def on_slice(
    hidden_in,
    out_grad,
    parents,
    routes,
    attn_gain,
    w_query,
    w_key,
    w_value,
    b_query,
    b_key,
    b_value,
    w_out,
    ffn_gain,
    w_router,
    shared_gate,
    shared_w_gate,
    shared_w_up,
    shared_w_down,
    expert_w_gate,
    expert_w_up,
    expert_w_down,
):
    tok_rows, model_width = hidden_in.shape
    devices = lax.axis_size("dp")
    columns = lax.axis_size("tensor")
    place, column = lax.axis_index("dp"), lax.axis_index("tensor")
    all_rows = tok_rows * devices
    part_rows = tok_rows // columns
    local_width = w_query.shape[1]
    experts = w_router.shape[1]
    top_count = routes.shape[1]
    capacity = 5 * tok_rows * top_count // 4
    score_scale = HEAD_DIM ** (-0.5)
    bf16, f32 = jnp.bfloat16, jnp.float32

    expert_units = expert_w_gate.shape[2]
    shared_units = shared_w_gate.shape[1] // devices
    shared_pad = -(-shared_units // 128) * 128
    units = shared_pad + expert_units
    units_pad = -(-(units + experts + 1) // 128) * 128

    def own_units(matrix):
        return lax.dynamic_slice_in_dim(matrix, place * shared_units, shared_units, 1)

    def pad_to(matrix, columns):
        return jnp.pad(matrix, ((0, 0), (0, columns - matrix.shape[1])))

    def side_by_side(shared, expert):
        joined = jnp.concatenate([pad_to(own_units(shared), shared_pad), expert[0]], 1)
        return joined

    w_pre = jnp.concatenate(
        [
            pad_to(
                jnp.concatenate(
                    [side_by_side(shared_w_gate, expert_w_gate), w_router, shared_gate[:, None]], 1
                ),
                units_pad,
            ),
            pad_to(side_by_side(shared_w_up, expert_w_up), units_pad),
        ],
        1,
    )
    w_down = pad_to(side_by_side(shared_w_down, expert_w_down), units_pad)

    out_all = gather_dp(out_grad)

    routes_all = lax.all_gather(routes, "dp", axis=0, tiled=True)
    pair_onehot = routes_all[:, :, None] == jnp.arange(experts, dtype=jnp.int32)[None, None, :]
    hits = jnp.any(pair_onehot, 1)
    hit_blocks = hits.astype(bf16).reshape(devices, tok_rows, experts)
    below = (
        jnp.arange(tok_rows)[None, :] < jnp.arange(tok_rows)[:, None]
    ).astype(bf16)
    within = jnp.einsum("ij,bje->bie", below, hit_blocks, preferred_element_type=f32)
    block_sums = jnp.sum(hit_blocks.astype(f32), 1)
    before = jnp.cumsum(block_sums, 0) - block_sums
    slots = (within + before[:, None, :]).reshape(all_rows, experts)
    kept = (hits & (slots < capacity)).astype(f32)

    path = path_of(parents, place * tok_rows // SEG)
    reachable = path >= 0
    path_rows = jnp.maximum(path, 0)
    row_ids = jnp.arange(tok_rows, dtype=jnp.int32)
    depth = jnp.sum(reachable.astype(f32)) - 1.0
    cosine, sine = rope_tables(depth * SEG + row_ids.astype(f32))
    allowed = jnp.concatenate(
        [
            row_ids[:, None] >= row_ids[None, :],
            jnp.broadcast_to(
                jnp.repeat(reachable[1:], tok_rows)[None, :], (tok_rows, (LEVELS - 1) * tok_rows)
            ),
        ],
        1,
    )
    hidden_f = hidden_in.astype(f32)
    attn_scale, attn_unit = norm_parts(hidden_f)
    attn_normed = (attn_unit * attn_gain).astype(bf16)
    query_rot = turn_heads(
        product(attn_normed, w_query) + b_query.reshape(-1), cosine, sine, 1.0
    ).astype(bf16)
    key_rot = turn_heads(
        product(attn_normed, w_key) + b_key.reshape(-1), cosine, sine, 1.0
    ).astype(bf16)
    value_rows = (product(attn_normed, w_value) + b_value.reshape(-1)).astype(bf16)
    gathered = gather_dp(jnp.concatenate([key_rot, value_rows], 1))
    kv_blocks = gathered.reshape(devices, tok_rows, 2 * local_width)
    kv_path = jnp.take(kv_blocks, path_rows, axis=0).reshape(LEVELS * tok_rows, 2 * local_width)
    key_path, value_path = kv_path[:, :local_width], kv_path[:, local_width:]
    attended, log_total = attend_forward(query_rot, key_path, value_path, allowed, score_scale)
    attended_low = attended.astype(bf16)
    attn_part = product_nt(attended_low, w_out).astype(bf16)

    hidden_own = lax.dynamic_slice_in_dim(hidden_in, column * part_rows, part_rows, 0)
    grad_own = lax.dynamic_slice_in_dim(out_grad, column * part_rows, part_rows, 0)
    layout = (shared_units, shared_pad, expert_units, experts, units_pad)
    (
        residual,
        residual_grad,
        residual_low,
        ffn_part,
        grad_expert_gate,
        grad_expert_up,
        grad_expert_down,
        grad_shared,
        grad_side,
        grad_ffn_gain,
    ) = ffn_plain(
        attn_part, hidden_own, grad_own, ffn_gain, kept, out_all, w_pre, w_down, layout
    )
    grad_shared = grad_shared[:, :, :shared_units]
    ffn_own = scatter_all(ffn_part).astype(f32)
    hidden_out = gather_tensor((residual + ffn_own).astype(bf16))
    residual_low = gather_tensor(residual_low)
    grad_out_proj = product_tn(residual_low, attended_low)
    attended_grad = product(residual_low, w_out).astype(bf16)

    query_grad, key_grad, value_grad = attend_backward(
        query_rot, key_path, value_path, allowed, log_total, attended_grad, score_scale
    )
    kv_grad = jnp.concatenate([key_grad, value_grad], 1).reshape(
        LEVELS, tok_rows, 2 * local_width
    )
    kv_all = jnp.zeros((devices, tok_rows, 2 * local_width), f32)
    for level in range(LEVELS):
        kv_all = kv_all.at[path_rows[level]].add(kv_grad[level])
    kv_own = scatter_dp(
        kv_all.reshape(all_rows, 2 * local_width).astype(bf16)
    ).astype(f32)
    query_pre_grad = turn_heads(query_grad, cosine, sine, -1.0).astype(bf16)
    key_pre_grad = turn_heads(kv_own[:, :local_width], cosine, sine, -1.0).astype(bf16)
    value_pre_grad = kv_own[:, local_width:].astype(bf16)
    qkv_pre_grad = jnp.concatenate([query_pre_grad, key_pre_grad, value_pre_grad], 1)
    grad_qkv = product_tn(attn_normed, qkv_pre_grad)
    bias_grads = jnp.sum(qkv_pre_grad.astype(f32), 0).reshape(3, -1, HEAD_DIM)
    attn_part_grad = (
        product_nt(query_pre_grad, w_query)
        + product_nt(key_pre_grad, w_key)
        + product_nt(value_pre_grad, w_value)
    )
    grad_attn_gain = jnp.sum(attn_part_grad * attn_unit, 0)
    attn_own_grad = scatter_tensor(attn_part_grad.astype(bf16)).astype(f32)
    own_rows = lambda array: lax.dynamic_slice_in_dim(
        array, column * part_rows, part_rows, 0
    )
    hidden_in_grad = gather_tensor(
        (
            residual_grad
            + norm_back(attn_own_grad, own_rows(attn_unit), own_rows(attn_scale), attn_gain)
        ).astype(bf16)
    )

    small = jnp.concatenate(
        [grad_side, grad_ffn_gain[:, None], grad_attn_gain[:, None]], 1
    )
    small = scatter_dp(lax.psum(small, "tensor"))
    bias_sums = lax.psum_scatter(bias_grads, "dp", scatter_dimension=2, tiled=True)
    grad_attn = scatter_dp(jnp.concatenate([grad_qkv, grad_out_proj], 1).astype(bf16)).astype(f32)
    shared_grads = lax.all_to_all(
        grad_shared, "dp", split_axis=1, concat_axis=2, tiled=True
    ).astype(f32)
    return (
        hidden_out,
        hidden_in_grad,
        small[:, experts + 2],
        grad_attn[:, :local_width],
        grad_attn[:, local_width : 2 * local_width],
        grad_attn[:, 2 * local_width : 3 * local_width],
        bias_sums[0],
        bias_sums[1],
        bias_sums[2],
        grad_attn[:, 3 * local_width :],
        small[:, experts + 1],
        small[:, :experts],
        small[:, experts],
        shared_grads[0],
        shared_grads[1],
        shared_grads[2],
        grad_expert_gate[None],
        grad_expert_up[None],
        grad_expert_down[None],
    )


def finish_kernel(
    hidden_out_in,
    hidden_grad_in,
    query_in,
    key_in,
    value_in,
    out_in,
    shared_in,
    gate_in,
    up_in,
    down_in,
    small_in,
    hidden_out,
    hidden_grad,
    query_out,
    key_out,
    value_out,
    out_out,
    s_gate_out,
    s_up_out,
    s_down_out,
    gate_out,
    up_out,
    down_out,
    router_out,
    shared_gate_out,
    ffn_gain_out,
    attn_gain_out,
):
    f32 = jnp.float32
    experts = router_out.shape[0]
    hidden_out[...] = hidden_out_in[...]
    hidden_grad[...] = hidden_grad_in[...]
    for source, target in (
        (query_in, query_out),
        (key_in, key_out),
        (value_in, value_out),
        (out_in, out_out),
        (gate_in, gate_out),
        (up_in, up_out),
        (down_in, down_out),
    ):
        target[...] = source[...].astype(f32)

    for which, target in enumerate((s_gate_out, s_up_out, s_down_out)):
        units = shared_in[:, which]
        target[...] = units.reshape(-1, units.shape[-1]).T.astype(f32)

    router_out[...] = small_in[0:experts]
    shared_gate_out[...] = small_in[experts : experts + 1]
    ffn_gain_out[...] = small_in[experts + 1 : experts + 2]
    attn_gain_out[...] = small_in[experts + 2 : experts + 3]


def finish_layer(hidden_out, hidden_grad, grads, shared, expert_grads, small, experts):
    steps = 2
    tok_rows, width = hidden_out.shape
    local_width = grads[0].shape[1]
    units = shared.shape[2]
    expert_units = expert_grads[0].shape[0]
    f32, bf16 = jnp.float32, jnp.bfloat16
    shape = jax.ShapeDtypeStruct
    row = lambda wide: pl.BlockSpec((tok_rows // steps, wide), lambda i: (i, 0))
    column = pl.BlockSpec((expert_units, width // steps), lambda i: (0, i))
    whole = lambda *dims: pl.BlockSpec(dims, lambda i: (0,) * len(dims))
    return pl.pallas_call(
        finish_kernel,
        grid=(steps,),
        in_specs=[row(width)] * 2
        + [row(local_width)] * 4
        + [pl.BlockSpec((8, 3, units, tok_rows // steps), lambda i: (0, 0, 0, i))]
        + [column] * 3
        + [whole(16, tok_rows)],
        out_specs=[row(width)] * 2
        + [row(local_width)] * 4
        + [pl.BlockSpec((tok_rows // steps, 8 * units), lambda i: (i, 0))] * 3
        + [column] * 3
        + [whole(experts, tok_rows)]
        + [whole(1, tok_rows)] * 3,
        out_shape=[shape((tok_rows, width), bf16)] * 2
        + [shape((tok_rows, local_width), f32)] * 4
        + [shape((tok_rows, 8 * units), f32)] * 3
        + [shape((expert_units, width), f32)] * 3
        + [shape((experts, tok_rows), f32)]
        + [shape((1, tok_rows), f32)] * 3,
        compiler_params=pltpu.CompilerParams(vmem_limit_bytes=63 * 2**20),
        cost_estimate=pl.CostEstimate(flops=0, bytes_accessed=26 * 2**20, transcendentals=0),
    )(hidden_out, hidden_grad, *grads, shared, *expert_grads, small)


def on_cube(
    hidden_in,
    out_grad,
    parents,
    routes,
    attn_gain,
    w_query,
    w_key,
    w_value,
    b_query,
    b_key,
    b_value,
    w_out,
    ffn_gain,
    w_router,
    shared_gate,
    shared_w_gate,
    shared_w_up,
    shared_w_down,
    expert_w_gate,
    expert_w_up,
    expert_w_down,
):
    tok_rows, model_width = hidden_in.shape
    devices, columns = lax.axis_size("dp"), lax.axis_size("tensor")
    place = lax.axis_index("dp")
    experts, top_count = w_router.shape[1], routes.shape[1]
    capacity = 5 * tok_rows * top_count // 4
    score_scale = HEAD_DIM ** (-0.5)
    bf16, f32 = jnp.bfloat16, jnp.float32
    expert_units = expert_w_gate.shape[2]
    shared_units = shared_w_gate.shape[1] // devices
    shared_pad = -(-shared_units // 128) * 128
    units = shared_pad + expert_units
    units_pad = -(-(units + experts + 1) // 128) * 128
    layout = (shared_units, shared_pad, expert_units, experts, units_pad)
    part_rows = tok_rows // columns

    powers = np.arange(0, HEAD_DIM, 2, dtype=np.float32) / np.float32(HEAD_DIM)
    freqs = np.float32(rope_base) ** -powers
    (
        residual,
        query_rot,
        key_path,
        value_path,
        log_total,
        attended,
        attn_normed,
        cosine,
        sine,
        hits_all,
        grad_all,
        shared_w,
    ) = front_layer(
        score_scale,
        shared_units,
        (
            parents,
            hidden_in,
            attn_gain[None, :],
            b_query,
            b_key,
            b_value,
            np.concatenate([freqs, freqs])[None, :],
            routes.T,
            out_grad.reshape(columns, part_rows, model_width),
            w_query,
            w_key,
            w_value,
            w_out,
            shared_w_gate,
            shared_w_up,
            shared_w_down,
        ),
    )
    (
        residual_grad,
        residual_low,
        ffn_part,
        grad_expert_gate,
        grad_expert_up,
        grad_expert_down,
        grad_shared,
        small,
    ) = ffn_layer(
        residual,
        ffn_gain[None, :],
        hits_all,
        grad_all.reshape(2, 2, 2, columns, part_rows, model_width),
        w_router.T,
        shared_gate[None, :],
        shared_w,
        (expert_w_gate[0].T, expert_w_up[0].T, expert_w_down[0].T),
        layout,
        capacity,
    )
    (
        hidden_out,
        hidden_in_grad,
        sum_query,
        sum_key,
        sum_value,
        sum_out,
        grad_shared,
        small,
        bias_sums,
    ) = back_layer(
        score_scale,
        experts + 2,
        (
            residual,
            residual_grad,
            residual_low,
            ffn_part,
            grad_shared,
            small,
            query_rot,
            key_path,
            value_path,
            parents,
            log_total,
            attended,
            attn_normed,
            hidden_in,
            attn_gain[None, :],
            cosine,
            sine,
            w_out,
            w_query,
            w_key,
            w_value,
        ),
    )
    bias_sums = lax.dynamic_slice_in_dim(
        bias_sums[: 3 * b_query.shape[0]].reshape(3, *b_query.shape),
        place * (HEAD_DIM // devices),
        HEAD_DIM // devices,
        2,
    )
    (
        hidden_out,
        hidden_in_grad,
        sum_query,
        sum_key,
        sum_value,
        sum_out,
        sum_s_gate,
        sum_s_up,
        sum_s_down,
        grad_expert_gate,
        grad_expert_up,
        grad_expert_down,
        sum_router,
        sum_shared_gate,
        sum_ffn_gain,
        sum_attn_gain,
    ) = finish_layer(
        hidden_out.reshape(tok_rows, model_width),
        hidden_in_grad.reshape(tok_rows, model_width),
        (sum_query, sum_key, sum_value, sum_out),
        grad_shared,
        (grad_expert_gate, grad_expert_up, grad_expert_down),
        small,
        experts,
    )
    return (
        hidden_out,
        hidden_in_grad,
        sum_attn_gain[0],
        sum_query,
        sum_key,
        sum_value,
        bias_sums[0],
        bias_sums[1],
        bias_sums[2],
        sum_out,
        sum_ffn_gain[0],
        sum_router.T,
        sum_shared_gate[0],
        sum_s_gate,
        sum_s_up,
        sum_s_down,
        grad_expert_gate.T[None],
        grad_expert_up.T[None],
        grad_expert_down.T[None],
    )


def on_device(*arrays):
    devices, columns = lax.axis_size("dp"), lax.axis_size("tensor")
    tok_rows, model_width = arrays[0].shape
    cube = devices == 8 and columns == 4 and tok_rows == SEG
    if cube and tok_rows * devices * model_width <= 2**22:
        return on_cube(*arrays)
    return on_slice(*arrays)


def solution(mesh):
    return jax.shard_map(
        on_device,
        mesh=mesh,
        in_specs=(
            P("dp", None),
            P("dp", None),
            P(),
            P("dp", None),
            P(),
            P(None, "tensor"),
            P(None, "tensor"),
            P(None, "tensor"),
            P("tensor", None),
            P("tensor", None),
            P("tensor", None),
            P(None, "tensor"),
            P(),
            P(),
            P(),
            P(None, "tensor"),
            P(None, "tensor"),
            P(None, "tensor"),
            P("dp", None, "tensor"),
            P("dp", None, "tensor"),
            P("dp", None, "tensor"),
        ),
        out_specs=(
            P("dp", None),
            P("dp", None),
            P("dp"),
            P("dp", "tensor"),
            P("dp", "tensor"),
            P("dp", "tensor"),
            P("tensor", "dp"),
            P("tensor", "dp"),
            P("tensor", "dp"),
            P("dp", "tensor"),
            P("dp"),
            P("dp", None),
            P("dp"),
            P("dp", "tensor"),
            P("dp", "tensor"),
            P("dp", "tensor"),
            P("dp", None, "tensor"),
            P("dp", None, "tensor"),
            P("dp", None, "tensor"),
        ),
        check_vma=False,
    )
```

```python
import functools

import jax
import jax.numpy as jnp
import numpy as np
from jax import lax
from jax.experimental import pallas as pl
from jax.experimental.pallas import tpu as pltpu
from jax.sharding import PartitionSpec as P

HEAD_DIM = 128
SEG = 256
MESH = pl.DeviceIdType.MESH


epsilon = 1e-06
rope_base = 1000000.0
highest = lax.Precision.HIGHEST


def product(left, right):
    return jnp.dot(left, right, preferred_element_type=jnp.float32)


def product_tn(left, right):
    return lax.dot_general(
        left, right, (((0,), (0,)), ((), ())), preferred_element_type=jnp.float32
    )


def product_nt(left, right):
    return lax.dot_general(
        left, right, (((1,), (1,)), ((), ())), preferred_element_type=jnp.float32
    )


def ancestry(parents):
    seg_count = parents.shape[0]
    labels = jnp.arange(seg_count, dtype=jnp.int32)

    def climb(level, carry):
        current, reach = carry
        upward = jnp.where(current >= 0, parents[jnp.maximum(current, 0)], -1)
        reach = jnp.maximum(reach, (upward[:, None] == labels[None, :]).astype(jnp.float32))
        return (upward, reach)

    start = (labels, jnp.eye(seg_count, dtype=jnp.float32))
    return lax.fori_loop(0, seg_count, climb, start)[1]


def rope_tables(positions):
    freqs = rope_base ** (-jnp.arange(0, HEAD_DIM, 2, dtype=jnp.float32) / HEAD_DIM)
    angles = positions[:, None] * freqs[None, :]
    angles = jnp.concatenate([angles, angles], 1)
    return (jnp.cos(angles)[:, None, :], jnp.sin(angles)[:, None, :])


def turn_heads(matrix, cosine, sine, sign_value):
    shaped = matrix.reshape(matrix.shape[0], matrix.shape[1] // HEAD_DIM, HEAD_DIM)
    half = HEAD_DIM // 2
    turned = jnp.concatenate([-shaped[..., half:], shaped[..., :half]], -1)
    return (shaped * cosine + sign_value * turned * sine).reshape(matrix.shape)


def norm_parts(values):
    scale_rows = lax.rsqrt(jnp.mean(values * values, 1, keepdims=True) + epsilon)
    return (scale_rows, values * scale_rows)


def norm_back(grad_rows, unit_rows, scale_rows, gain):
    unit_grad = grad_rows * gain
    return scale_rows * (unit_grad - unit_rows * jnp.mean(unit_grad * unit_rows, 1, keepdims=True))


LEVELS = 4


def gather_dp(rows):
    return lax.all_gather(rows, "dp", axis=0, tiled=True)


def gather_tensor(rows):
    return lax.all_gather(rows, "tensor", axis=0, tiled=True)


def gather_all(rows):
    return gather_dp(gather_tensor(rows))


def scatter_dp(rows):
    return lax.psum_scatter(rows, "dp", scatter_dimension=0, tiled=True)


def scatter_tensor(rows):
    return lax.psum_scatter(rows, "tensor", scatter_dimension=0, tiled=True)


def scatter_all(rows):
    return scatter_tensor(scatter_dp(rows))


def path_of(parents, segment):
    path = [segment]
    for _ in range(LEVELS - 1):
        last = path[-1]
        path.append(jnp.where(last >= 0, parents[jnp.maximum(last, 0)], -1))
    return jnp.stack(path)


def heads_of(matrix):
    return matrix.reshape(matrix.shape[0], -1, HEAD_DIM)


def attend_forward(query_rot, key_path, value_path, allowed, score_scale):
    scores = (
        jnp.einsum(
            "qhd,khd->hqk",
            heads_of(query_rot),
            heads_of(key_path),
            preferred_element_type=jnp.float32,
        )
        * score_scale
    )
    scores = jnp.where(allowed[None], scores, -jnp.inf)
    peak = jnp.max(scores, 2, keepdims=True)
    log_total = peak + jnp.log(jnp.sum(jnp.exp(scores - peak), 2, keepdims=True))
    weights = jnp.exp(scores - log_total).astype(jnp.bfloat16)
    attended = jnp.einsum(
        "hqk,khd->qhd", weights, heads_of(value_path), preferred_element_type=jnp.float32
    )
    return attended.reshape(query_rot.shape), log_total


def attend_backward(
    query_rot, key_path, value_path, allowed, log_total, attended_grad, score_scale
):
    query, key, value = heads_of(query_rot), heads_of(key_path), heads_of(value_path)
    grad = heads_of(attended_grad)
    scores = jnp.einsum("qhd,khd->hqk", query, key, preferred_element_type=jnp.float32)
    weights = jnp.exp(jnp.where(allowed[None], scores * score_scale, -jnp.inf) - log_total)
    weight_grad = jnp.einsum("qhd,khd->hqk", grad, value, preferred_element_type=jnp.float32)
    center = jnp.sum(weights * weight_grad, 2, keepdims=True)
    score_grad = (weights * (weight_grad - center)).astype(jnp.bfloat16)
    query_grad = (
        jnp.einsum("hqk,khd->qhd", score_grad, key, preferred_element_type=jnp.float32)
        * score_scale
    )
    key_grad = (
        jnp.einsum("hqk,qhd->khd", score_grad, query, preferred_element_type=jnp.float32)
        * score_scale
    )
    value_grad = jnp.einsum(
        "hqk,qhd->khd",
        weights.astype(jnp.bfloat16),
        grad,
        preferred_element_type=jnp.float32,
    )
    return (
        query_grad.reshape(query_rot.shape),
        key_grad.reshape(key_path.shape),
        value_grad.reshape(value_path.shape),
    )


def ffn_plain(attn_part, hidden_own, grad_own, ffn_gain, kept, out_all, w_pre, w_down, layout):
    _, shared_pad, expert_units, experts, units_pad = layout
    units = shared_pad + expert_units
    bf16, f32 = jnp.bfloat16, jnp.float32
    place, column = lax.axis_index("dp"), lax.axis_index("tensor")
    columns, part_rows = lax.axis_size("tensor"), hidden_own.shape[0]
    out_own = grad_own.astype(f32)
    residual = hidden_own.astype(f32) + scatter_tensor(attn_part).astype(f32)
    ffn_scale, ffn_unit = norm_parts(residual)
    ffn_normed = (ffn_unit * ffn_gain).astype(bf16)
    normed_all = gather_all(ffn_normed)

    pre = product(normed_all, w_pre)
    pre_gate, pre_up = pre[:, :units_pad], pre[:, units_pad:]
    logits = pre[:, units : units + experts]
    probs = jax.nn.softmax(logits, 1)
    shared_weight = jax.nn.sigmoid(pre[:, units + experts])
    own_expert = jnp.arange(experts, dtype=jnp.int32)[None, :] == place
    gate_own = jnp.sum(jnp.where(own_expert, probs * kept, 0.0), 1)
    lane = jnp.arange(units_pad)[None, :]
    weight = jnp.where(
        lane < shared_pad,
        shared_weight[:, None],
        jnp.where(lane < units, gate_own[:, None], 0.0),
    )
    down_back = product(out_all, w_down)
    sigmoid_gate = jax.nn.sigmoid(pre_gate)
    hidden = (pre_gate * sigmoid_gate * pre_up).astype(bf16).astype(f32)
    hidden_scaled = (hidden * weight).astype(bf16)
    hidden_grad = down_back * weight
    up_rows = (hidden_grad * pre_gate * sigmoid_gate).astype(bf16)
    gate_rows = (
        hidden_grad * pre_up * sigmoid_gate * (1.0 + pre_gate * (1.0 - sigmoid_gate))
    ).astype(bf16)
    both_rows = jnp.concatenate([gate_rows, up_rows], 1)
    dots = hidden * down_back
    gate_dot = jnp.sum(jnp.where((lane >= shared_pad) & (lane < units), dots, 0.0), 1)
    shared_dot = jnp.sum(jnp.where(lane < shared_pad, dots, 0.0), 1)
    dot_parts = jnp.concatenate(
        [jnp.where(own_expert, gate_dot[:, None] * kept, 0.0), shared_dot[:, None]], 1
    )
    ffn_part = product_nt(hidden_scaled, w_down).astype(bf16)
    normed_part = product_nt(both_rows, w_pre).astype(bf16)
    grad_pre = product_tn(normed_all, both_rows)
    grad_down = product_tn(out_all, hidden_scaled)

    dot_own = scatter_all(dot_parts)
    normed_own = scatter_all(normed_part).astype(f32)

    first = (place * columns + column) * part_rows
    own = lambda array: lax.dynamic_slice_in_dim(array, first, part_rows, 0)
    probs_own, shared_own = own(probs), own(shared_weight)
    prob_grad = dot_own[:, :experts]
    logit_grad = (
        probs_own * (prob_grad - jnp.sum(probs_own * prob_grad, 1, keepdims=True))
    ).astype(bf16)
    weight_logit_grad = (dot_own[:, experts] * shared_own * (1.0 - shared_own)).astype(bf16)
    side_grad = jnp.concatenate([logit_grad, weight_logit_grad[:, None]], 1)
    side_w = w_pre[:, units : units + experts + 1]
    normed_grad = normed_own + product_nt(side_grad, side_w)
    grad_side = product_tn(ffn_normed, side_grad)
    grad_ffn_gain = jnp.sum(normed_grad * ffn_unit, 0)
    residual_grad = out_own + norm_back(normed_grad, ffn_unit, ffn_scale, ffn_gain)
    expert = slice(shared_pad, units)
    expert_up = slice(units_pad + shared_pad, units_pad + units)
    grad_shared = jnp.stack(
        [
            grad_pre[:, : shared_pad],
            grad_pre[:, units_pad : units_pad + shared_pad],
            grad_down[:, : shared_pad],
        ]
    ).astype(bf16)
    return (
        residual,
        residual_grad,
        residual_grad.astype(bf16),
        ffn_part,
        grad_pre[:, expert],
        grad_pre[:, expert_up],
        grad_down[:, expert],
        grad_shared,
        grad_side,
        grad_ffn_gain,
    )


def flip(bit):
    return 1 - bit


def other(index, step):
    result, place = index, 1
    while place <= step:
        if step & place:
            result = result + place - 2 * place * ((index // place) % 2)
        place *= 2
    return result


def ffn_kernel(
    units,
    residual_ref,
    gain_ref,
    hits_ref,
    grad_all_ref,
    router_ref,
    shared_gate_ref,
    shared_w_ref,
    e_gate_w_ref,
    e_up_w_ref,
    e_down_w_ref,
    res_grad_ref,
    res_low_ref,
    ffn_part_ref,
    e_gate_ref,
    e_up_ref,
    e_down_ref,
    shared_ref,
    small_ref,
    rows_all,
    dy_all,
    w_pre,
    w_down,
    both_all,
    scaled_all,
    scaled_now,
    down_back_all,
    sums,
    got_core,
    got_x1,
    got_y1,
    got_y2,
    got_x2,
    got_z,
    kept_ref,
    out_send,
    out_own,
    got_out,
    tile_gate,
    tile_up,
    tile_down,
    tile_shared,
    load_sems,
    store_sems,
    tile_sems,
    zs,
    links,
    cores,
    rs_core,
    rs_links,
    rs_z,
    rs_out,
):
    shared_units, shared_pad, expert_units, experts, unit_pad, half, wide, capacity = units
    bf16, f32 = jnp.bfloat16, jnp.float32
    place, column = lax.axis_index("dp"), lax.axis_index("tensor")
    core, east, north = place % 2, (place // 2) % 2, place // 4
    rows, width = residual_ref.shape
    sibling = {"dp": other(place, 1)}
    x_side = {"dp": other(place, 2)}
    y_side = {"dp": other(place, 4)}
    levels = [{"tensor": other(column, k)} for k in range(4)]

    def level_of(k):
        low_i, high_i, low_k, high_k = column % 2, column // 2, k % 2, k // 2
        return (low_i + low_k - 2 * low_i * low_k) + 2 * (high_i + high_k - 2 * high_i * high_k)

    def remote(src, dst, sems, which, device):
        return pltpu.make_async_remote_copy(
            src_ref=src,
            dst_ref=dst,
            send_sem=sems.at[(0, *which)],
            recv_sem=sems.at[(1, *which)],
            device_id=device,
            device_id_type=MESH,
        )

    expert_first, side_first = shared_pad, shared_pad + expert_units
    loads = []
    for j, (target, first, ref) in enumerate(
        ((w_pre, 0, e_gate_w_ref), (w_pre, unit_pad, e_up_w_ref), (w_down, 0, e_down_w_ref))
    ):
        own_rows = pl.ds(first + expert_first, expert_units)
        shared_rows = pl.ds(first, shared_units)
        loads += [
            pltpu.make_async_copy(ref, target.at[own_rows], load_sems.at[8 + 2 * j]),
            pltpu.make_async_copy(
                shared_w_ref.at[j], target.at[shared_rows], load_sems.at[9 + 2 * j]
            ),
        ]
    for copy in loads:
        copy.start()
    for target, first in ((w_pre, 0), (w_pre, unit_pad), (w_down, 0)):
        gap = shared_pad - shared_units
        target[first + shared_units : first + shared_pad, :] = jnp.zeros((gap, width), bf16)
        rest = unit_pad - side_first
        target[first + side_first : first + unit_pad, :] = jnp.zeros((rest, width), bf16)
    side_rows = [router_ref[...].astype(f32), shared_gate_ref[...].astype(f32)]
    side_rows.append(jnp.zeros((16 - experts - 1, width), f32))
    w_pre[side_first : side_first + 16, :] = jnp.concatenate(side_rows, 0).astype(bf16)

    def load_grad(c, z):
        return pltpu.make_async_copy(
            grad_all_ref.at[:, :, c, z], dy_all.at[z, c], load_sems.at[c * 4 + z]
        )

    for c in range(2):
        for z in range(4):
            load_grad(c, z).start()

    barrier = pltpu.get_barrier_semaphore()
    partners = [sibling, x_side, y_side] + levels[1:]
    for partner in partners:
        pl.semaphore_signal(barrier, inc=1, device_id=partner, device_id_type=MESH)
    pl.semaphore_wait(barrier, len(partners))

    residual = residual_ref[...]
    scale_rows = lax.rsqrt(jnp.mean(residual * residual, 1, keepdims=True) + epsilon)
    normed = (residual * scale_rows * gain_ref[...]).astype(bf16)
    rows_all[column, core, north, east] = normed

    own_slot = rows_all.at[column, core, north, east]

    def z_copy(k):
        return remote(own_slot, own_slot, zs, (k,), levels[k])

    def block(k, c, y, x, cols=slice(None)):
        return rows_all.at[level_of(k), c, y, x, :, cols]

    first_half, second_half = pl.ds(0, half), pl.ds(half, width - half)

    def direct_copies(k):
        own = block(k, core, north, east)
        return [
            remote(own, own, links, (0, k), x_side),
            remote(own, own, links, (1, k), y_side),
            remote(own, own, cores, (0, k), sibling),
        ]

    def forward_copies(k):
        from_x = block(k, core, north, flip(east), first_half)
        from_y = block(k, core, flip(north), east, second_half)
        all_x = block(k, core, north, flip(east))
        all_y = block(k, core, flip(north), east)
        return [
            remote(from_x, from_x, links, (2, k), y_side),
            remote(from_y, from_y, links, (3, k), x_side),
            remote(all_x, all_x, cores, (1, k), sibling),
            remote(all_y, all_y, cores, (2, k), sibling),
        ]

    def corner_copy(k):
        corner = block(k, core, flip(north), flip(east))
        return remote(corner, corner, cores, (3, k), sibling)

    def start_direct(k):
        for copy in direct_copies(k):
            copy.start()

    def start_forward(k):
        for copy in direct_copies(k)[:2]:
            copy.wait_recv()
        for copy in forward_copies(k):
            copy.start()

    def start_corner(k):
        for copy in forward_copies(k)[:2]:
            copy.wait_recv()
        corner_copy(k).start()

    def finish_gather(k):
        direct_copies(k)[2].wait_recv()
        for copy in forward_copies(k)[2:]:
            copy.wait_recv()
        corner_copy(k).wait_recv()

    def core_copy(k):
        return remote(sums.at[k, flip(core)], got_core.at[k % 2], rs_core, (k,), sibling)

    left, right = pl.ds(0, half), pl.ds(half, wide - half)

    def first_copies(k):
        return [
            remote(
                sums.at[k, core, :, flip(east), :, left],
                got_x1.at[k % 2],
                rs_links, (0, k),
                x_side,
            ),
            remote(
                sums.at[k, core, flip(north), :, :, right],
                got_y1.at[k % 2],
                rs_links, (1, k),
                y_side,
            ),
        ]

    def second_copies(k):
        return [
            remote(
                sums.at[k, core, flip(north), east, :, left],
                got_y2.at[k % 2],
                rs_links, (2, k),
                y_side,
            ),
            remote(
                sums.at[k, core, north, flip(east), :, right],
                got_x2.at[k % 2],
                rs_links, (3, k),
                x_side,
            ),
        ]

    def level_copy(k, device):
        return remote(sums.at[k, core, north, east], got_z.at[k], rs_z, (k,), device)

    def add(ref, value):
        ref[...] = (ref[...].astype(f32) + value.astype(f32)).astype(bf16)

    def after_core(k):
        core_copy(k).wait_recv()
        for y in range(2):
            for x in range(2):
                add(sums.at[k, core, y, x], got_core[k % 2, y, x])
        for copy in first_copies(k):
            copy.start()

    def after_first(k):
        x_copy, y_copy = first_copies(k)
        x_copy.wait_recv()
        for y in range(2):
            add(sums.at[k, core, y, east, :, left], got_x1[k % 2, y])
        y_copy.wait_recv()
        for x in range(2):
            add(sums.at[k, core, north, x, :, right], got_y1[k % 2, x])
        for copy in second_copies(k):
            copy.start()

    def after_second(k):
        y_copy, x_copy = second_copies(k)
        y_copy.wait_recv()
        add(sums.at[k, core, north, east, :, left], got_y2[k % 2])
        x_copy.wait_recv()
        add(sums.at[k, core, north, east, :, right], got_x2[k % 2])
        for level in range(1, 4):

            @pl.when(k == level)
            def _():
                level_copy(k, levels[level]).start()

    start_direct(0)
    for k in (1, 2, 3):
        z_copy(k).start()

    tokens_dev = 4 * rows
    expert_id = lax.broadcasted_iota(jnp.int32, hits_ref.shape, 1)
    hits = jnp.sum(jnp.where(expert_id == place, hits_ref[...], 0.0), 1)
    earlier = lax.broadcasted_iota(jnp.int32, (tokens_dev, tokens_dev), 0)
    later = lax.broadcasted_iota(jnp.int32, (tokens_dev, tokens_dev), 1)
    slots = product(hits.astype(bf16), (earlier < later).astype(bf16))
    counts = jnp.sum(hits, 1, keepdims=True)
    counts_wide = jnp.broadcast_to(counts, (8, 128))
    order_row = lax.broadcasted_iota(jnp.int32, (8, 8), 0)
    order_col = lax.broadcasted_iota(jnp.int32, (8, 8), 1)
    before = lax.dot_general(
        (order_col < order_row).astype(f32),
        counts_wide,
        (((1,), (0,)), ((), ())),
        precision=highest,
        preferred_element_type=f32,
    )
    kept = jnp.where(slots + before[:, :1] < capacity, hits, 0.0).astype(bf16)
    eye = (
        lax.broadcasted_iota(jnp.int32, (8, 128), 0)
        == lax.broadcasted_iota(jnp.int32, (8, 128), 1)
    ).astype(bf16)
    kept_columns = product_tn(kept, eye)
    for d in range(8):
        y, x, c = d // 4, (d // 2) % 2, d % 2
        for z in range(4):
            first = (2 * y + x) * rows
            kept_ref[z, c, first : first + rows, :] = kept_columns[
                z * rows : (z + 1) * rows, d : d + 1
            ]

    for copy in loads:
        copy.wait()
    for c in range(2):
        for z in range(4):
            load_grad(c, z).wait()

    def back_down(i, carry):
        z, c = i // 2, i % 2
        dy_block = dy_all[z, c].reshape(4 * rows, width)
        down_back_all[z, c] = product_nt(dy_block, w_down[...]).astype(bf16)
        return carry

    lax.fori_loop(0, 3, back_down, 0)
    start_forward(0)
    z_copy(1).wait_recv()
    start_direct(1)
    lax.fori_loop(3, 5, back_down, 0)
    start_corner(0)
    lax.fori_loop(5, 8, back_down, 0)

    last = unit_pad - 128
    lane = lax.broadcasted_iota(jnp.int32, (1, 128), 1)
    first_lane = shared_pad + expert_units - last
    in_router = (lane >= first_lane) & (lane < first_lane + experts)
    is_shared = lane == first_lane + experts

    def routing(logit_block):
        top = jnp.max(jnp.where(in_router, logit_block, -jnp.inf), 1, keepdims=True)
        powers = jnp.where(in_router, jnp.exp(jnp.where(in_router, logit_block - top, 0.0)), 0.0)
        probs = powers / jnp.sum(powers, 1, keepdims=True)
        shared_logit = jnp.sum(jnp.where(is_shared, logit_block, 0.0), 1, keepdims=True)
        return probs, jax.nn.sigmoid(shared_logit)

    def compute(k, c):
        z = level_of(k)
        row_block = rows_all[z, c].reshape(4 * rows, width)
        pre_gate = product_nt(row_block, w_pre[:unit_pad])
        pre_up = product_nt(row_block, w_pre[unit_pad:])
        down_back = down_back_all[z, c].astype(f32)
        probs, shared_weight = routing(pre_gate[:, last:])
        kept = kept_ref[z, c]
        gate = (
            jnp.sum(jnp.where(lane == first_lane + place, probs, 0.0), 1, keepdims=True) * kept
        )
        dots, scaled, gate_rows, up_rows = [], [], [], []
        for begin, end, weight in (
            (0, shared_pad, shared_weight),
            (shared_pad, unit_pad, gate),
        ):
            cols = slice(begin, end)
            a, b, back = pre_gate[:, cols], pre_up[:, cols], down_back[:, cols]
            sig = jax.nn.sigmoid(a)
            silu = a * sig
            hidden = (silu * b).astype(bf16).astype(f32)
            dots.append(jnp.sum(hidden * back, 1, keepdims=True))
            scaled.append((hidden * weight).astype(bf16))
            grad = back * weight
            up_rows.append((grad * silu).astype(bf16))
            gate_rows.append((grad * b * sig * (1.0 + a * (1.0 - sig))).astype(bf16))
        both = jnp.concatenate(gate_rows + up_rows, 1)
        own_scaled = jnp.concatenate(scaled, 1)
        first_token = pl.multiple_of((2 * z + c) * 4 * rows, 4 * rows)
        both_all[:, pl.ds(first_token, 4 * rows)] = both.T
        scaled_all[:, pl.ds(first_token, 4 * rows)] = own_scaled.T
        scaled_now[c] = own_scaled
        dot_block = jnp.where(is_shared, dots[0], 0.0) + jnp.where(
            lane == first_lane + place, dots[1] * kept, 0.0
        )
        normed_grad = product(both, w_pre[...]).astype(bf16)
        sums[k, c, :, :, :, 0:width] = normed_grad.reshape(2, 2, rows, width)
        sums[k, c, :, :, :, width:wide] = dot_block.astype(bf16).reshape(2, 2, rows, wide - width)

    def store_chunk(k):
        return pltpu.make_async_copy(out_own, ffn_part_ref.at[level_of(k)], store_sems.at[0])

    def out_core_copy(k):
        return remote(out_send, got_out.at[k % 2], rs_out, (k,), sibling)

    def chunk(k, carry):
        @pl.when(k < 3)
        def _():
            start_forward(k + 1)

        @pl.when(k < 2)
        def _():
            for level in (2, 3):

                @pl.when(k + 2 == level)
                def _():
                    z_copy(level).wait_recv()

            start_direct(k + 2)

        finish_gather(k)
        def rows_of(i, carry):
            compute(k, (i + 1 + core) % 2)

            @pl.when(i == 0)
            def _():
                core_copy(k).start()

            return carry

        lax.fori_loop(0, 2, rows_of, 0)

        @pl.when(k >= 1)
        def _():
            after_first(k - 1)
            store_chunk(k - 1).wait()
            out_core_copy(k - 1).wait_send()

        def outputs(i, carry):
            part = product(scaled_now[(i + 1 + core) % 2], w_down[...]).astype(bf16)

            @pl.when(i == 0)
            def _():
                out_send[...] = part.reshape(2, 2, rows, width)
                out_core_copy(k).start()

            @pl.when(i == 1)
            def _():
                out_own[...] = part.reshape(2, 2, rows, width)

            return carry

        lax.fori_loop(0, 2, outputs, 0)

        @pl.when(k < 3)
        def _():
            start_corner(k + 1)

        after_core(k)
        out_core_copy(k).wait_recv()
        for y in range(2):
            for x in range(2):
                add(out_own.at[y, x], got_out[k % 2, y, x])
        store_chunk(k).start()

        @pl.when(k >= 1)
        def _():
            after_second(k - 1)

        return carry

    lax.fori_loop(0, 4, chunk, 0)
    store_chunk(3).wait()
    out_core_copy(3).wait_send()

    tile = tile_gate.shape[2]
    tiles = width // tile

    def tile_copies(i, slot):
        window = pl.ds(pl.multiple_of(i * tile, tile), tile)
        return [
            pltpu.make_async_copy(tile_gate.at[slot], e_gate_ref.at[:, window], tile_sems.at[slot, 0]),
            pltpu.make_async_copy(tile_up.at[slot], e_up_ref.at[:, window], tile_sems.at[slot, 1]),
            pltpu.make_async_copy(tile_down.at[slot], e_down_ref.at[:, window], tile_sems.at[slot, 2]),
            pltpu.make_async_copy(
                tile_shared.at[slot], shared_ref.at[i], tile_sems.at[slot, 3]
            ),
        ]

    tokens = rows * 32

    def weight_tile(i, carry):
        slot = i % 2

        @pl.when(i >= 2)
        def _():
            for copy in tile_copies(i - 2, slot):
                copy.wait()

        window = pl.ds(pl.multiple_of(i * tile, tile), tile)
        expert = slice(shared_pad, shared_pad + expert_units)
        row_tile = rows_all[:, :, :, :, :, window].reshape(tokens, tile)
        for j, (first, target) in enumerate(((0, tile_gate), (unit_pad, tile_up))):
            grad = product(both_all[first : first + unit_pad], row_tile).astype(bf16)
            target[slot] = grad[expert]
            tile_shared[slot, j] = grad[:shared_units]
        dy_tile = dy_all[:, :, :, :, :, window].reshape(tokens, tile)
        grad = product(scaled_all[...], dy_tile).astype(bf16)
        tile_down[slot] = grad[expert]
        tile_shared[slot, 2] = grad[:shared_units]
        for copy in tile_copies(i, slot):
            copy.start()

        @pl.when(i == 1)
        def _():
            after_first(3)

        @pl.when(i == 3)
        def _():
            after_second(3)

        return carry

    lax.fori_loop(0, tiles, weight_tile, 0)
    for i in (tiles - 2, tiles - 1):
        for copy in tile_copies(i, i % 2):
            copy.wait()

    total = sums[0, core, north, east].astype(f32)
    for k in (1, 2, 3):
        level_copy(k, levels[k]).wait_recv()
        total = total + got_z[k].astype(f32)
    dots = total[:, width:]
    unit = residual_ref[...] * scale_rows
    own_normed = rows_all[column, core, north, east]
    side_w = w_pre[last:unit_pad]
    probs, shared_weight = routing(product_nt(own_normed, side_w))
    router_dots = jnp.where(in_router, dots, 0.0)
    center = jnp.sum(probs * router_dots, 1, keepdims=True)
    side = jnp.where(in_router, probs * (router_dots - center), 0.0) + jnp.where(
        is_shared, dots * shared_weight * (1.0 - shared_weight), 0.0
    )
    side = side.astype(bf16)
    normed_grad = total[:, :width] + product(side, side_w)
    side_rows = product_tn(side, own_normed)
    small_ref[...] = side_rows[first_lane : first_lane + small_ref.shape[0]]
    small_ref[experts + 1 : experts + 2, :] = jnp.sum(normed_grad * unit, 0, keepdims=True)
    own_grad = dy_all[column, core, north, east].astype(f32)
    grad_f = own_grad + norm_back(normed_grad, unit, scale_rows, gain_ref[...])
    res_grad_ref[...] = grad_f
    res_low_ref[...] = grad_f.astype(bf16)

    for k in (1, 2, 3):
        z_copy(k).wait_send()
        level_copy(k, levels[k]).wait_send()
    for k in range(4):
        for copy in direct_copies(k) + forward_copies(k) + [corner_copy(k), core_copy(k)]:
            copy.wait_send()
        for copy in first_copies(k) + second_copies(k):
            copy.wait_send()


def ffn_layer(
    residual, ffn_gain, hits, grad_all, router, shared_gate, shared_w, expert_w, layout, capacity
):
    shared_units, shared_pad, expert_units, experts, unit_pad = layout
    rows, width = residual.shape
    bf16, f32 = jnp.bfloat16, jnp.float32
    half = width // 2
    wide = width + 128
    tile = 256
    shape = jax.ShapeDtypeStruct
    vmem, anywhere = pl.BlockSpec(memory_space=pltpu.VMEM), pl.BlockSpec(memory_space=pl.ANY)
    dma = pltpu.SemaphoreType.DMA
    cost = pl.CostEstimate(
        flops=2 * 24 * 2048 * 2048 * 256, bytes_accessed=60 * 2**20, transcendentals=3 * 2**20
    )
    return pl.pallas_call(
        functools.partial(
            ffn_kernel,
            (shared_units, shared_pad, expert_units, experts, unit_pad, half, wide, capacity),
        ),
        out_shape=[
            shape((rows, width), f32),
            shape((rows, width), bf16),
            shape((4, 2, 2, rows, width), bf16),
            shape((expert_units, width), bf16),
            shape((expert_units, width), bf16),
            shape((expert_units, width), bf16),
            shape((width // tile, 3, shared_units, tile), bf16),
            shape((16, width), f32),
        ],
        in_specs=[vmem, vmem, vmem, anywhere, vmem, vmem] + [anywhere] * 4,
        out_specs=[vmem, vmem] + [anywhere] * 5 + [vmem],
        scratch_shapes=[
            pltpu.VMEM((4, 2, 2, 2, rows, width), bf16),
            pltpu.VMEM((4, 2, 2, 2, rows, width), bf16),
            pltpu.VMEM((2 * unit_pad, width), bf16),
            pltpu.VMEM((unit_pad, width), bf16),
            pltpu.VMEM((2 * unit_pad, 32 * rows), bf16),
            pltpu.VMEM((unit_pad, 32 * rows), bf16),
            pltpu.VMEM((2, 4 * rows, unit_pad), bf16),
            pltpu.VMEM((4, 2, 4 * rows, unit_pad), bf16),
            pltpu.VMEM((4, 2, 2, 2, rows, wide), bf16),
            pltpu.VMEM((2, 2, 2, rows, wide), bf16),
            pltpu.VMEM((2, 2, rows, half), bf16),
            pltpu.VMEM((2, 2, rows, wide - half), bf16),
            pltpu.VMEM((2, rows, half), bf16),
            pltpu.VMEM((2, rows, wide - half), bf16),
            pltpu.VMEM((4, rows, wide), bf16),
            pltpu.VMEM((4, 2, 4 * rows, 1), f32),
            pltpu.VMEM((2, 2, rows, width), bf16),
            pltpu.VMEM((2, 2, rows, width), bf16),
            pltpu.VMEM((2, 2, 2, rows, width), bf16),
            pltpu.VMEM((2, expert_units, tile), bf16),
            pltpu.VMEM((2, expert_units, tile), bf16),
            pltpu.VMEM((2, expert_units, tile), bf16),
            pltpu.VMEM((2, 3, shared_units, tile), bf16),
            dma((14,)),
            dma((2,)),
            dma((2, 4)),
            dma((2, 4)),
            dma((2, 4, 4)),
            dma((2, 4, 4)),
            dma((2, 4)),
            dma((2, 4, 4)),
            dma((2, 4)),
            dma((2, 4)),
        ],
        compiler_params=pltpu.CompilerParams(
            collective_id=0, has_side_effects=True, vmem_limit_bytes=63 * 2**20
        ),
        cost_estimate=cost,
    )(residual, ffn_gain, hits, grad_all, router, shared_gate, shared_w, *expert_w)


def path_scalars(parents_ref, segment):
    path = [segment]
    for _ in range(LEVELS - 1):
        last = path[-1]
        parent = parents_ref[jnp.maximum(last, 0)]
        path.append(jnp.where(last >= 0, parent, -1))
    return path


class Line:
    def __init__(self, sems):
        self.sems = sems
        self.column = lax.axis_index("tensor")
        self.levels = [{"tensor": other(self.column, k)} for k in range(4)]
        self.outer = (self.column % 3) == 0
        self.inner = (self.column % 3) != 0

    def remote(self, src, dst, send, receive, device):
        return pltpu.make_async_remote_copy(
            src_ref=src,
            dst_ref=dst,
            send_sem=self.sems.at[0, send],
            recv_sem=self.sems.at[1, receive],
            device_id=device,
            device_id_type=MESH,
        )


class LineGather(Line):
    def __init__(self, slot, sems):
        super().__init__(sems)
        self.slot = slot

    def own(self, k):
        ref = self.slot(self.column)
        return self.remote(ref, ref, k, k, self.levels[k])

    def passed(self):
        ref = self.slot(other(self.column, 2))
        return self.remote(ref, ref, 0, 3, self.levels[1])

    def start(self):
        self.own(2).start()
        self.own(1).start()

        @pl.when(self.inner)
        def _():
            self.own(3).start()

    def forward(self):
        self.own(2).wait_recv()

        @pl.when(self.inner)
        def _():
            self.passed().start()

    def finish(self):
        self.own(1).wait_recv()
        self.own(3).wait_recv()

    def wait_sends(self):
        self.own(1).wait_send()
        self.own(2).wait_send()

        @pl.when(self.inner)
        def _():
            self.own(3).wait_send()
            self.passed().wait_send()


class LineSum(Line):
    def __init__(self, part, got, sems):
        super().__init__(sems)
        self.part, self.got = part, got

    def own(self, k):
        part = self.part(other(self.column, k))
        return self.remote(part, self.got.at[k], k, k, self.levels[k])

    def passed(self):
        part = self.part(other(self.column, 3))
        return self.remote(part, self.got.at[0], 0, 0, self.levels[1])

    def start(self):
        @pl.when(self.outer)
        def _():
            self.passed().start()
            self.own(2).start()
            self.got[3] = jnp.zeros(self.got.shape[1:], self.got.dtype)

        @pl.when(self.inner)
        def _():
            self.own(3).start()

        self.own(1).start()

    def forward(self):
        @pl.when(self.inner)
        def _():
            self.passed().wait_recv()
            part = self.part(other(self.column, 2))
            total = part[...].astype(jnp.float32) + self.got[0].astype(jnp.float32)
            part[...] = total.astype(part.dtype)
            self.own(2).start()

    def finish(self):
        self.own(1).wait_recv()
        self.own(2).wait_recv()

        @pl.when(self.inner)
        def _():
            self.own(3).wait_recv()

        total = self.part(self.column)[...].astype(jnp.float32)
        for k in (1, 2, 3):
            total = total + self.got[k].astype(jnp.float32)
        return total

    def wait_sends(self):
        self.own(1).wait_send()
        self.own(2).wait_send()

        @pl.when(self.outer)
        def _():
            self.passed().wait_send()

        @pl.when(self.inner)
        def _():
            self.own(3).wait_send()


class PlaneGather:
    def __init__(self, block, width, link_sems, core_sems):
        self.block, self.link_sems, self.core_sems = block, link_sems, core_sems
        place = lax.axis_index("dp")
        self.x, self.y, self.corner = other(place, 2), other(place, 4), other(place, 6)
        self.place = place
        self.x_side, self.y_side = {"dp": self.x}, {"dp": self.y}
        self.sibling = {"dp": other(place, 1)}
        self.halves = (pl.ds(0, width // 2), pl.ds(width // 2, width - width // 2))

    def copy(self, ref, sems, which, device):
        return pltpu.make_async_remote_copy(
            src_ref=ref,
            dst_ref=ref,
            send_sem=sems.at[0, which],
            recv_sem=sems.at[1, which],
            device_id=device,
            device_id_type=MESH,
        )

    def direct(self):
        own = self.block(self.place)
        return [
            self.copy(own, self.link_sems, 0, self.x_side),
            self.copy(own, self.link_sems, 1, self.y_side),
            self.copy(own, self.core_sems, 0, self.sibling),
        ]

    def forward(self):
        return [
            self.copy(self.block(self.x, self.halves[0]), self.link_sems, 2, self.y_side),
            self.copy(self.block(self.y, self.halves[1]), self.link_sems, 3, self.x_side),
            self.copy(self.block(self.x), self.core_sems, 1, self.sibling),
            self.copy(self.block(self.y), self.core_sems, 2, self.sibling),
        ]

    def last(self):
        return self.copy(self.block(self.corner), self.core_sems, 3, self.sibling)

    def start(self):
        for copy in self.direct():
            copy.start()

    def start_forward(self):
        for copy in self.direct()[:2]:
            copy.wait_recv()
        for copy in self.forward():
            copy.start()

    def start_last(self):
        for copy in self.forward()[:2]:
            copy.wait_recv()
        self.last().start()

    def finish(self):
        self.direct()[2].wait_recv()
        for copy in self.forward()[2:]:
            copy.wait_recv()
        self.last().wait_recv()

    def wait_sends(self):
        for copy in self.direct() + self.forward() + [self.last()]:
            copy.wait_send()


def turn(values, cosine, sine):
    heads = []
    for begin in range(0, values.shape[1], HEAD_DIM):
        head = values[:, begin : begin + HEAD_DIM]
        heads.append(head * cosine + pltpu.roll(head, HEAD_DIM // 2, 1) * sine)
    return jnp.concatenate(heads, 1)


def front_kernel(
    score_scale,
    shared_units,
    parents_ref,
    hidden_ref,
    gain_ref,
    b_query_ref,
    b_key_ref,
    b_value_ref,
    freqs_ref,
    routes_ref,
    out_grad_ref,
    w_query_ref,
    w_key_ref,
    w_value_ref,
    w_out_ref,
    s_gate_ref,
    s_up_ref,
    s_down_ref,
    residual_ref,
    query_ref,
    key_out,
    value_out,
    log_total_ref,
    attended_ref,
    normed_out,
    cosine_ref,
    sine_ref,
    hits_all_ref,
    grad_all_ref,
    shared_ref,
    weights,
    kv_all,
    hits_all,
    part_send,
    part_z,
    s_tiles,
    t_tiles,
    key_ref,
    value_ref,
    normed_ref,
    load_sems,
    tile_sems,
    store_sems,
    hit_sems,
    part_sems,
    kv_links,
    kv_cores,
    head_links,
    head_cores,
    tail_links,
    tail_cores,
):
    bf16, f32 = jnp.bfloat16, jnp.float32
    place, column = lax.axis_index("dp"), lax.axis_index("tensor")
    tok_rows, width = hidden_ref.shape
    rows = tok_rows // 4
    local_width = w_query_ref.shape[1]
    levels = [{"tensor": other(column, k)} for k in range(4)]
    peers = [{"dp": other(place, j)} for j in range(8)]

    loads = [
        pltpu.make_async_copy(ref, weights.at[i], load_sems.at[i])
        for i, ref in enumerate((w_query_ref, w_key_ref, w_value_ref, w_out_ref))
    ]
    own_grad = pltpu.make_async_copy(out_grad_ref, grad_all_ref.at[place], load_sems.at[4])
    for copy in loads:
        copy.start()
    own_grad.start()
    expert_id = lax.broadcasted_iota(jnp.int32, hits_all.shape[1:], 0)
    hits = jnp.zeros(hits_all.shape[1:], f32)
    for choice in range(routes_ref.shape[0]):
        hits = hits + jnp.where(expert_id == routes_ref[choice : choice + 1, :], 1.0, 0.0)
    hits_all[place] = hits

    barrier = pltpu.get_barrier_semaphore()
    partners = peers[1:] + levels[1:]
    for partner in partners:
        pl.semaphore_signal(barrier, inc=1, device_id=partner, device_id_type=MESH)
    pl.semaphore_wait(barrier, len(partners))

    def grad_block(first, count):
        def block(d, cols=slice(None)):
            return grad_all_ref.at[d, pl.ds(first, count), :, cols]

        return block

    head_gather = PlaneGather(grad_block(0, 1), width, head_links, head_cores)
    tail_gather = PlaneGather(grad_block(1, 3), width, tail_links, tail_cores)
    kv_gather = PlaneGather(
        lambda d, cols=slice(None): kv_all.at[d, :, cols], 2 * local_width, kv_links, kv_cores
    )
    own_grad.wait()
    head_gather.start()

    def hit_copy(j):
        return pltpu.make_async_remote_copy(
            src_ref=hits_all.at[place],
            dst_ref=hits_all.at[place],
            send_sem=hit_sems.at[0, j],
            recv_sem=hit_sems.at[1, j],
            device_id=peers[j],
            device_id_type=MESH,
        )

    for j in range(1, 8):
        hit_copy(j).start()

    def row_of(ref):
        return jnp.concatenate([ref[h : h + 1, :] for h in range(ref.shape[0])], 1)

    path = path_scalars(parents_ref, place)
    depth = jnp.float32(-1.0)
    for segment in path:
        depth = depth + jnp.where(segment >= 0, 1.0, 0.0)
    row_ids = lax.broadcasted_iota(jnp.int32, (tok_rows, HEAD_DIM), 0).astype(f32)
    lane = lax.broadcasted_iota(jnp.int32, (tok_rows, HEAD_DIM), 1)
    angles = (depth * SEG + row_ids) * freqs_ref[...]
    cosine = jnp.cos(angles)
    sine = jnp.where(lane < HEAD_DIM // 2, -1.0, 1.0) * jnp.sin(angles)
    cosine_ref[...] = cosine
    sine_ref[...] = sine
    hidden_f = hidden_ref[...].astype(f32)
    scale_rows = lax.rsqrt(jnp.mean(hidden_f * hidden_f, 1, keepdims=True) + epsilon)
    normed_ref[...] = (hidden_f * scale_rows * gain_ref[...]).astype(bf16)
    results = [
        pltpu.make_async_copy(source, target, load_sems.at[5 + i])
        for i, (source, target) in enumerate(
            ((normed_ref, normed_out), (key_ref, key_out), (value_ref, value_out))
        )
    ]
    results[0].start()
    for copy in loads[1:3]:
        copy.wait()
    key = product(normed_ref[...], weights[1]) + row_of(b_key_ref)
    kv_all[place, :, :local_width] = turn(key, cosine, sine).astype(bf16)
    value = product(normed_ref[...], weights[2]) + row_of(b_value_ref)
    kv_all[place, :, local_width:] = value.astype(bf16)
    kv_gather.start()
    loads[0].wait()
    query = product(normed_ref[...], weights[0]) + row_of(b_query_ref)
    query_ref[...] = turn(query, cosine, sine).astype(bf16)

    tile, span = s_tiles.shape[2:]
    shared_first = place * shared_units
    shared_base = jnp.minimum(shared_first // 128 * 128, s_gate_ref.shape[1] - span)
    shared_skip = shared_first - shared_base

    def tile_loads(i, slot):
        window = pl.ds(pl.multiple_of(i * tile, tile), tile)
        columns = pl.ds(pl.multiple_of(shared_base, 128), span)
        return [
            pltpu.make_async_copy(
                ref.at[window, columns], s_tiles.at[slot, j], tile_sems.at[slot, j]
            )
            for j, ref in enumerate((s_gate_ref, s_up_ref, s_down_ref))
        ]

    def tile_stores(i, slot):
        window = pl.ds(pl.multiple_of(i * tile, tile), tile)
        units = pl.ds(pl.multiple_of(shared_skip, 16), shared_units)
        return [
            pltpu.make_async_copy(
                t_tiles.at[slot, j, units], shared_ref.at[j, :, window], store_sems.at[slot, j]
            )
            for j in range(3)
        ]

    tiles = width // tile

    def pack(i, carry):
        slot = i % 2

        @pl.when(i + 1 < tiles)
        def _():
            for copy in tile_loads(i + 1, (i + 1) % 2):
                copy.start()

        for copy in tile_loads(i, slot):
            copy.wait()

        @pl.when(i >= 2)
        def _():
            for copy in tile_stores(i - 2, slot):
                copy.wait()

        for j in range(3):
            t_tiles[slot, j] = s_tiles[slot, j].T
        for copy in tile_stores(i, slot):
            copy.start()
        return carry

    for copy in tile_loads(0, 0):
        copy.start()
    lax.fori_loop(0, tiles // 2, pack, 0)
    kv_gather.start_forward()
    lax.fori_loop(tiles // 2, tiles, pack, 0)
    kv_gather.start_last()
    tail_gather.start()
    head_gather.start_forward()
    for i in (tiles - 2, tiles - 1):
        for copy in tile_stores(i, i % 2):
            copy.wait()
    kv_gather.finish()

    for level, segment in enumerate(path):
        block = kv_all[jnp.maximum(segment, 0)]
        key_ref[level * tok_rows : (level + 1) * tok_rows, :] = block[:, :local_width]
        value_ref[level * tok_rows : (level + 1) * tok_rows, :] = block[:, local_width:]
    for copy in results[1:]:
        copy.start()
    key_rows = key_ref.shape[0]
    row_id = lax.broadcasted_iota(jnp.int32, (tok_rows, key_rows), 0)
    col_id = lax.broadcasted_iota(jnp.int32, (tok_rows, key_rows), 1)
    allowed = row_id >= col_id
    for level in range(1, LEVELS):
        barred = jnp.where(path[level] >= 0, key_rows, 0)
        inside = (col_id >= level * tok_rows) & (col_id < (level + 1) * tok_rows)
        allowed = allowed | (inside & (col_id < barred))

    def head(h, carry):
        cols = pl.ds(pl.multiple_of(h * HEAD_DIM, HEAD_DIM), HEAD_DIM)
        scores = product_nt(query_ref[:, cols], key_ref[:, cols]) * score_scale
        scores = jnp.where(allowed, scores, -jnp.inf)
        top = jnp.max(scores, 1, keepdims=True)
        powers = jnp.exp(scores - top)
        total = jnp.sum(powers, 1, keepdims=True)
        log_total_ref[h] = top + jnp.log(total)
        probs = (powers * (1.0 / total)).astype(bf16)
        attended_ref[:, cols] = product(probs, value_ref[:, cols]).astype(bf16)
        return carry

    lax.fori_loop(0, local_width // HEAD_DIM, head, 0)

    loads[3].wait()
    for quarter in range(4):
        mine = slice(quarter * rows, (quarter + 1) * rows)
        part_send[quarter] = product_nt(attended_ref[mine, :], weights[3]).astype(bf16)

    line = LineSum(lambda z: part_send.at[z], part_z, part_sems)
    line.start()
    head_gather.start_last()
    tail_gather.start_forward()
    line.forward()
    attn = line.finish()
    own_rows = pl.ds(pl.multiple_of(column * rows, rows), rows)
    residual_ref[...] = hidden_ref[own_rows, :].astype(f32) + attn
    tail_gather.start_last()
    head_gather.finish()
    for j in range(1, 8):
        hit_copy(j).wait_recv()
    hits_all_ref[...] = hits_all[...]
    tail_gather.finish()

    for copy in results:
        copy.wait()

    for gather in (kv_gather, head_gather, tail_gather):
        gather.wait_sends()
    for j in range(1, 8):
        hit_copy(j).wait_send()
    line.wait_sends()


def front_layer(score_scale, shared_units, operands):
    hidden, w_query = operands[1], operands[9]
    tok_rows, width = hidden.shape
    rows, local_width = tok_rows // 4, w_query.shape[1]
    heads = local_width // HEAD_DIM
    tile, span = 256, 384
    bf16, f32 = jnp.bfloat16, jnp.float32
    shape = jax.ShapeDtypeStruct
    vmem, anywhere = pl.BlockSpec(memory_space=pltpu.VMEM), pl.BlockSpec(memory_space=pl.ANY)
    smem = pl.BlockSpec(memory_space=pltpu.SMEM)
    dma = pltpu.SemaphoreType.DMA
    return pl.pallas_call(
        functools.partial(front_kernel, score_scale, shared_units),
        out_shape=[
            shape((rows, width), f32),
            shape((tok_rows, local_width), bf16),
            shape((LEVELS * tok_rows, local_width), bf16),
            shape((LEVELS * tok_rows, local_width), bf16),
            shape((heads, tok_rows, 1), f32),
            shape((tok_rows, local_width), bf16),
            shape((tok_rows, width), bf16),
            shape((tok_rows, HEAD_DIM), f32),
            shape((tok_rows, HEAD_DIM), f32),
            shape((8, 16, tok_rows), f32),
            shape((8, 4, rows, width), bf16),
            shape((3, shared_units, width), bf16),
        ],
        in_specs=[smem] + [vmem] * 8 + [anywhere] * 7,
        out_specs=[vmem, vmem, anywhere, anywhere, vmem, vmem, anywhere]
        + [vmem] * 3
        + [anywhere] * 2,
        scratch_shapes=[
            pltpu.VMEM((4, width, local_width), bf16),
            pltpu.VMEM((8, tok_rows, 2 * local_width), bf16),
            pltpu.VMEM((8, 16, tok_rows), f32),
            pltpu.VMEM((4, rows, width), bf16),
            pltpu.VMEM((4, rows, width), bf16),
            pltpu.VMEM((2, 3, tile, span), bf16),
            pltpu.VMEM((2, 3, span, tile), bf16),
            pltpu.VMEM((LEVELS * tok_rows, local_width), bf16),
            pltpu.VMEM((LEVELS * tok_rows, local_width), bf16),
            pltpu.VMEM((tok_rows, width), bf16),
            dma((8,)),
            dma((2, 3)),
            dma((2, 3)),
            dma((2, 8)),
            dma((2, 4)),
        ]
        + [dma((2, 4))] * 6,
        compiler_params=pltpu.CompilerParams(
            collective_id=2, has_side_effects=True, vmem_limit_bytes=56 * 2**20
        ),
        cost_estimate=pl.CostEstimate(
            flops=2 * 2**31, bytes_accessed=40 * 2**20, transcendentals=2**21
        ),
    )(*operands)


class PlaneSum:
    def __init__(self, mine, theirs, got_core, got_x1, got_y1, got_y2, got_x2, core_sems, sems):
        self.mine, self.theirs = mine, theirs
        self.got = (got_core, got_x1, got_y1, got_y2, got_x2)
        self.core_sems, self.sems = core_sems, sems
        self.half = got_x1.shape[-1]
        self.wide = self.half + got_y1.shape[-1]
        self.left, self.right = pl.ds(0, self.half), pl.ds(self.half, self.wide - self.half)
        place = lax.axis_index("dp")
        self.core, self.east, self.north = place % 2, (place // 2) % 2, place // 4
        self.sibling = {"dp": other(place, 1)}
        self.x_side, self.y_side = {"dp": other(place, 2)}, {"dp": other(place, 4)}

    def remote(self, src, dst, sems, which, device):
        return pltpu.make_async_remote_copy(
            src_ref=src,
            dst_ref=dst,
            send_sem=sems.at[(0, *which)],
            recv_sem=sems.at[(1, *which)],
            device_id=device,
            device_id_type=MESH,
        )

    def core_copy(self, k):
        return self.remote(
            self.theirs(k), self.got[0].at[k], self.core_sems, (k,), self.sibling
        )

    def first_copies(self, k):
        mine = self.mine(k)
        return [
            self.remote(
                mine.at[:, flip(self.east), :, self.left],
                self.got[1].at[k],
                self.sems,
                (0, k),
                self.x_side,
            ),
            self.remote(
                mine.at[flip(self.north), :, :, self.right],
                self.got[2].at[k],
                self.sems,
                (1, k),
                self.y_side,
            ),
        ]

    def second_copies(self, k):
        mine = self.mine(k)
        return [
            self.remote(
                mine.at[flip(self.north), self.east, :, self.left],
                self.got[3].at[k],
                self.sems,
                (2, k),
                self.y_side,
            ),
            self.remote(
                mine.at[self.north, flip(self.east), :, self.right],
                self.got[4].at[k],
                self.sems,
                (3, k),
                self.x_side,
            ),
        ]

    def add(self, ref, value):
        ref[...] = (ref[...].astype(jnp.float32) + value.astype(jnp.float32)).astype(jnp.bfloat16)

    def start(self, k):
        self.core_copy(k).start()

    def after_core(self, k):
        self.core_copy(k).wait_recv()
        mine = self.mine(k)
        for y in range(2):
            for x in range(2):
                self.add(mine.at[y, x], self.got[0][k, y, x])
        self.start_first(k)

    def start_first(self, k):
        for copy in self.first_copies(k):
            copy.start()

    def after_first(self, k):
        x_copy, y_copy = self.first_copies(k)
        mine = self.mine(k)
        x_copy.wait_recv()
        for y in range(2):
            self.add(mine.at[y, self.east, :, self.left], self.got[1][k, y])
        y_copy.wait_recv()
        for x in range(2):
            self.add(mine.at[self.north, x, :, self.right], self.got[2][k, x])
        for copy in self.second_copies(k):
            copy.start()

    def after_second(self, k):
        y_copy, x_copy = self.second_copies(k)
        own = self.mine(k).at[self.north, self.east]
        y_copy.wait_recv()
        self.add(own.at[:, self.left], self.got[3][k])
        x_copy.wait_recv()
        self.add(own.at[:, self.right], self.got[4][k])
        return own

    def wait_sends(self, k):
        if self.theirs is not None:
            self.core_copy(k).wait_send()
        for copy in self.first_copies(k) + self.second_copies(k):
            copy.wait_send()


def plane_scratch(count, rows, wide):
    half = wide // 2
    bf16, dma = jnp.bfloat16, pltpu.SemaphoreType.DMA
    return [
        pltpu.VMEM((count, 2, 2, rows, wide), bf16),
        pltpu.VMEM((count, 2, rows, half), bf16),
        pltpu.VMEM((count, 2, rows, wide - half), bf16),
        pltpu.VMEM((count, rows, half), bf16),
        pltpu.VMEM((count, rows, wide - half), bf16),
        dma((2, count)),
        dma((2, 4, count)),
    ]


def unturn(grad, cosine, sine):
    heads = []
    for begin in range(0, grad.shape[1], HEAD_DIM):
        head = grad[:, begin : begin + HEAD_DIM]
        heads.append(head * cosine - pltpu.roll(head, HEAD_DIM // 2, 1) * sine)
    return jnp.concatenate(heads, 1)


def back_kernel(
    score_scale,
    gain_row,
    residual_in,
    res_grad_in,
    res_low_ref,
    ffn_part_ref,
    shared_ref,
    small_ref,
    query_ref,
    key_in,
    value_in,
    parents_ref,
    log_total_ref,
    attended_ref,
    normed_in,
    hidden_in,
    gain_ref,
    cosine_ref,
    sine_ref,
    w_out_ref,
    w_query_ref,
    w_key_ref,
    w_value_ref,
    hidden_out_ref,
    hidden_grad_ref,
    grad_query_ref,
    grad_key_ref,
    grad_value_ref,
    grad_out_ref,
    shared_got,
    small_out_ref,
    bias_out_ref,
    low_all,
    w_qkv,
    out_mine,
    out_z,
    kv_sums,
    w_sums,
    kv_path,
    attended_grad,
    query_grad,
    pre_grads,
    part,
    part_send,
    part_z,
    hidden_stage,
    shared_stage,
    small_send,
    small_got,
    small_z,
    residual_ref,
    res_grad_ref,
    key_ref,
    value_ref,
    normed_ref,
    hidden_ref,
    *rest,
):
    bf16, f32 = jnp.bfloat16, jnp.float32
    out_scr, rest = rest[:5], rest[5:]
    kv_scr, rest = rest[:7], rest[7:]
    w_scr, rest = rest[:7], rest[7:]
    wkv_sems, rest = rest[:2], rest[2:]
    load_sems, low_sems, out_sems, part_sems, end_sems, shared_sems, small_sems, small_z_sems = rest
    place, column = lax.axis_index("dp"), lax.axis_index("tensor")
    core, east, north = place % 2, (place // 2) % 2, place // 4
    rows, width = residual_ref.shape
    tok_rows, local_width = query_ref.shape
    levels = [{"tensor": other(column, k)} for k in range(4)]
    peers = [{"dp": other(place, j)} for j in range(8)]

    def remote(src, dst, sems, which, device):
        return pltpu.make_async_remote_copy(
            src_ref=src,
            dst_ref=dst,
            send_sem=sems.at[(0, *which)],
            recv_sem=sems.at[(1, *which)],
            device_id=device,
            device_id_type=MESH,
        )

    def load_out(z):
        return pltpu.make_async_copy(ffn_part_ref.at[z], out_mine.at[z], load_sems.at[z])

    loads = [
        pltpu.make_async_copy(w_query_ref, w_qkv.at[0], load_sems.at[5]),
        pltpu.make_async_copy(w_key_ref, w_qkv.at[1], load_sems.at[6]),
        pltpu.make_async_copy(w_out_ref, w_qkv.at[2], load_sems.at[4]),
    ]
    fetches = [
        pltpu.make_async_copy(source, target, load_sems.at[12 + i])
        for i, (source, target) in enumerate(
            (
                (key_in, key_ref),
                (value_in, value_ref),
                (normed_in, normed_ref),
                (hidden_in, hidden_ref),
                (residual_in, residual_ref),
                (res_grad_in, res_grad_ref),
            )
        )
    ]
    for copy in fetches:
        copy.start()
    load_value = pltpu.make_async_copy(w_value_ref, w_qkv.at[2], load_sems.at[7])
    load_shared = pltpu.make_async_copy(shared_ref.at[place], shared_stage, load_sems.at[9])
    load_shared.start()
    for z in range(4):
        load_out(z).start()
    for copy in loads:
        copy.start()

    barrier = pltpu.get_barrier_semaphore()
    partners = peers[1:] + levels[1:]
    for partner in partners:
        pl.semaphore_signal(barrier, inc=1, device_id=partner, device_id_type=MESH)
    pl.semaphore_wait(barrier, len(partners))

    out_sum = PlaneSum(lambda k: out_mine.at[k], None, None, *out_scr[:4], None, out_scr[4])
    kv_sum = PlaneSum(
        lambda k: kv_sums.at[k, core], lambda k: kv_sums.at[k, flip(core)], *kv_scr
    )
    w_sum = PlaneSum(
        lambda k: w_sums.at[k, core], lambda k: w_sums.at[k, flip(core)], *w_scr
    )
    wkv_sum = PlaneSum(
        lambda k: kv_sums.at[k, core],
        lambda k: kv_sums.at[k, flip(core)],
        *kv_scr[:5],
        *wkv_sems,
    )

    low_all[column] = res_low_ref[...]
    low_line = LineGather(lambda z: low_all.at[z], low_sems)
    low_line.start()
    order = [other(column, k) for k in (1, 3, 2, 0)]
    for z in range(4):
        load_out(z).wait()
    for z in order:
        out_sum.start_first(z)
    kv_path[...] = jnp.zeros(kv_path.shape, f32)
    for copy in loads + fetches:
        copy.wait()

    out_line = LineSum(lambda z: out_mine.at[z, north, east], out_z, out_sems)
    low_line.forward()

    half_rows = tok_rows // 2
    key_rows = key_ref.shape[0]
    row_id = lax.broadcasted_iota(jnp.int32, (half_rows, key_rows), 0)
    col_id = lax.broadcasted_iota(jnp.int32, (half_rows, key_rows), 1)
    path = path_scalars(parents_ref, place)
    reached = col_id < 0
    for level in range(1, LEVELS):
        barred = jnp.where(path[level] >= 0, key_rows, 0)
        inside = (col_id >= level * tok_rows) & (col_id < (level + 1) * tok_rows)
        reached = reached | (inside & (col_id < barred))

    def half(i, carry):
        pair = (column // 2 + i) % 2
        first = pl.multiple_of(pair * half_rows, half_rows)
        window = pl.ds(first, half_rows)

        @pl.when(i == 0)
        def _():
            low_line.own(1).wait_recv()

        @pl.when(i == 1)
        def _():
            low_line.own(3).wait_recv()

        low_rows = low_all[pl.ds(2 * pair, 2)].reshape(half_rows, width)
        attended_grad[window, :] = product(low_rows, w_qkv[2]).astype(bf16)
        allowed = (row_id + first >= col_id) | reached

        def head(h, carry):
            cols = pl.ds(pl.multiple_of(h * HEAD_DIM, HEAD_DIM), HEAD_DIM)
            value_cols = pl.ds(pl.multiple_of(local_width + h * HEAD_DIM, HEAD_DIM), HEAD_DIM)
            query, key, value = query_ref[window, cols], key_ref[:, cols], value_ref[:, cols]
            grad = attended_grad[window, cols]
            scores = jnp.where(allowed, product_nt(query, key) * score_scale, -jnp.inf)
            weights = jnp.exp(scores - log_total_ref[h, window])
            weight_grad = product_nt(grad, value)
            center = jnp.sum(weights * weight_grad, 1, keepdims=True)
            score_grad = (weights * (weight_grad - center)).astype(bf16)
            query_grad[window, cols] = product(score_grad, key) * score_scale
            kv_path[:, cols] += product_tn(score_grad, query) * score_scale
            kv_path[:, value_cols] += product_tn(weights.astype(bf16), grad)
            return carry

        lax.fori_loop(0, local_width // HEAD_DIM, head, 0)

        @pl.when(i == 0)
        def _():
            out_sum.after_first(order[0])
            out_sum.after_first(order[1])

        return carry

    lax.fori_loop(0, 2, half, 0)
    for z in order[2:]:
        out_sum.after_first(z)
    load_value.start()

    part_rows = rows // 2

    def kv_blocks(i, c):
        which, y, x = i // 4, (i // 2) % 2, i % 2
        segment = 4 * y + 2 * x + c
        total = jnp.zeros((4, part_rows, 2 * local_width), f32)
        for level in range(1, LEVELS):
            spot = jnp.where(path[level] == segment, 1.0, 0.0)
            total = total + spot * kv_rows(level, which)
        kv_sums[which, c, y, x] = total.reshape(4 * part_rows, 2 * local_width).astype(bf16)
        return c

    def kv_rows(level, which):
        rows_view = kv_path.at[level * tok_rows : (level + 1) * tok_rows]
        pieces = []
        for z in range(4):
            start = pl.multiple_of(z * rows + which * part_rows, part_rows)
            pieces.append(rows_view[pl.ds(start, part_rows), :])
        return jnp.stack(pieces)

    lax.fori_loop(0, 4, kv_blocks, flip(core))
    kv_sum.start(0)
    lax.fori_loop(4, 8, kv_blocks, flip(core))
    kv_sum.start(1)
    lax.fori_loop(0, 8, kv_blocks, core)
    for which in range(2):
        own_kv = kv_sums.at[which, core, north, east]
        added = own_kv[...].astype(f32) + kv_rows(0, which).reshape(4 * part_rows, -1)
        own_kv[...] = added.astype(bf16)
        kv_sum.after_core(which)
    for z in order:
        out_sum.after_second(z)
    out_line.start()

    def bias_of(which, grad, begin):
        bias = jnp.sum(grad.astype(f32), 0, keepdims=True)
        for h in range(local_width // HEAD_DIM):
            spot = slice(4 * which + h, 4 * which + h + 1)
            added = bias[:, h * HEAD_DIM : (h + 1) * HEAD_DIM]
            if not begin:
                added = added + small_send[0, spot, 2 * HEAD_DIM :]
            small_send[0, spot, 2 * HEAD_DIM :] = added

    small_send[0, :, 2 * HEAD_DIM :] = jnp.zeros((16, HEAD_DIM), f32)
    query_pre = unturn(query_grad[...], cosine_ref[...], sine_ref[...]).astype(bf16)
    pre_grads[0] = query_pre.reshape(4, 2, part_rows, local_width)
    bias_of(0, query_pre, True)
    part[...] = product_nt(query_pre, w_qkv[0]).reshape(4, 2, part_rows, width)
    def block_index(place_of):
        return place_of % 2, place_of // 4, (place_of // 2) % 2

    def out_weights(i, carry):
        c, y, x = block_index(i)
        window = pl.ds(pl.multiple_of(i * tok_rows, tok_rows), tok_rows)
        lhs = low_all[:, :, window].reshape(tok_rows, tok_rows)
        w_sums[0, c, y, x] = product_tn(lhs, attended_ref[...]).astype(bf16)
        return carry

    def query_weights(i, carry):
        c, y, x = block_index(i)
        window = pl.ds(pl.multiple_of(i * tok_rows, tok_rows), tok_rows)
        rows_pre = pre_grads[0].reshape(tok_rows, local_width)
        w_sums[1, c, y, x] = product_tn(normed_ref[:, window], rows_pre).astype(bf16)
        return carry

    lax.fori_loop(0, 8, out_weights, 0)
    w_sum.start(0)
    lax.fori_loop(0, 8, query_weights, 0)
    w_sum.start(1)
    kv_sum.after_first(0)
    kv_sum.after_first(1)

    load_value.wait()
    hidden_f = hidden_ref[...].astype(f32)
    unit_scale = lax.rsqrt(jnp.mean(hidden_f * hidden_f, 1, keepdims=True) + epsilon)

    part_lines = [
        LineSum(
            lambda z, which=which: part_send.at[which, z],
            part_z.at[which],
            part_sems.at[which],
        )
        for which in range(2)
    ]

    for which in range(2):
        own_kv = kv_sum.after_second(which)
        cos_rows = cosine_ref[...].reshape(4, 2, part_rows, HEAD_DIM)[:, which]
        sin_rows = sine_ref[...].reshape(4, 2, part_rows, HEAD_DIM)[:, which]
        key_pre = unturn(
            own_kv[:, :local_width].astype(f32),
            cos_rows.reshape(4 * part_rows, HEAD_DIM),
            sin_rows.reshape(4 * part_rows, HEAD_DIM),
        ).astype(bf16)
        value_pre = own_kv[:, local_width:]
        pre_grads[1, :, which] = key_pre.reshape(4, part_rows, local_width)
        pre_grads[2, :, which] = value_pre.reshape(4, part_rows, local_width)
        bias_of(1, key_pre, which == 0)
        bias_of(2, value_pre, which == 0)
        added = product_nt(key_pre, w_qkv[1]) + product_nt(value_pre, w_qkv[2])
        whole = part[:, which] + added.reshape(4, part_rows, width)
        part[:, which] = whole
        part_send[which] = whole.astype(bf16)
        part_lines[which].start()
        if which == 0:
            out_line.forward()


    def shared_copy(j):
        return remote(
            shared_ref.at[other(place, j)], shared_got.at[place], shared_sems, (j,), peers[j]
        )

    for k in range(2):
        w_sum.after_core(k)
    part_lines[0].forward()
    attn_gain_row = jnp.sum(
        part[...].reshape(tok_rows, width) * (hidden_f * unit_scale), 0, keepdims=True
    )
    def key_value_weights(i, carry):
        c, y, x = block_index(i)
        window = pl.ds(pl.multiple_of(i * tok_rows, tok_rows), tok_rows)
        lhs = normed_ref[:, window]
        for which, cols in ((1, slice(0, local_width)), (2, slice(local_width, None))):
            rows_pre = pre_grads[which].reshape(tok_rows, local_width)
            grad = product_tn(lhs, rows_pre).astype(bf16)
            for k in range(2):
                piece = slice(k * half_rows, (k + 1) * half_rows)
                kv_sums[k, c, y, x, :, cols] = grad[piece]
        return carry

    for k in range(2):
        kv_sum.wait_sends(k)
    lax.fori_loop(0, 8, key_value_weights, 0)
    for k in range(2):
        wkv_sum.start(k)
    part_lines[1].forward()

    bias_rows = small_send[0, :, 2 * HEAD_DIM :]
    for d in range(8):
        small_send[d, :, : 2 * HEAD_DIM] = small_ref[:, d * tok_rows : (d + 1) * tok_rows]
        small_send[d, gain_row : gain_row + 1, : 2 * HEAD_DIM] = attn_gain_row[
            :, d * tok_rows : (d + 1) * tok_rows
        ]
        small_send[d, :, 2 * HEAD_DIM :] = bias_rows

    def small_copy(j):
        return remote(
            small_send.at[other(place, j)], small_got.at[j], small_sems, (j,), peers[j]
        )

    for j in range(1, 8):
        small_copy(j).start()

    w_sum.after_first(0)
    for k in range(2):
        wkv_sum.after_core(k)
    w_sum.after_first(1)
    own_shared = pltpu.make_async_copy(shared_stage, shared_got.at[place], load_sems.at[8])
    load_shared.wait()
    own_shared.start()

    total = small_send[place]
    for j in range(1, 8):
        small_copy(j).wait_recv()
        total = total + small_got[j]
    bias_out_ref[...] = total[:, 2 * HEAD_DIM :]
    small_z[column] = total[:, : 2 * HEAD_DIM]
    own_small = small_z.at[column]
    small_levels = [
        remote(own_small, own_small, small_z_sems, (k,), levels[k]) for k in (1, 2, 3)
    ]
    for copy in small_levels:
        copy.start()

    end_lines = [
        LineGather(
            lambda z, which=which, piece=piece: hidden_stage.at[which, z, piece],
            end_sems.at[which, piece],
        )
        for which in range(2)
        for piece in range(2)
    ]

    for which in range(2):
        attn_grad = part_lines[which].finish()
        start = pl.multiple_of(column * rows + which * part_rows, part_rows)
        own_hidden = hidden_ref[pl.ds(start, part_rows), :].astype(f32)
        own_scale = lax.rsqrt(jnp.mean(own_hidden * own_hidden, 1, keepdims=True) + epsilon)
        own_grad = res_grad_ref[which * part_rows : (which + 1) * part_rows, :]
        hidden_stage[0, column, which] = (
            own_grad + norm_back(attn_grad, own_hidden * own_scale, own_scale, gain_ref[...])
        ).astype(bf16)
        end_lines[which].start()
        if which == 0:
            grad_out_ref[...] = w_sum.after_second(0)[...]
            for k in range(2):
                wkv_sum.after_first(k)
            for j in (6, 7, 2, 3, 4, 5, 1):
                shared_copy(j).start()

    end_lines[0].forward()
    out = residual_ref[...] + out_line.finish()
    hidden_stage[1, column] = out.astype(bf16).reshape(2, part_rows, width)
    end_lines[1].forward()
    end_lines[2].start()
    end_lines[3].start()

    grad_query_ref[...] = w_sum.after_second(1)[...]
    for copy in small_levels:
        copy.wait_recv()
    small_out_ref[...] = (small_z[0] + small_z[1]) + (small_z[2] + small_z[3])
    for k in range(2):
        own_wkv = wkv_sum.after_second(k)
        piece = slice(k * half_rows, (k + 1) * half_rows)
        grad_key_ref[piece, :] = own_wkv[:, :local_width]
        grad_value_ref[piece, :] = own_wkv[:, local_width:]

    end_lines[2].forward()
    end_lines[3].forward()
    own_shared.wait()
    for j in range(1, 8):
        shared_copy(j).wait_recv()
    for line in end_lines:
        line.finish()
    ends = [
        pltpu.make_async_copy(hidden_stage.at[0], hidden_grad_ref, load_sems.at[10]),
        pltpu.make_async_copy(hidden_stage.at[1], hidden_out_ref, load_sems.at[11]),
    ]
    for copy in ends:
        copy.start()
    for copy in ends:
        copy.wait()

    for copy in small_levels:
        copy.wait_send()
    for line in [low_line, out_line] + part_lines + end_lines:
        line.wait_sends()
    for z in range(4):
        out_sum.wait_sends(z)
    for k in range(2):
        w_sum.wait_sends(k)
        wkv_sum.wait_sends(k)
    for j in range(1, 8):
        small_copy(j).wait_send()
        shared_copy(j).wait_send()


def back_layer(score_scale, gain_row, operands):
    (
        residual,
        res_grad,
        res_low,
        ffn_part,
        grad_shared,
        small,
        query,
        key,
        value,
        parents,
        log_total,
        attended,
        normed,
        hidden,
        gain,
        cosine,
        sine,
        w_out,
        w_query,
        w_key,
        w_value,
    ) = operands
    rows, width = residual.shape
    tok_rows, local_width = query.shape
    units = grad_shared.shape[2]
    bf16, f32 = jnp.bfloat16, jnp.float32
    shape = jax.ShapeDtypeStruct
    vmem, anywhere = pl.BlockSpec(memory_space=pltpu.VMEM), pl.BlockSpec(memory_space=pl.ANY)
    smem = pl.BlockSpec(memory_space=pltpu.SMEM)
    dma = pltpu.SemaphoreType.DMA
    return pl.pallas_call(
        functools.partial(back_kernel, score_scale, gain_row),
        out_shape=[
            shape((4, 2, rows // 2, width), bf16),
            shape((4, 2, rows // 2, width), bf16),
            shape((tok_rows, local_width), bf16),
            shape((tok_rows, local_width), bf16),
            shape((tok_rows, local_width), bf16),
            shape((tok_rows, local_width), bf16),
            shape((8, 3, units, tok_rows), bf16),
            shape((16, tok_rows), f32),
            shape((16, HEAD_DIM), f32),
        ],
        in_specs=[anywhere, anywhere, vmem, anywhere, anywhere, vmem]
        + [vmem, anywhere, anywhere]
        + [smem]
        + [vmem, vmem, anywhere, anywhere, vmem, vmem, vmem]
        + [anywhere] * 4,
        out_specs=[anywhere] * 2 + [vmem] * 4 + [anywhere] + [vmem] * 2,
        scratch_shapes=[
            pltpu.VMEM((4, rows, width), bf16),
            pltpu.VMEM((3, width, local_width), bf16),
            pltpu.VMEM((4, 2, 2, rows, width), bf16),
            pltpu.VMEM((4, rows, width), bf16),
            pltpu.VMEM((2, 2, 2, 2, tok_rows // 2, 2 * local_width), bf16),
            pltpu.VMEM((2, 2, 2, 2, tok_rows, local_width), bf16),
            pltpu.VMEM((LEVELS * tok_rows, 2 * local_width), f32),
            pltpu.VMEM((tok_rows, local_width), bf16),
            pltpu.VMEM((tok_rows, local_width), f32),
            pltpu.VMEM((3, 4, 2, rows // 2, local_width), bf16),
            pltpu.VMEM((4, 2, rows // 2, width), f32),
            pltpu.VMEM((2, 4, rows // 2, width), bf16),
            pltpu.VMEM((2, 4, rows // 2, width), bf16),
            pltpu.VMEM((2, 4, 2, rows // 2, width), bf16),
            pltpu.VMEM((3, units, tok_rows), bf16),
            pltpu.VMEM((8, 16, 2 * HEAD_DIM + HEAD_DIM), f32),
            pltpu.VMEM((8, 16, 2 * HEAD_DIM + HEAD_DIM), f32),
            pltpu.VMEM((4, 16, 2 * HEAD_DIM), f32),
            pltpu.VMEM(residual.shape, f32),
            pltpu.VMEM(res_grad.shape, f32),
            pltpu.VMEM(key.shape, bf16),
            pltpu.VMEM(value.shape, bf16),
            pltpu.VMEM(normed.shape, bf16),
            pltpu.VMEM(hidden.shape, bf16),
        ]
        + plane_scratch(4, rows, width)[1:5]
        + plane_scratch(4, rows, width)[6:]
        + plane_scratch(2, tok_rows // 2, 2 * local_width)
        + plane_scratch(2, tok_rows, local_width)
        + plane_scratch(2, tok_rows // 2, 2 * local_width)[5:]
        + [
            dma((18,)),
            dma((2, 4)),
            dma((2, 4)),
            dma((2, 2, 4)),
            dma((2, 2, 2, 4)),
            dma((2, 8)),
            dma((2, 8)),
            dma((2, 4)),
        ],
        compiler_params=pltpu.CompilerParams(
            collective_id=1, has_side_effects=True, vmem_limit_bytes=63 * 2**20
        ),
        cost_estimate=pl.CostEstimate(
            flops=2 * 12 * 2**30, bytes_accessed=40 * 2**20, transcendentals=2**20
        ),
    )(*operands)


def on_slice(
    hidden_in,
    out_grad,
    parents,
    routes,
    attn_gain,
    w_query,
    w_key,
    w_value,
    b_query,
    b_key,
    b_value,
    w_out,
    ffn_gain,
    w_router,
    shared_gate,
    shared_w_gate,
    shared_w_up,
    shared_w_down,
    expert_w_gate,
    expert_w_up,
    expert_w_down,
):
    tok_rows, model_width = hidden_in.shape
    devices = lax.axis_size("dp")
    columns = lax.axis_size("tensor")
    place, column = lax.axis_index("dp"), lax.axis_index("tensor")
    all_rows = tok_rows * devices
    part_rows = tok_rows // columns
    local_width = w_query.shape[1]
    experts = w_router.shape[1]
    top_count = routes.shape[1]
    capacity = 5 * tok_rows * top_count // 4
    score_scale = HEAD_DIM ** (-0.5)
    bf16, f32 = jnp.bfloat16, jnp.float32

    expert_units = expert_w_gate.shape[2]
    shared_units = shared_w_gate.shape[1] // devices
    shared_pad = -(-shared_units // 128) * 128
    units = shared_pad + expert_units
    units_pad = -(-(units + experts + 1) // 128) * 128

    def own_units(matrix):
        return lax.dynamic_slice_in_dim(matrix, place * shared_units, shared_units, 1)

    def pad_to(matrix, columns):
        return jnp.pad(matrix, ((0, 0), (0, columns - matrix.shape[1])))

    def side_by_side(shared, expert):
        joined = jnp.concatenate([pad_to(own_units(shared), shared_pad), expert[0]], 1)
        return joined

    w_pre = jnp.concatenate(
        [
            pad_to(
                jnp.concatenate(
                    [side_by_side(shared_w_gate, expert_w_gate), w_router, shared_gate[:, None]], 1
                ),
                units_pad,
            ),
            pad_to(side_by_side(shared_w_up, expert_w_up), units_pad),
        ],
        1,
    )
    w_down = pad_to(side_by_side(shared_w_down, expert_w_down), units_pad)

    out_all = gather_dp(out_grad)

    routes_all = lax.all_gather(routes, "dp", axis=0, tiled=True)
    pair_onehot = routes_all[:, :, None] == jnp.arange(experts, dtype=jnp.int32)[None, None, :]
    hits = jnp.any(pair_onehot, 1)
    hit_blocks = hits.astype(bf16).reshape(devices, tok_rows, experts)
    below = (
        jnp.arange(tok_rows)[None, :] < jnp.arange(tok_rows)[:, None]
    ).astype(bf16)
    within = jnp.einsum("ij,bje->bie", below, hit_blocks, preferred_element_type=f32)
    block_sums = jnp.sum(hit_blocks.astype(f32), 1)
    before = jnp.cumsum(block_sums, 0) - block_sums
    slots = (within + before[:, None, :]).reshape(all_rows, experts)
    kept = (hits & (slots < capacity)).astype(f32)

    path = path_of(parents, place * tok_rows // SEG)
    reachable = path >= 0
    path_rows = jnp.maximum(path, 0)
    row_ids = jnp.arange(tok_rows, dtype=jnp.int32)
    depth = jnp.sum(reachable.astype(f32)) - 1.0
    cosine, sine = rope_tables(depth * SEG + row_ids.astype(f32))
    allowed = jnp.concatenate(
        [
            row_ids[:, None] >= row_ids[None, :],
            jnp.broadcast_to(
                jnp.repeat(reachable[1:], tok_rows)[None, :], (tok_rows, (LEVELS - 1) * tok_rows)
            ),
        ],
        1,
    )
    hidden_f = hidden_in.astype(f32)
    attn_scale, attn_unit = norm_parts(hidden_f)
    attn_normed = (attn_unit * attn_gain).astype(bf16)
    query_rot = turn_heads(
        product(attn_normed, w_query) + b_query.reshape(-1), cosine, sine, 1.0
    ).astype(bf16)
    key_rot = turn_heads(
        product(attn_normed, w_key) + b_key.reshape(-1), cosine, sine, 1.0
    ).astype(bf16)
    value_rows = (product(attn_normed, w_value) + b_value.reshape(-1)).astype(bf16)
    gathered = gather_dp(jnp.concatenate([key_rot, value_rows], 1))
    kv_blocks = gathered.reshape(devices, tok_rows, 2 * local_width)
    kv_path = jnp.take(kv_blocks, path_rows, axis=0).reshape(LEVELS * tok_rows, 2 * local_width)
    key_path, value_path = kv_path[:, :local_width], kv_path[:, local_width:]
    attended, log_total = attend_forward(query_rot, key_path, value_path, allowed, score_scale)
    attended_low = attended.astype(bf16)
    attn_part = product_nt(attended_low, w_out).astype(bf16)

    hidden_own = lax.dynamic_slice_in_dim(hidden_in, column * part_rows, part_rows, 0)
    grad_own = lax.dynamic_slice_in_dim(out_grad, column * part_rows, part_rows, 0)
    layout = (shared_units, shared_pad, expert_units, experts, units_pad)
    (
        residual,
        residual_grad,
        residual_low,
        ffn_part,
        grad_expert_gate,
        grad_expert_up,
        grad_expert_down,
        grad_shared,
        grad_side,
        grad_ffn_gain,
    ) = ffn_plain(
        attn_part, hidden_own, grad_own, ffn_gain, kept, out_all, w_pre, w_down, layout
    )
    grad_shared = grad_shared[:, :, :shared_units]
    ffn_own = scatter_all(ffn_part).astype(f32)
    hidden_out = gather_tensor((residual + ffn_own).astype(bf16))
    residual_low = gather_tensor(residual_low)
    grad_out_proj = product_tn(residual_low, attended_low)
    attended_grad = product(residual_low, w_out).astype(bf16)

    query_grad, key_grad, value_grad = attend_backward(
        query_rot, key_path, value_path, allowed, log_total, attended_grad, score_scale
    )
    kv_grad = jnp.concatenate([key_grad, value_grad], 1).reshape(
        LEVELS, tok_rows, 2 * local_width
    )
    kv_all = jnp.zeros((devices, tok_rows, 2 * local_width), f32)
    for level in range(LEVELS):
        kv_all = kv_all.at[path_rows[level]].add(kv_grad[level])
    kv_own = scatter_dp(
        kv_all.reshape(all_rows, 2 * local_width).astype(bf16)
    ).astype(f32)
    query_pre_grad = turn_heads(query_grad, cosine, sine, -1.0).astype(bf16)
    key_pre_grad = turn_heads(kv_own[:, :local_width], cosine, sine, -1.0).astype(bf16)
    value_pre_grad = kv_own[:, local_width:].astype(bf16)
    qkv_pre_grad = jnp.concatenate([query_pre_grad, key_pre_grad, value_pre_grad], 1)
    grad_qkv = product_tn(attn_normed, qkv_pre_grad)
    bias_grads = jnp.sum(qkv_pre_grad.astype(f32), 0).reshape(3, -1, HEAD_DIM)
    attn_part_grad = (
        product_nt(query_pre_grad, w_query)
        + product_nt(key_pre_grad, w_key)
        + product_nt(value_pre_grad, w_value)
    )
    grad_attn_gain = jnp.sum(attn_part_grad * attn_unit, 0)
    attn_own_grad = scatter_tensor(attn_part_grad.astype(bf16)).astype(f32)
    own_rows = lambda array: lax.dynamic_slice_in_dim(
        array, column * part_rows, part_rows, 0
    )
    hidden_in_grad = gather_tensor(
        (
            residual_grad
            + norm_back(attn_own_grad, own_rows(attn_unit), own_rows(attn_scale), attn_gain)
        ).astype(bf16)
    )

    small = jnp.concatenate(
        [grad_side, grad_ffn_gain[:, None], grad_attn_gain[:, None]], 1
    )
    small = scatter_dp(lax.psum(small, "tensor"))
    bias_sums = lax.psum_scatter(bias_grads, "dp", scatter_dimension=2, tiled=True)
    grad_attn = scatter_dp(jnp.concatenate([grad_qkv, grad_out_proj], 1).astype(bf16)).astype(f32)
    shared_grads = lax.all_to_all(
        grad_shared, "dp", split_axis=1, concat_axis=2, tiled=True
    ).astype(f32)
    return (
        hidden_out,
        hidden_in_grad,
        small[:, experts + 2],
        grad_attn[:, :local_width],
        grad_attn[:, local_width : 2 * local_width],
        grad_attn[:, 2 * local_width : 3 * local_width],
        bias_sums[0],
        bias_sums[1],
        bias_sums[2],
        grad_attn[:, 3 * local_width :],
        small[:, experts + 1],
        small[:, :experts],
        small[:, experts],
        shared_grads[0],
        shared_grads[1],
        shared_grads[2],
        grad_expert_gate[None],
        grad_expert_up[None],
        grad_expert_down[None],
    )


def finish_kernel(
    hidden_out_in,
    hidden_grad_in,
    query_in,
    key_in,
    value_in,
    out_in,
    shared_in,
    gate_in,
    up_in,
    down_in,
    small_in,
    hidden_out,
    hidden_grad,
    query_out,
    key_out,
    value_out,
    out_out,
    s_gate_out,
    s_up_out,
    s_down_out,
    gate_out,
    up_out,
    down_out,
    router_out,
    shared_gate_out,
    ffn_gain_out,
    attn_gain_out,
):
    f32 = jnp.float32
    experts = router_out.shape[0]
    hidden_out[...] = hidden_out_in[...]
    hidden_grad[...] = hidden_grad_in[...]
    for source, target in (
        (query_in, query_out),
        (key_in, key_out),
        (value_in, value_out),
        (out_in, out_out),
        (gate_in, gate_out),
        (up_in, up_out),
        (down_in, down_out),
    ):
        target[...] = source[...].astype(f32)

    for which, target in enumerate((s_gate_out, s_up_out, s_down_out)):
        units = shared_in[:, which]
        target[...] = units.reshape(-1, units.shape[-1]).T.astype(f32)

    router_out[...] = small_in[0:experts]
    shared_gate_out[...] = small_in[experts : experts + 1]
    ffn_gain_out[...] = small_in[experts + 1 : experts + 2]
    attn_gain_out[...] = small_in[experts + 2 : experts + 3]


def finish_layer(hidden_out, hidden_grad, grads, shared, expert_grads, small, experts):
    steps = 2
    tok_rows, width = hidden_out.shape
    local_width = grads[0].shape[1]
    units = shared.shape[2]
    expert_units = expert_grads[0].shape[0]
    f32, bf16 = jnp.float32, jnp.bfloat16
    shape = jax.ShapeDtypeStruct
    row = lambda wide: pl.BlockSpec((tok_rows // steps, wide), lambda i: (i, 0))
    column = pl.BlockSpec((expert_units, width // steps), lambda i: (0, i))
    whole = lambda *dims: pl.BlockSpec(dims, lambda i: (0,) * len(dims))
    return pl.pallas_call(
        finish_kernel,
        grid=(steps,),
        in_specs=[row(width)] * 2
        + [row(local_width)] * 4
        + [pl.BlockSpec((8, 3, units, tok_rows // steps), lambda i: (0, 0, 0, i))]
        + [column] * 3
        + [whole(16, tok_rows)],
        out_specs=[row(width)] * 2
        + [row(local_width)] * 4
        + [pl.BlockSpec((tok_rows // steps, 8 * units), lambda i: (i, 0))] * 3
        + [column] * 3
        + [whole(experts, tok_rows)]
        + [whole(1, tok_rows)] * 3,
        out_shape=[shape((tok_rows, width), bf16)] * 2
        + [shape((tok_rows, local_width), f32)] * 4
        + [shape((tok_rows, 8 * units), f32)] * 3
        + [shape((expert_units, width), f32)] * 3
        + [shape((experts, tok_rows), f32)]
        + [shape((1, tok_rows), f32)] * 3,
        compiler_params=pltpu.CompilerParams(vmem_limit_bytes=63 * 2**20),
        cost_estimate=pl.CostEstimate(flops=0, bytes_accessed=26 * 2**20, transcendentals=0),
    )(hidden_out, hidden_grad, *grads, shared, *expert_grads, small)


def on_cube(
    hidden_in,
    out_grad,
    parents,
    routes,
    attn_gain,
    w_query,
    w_key,
    w_value,
    b_query,
    b_key,
    b_value,
    w_out,
    ffn_gain,
    w_router,
    shared_gate,
    shared_w_gate,
    shared_w_up,
    shared_w_down,
    expert_w_gate,
    expert_w_up,
    expert_w_down,
):
    tok_rows, model_width = hidden_in.shape
    devices, columns = lax.axis_size("dp"), lax.axis_size("tensor")
    place = lax.axis_index("dp")
    experts, top_count = w_router.shape[1], routes.shape[1]
    capacity = 5 * tok_rows * top_count // 4
    score_scale = HEAD_DIM ** (-0.5)
    bf16, f32 = jnp.bfloat16, jnp.float32
    expert_units = expert_w_gate.shape[2]
    shared_units = shared_w_gate.shape[1] // devices
    shared_pad = -(-shared_units // 128) * 128
    units = shared_pad + expert_units
    units_pad = -(-(units + experts + 1) // 128) * 128
    layout = (shared_units, shared_pad, expert_units, experts, units_pad)
    part_rows = tok_rows // columns

    powers = np.arange(0, HEAD_DIM, 2, dtype=np.float32) / np.float32(HEAD_DIM)
    freqs = np.float32(rope_base) ** -powers
    (
        residual,
        query_rot,
        key_path,
        value_path,
        log_total,
        attended,
        attn_normed,
        cosine,
        sine,
        hits_all,
        grad_all,
        shared_w,
    ) = front_layer(
        score_scale,
        shared_units,
        (
            parents,
            hidden_in,
            attn_gain[None, :],
            b_query,
            b_key,
            b_value,
            np.concatenate([freqs, freqs])[None, :],
            routes.T,
            out_grad.reshape(columns, part_rows, model_width),
            w_query,
            w_key,
            w_value,
            w_out,
            shared_w_gate,
            shared_w_up,
            shared_w_down,
        ),
    )
    (
        residual_grad,
        residual_low,
        ffn_part,
        grad_expert_gate,
        grad_expert_up,
        grad_expert_down,
        grad_shared,
        small,
    ) = ffn_layer(
        residual,
        ffn_gain[None, :],
        hits_all,
        grad_all.reshape(2, 2, 2, columns, part_rows, model_width),
        w_router.T,
        shared_gate[None, :],
        shared_w,
        (expert_w_gate[0].T, expert_w_up[0].T, expert_w_down[0].T),
        layout,
        capacity,
    )
    (
        hidden_out,
        hidden_in_grad,
        sum_query,
        sum_key,
        sum_value,
        sum_out,
        grad_shared,
        small,
        bias_sums,
    ) = back_layer(
        score_scale,
        experts + 2,
        (
            residual,
            residual_grad,
            residual_low,
            ffn_part,
            grad_shared,
            small,
            query_rot,
            key_path,
            value_path,
            parents,
            log_total,
            attended,
            attn_normed,
            hidden_in,
            attn_gain[None, :],
            cosine,
            sine,
            w_out,
            w_query,
            w_key,
            w_value,
        ),
    )
    bias_sums = lax.dynamic_slice_in_dim(
        bias_sums[: 3 * b_query.shape[0]].reshape(3, *b_query.shape),
        place * (HEAD_DIM // devices),
        HEAD_DIM // devices,
        2,
    )
    (
        hidden_out,
        hidden_in_grad,
        sum_query,
        sum_key,
        sum_value,
        sum_out,
        sum_s_gate,
        sum_s_up,
        sum_s_down,
        grad_expert_gate,
        grad_expert_up,
        grad_expert_down,
        sum_router,
        sum_shared_gate,
        sum_ffn_gain,
        sum_attn_gain,
    ) = finish_layer(
        hidden_out.reshape(tok_rows, model_width),
        hidden_in_grad.reshape(tok_rows, model_width),
        (sum_query, sum_key, sum_value, sum_out),
        grad_shared,
        (grad_expert_gate, grad_expert_up, grad_expert_down),
        small,
        experts,
    )
    return (
        hidden_out,
        hidden_in_grad,
        sum_attn_gain[0],
        sum_query,
        sum_key,
        sum_value,
        bias_sums[0],
        bias_sums[1],
        bias_sums[2],
        sum_out,
        sum_ffn_gain[0],
        sum_router.T,
        sum_shared_gate[0],
        sum_s_gate,
        sum_s_up,
        sum_s_down,
        grad_expert_gate.T[None],
        grad_expert_up.T[None],
        grad_expert_down.T[None],
    )


def on_device(*arrays):
    devices, columns = lax.axis_size("dp"), lax.axis_size("tensor")
    tok_rows, model_width = arrays[0].shape
    cube = devices == 8 and columns == 4 and tok_rows == SEG
    if cube and tok_rows * devices * model_width <= 2**22:
        return on_cube(*arrays)
    return on_slice(*arrays)


def solution(mesh):
    return jax.shard_map(
        on_device,
        mesh=mesh,
        in_specs=(
            P("dp", None),
            P("dp", None),
            P(),
            P("dp", None),
            P(),
            P(None, "tensor"),
            P(None, "tensor"),
            P(None, "tensor"),
            P("tensor", None),
            P("tensor", None),
            P("tensor", None),
            P(None, "tensor"),
            P(),
            P(),
            P(),
            P(None, "tensor"),
            P(None, "tensor"),
            P(None, "tensor"),
            P("dp", None, "tensor"),
            P("dp", None, "tensor"),
            P("dp", None, "tensor"),
        ),
        out_specs=(
            P("dp", None),
            P("dp", None),
            P("dp"),
            P("dp", "tensor"),
            P("dp", "tensor"),
            P("dp", "tensor"),
            P("tensor", "dp"),
            P("tensor", "dp"),
            P("tensor", "dp"),
            P("dp", "tensor"),
            P("dp"),
            P("dp", None),
            P("dp"),
            P("dp", "tensor"),
            P("dp", "tensor"),
            P("dp", "tensor"),
            P("dp", None, "tensor"),
            P("dp", None, "tensor"),
            P("dp", None, "tensor"),
        ),
        check_vma=False,
    )
```
